32 devices in a mesh: groups: 2 (over x), win: 4 (over y, core), rcv: 4 (over z).
Axes of the slice: x: 2, y: 2, z: 4, core: 2. Of those that a mesh axis runs over, the one named last changes fastest.
Arguments:
- traces: bfloat16 [32, 768, 4096], P('win', ('groups', 'rcv')), parts along dimension 1, may hold values from -6 to 6
- valid: int32 [64], P(('groups', 'win')), parts along dimension 0, may hold values 0 or 1
- src_station: int32 [64], P('groups'), parts along dimension 0, may hold values from 0 to 383, as said below
Outputs:
- stacks: float32 [32, 768, 2, 512], P(None, ('groups', 'rcv'), None, 'win'), parts along dimension 1
The draws below stay inside these ranges and needn't reach their ends.
There are 2 independent parts, one for each index of `groups`. The reference program is written for one: setup_inputs(seed, part) draws one part's arguments, and reference() takes and returns one part's arrays. A program takes and returns all parts, laid end to end along the dimension named above; each array names one. Nothing has to cross between parts.
Inputs may be any that keep to these rules, and one draw needn't show every extreme that they name: `src_station`: distinct stations; station 0 and station 384 - 1 are always among them.
All inputs are finite; a program needn't handle non-finite values. No bound on the sum of `valid` on one device may be relied on, other than what follows from the above.
Results may differ from the reference program's by a relative error of at most 0.0049.
Values may be sent and summed in bfloat16 or wider, within the bound.
No kernel may reach another device: no remote copies, remote signals or barrier semaphores. Data moves between devices by JAX's collectives and lax.ppermute only.
A program may use at most 128 MiB of HBM per device.

```python
import math
import jax
import jax.numpy as jnp
from jax import lax

NT = 4096
F = 512
K0 = 256
SOURCES = 32
WINDOWS = 32
RECEIVERS = 384


def draw_src_station(key, part):
    inner = jax.random.permutation(key, RECEIVERS - 2)[:SOURCES - 2].astype(jnp.int32) + 1
    ends = jnp.array([0, RECEIVERS - 1], dtype=jnp.int32)
    picked = jnp.concatenate([ends, inner])
    return jax.random.permutation(jax.random.fold_in(key, 7), picked).astype(jnp.int32)


def place_ends(entries, rng, smallest, top_value):
    place = [jax.random.randint(jax.random.fold_in(rng, axis), (), 0, length) for axis, length in enumerate(entries.shape)]
    longest = entries.shape.index(max(entries.shape))
    beside = place[:longest] + [(place[longest] + 1) % entries.shape[longest]] + place[longest + 1:]
    return entries.at[tuple(place)].set(smallest).at[tuple(beside)].set(top_value)


def block_levels(key, dims, pieces, least, largest):
    def one(dim, shards_of):
        draws = jax.random.uniform(jax.random.fold_in(jax.random.fold_in(key, 6), dim), (shards_of,), jnp.float32, least / len(pieces), largest / len(pieces))
        return jnp.repeat(jnp.exp(draws), dims[dim] // shards_of).reshape((-1,) + (1,) * (len(dims) - dim - 1))

    factor_of = one(*pieces[0])
    for cut in pieces[1:]:
        factor_of = factor_of * one(*cut)
    return factor_of


def scatter_about(rng, dims, scale, bound, shards=(), kind=jnp.bfloat16):
    level = block_levels(rng, dims, shards, -0.22, 0.18) if shards else 1.0
    entries = jax.random.normal(rng, dims, jnp.float32) * scale * level
    return jnp.minimum(jnp.maximum(entries, -bound), bound).astype(kind)


def setup_inputs(seed: int = 0, part: int = 0) -> dict:
    key_of = jax.random.split(jax.random.key(seed), 4)
    own_keys = jax.random.split(jax.random.fold_in(key_of[3], part), 4)
    traces = scatter_about(own_keys[0], (WINDOWS, RECEIVERS, NT), 1.0, 6.0, ((0, 4), (1, 4)))
    valid = place_ends((jax.random.randint(own_keys[1], (WINDOWS,), 0, 4) < 3).astype(jnp.int32), jax.random.fold_in(own_keys[1], 1), 0, 1)
    src_station = draw_src_station(jax.random.fold_in(jax.random.fold_in(key_of[3], part), 71), part)
    return dict(traces=traces, valid=valid, src_station=src_station)


def band_table(count, bins, first):
    samples = jnp.arange(count, dtype=jnp.int32)
    freqs = first + jnp.arange(bins, dtype=jnp.int32)
    phase = samples[:, None] * freqs[None, :] % count
    angle = phase.astype(jnp.float32) * (2.0 * math.pi / count)
    return jnp.concatenate([jnp.cos(angle), -jnp.sin(angle)], axis=1).astype(jnp.bfloat16)

def reference(traces, valid, src_station):
    table = band_table(NT, F, K0)

    def whiten(window):
        spectra = jnp.dot(window, table, preferred_element_type=jnp.float32)
        spectra = spectra.reshape(window.shape[0], 2, F)
        power = lax.optimization_barrier(jnp.sum(spectra * spectra, axis=(1, 2), keepdims=True)) / F
        return (spectra * lax.rsqrt(power + 1e-06)).astype(jnp.bfloat16)
    white = lax.map(whiten, traces)
    received = white * valid.astype(jnp.bfloat16)[:, None, None, None]
    sources = white[:, src_station]
    rr = received[:, :, 0].astype(jnp.float32)
    ri = received[:, :, 1].astype(jnp.float32)
    sr = sources[:, :, 0].astype(jnp.float32)
    si = sources[:, :, 1].astype(jnp.float32)
    real = jnp.einsum('wsf,wrf->srf', sr, rr) + jnp.einsum('wsf,wrf->srf', si, ri)
    imag = jnp.einsum('wsf,wrf->srf', sr, ri) - jnp.einsum('wsf,wrf->srf', si, rr)
    return jnp.stack([real, imag], axis=2) * (1.0 / math.sqrt(WINDOWS))
```

```python
import math

import jax
import jax.numpy as jnp
import numpy as np
from jax import lax
from jax.sharding import PartitionSpec as P

F = 512


def band_table(count, bins, first):
    samples = np.arange(count, dtype=np.int64)
    freqs = first + np.arange(bins, dtype=np.int64)
    phase = samples[:, None] * freqs[None, :] % count
    angle = phase.astype(np.float64) * (2.0 * math.pi / count)
    return np.concatenate([np.cos(angle), -np.sin(angle)], axis=1).astype(jnp.bfloat16)


def correlate(received, sources):
    rr = received[:, :, 0]
    ri = received[:, :, 1]
    sr = sources[:, :, 0]
    si = sources[:, :, 1]
    real = jnp.einsum("wsf,wrf->srf", sr, rr, preferred_element_type=jnp.float32)
    real = real + jnp.einsum("wsf,wrf->srf", si, ri, preferred_element_type=jnp.float32)
    imag = jnp.einsum("wsf,wrf->srf", sr, ri, preferred_element_type=jnp.float32)
    imag = imag - jnp.einsum("wsf,wrf->srf", si, rr, preferred_element_type=jnp.float32)
    return jnp.stack([real, imag], axis=2)


def body(traces, valid, src_station):
    w_dev, r_dev, samples = traces.shape
    bins = F
    n_win = lax.axis_size("win")
    n_rcv = lax.axis_size("rcv")
    bins_dev = bins // n_win
    table = jnp.asarray(band_table(samples, bins, samples // 16))
    spectra = jnp.dot(
        traces.reshape(w_dev * r_dev, samples), table, preferred_element_type=jnp.float32
    )
    spectra = spectra.reshape(w_dev, r_dev, 2, bins)
    power = jnp.sum(spectra * spectra, axis=(2, 3), keepdims=True) / bins
    gain = lax.rsqrt(power + 1e-06)
    keep = valid.astype(jnp.float32)[:, None, None, None]
    white = ((spectra * gain) * keep).astype(jnp.bfloat16)
    blocks = white.reshape(w_dev, r_dev, 2, n_win, bins_dev).transpose(3, 0, 1, 2, 4)

    me = lax.axis_index("win")
    parts = []
    for j in range(n_win):
        block = lax.dynamic_index_in_dim(blocks, me ^ j, 0, keepdims=False)
        if j:
            block = lax.ppermute(block, "win", [(i, i ^ j) for i in range(n_win)])
        parts.append(block)

    offset = lax.axis_index("rcv") * r_dev
    station_ids = offset + jnp.arange(r_dev, dtype=jnp.int32)
    selector = (src_station[:, None] == station_ids[None, :]).astype(jnp.bfloat16)
    sources = []
    for part in parts:
        rows = jnp.einsum("sr,wrcf->wscf", selector, part, preferred_element_type=jnp.float32)
        rows = rows.astype(jnp.bfloat16)
        rows = lax.all_to_all(rows, "rcv", 0, 0, tiled=True)
        rows = rows.reshape((n_rcv, w_dev // n_rcv) + rows.shape[1:])
        merged = jnp.sum(rows.astype(jnp.float32), axis=0).astype(jnp.bfloat16)
        sources.append(lax.all_gather(merged, "rcv", axis=0, tiled=True))
    scale = 1.0 / math.sqrt(w_dev * n_win)
    stacks = correlate(jnp.concatenate(parts, axis=0), jnp.concatenate(sources, axis=0))
    return stacks * scale


def solution(mesh):
    return jax.shard_map(
        body,
        mesh=mesh,
        in_specs=(P("win", ("groups", "rcv"), None), P(("groups", "win")), P("groups")),
        out_specs=P(None, ("groups", "rcv"), None, "win"),
        check_vma=False,
    )
```

```python
import functools
import math

import jax
import jax.numpy as jnp
import numpy as np
from jax import lax
from jax.experimental import pallas as pl
from jax.experimental.pallas import tpu as pltpu
from jax.sharding import PartitionSpec as P

F = 512
SMEM = pltpu.MemorySpace.SMEM
VMEM = pltpu.MemorySpace.VMEM


def angles(samples, freqs, count):
    phase = samples[:, None] * freqs[None, :] % count
    return phase.astype(np.float64) * (2.0 * math.pi / count)


def band_table(count, bins, first):
    angle = angles(np.arange(count), first + np.arange(bins), count)
    return np.concatenate([np.cos(angle), -np.sin(angle)], axis=1).astype(jnp.bfloat16)


def quarter_tables(count, bins, first, n_win):
    j = np.arange(bins // 4)

    def columns(re, im):
        both = np.stack([re, im], axis=1).reshape(re.shape[0], 2, n_win, -1)
        return both.transpose(0, 2, 1, 3).reshape(re.shape[0], -1)

    tables = []
    for m in range(4):
        angle = angles(np.arange(count // 4), first + 4 * j + m, count)
        cos, sin = np.cos(angle), np.sin(angle)
        rows = [columns(cos, -sin)]
        if m == 1:
            rows.append(columns(-sin, -cos))
        if m == 3:
            rows.append(columns(sin, cos))
        tables.append(np.concatenate(rows, axis=0))
    return [np.concatenate(tables[:1] + tables[2:3], axis=0).astype(jnp.bfloat16),
            np.concatenate(tables[1:2] + tables[3:], axis=0).astype(jnp.bfloat16)]


def spectra_kernel(n_win, n_rcv, r_dev, n_src, valid_ref, src_ref, x_ref, even_ref, odd_ref, *refs):
    r_refs = refs[:n_win]
    q_refs = refs[n_win:n_win + n_rcv]
    y_ref, white_ref, sel_ref = refs[n_win + n_rcv:]
    step = pl.program_id(0)
    rows, samples = x_ref.shape
    per_step = rows // r_dev
    quarter = samples // 4
    win = lax.axis_index("win")
    rcv = lax.axis_index("rcv")

    @pl.when(step == 0)
    def _():
        shape = (per_step * n_src, rows)
        out_row = lax.broadcasted_iota(jnp.int32, shape, 0)
        column = lax.broadcasted_iota(jnp.int32, shape, 1)
        wanted = jnp.zeros(shape, jnp.int32)
        for s in range(n_src):
            wanted = jnp.where(out_row % n_src == s, src_ref[s] - rcv * r_dev, wanted)
        inside = (wanted >= 0) & (wanted < r_dev)
        hit = inside & (column == wanted + (out_row // n_src) * r_dev)
        sel_ref[...] = hit.astype(jnp.float32).astype(jnp.bfloat16)

    x0, x1, x2, x3 = (
        x_ref[:, q * quarter:(q + 1) * quarter].astype(jnp.float32) for q in range(4)
    )
    y_ref[:, :quarter] = ((x0 + x2) + (x1 + x3)).astype(jnp.bfloat16)
    y_ref[:, quarter:2 * quarter] = ((x0 + x2) - (x1 + x3)).astype(jnp.bfloat16)
    y_ref[:, 2 * quarter:3 * quarter] = (x0 - x2).astype(jnp.bfloat16)
    y_ref[:, 3 * quarter:] = (x1 - x3).astype(jnp.bfloat16)

    def product(lhs, table):
        return jnp.dot(lhs, table, preferred_element_type=jnp.float32)

    spectra = [
        product(y_ref[:, :quarter], even_ref[:quarter]),
        product(y_ref[:, 2 * quarter:], odd_ref[:2 * quarter]),
        product(y_ref[:, quarter:2 * quarter], even_ref[quarter:]),
        product(y_ref[:, 2 * quarter:], odd_ref[2 * quarter:]),
    ]
    squares = sum(jnp.sum(s * s, axis=1, keepdims=True) for s in spectra)
    gain = lax.rsqrt(squares / F + 1e-06)
    row = lax.broadcasted_iota(jnp.int32, (rows, 1), 0)
    keep = jnp.zeros((rows, 1), jnp.float32)
    for t in range(per_step):
        own = (row >= t * r_dev) & (row < (t + 1) * r_dev)
        keep = jnp.where(own, valid_ref[step * per_step + t].astype(jnp.float32), keep)
    gain = gain * keep
    white = [s * gain for s in spectra]
    piece = white[0].shape[1] // n_win
    for d in range(n_win):
        columns = slice(d * piece, (d + 1) * piece)
        block = jnp.concatenate([part[:, columns] for part in white], axis=1)
        white_ref[d] = block.astype(jnp.bfloat16)
    for j in range(n_win):
        r_refs[j][...] = white_ref[win ^ j]
    for i in range(n_rcv):
        @pl.when((step ^ rcv) == i)
        def _(q_ref=q_refs[i]):
            for j in range(n_win):
                q_ref[j] = product(sel_ref[...], white_ref[win ^ j]).astype(jnp.bfloat16)


def spectra_call(traces, valid, src_station, n_win, n_rcv):
    w_dev, r_dev, samples = traces.shape
    n_src = src_station.shape[0]
    per_step = w_dev // n_rcv
    rows = per_step * r_dev
    lanes = 2 * F // n_win
    even, odd = (jnp.asarray(t) for t in quarter_tables(samples, F, samples // 16, n_win))
    block = jax.ShapeDtypeStruct((w_dev * r_dev, lanes), jnp.bfloat16)
    picked = jax.ShapeDtypeStruct((n_win, per_step * n_src, lanes), jnp.bfloat16)
    flops = 2 * w_dev * r_dev * (samples // 4) * 6 * (F // 2)
    return pl.pallas_call(
        functools.partial(spectra_kernel, n_win, n_rcv, r_dev, n_src),
        grid=(n_rcv,),
        in_specs=[
            pl.BlockSpec(memory_space=SMEM),
            pl.BlockSpec(memory_space=SMEM),
            pl.BlockSpec((rows, samples), lambda g: (g, 0)),
            pl.BlockSpec(even.shape, lambda g: (0, 0)),
            pl.BlockSpec(odd.shape, lambda g: (0, 0)),
        ],
        out_specs=[pl.BlockSpec((rows, lanes), lambda g: (g, 0))] * n_win
        + [pl.BlockSpec(picked.shape, lambda g: (0, 0, 0))] * n_rcv,
        out_shape=[block] * n_win + [picked] * n_rcv,
        scratch_shapes=[
            pltpu.VMEM((rows, samples), jnp.bfloat16),
            pltpu.VMEM((n_win, rows, lanes), jnp.bfloat16),
            pltpu.VMEM((per_step * n_src, rows), jnp.bfloat16),
        ],
        compiler_params=pltpu.CompilerParams(vmem_limit_bytes=48 * 2**20),
        cost_estimate=pl.CostEstimate(
            flops=flops, bytes_accessed=w_dev * r_dev * samples * 2, transcendentals=0
        ),
        name="spectra",
    )(valid, src_station, traces.reshape(w_dev * r_dev, samples), even, odd)


def stacks_kernel(n_win, n_rcv, w_dev, r_dev, n_src, bins, *refs):
    r_refs = refs[:n_win]
    s_refs = refs[n_win:n_win + n_rcv]
    out_ref, rows_ref, srow_ref, left_ref, prod_ref = refs[n_win + n_rcv:]
    lanes = 2 * bins
    windows = n_win * w_dev
    per = w_dev // n_rcv
    pad = 128
    step = pl.program_id(0)
    rcv = lax.axis_index("rcv")
    nt = (((1,), (1,)), ((), ()))

    def product(lhs, rhs, dims=(((1,), (0,)), ((), ()))):
        return lax.dot_general(lhs, rhs, dims, preferred_element_type=jnp.float32)

    @pl.when(step == 0)
    def _():
        lane = lax.broadcasted_iota(jnp.int32, (lanes, lanes), 1)
        row = lax.broadcasted_iota(jnp.int32, (lanes, lanes), 0)
        quarter = bins // 4
        part = (lane // quarter) % 2
        bin_of = 4 * (lane % quarter) + lane // (2 * quarter)
        order = (row == part * bins + bin_of).astype(jnp.float32).astype(jnp.bfloat16)
        both = order[:bins] + order[bins:]

        for j in range(n_win):
            for w in range(w_dev):
                block = r_refs[j][w * r_dev:(w + 1) * r_dev]
                turned = product(order, block, nt)
                rows_ref[pl.ds(j * w_dev + w, lanes, stride=windows), :r_dev] = turned

        for i in range(n_rcv):
            for j in range(n_win):
                start = pl.multiple_of((j * w_dev + per * (i ^ rcv)) * n_src, per * n_src)
                block = s_refs[i][j].astype(jnp.float32)
                for h in range(lanes // pad):
                    half = block[:, h * pad:(h + 1) * pad]
                    srow_ref[h, pl.ds(start, per * n_src), :] = half
        lane = lax.broadcasted_iota(jnp.int32, (windows, lanes), 1)
        real = (lane // quarter) % 2 == 0
        for s in range(n_src):
            values = jnp.concatenate(
                [srow_ref[h, pl.ds(s, windows, stride=n_src), :] for h in range(lanes // pad)],
                axis=1,
            )
            stacked = jnp.concatenate(
                [jnp.where(real, values, 0.0), jnp.where(real, 0.0, values)], axis=0
            )
            turned = product(both, stacked.astype(jnp.bfloat16), nt)
            left_ref[pl.ds(s, bins, stride=n_src), :2 * windows] = turned

        for f in range(bins):
            rr = rows_ref[pl.ds(f * windows, windows), :]
            ri = rows_ref[pl.ds((bins + f) * windows, windows), :]
            right = jnp.concatenate(
                [jnp.concatenate([rr, ri], axis=0), jnp.concatenate([ri, -rr], axis=0)], axis=1
            ).astype(jnp.bfloat16)
            left = left_ref[pl.ds(f * n_src, n_src), :2 * windows].astype(jnp.bfloat16)
            result = product(left, right)
            for c in range(2):
                prod_ref[c, pl.ds(f, n_src, stride=bins), :] = result[:, c * pad:(c + 1) * pad]

    scale = 1.0 / math.sqrt(windows)
    s_step = out_ref.shape[0]
    for k in range(s_step):
        start = pl.multiple_of((step * s_step + k) * bins, bins)
        for c in range(2):
            turned = prod_ref[c, pl.ds(start, bins), :].T
            out_ref[k, pl.ds(c, r_dev, stride=2), :] = turned[:r_dev] * scale


def stacks_call(received, sources, w_dev, r_dev, n_src, bins):
    n_win, n_rcv = len(received), len(sources)
    windows = n_win * w_dev
    steps = 4
    whole = pl.BlockSpec(memory_space=VMEM)
    out = pl.pallas_call(
        functools.partial(stacks_kernel, n_win, n_rcv, w_dev, r_dev, n_src, bins),
        grid=(steps,),
        in_specs=[whole] * (n_win + n_rcv),
        out_specs=pl.BlockSpec((n_src // steps, 2 * r_dev, bins), lambda g: (g, 0, 0)),
        out_shape=jax.ShapeDtypeStruct((n_src, 2 * r_dev, bins), jnp.float32),
        scratch_shapes=[
            pltpu.VMEM((2 * bins * windows, 128), jnp.float32),
            pltpu.VMEM((2 * bins // 128, windows * n_src, 128), jnp.float32),
            pltpu.VMEM((bins * n_src, 128), jnp.float32),
            pltpu.VMEM((2, n_src * bins, 128), jnp.float32),
        ],
        compiler_params=pltpu.CompilerParams(vmem_limit_bytes=48 * 2**20),
        cost_estimate=pl.CostEstimate(
            flops=8 * windows * n_src * r_dev * bins, bytes_accessed=6 * 2**20, transcendentals=0
        ),
        name="stacks",
    )(*received, *sources)
    return out.reshape(n_src, r_dev, 2, bins)


def swap(value, axis, by):
    size = lax.axis_size(axis)
    return lax.ppermute(value, axis, [(i, i ^ by) for i in range(size)])


def body(traces, valid, src_station):
    w_dev, r_dev, samples = traces.shape
    n_src = src_station.shape[0]
    n_win = lax.axis_size("win")
    n_rcv = lax.axis_size("rcv")
    bins = F // n_win

    out = spectra_call(traces, valid, src_station, n_win, n_rcv)
    received, picked = out[:n_win], out[n_win:]

    picked = [picked[0]] + [swap(picked[i], "rcv", i) for i in range(1, n_rcv)]
    received = [received[0]] + [swap(received[j], "win", j) for j in range(1, n_win)]
    merged = sum(picked[1:], picked[0])
    blocks = [merged[0]] + [swap(merged[j], "win", j) for j in range(1, n_win)]
    blocks = jnp.stack(blocks, axis=0)
    sources = [blocks] + [swap(blocks, "rcv", i) for i in range(1, n_rcv)]
    return stacks_call(received, sources, w_dev, r_dev, n_src, bins)


def correlate(received, sources):
    rr = received[:, :, 0]
    ri = received[:, :, 1]
    sr = sources[:, :, 0]
    si = sources[:, :, 1]
    real = jnp.einsum("wsf,wrf->srf", sr, rr, preferred_element_type=jnp.float32)
    real = real + jnp.einsum("wsf,wrf->srf", si, ri, preferred_element_type=jnp.float32)
    imag = jnp.einsum("wsf,wrf->srf", sr, ri, preferred_element_type=jnp.float32)
    imag = imag - jnp.einsum("wsf,wrf->srf", si, rr, preferred_element_type=jnp.float32)
    return jnp.stack([real, imag], axis=2)


def body_any(traces, valid, src_station):
    w_dev, r_dev, samples = traces.shape
    n_win = lax.axis_size("win")
    n_rcv = lax.axis_size("rcv")
    bins = F // n_win
    table = jnp.asarray(band_table(samples, F, samples // 16))
    spectra = jnp.dot(
        traces.reshape(w_dev * r_dev, samples), table, preferred_element_type=jnp.float32
    )
    spectra = spectra.reshape(w_dev, r_dev, 2, F)
    power = jnp.sum(spectra * spectra, axis=(2, 3), keepdims=True) / F
    keep = valid.astype(jnp.float32)[:, None, None, None]
    white = (spectra * lax.rsqrt(power + 1e-06) * keep).astype(jnp.bfloat16)
    blocks = white.reshape(w_dev, r_dev, 2, n_win, bins).transpose(3, 0, 1, 2, 4)
    me = lax.axis_index("win")
    offset = lax.axis_index("rcv") * r_dev
    station_ids = offset + jnp.arange(r_dev, dtype=jnp.int32)
    selector = (src_station[:, None] == station_ids[None, :]).astype(jnp.bfloat16)
    received = []
    for j in range(n_win):
        block = lax.dynamic_index_in_dim(blocks, me ^ j, 0, keepdims=False)
        received.append(swap(block, "win", j) if j else block)
    received = jnp.concatenate(received, axis=0)
    rows = jnp.einsum("sr,wrcf->wscf", selector, received, preferred_element_type=jnp.float32)
    rows = lax.all_to_all(rows.astype(jnp.bfloat16), "rcv", 0, 0, tiled=True)
    rows = rows.reshape((n_rcv, -1) + rows.shape[1:])
    merged = jnp.sum(rows.astype(jnp.float32), axis=0).astype(jnp.bfloat16)
    sources = lax.all_gather(merged, "rcv", axis=0, tiled=True)
    return correlate(received, sources) * (1.0 / math.sqrt(w_dev * n_win))


def solution(mesh):
    sizes = (mesh.shape["win"], mesh.shape["rcv"])
    return jax.shard_map(
        body if sizes == (4, 4) else body_any,
        mesh=mesh,
        in_specs=(P("win", ("groups", "rcv"), None), P(("groups", "win")), P("groups")),
        out_specs=P(None, ("groups", "rcv"), None, "win"),
        check_vma=False,
    )
```

```python
import functools
import math

import jax
import jax.numpy as jnp
import numpy as np
from jax import lax
from jax.experimental import pallas as pl
from jax.experimental.pallas import tpu as pltpu
from jax.sharding import PartitionSpec as P

F = 512
SMEM = pltpu.MemorySpace.SMEM
VMEM = pltpu.MemorySpace.VMEM


def angles(samples, freqs, count):
    phase = samples[:, None] * freqs[None, :] % count
    return phase.astype(np.float64) * (2.0 * math.pi / count)


def band_table(count, bins, first):
    angle = angles(np.arange(count), first + np.arange(bins), count)
    return np.concatenate([np.cos(angle), -np.sin(angle)], axis=1).astype(jnp.bfloat16)


def quarter_tables(count, bins, first, n_win):
    j = np.arange(bins // 4)

    def columns(re, im):
        both = np.stack([re, im], axis=1).reshape(re.shape[0], 2, n_win, -1)
        return both.transpose(0, 2, 1, 3).reshape(re.shape[0], -1)

    tables = []
    for m in range(4):
        angle = angles(np.arange(count // 4), first + 4 * j + m, count)
        cos, sin = np.cos(angle), np.sin(angle)
        rows = [columns(cos, -sin)]
        if m == 1:
            rows.append(columns(-sin, -cos))
        if m == 3:
            rows.append(columns(sin, cos))
        tables.append(np.concatenate(rows, axis=0))
    return [np.concatenate(tables[:1] + tables[2:3], axis=0).astype(jnp.bfloat16),
            np.concatenate(tables[1:2] + tables[3:], axis=0).astype(jnp.bfloat16)]


def in_hbm(value):
    return pltpu.with_memory_space_constraint(value, pltpu.HBM)


def spectra_kernel(n_win, n_rcv, w_dev, r_dev, n_src, valid_hbm, src_hbm, x_ref, even_hbm, odd_hbm, *refs):
    r_refs = refs[:n_win]
    q_refs = refs[n_win:n_win + n_rcv]
    y_ref, white_ref, sel_ref, even_ref, odd_ref, valid_ref, src_ref, sems = refs[n_win + n_rcv:]
    step = pl.program_id(0)
    rows, samples = x_ref.shape
    w_step = rows // r_dev
    per = w_dev // n_rcv
    share = per * r_dev
    quarter = samples // 4
    win = lax.axis_index("win")
    rcv = lax.axis_index("rcv")
    pairs = ((valid_hbm, valid_ref), (src_hbm, src_ref), (even_hbm, even_ref), (odd_hbm, odd_ref))
    copies = [pltpu.make_async_copy(a, b, sems.at[k]) for k, (a, b) in enumerate(pairs)]

    @pl.when(step == 0)
    def _():
        for copy in copies:
            copy.start()

    x0, x1, x2, x3 = (
        x_ref[:, q * quarter:(q + 1) * quarter].astype(jnp.float32) for q in range(4)
    )
    y_ref[:, :quarter] = ((x0 + x2) + (x1 + x3)).astype(jnp.bfloat16)
    y_ref[:, quarter:2 * quarter] = ((x0 + x2) - (x1 + x3)).astype(jnp.bfloat16)
    y_ref[:, 2 * quarter:3 * quarter] = (x0 - x2).astype(jnp.bfloat16)
    y_ref[:, 3 * quarter:] = (x1 - x3).astype(jnp.bfloat16)

    @pl.when(step == 0)
    def _():
        for copy in copies:
            copy.wait()
        shape = (per * n_src, share)
        out_row = lax.broadcasted_iota(jnp.int32, shape, 0)
        column = lax.broadcasted_iota(jnp.int32, shape, 1)
        wanted = jnp.zeros(shape, jnp.int32)
        for s in range(n_src):
            wanted = jnp.where(out_row % n_src == s, src_ref[s] - rcv * r_dev, wanted)
        inside = (wanted >= 0) & (wanted < r_dev)
        hit = inside & (column == wanted + (out_row // n_src) * r_dev)
        sel_ref[...] = hit.astype(jnp.float32).astype(jnp.bfloat16)

    def product(lhs, table):
        return jnp.dot(lhs, table, preferred_element_type=jnp.float32)

    spectra = [
        product(y_ref[:, :quarter], even_ref[:quarter]),
        product(y_ref[:, 2 * quarter:], odd_ref[:2 * quarter]),
        product(y_ref[:, quarter:2 * quarter], even_ref[quarter:]),
        product(y_ref[:, 2 * quarter:], odd_ref[2 * quarter:]),
    ]
    squares = sum(jnp.sum(s * s, axis=1, keepdims=True) for s in spectra)
    gain = lax.rsqrt(squares / F + 1e-06)
    row = lax.broadcasted_iota(jnp.int32, (rows, 1), 0)
    keep = jnp.zeros((rows, 1), jnp.float32)
    for t in range(w_step):
        own = (row >= t * r_dev) & (row < (t + 1) * r_dev)
        keep = jnp.where(own, valid_ref[step * w_step + t].astype(jnp.float32), keep)
    gain = gain * keep
    white = [s * gain for s in spectra]
    piece = white[0].shape[1] // n_win
    for d in range(n_win):
        columns = slice(d * piece, (d + 1) * piece)
        block = jnp.concatenate([part[:, columns] for part in white], axis=1)
        white_ref[d] = block.astype(jnp.bfloat16)
    for j in range(n_win):
        r_refs[j][...] = white_ref[win ^ j]
    for k in range(rows // share):
        for i in range(n_rcv):
            @pl.when(((step * (rows // share) + k) ^ rcv) == i)
            def _(q_ref=q_refs[i]):
                for j in range(n_win):
                    block = white_ref[win ^ j, k * share:(k + 1) * share]
                    q_ref[j] = product(sel_ref[...], block).astype(jnp.bfloat16)


def spectra_call(traces, valid, src_station, n_win, n_rcv):
    w_dev, r_dev, samples = traces.shape
    n_src = src_station.shape[0]
    per = w_dev // n_rcv
    steps = 2
    rows = w_dev * r_dev // steps
    lanes = 2 * F // n_win
    even, odd = (jnp.asarray(t) for t in quarter_tables(samples, F, samples // 16, n_win))
    block = jax.ShapeDtypeStruct((w_dev * r_dev, lanes), jnp.bfloat16)
    picked = jax.ShapeDtypeStruct((n_win, per * n_src, lanes), jnp.bfloat16)
    flops = 2 * w_dev * r_dev * (samples // 4) * 6 * (F // 2)
    hbm = pl.BlockSpec(memory_space=pltpu.HBM)
    return pl.pallas_call(
        functools.partial(spectra_kernel, n_win, n_rcv, w_dev, r_dev, n_src),
        grid=(steps,),
        in_specs=[hbm, hbm, pl.BlockSpec((rows, samples), lambda g: (g, 0)), hbm, hbm],
        out_specs=[pl.BlockSpec((rows, lanes), lambda g: (g, 0))] * n_win
        + [pl.BlockSpec(picked.shape, lambda g: (0, 0, 0))] * n_rcv,
        out_shape=[block] * n_win + [picked] * n_rcv,
        scratch_shapes=[
            pltpu.VMEM((rows, samples), jnp.bfloat16),
            pltpu.VMEM((n_win, rows, lanes), jnp.bfloat16),
            pltpu.VMEM((per * n_src, per * r_dev), jnp.bfloat16),
            pltpu.VMEM(even.shape, jnp.bfloat16),
            pltpu.VMEM(odd.shape, jnp.bfloat16),
            pltpu.SMEM(valid.shape, jnp.int32),
            pltpu.SMEM(src_station.shape, jnp.int32),
            pltpu.SemaphoreType.DMA((4,)),
        ],
        compiler_params=pltpu.CompilerParams(vmem_limit_bytes=48 * 2**20),
        cost_estimate=pl.CostEstimate(
            flops=flops, bytes_accessed=w_dev * r_dev * samples * 2, transcendentals=0
        ),
        name="spectra",
    )(*(in_hbm(x) for x in (valid, src_station, traces.reshape(w_dev * r_dev, samples), even, odd)))


def bin_order(lanes):
    quarter = lanes // 8
    lane = lax.broadcasted_iota(jnp.int32, (lanes, lanes), 1)
    row = lax.broadcasted_iota(jnp.int32, (lanes, lanes), 0)
    part = (lane // quarter) % 2
    bin_of = 4 * (lane % quarter) + lane // (2 * quarter)
    hit = row == part * (lanes // 2) + bin_of
    return hit.astype(jnp.float32).astype(jnp.bfloat16)


def turn_kernel(w_dev, r_dev, x_ref, out_ref, rows_ref):
    lanes = x_ref.shape[1]
    bins = lanes // 2
    pad = out_ref.shape[2] // 2
    order = bin_order(lanes)
    for w in range(w_dev):
        turned = lax.dot_general(
            order, x_ref[w * r_dev:(w + 1) * r_dev], (((1,), (1,)), ((), ())),
            preferred_element_type=jnp.float32,
        )
        rows_ref[pl.ds(w, lanes, stride=w_dev), :r_dev] = turned
    rr = rows_ref[:bins * w_dev].reshape(bins, w_dev, pad)
    ri = rows_ref[bins * w_dev:].reshape(bins, w_dev, pad)
    out_ref[:, :, :pad] = jnp.concatenate([rr, ri], axis=1).astype(jnp.bfloat16)
    out_ref[:, :, pad:] = jnp.concatenate([ri, -rr], axis=1).astype(jnp.bfloat16)


def turn_call(block, w_dev, r_dev):
    lanes = block.shape[1]
    pad = 128
    return pl.pallas_call(
        functools.partial(turn_kernel, w_dev, r_dev),
        in_specs=[pl.BlockSpec(memory_space=VMEM)],
        out_specs=pl.BlockSpec(memory_space=VMEM),
        out_shape=jax.ShapeDtypeStruct((lanes // 2, 2 * w_dev, 2 * pad), jnp.bfloat16),
        scratch_shapes=[pltpu.VMEM((lanes * w_dev, pad), jnp.float32)],
        compiler_params=pltpu.CompilerParams(vmem_limit_bytes=16 * 2**20),
        cost_estimate=pl.CostEstimate(
            flops=2 * w_dev * lanes * lanes * pad, bytes_accessed=2 * 2**20, transcendentals=0
        ),
        name="turn",
    )(block)


def merge_kernel(*refs):
    picked = refs[:-5]
    outs = refs[-4:]
    for j, out_ref in enumerate(outs):
        total = picked[0][j].astype(jnp.float32)
        for q_ref in picked[1:]:
            total = total + q_ref[j].astype(jnp.float32)
        out_ref[...] = total.astype(jnp.bfloat16)


def merge_call(picked, after):
    n_win, rows, lanes = picked[0].shape
    vmem = pl.BlockSpec(memory_space=VMEM)
    return pl.pallas_call(
        merge_kernel,
        in_specs=[vmem] * len(picked) + [pl.BlockSpec(memory_space=pl.ANY)],
        out_specs=[vmem] * n_win,
        out_shape=[jax.ShapeDtypeStruct((rows, lanes), jnp.bfloat16)] * n_win,
        cost_estimate=pl.CostEstimate(flops=2**18, bytes_accessed=2**19, transcendentals=0),
        name="merge",
    )(*picked, after)


def stacks_kernel(n_win, n_rcv, w_dev, r_dev, n_src, bins, *refs):
    t_refs = refs[:n_win]
    s_refs = refs[n_win:n_win + n_rcv]
    out_ref, srow_ref, left_ref, prod_ref = refs[n_win + n_rcv:]
    lanes = 2 * bins
    windows = n_win * w_dev
    per = w_dev // n_rcv
    pad = 128
    step = pl.program_id(0)
    rcv = lax.axis_index("rcv")

    def product(lhs, rhs, dims=(((1,), (0,)), ((), ()))):
        return lax.dot_general(lhs, rhs, dims, preferred_element_type=jnp.float32)

    @pl.when(step == 0)
    def _():
        order = bin_order(lanes)
        both = order[:bins] + order[bins:]

        for i in range(n_rcv):
            for j in range(n_win):
                start = pl.multiple_of((j * w_dev + per * (i ^ rcv)) * n_src, per * n_src)
                block = s_refs[i][j].astype(jnp.float32)
                for h in range(lanes // pad):
                    half = block[:, h * pad:(h + 1) * pad]
                    srow_ref[h, pl.ds(start, per * n_src), :] = half
        lane = lax.broadcasted_iota(jnp.int32, (w_dev, lanes), 1)
        real = (lane // (bins // 4)) % 2 == 0
        for s in range(n_src):
            values = jnp.concatenate(
                [srow_ref[h, pl.ds(s, windows, stride=n_src), :] for h in range(lanes // pad)],
                axis=1,
            )
            stacked = []
            for j in range(n_win):
                own = values[j * w_dev:(j + 1) * w_dev]
                stacked += [jnp.where(real, own, 0.0), jnp.where(real, 0.0, own)]
            stacked = jnp.concatenate(stacked, axis=0).astype(jnp.bfloat16)
            turned = product(both, stacked, (((1,), (1,)), ((), ())))
            left_ref[pl.ds(s, bins, stride=n_src), :2 * windows] = turned

        for f in range(bins):
            right = jnp.concatenate([t_ref[f] for t_ref in t_refs], axis=0)
            left = left_ref[pl.ds(f * n_src, n_src), :2 * windows].astype(jnp.bfloat16)
            result = product(left, right)
            for c in range(2):
                prod_ref[c, pl.ds(f, n_src, stride=bins), :] = result[:, c * pad:(c + 1) * pad]

    scale = 1.0 / math.sqrt(windows)
    s_step = out_ref.shape[0]
    for k in range(s_step):
        start = pl.multiple_of((step * s_step + k) * bins, bins)
        for c in range(2):
            turned = prod_ref[c, pl.ds(start, bins), :].T
            out_ref[k, pl.ds(c, r_dev, stride=2), :] = turned[:r_dev] * scale


def stacks_call(turned, sources, w_dev, r_dev, n_src, bins):
    n_win, n_rcv = len(turned), len(sources)
    windows = n_win * w_dev
    steps = 4
    whole = pl.BlockSpec(memory_space=VMEM)
    out = pl.pallas_call(
        functools.partial(stacks_kernel, n_win, n_rcv, w_dev, r_dev, n_src, bins),
        grid=(steps,),
        in_specs=[whole] * (n_win + n_rcv),
        out_specs=pl.BlockSpec((n_src // steps, 2 * r_dev, bins), lambda g: (g, 0, 0)),
        out_shape=jax.ShapeDtypeStruct((n_src, 2 * r_dev, bins), jnp.float32),
        scratch_shapes=[
            pltpu.VMEM((2 * bins // 128, windows * n_src, 128), jnp.float32),
            pltpu.VMEM((bins * n_src, 128), jnp.float32),
            pltpu.VMEM((2, n_src * bins, 128), jnp.float32),
        ],
        compiler_params=pltpu.CompilerParams(vmem_limit_bytes=32 * 2**20),
        cost_estimate=pl.CostEstimate(
            flops=8 * windows * n_src * r_dev * bins, bytes_accessed=6 * 2**20, transcendentals=0
        ),
        name="stacks",
    )(*turned, *sources)
    return out.reshape(n_src, r_dev, 2, bins)


def swap(value, axis, by):
    size = lax.axis_size(axis)
    return lax.ppermute(value, axis, [(i, i ^ by) for i in range(size)])


def body(traces, valid, src_station):
    w_dev, r_dev, samples = traces.shape
    n_src = src_station.shape[0]
    n_win = lax.axis_size("win")
    n_rcv = lax.axis_size("rcv")
    bins = F // n_win

    out = spectra_call(traces, valid, src_station, n_win, n_rcv)
    received, picked = out[:n_win], out[n_win:]

    picked = [picked[0]] + [swap(picked[i], "rcv", i) for i in range(1, n_rcv)]
    received = [received[0]] + [swap(received[j], "win", j) for j in range(1, n_win)]
    merged = merge_call(picked, received[2])
    blocks = [merged[0]] + [swap(merged[j], "win", j) for j in range(1, n_win)]
    blocks = jnp.stack(blocks, axis=0)
    sources = [blocks] + [swap(blocks, "rcv", i) for i in range(1, n_rcv)]
    turned = [turn_call(block, w_dev, r_dev) for block in received]
    return stacks_call(turned, sources, w_dev, r_dev, n_src, bins)


def correlate(received, sources):
    rr = received[:, :, 0]
    ri = received[:, :, 1]
    sr = sources[:, :, 0]
    si = sources[:, :, 1]
    real = jnp.einsum("wsf,wrf->srf", sr, rr, preferred_element_type=jnp.float32)
    real = real + jnp.einsum("wsf,wrf->srf", si, ri, preferred_element_type=jnp.float32)
    imag = jnp.einsum("wsf,wrf->srf", sr, ri, preferred_element_type=jnp.float32)
    imag = imag - jnp.einsum("wsf,wrf->srf", si, rr, preferred_element_type=jnp.float32)
    return jnp.stack([real, imag], axis=2)


def body_any(traces, valid, src_station):
    w_dev, r_dev, samples = traces.shape
    n_win = lax.axis_size("win")
    n_rcv = lax.axis_size("rcv")
    bins = F // n_win
    table = jnp.asarray(band_table(samples, F, samples // 16))
    spectra = jnp.dot(
        traces.reshape(w_dev * r_dev, samples), table, preferred_element_type=jnp.float32
    )
    spectra = spectra.reshape(w_dev, r_dev, 2, F)
    power = jnp.sum(spectra * spectra, axis=(2, 3), keepdims=True) / F
    keep = valid.astype(jnp.float32)[:, None, None, None]
    white = (spectra * lax.rsqrt(power + 1e-06) * keep).astype(jnp.bfloat16)
    blocks = white.reshape(w_dev, r_dev, 2, n_win, bins).transpose(3, 0, 1, 2, 4)
    me = lax.axis_index("win")
    offset = lax.axis_index("rcv") * r_dev
    station_ids = offset + jnp.arange(r_dev, dtype=jnp.int32)
    selector = (src_station[:, None] == station_ids[None, :]).astype(jnp.bfloat16)
    received = []
    for j in range(n_win):
        block = lax.dynamic_index_in_dim(blocks, me ^ j, 0, keepdims=False)
        received.append(swap(block, "win", j) if j else block)
    received = jnp.concatenate(received, axis=0)
    rows = jnp.einsum("sr,wrcf->wscf", selector, received, preferred_element_type=jnp.float32)
    rows = lax.all_to_all(rows.astype(jnp.bfloat16), "rcv", 0, 0, tiled=True)
    rows = rows.reshape((n_rcv, -1) + rows.shape[1:])
    merged = jnp.sum(rows.astype(jnp.float32), axis=0).astype(jnp.bfloat16)
    sources = lax.all_gather(merged, "rcv", axis=0, tiled=True)
    return correlate(received, sources) * (1.0 / math.sqrt(w_dev * n_win))


def solution(mesh):
    sizes = (mesh.shape["win"], mesh.shape["rcv"])
    return jax.shard_map(
        body if sizes == (4, 4) else body_any,
        mesh=mesh,
        in_specs=(P("win", ("groups", "rcv"), None), P(("groups", "win")), P("groups")),
        out_specs=P(None, ("groups", "rcv"), None, "win"),
        check_vma=False,
    )
```

```python
import functools
import math

import jax
import jax.numpy as jnp
import numpy as np
from jax import lax
from jax.experimental import pallas as pl
from jax.experimental.pallas import tpu as pltpu
from jax.sharding import PartitionSpec as P

F = 512
SMEM = pltpu.MemorySpace.SMEM
VMEM = pltpu.MemorySpace.VMEM


def angles(samples, freqs, count):
    phase = samples[:, None] * freqs[None, :] % count
    return phase.astype(np.float64) * (2.0 * math.pi / count)


def band_table(count, bins, first):
    angle = angles(np.arange(count), first + np.arange(bins), count)
    return np.concatenate([np.cos(angle), -np.sin(angle)], axis=1).astype(jnp.bfloat16)


def quarter_tables(count, bins, first, n_win):
    j = np.arange(bins // 4)

    def columns(re, im):
        both = np.stack([re, im], axis=1).reshape(re.shape[0], 2, n_win, -1)
        return both.transpose(0, 2, 1, 3).reshape(re.shape[0], -1)

    tables = []
    for m in range(4):
        angle = angles(np.arange(count // 4), first + 4 * j + m, count)
        cos, sin = np.cos(angle), np.sin(angle)
        rows = [columns(cos, -sin)]
        if m == 1:
            rows.append(columns(-sin, -cos))
        if m == 3:
            rows.append(columns(sin, cos))
        tables.append(np.concatenate(rows, axis=0))
    return [np.concatenate(tables[:1] + tables[2:3], axis=0).astype(jnp.bfloat16),
            np.concatenate(tables[1:2] + tables[3:], axis=0).astype(jnp.bfloat16)]


def in_hbm(value):
    return pltpu.with_memory_space_constraint(value, pltpu.HBM)


def spectra_kernel(n_win, n_rcv, w_dev, r_dev, n_src, valid_hbm, src_hbm, x_ref, even_hbm, odd_hbm, *refs):
    r_refs = refs[:n_win]
    q_refs = refs[n_win:n_win + n_rcv]
    y_ref, white_ref, sel_ref, even_ref, odd_ref, valid_ref, src_ref, sems = refs[n_win + n_rcv:]
    step = pl.program_id(0)
    rows, samples = x_ref.shape
    w_step = rows // r_dev
    n_own = n_src // n_rcv
    quarter = samples // 4
    win = lax.axis_index("win")
    rcv = lax.axis_index("rcv")
    pairs = ((valid_hbm, valid_ref), (src_hbm, src_ref), (even_hbm, even_ref), (odd_hbm, odd_ref))
    copies = [pltpu.make_async_copy(a, b, sems.at[k]) for k, (a, b) in enumerate(pairs)]

    @pl.when(step == 0)
    def _():
        for copy in copies:
            copy.start()

    b0, b1, b2, b3 = (x_ref[:, q * quarter:(q + 1) * quarter] for q in range(4))
    x0, x1, x2, x3 = (b.astype(jnp.float32) for b in (b0, b1, b2, b3))
    y_ref[:, :quarter] = ((x0 + x2) + (x1 + x3)).astype(jnp.bfloat16)
    y_ref[:, quarter:2 * quarter] = ((x0 + x2) - (x1 + x3)).astype(jnp.bfloat16)
    y_ref[:, 2 * quarter:3 * quarter] = b0 - b2
    y_ref[:, 3 * quarter:] = b1 - b3

    @pl.when(step == 0)
    def _():
        for copy in copies:
            copy.wait()
        shape = (n_rcv * w_step * n_own, rows)
        out_row = lax.broadcasted_iota(jnp.int32, shape, 0)
        column = lax.broadcasted_iota(jnp.int32, shape, 1)
        wanted = jnp.zeros(shape, jnp.int32)
        for i in range(n_rcv):
            for k in range(n_own):
                mine = (out_row // (w_step * n_own) == i) & (out_row % n_own == k)
                station = src_ref[(rcv ^ i) * n_own + k] - rcv * r_dev
                wanted = jnp.where(mine, station, wanted)
        inside = (wanted >= 0) & (wanted < r_dev)
        hit = inside & (column == wanted + (out_row // n_own) % w_step * r_dev)
        sel_ref[...] = hit.astype(jnp.float32).astype(jnp.bfloat16)

    def product(lhs, table):
        return jnp.dot(lhs, table, preferred_element_type=jnp.float32)

    spectra = [
        product(y_ref[:, :quarter], even_ref[:quarter]),
        product(y_ref[:, 2 * quarter:], odd_ref[:2 * quarter]),
        product(y_ref[:, quarter:2 * quarter], even_ref[quarter:]),
        product(y_ref[:, 2 * quarter:], odd_ref[2 * quarter:]),
    ]
    squares = sum(jnp.sum(s * s, axis=1, keepdims=True) for s in spectra)
    gain = lax.rsqrt(squares / F + 1e-06)
    row = lax.broadcasted_iota(jnp.int32, (rows, 1), 0)
    keep = jnp.zeros((rows, 1), jnp.float32)
    for t in range(w_step):
        own = (row >= t * r_dev) & (row < (t + 1) * r_dev)
        keep = jnp.where(own, valid_ref[step * w_step + t].astype(jnp.float32), keep)
    gain = gain * keep
    white = [s * gain for s in spectra]
    piece = white[0].shape[1] // n_win
    for d in range(n_win):
        columns = slice(d * piece, (d + 1) * piece)
        block = jnp.concatenate([part[:, columns] for part in white], axis=1)
        white_ref[d] = block.astype(jnp.bfloat16)
    for j in range(n_win):
        r_refs[j][...] = white_ref[win ^ j]
    count = w_step * n_own
    start = pl.multiple_of(step * count, count)
    for j in range(n_win):
        rows_of = product(sel_ref[...], white_ref[win ^ j]).astype(jnp.bfloat16)
        for i in range(n_rcv):
            q_refs[i][j, pl.ds(start, count), :] = rows_of[i * count:(i + 1) * count]


def spectra_call(traces, valid, src_station, n_win, n_rcv):
    w_dev, r_dev, samples = traces.shape
    n_src = src_station.shape[0]
    n_own = n_src // n_rcv
    steps = 4
    rows = w_dev * r_dev // steps
    lanes = 2 * F // n_win
    even, odd = (jnp.asarray(t) for t in quarter_tables(samples, F, samples // 16, n_win))
    block = jax.ShapeDtypeStruct((w_dev * r_dev, lanes), jnp.bfloat16)
    picked = jax.ShapeDtypeStruct((n_win, w_dev * n_own, lanes), jnp.bfloat16)
    flops = 2 * w_dev * r_dev * (samples // 4) * 6 * (F // 2)
    hbm = pl.BlockSpec(memory_space=pltpu.HBM)
    return pl.pallas_call(
        functools.partial(spectra_kernel, n_win, n_rcv, w_dev, r_dev, n_src),
        grid=(steps,),
        in_specs=[hbm, hbm, pl.BlockSpec((rows, samples), lambda g: (g, 0)), hbm, hbm],
        out_specs=[pl.BlockSpec((rows, lanes), lambda g: (g, 0))] * n_win
        + [pl.BlockSpec(picked.shape, lambda g: (0, 0, 0))] * n_rcv,
        out_shape=[block] * n_win + [picked] * n_rcv,
        scratch_shapes=[
            pltpu.VMEM((rows, samples), jnp.bfloat16),
            pltpu.VMEM((n_win, rows, lanes), jnp.bfloat16),
            pltpu.VMEM((n_src * (w_dev // steps), rows), jnp.bfloat16),
            pltpu.VMEM(even.shape, jnp.bfloat16),
            pltpu.VMEM(odd.shape, jnp.bfloat16),
            pltpu.SMEM(valid.shape, jnp.int32),
            pltpu.SMEM(src_station.shape, jnp.int32),
            pltpu.SemaphoreType.DMA((4,)),
        ],
        compiler_params=pltpu.CompilerParams(vmem_limit_bytes=48 * 2**20),
        cost_estimate=pl.CostEstimate(
            flops=flops, bytes_accessed=w_dev * r_dev * samples * 2, transcendentals=0
        ),
        name="spectra",
    )(*(in_hbm(x) for x in (valid, src_station, traces.reshape(w_dev * r_dev, samples), even, odd)))


def bin_order(lanes):
    quarter = lanes // 8
    lane = lax.broadcasted_iota(jnp.int32, (lanes, lanes), 1)
    row = lax.broadcasted_iota(jnp.int32, (lanes, lanes), 0)
    part = (lane // quarter) % 2
    bin_of = 4 * (lane % quarter) + lane // (2 * quarter)
    hit = row == part * (lanes // 2) + bin_of
    return hit.astype(jnp.float32).astype(jnp.bfloat16)


def turn_kernel(w_dev, r_dev, x_ref, out_ref, rows_ref):
    lanes = x_ref.shape[1]
    bins = lanes // 2
    pad = out_ref.shape[2] // 2
    order = bin_order(lanes)
    for w in range(w_dev):
        turned = lax.dot_general(
            order, x_ref[w * r_dev:(w + 1) * r_dev], (((1,), (1,)), ((), ())),
            preferred_element_type=jnp.float32,
        )
        rows_ref[pl.ds(w, lanes, stride=w_dev), :r_dev] = turned
    rr = rows_ref[:bins * w_dev].reshape(bins, w_dev, pad)
    ri = rows_ref[bins * w_dev:].reshape(bins, w_dev, pad)
    out_ref[:, :, :pad] = jnp.concatenate([rr, ri], axis=1).astype(jnp.bfloat16)
    out_ref[:, :, pad:] = jnp.concatenate([ri, -rr], axis=1).astype(jnp.bfloat16)


def turn_call(block, w_dev, r_dev):
    lanes = block.shape[1]
    pad = 128
    return pl.pallas_call(
        functools.partial(turn_kernel, w_dev, r_dev),
        in_specs=[pl.BlockSpec(memory_space=VMEM)],
        out_specs=pl.BlockSpec(memory_space=VMEM),
        out_shape=jax.ShapeDtypeStruct((lanes // 2, 2 * w_dev, 2 * pad), jnp.bfloat16),
        scratch_shapes=[pltpu.VMEM((lanes * w_dev, pad), jnp.float32)],
        compiler_params=pltpu.CompilerParams(vmem_limit_bytes=16 * 2**20),
        cost_estimate=pl.CostEstimate(
            flops=2 * w_dev * lanes * lanes * pad, bytes_accessed=2 * 2**20, transcendentals=0
        ),
        name="turn",
    )(block)


def merge_kernel(*refs):
    picked = refs[:-5]
    outs = refs[-4:]
    for j, out_ref in enumerate(outs):
        total = picked[0][j].astype(jnp.float32)
        for q_ref in picked[1:]:
            total = total + q_ref[j].astype(jnp.float32)
        out_ref[...] = total.astype(jnp.bfloat16)


def merge_call(picked, after):
    n_win, rows, lanes = picked[0].shape
    vmem = pl.BlockSpec(memory_space=VMEM)
    return pl.pallas_call(
        merge_kernel,
        in_specs=[vmem] * len(picked) + [pl.BlockSpec(memory_space=pl.ANY)],
        out_specs=[vmem] * n_win,
        out_shape=[jax.ShapeDtypeStruct((rows, lanes), jnp.bfloat16)] * n_win,
        compiler_params=pltpu.CompilerParams(vmem_limit_bytes=4 * 2**20),
        cost_estimate=pl.CostEstimate(flops=2**18, bytes_accessed=2**19, transcendentals=0),
        name="merge",
    )(*picked, after)


def stacks_kernel(shares, n_win, w_dev, r_dev, n_own, bins, *refs):
    t_refs = refs[:n_win]
    s_refs = refs[n_win:n_win + len(shares)]
    out_hbm, srow_ref, left_ref, prod_ref, out_ref, sems = refs[-6:]
    lanes = 2 * bins
    windows = n_win * w_dev
    count = len(shares) * n_own
    pad = 128
    rcv = lax.axis_index("rcv")

    def product(lhs, rhs, dims=(((1,), (0,)), ((), ()))):
        return lax.dot_general(lhs, rhs, dims, preferred_element_type=jnp.float32)

    order = bin_order(lanes)
    both = order[:bins] + order[bins:]
    lane = lax.broadcasted_iota(jnp.int32, (w_dev, lanes), 1)
    real = (lane // (bins // 4)) % 2 == 0

    for k, s_ref in enumerate(s_refs):
        for j in range(n_win):
            block = s_ref[j].astype(jnp.float32)
            for h in range(lanes // pad):
                half = block[:, h * pad:(h + 1) * pad]
                srow_ref[h, pl.ds((k * n_win + j) * w_dev * n_own, w_dev * n_own), :] = half
    for s in range(count):
        first = s // n_own * windows * n_own + s % n_own
        values = jnp.concatenate(
            [srow_ref[h, pl.ds(first, windows, stride=n_own), :] for h in range(lanes // pad)],
            axis=1,
        )
        stacked = []
        for j in range(n_win):
            own = values[j * w_dev:(j + 1) * w_dev]
            stacked += [jnp.where(real, own, 0.0), jnp.where(real, 0.0, own)]
        stacked = jnp.concatenate(stacked, axis=0).astype(jnp.bfloat16)
        turned = product(both, stacked, (((1,), (1,)), ((), ())))
        left_ref[pl.ds(s, bins, stride=count), :2 * windows] = turned

    for f in range(bins):
        right = jnp.concatenate([t_ref[f] for t_ref in t_refs], axis=0)
        left = left_ref[pl.ds(f * count, count), :2 * windows].astype(jnp.bfloat16)
        result = product(left, right)
        for c in range(2):
            prod_ref[c, pl.ds(f, count, stride=bins), :] = result[:, c * pad:(c + 1) * pad]

    scale = 1.0 / math.sqrt(windows)
    copies = []
    for s in range(count):
        for c in range(2):
            turned = prod_ref[c, s * bins:(s + 1) * bins, :].T
            out_ref[s, pl.ds(c, r_dev, stride=2), :] = turned[:r_dev] * scale
        row = (rcv ^ shares[s // n_own]) * n_own + s % n_own
        copies.append(pltpu.make_async_copy(out_ref.at[s], out_hbm.at[row], sems.at[s]))
        copies[-1].start()
    for copy in copies:
        copy.wait()


def stacks_call(out, turned, sources, shares, n_rcv, w_dev, r_dev, bins):
    n_win = len(turned)
    n_own = sources[0].shape[1] // w_dev
    windows = n_win * w_dev
    count = len(shares) * n_own
    whole = pl.BlockSpec(memory_space=VMEM)
    args = list(turned) + [sources[i] for i in shares]
    specs = [whole] * len(args)
    aliases = {}
    if out is not None:
        aliases = {len(args): 0}
        args.append(out)
        specs.append(pl.BlockSpec(memory_space=pl.ANY))
    return pl.pallas_call(
        functools.partial(stacks_kernel, shares, n_win, w_dev, r_dev, n_own, bins),
        in_specs=specs,
        out_specs=pl.BlockSpec(memory_space=pltpu.HBM),
        out_shape=jax.ShapeDtypeStruct((n_rcv * n_own, 2 * r_dev, bins), jnp.float32),
        input_output_aliases=aliases,
        scratch_shapes=[
            pltpu.VMEM((2 * bins // 128, windows * count, 128), jnp.float32),
            pltpu.VMEM((bins * count, 128), jnp.float32),
            pltpu.VMEM((2, count * bins, 128), jnp.float32),
            pltpu.VMEM((count, 2 * r_dev, bins), jnp.float32),
            pltpu.SemaphoreType.DMA((count,)),
        ],
        compiler_params=pltpu.CompilerParams(vmem_limit_bytes=20 * 2**20),
        cost_estimate=pl.CostEstimate(
            flops=8 * windows * count * r_dev * bins, bytes_accessed=6 * 2**20, transcendentals=0
        ),
        name="stacks",
    )(*args)


def swap(value, axis, by):
    size = lax.axis_size(axis)
    return lax.ppermute(value, axis, [(i, i ^ by) for i in range(size)])


def body(traces, valid, src_station):
    w_dev, r_dev, samples = traces.shape
    n_src = src_station.shape[0]
    n_win = lax.axis_size("win")
    n_rcv = lax.axis_size("rcv")
    bins = F // n_win

    out = spectra_call(traces, valid, src_station, n_win, n_rcv)
    received, picked = out[:n_win], out[n_win:]

    picked = [picked[0]] + [swap(picked[i], "rcv", i) for i in range(1, n_rcv)]
    received = [received[0]] + [swap(received[j], "win", j) for j in range(1, n_win)]
    merged = merge_call(picked, received[2])
    blocks = [merged[0]] + [swap(merged[j], "win", j) for j in range(1, n_win)]
    blocks = jnp.stack(blocks, axis=0)
    sources = [blocks] + [swap(blocks, "rcv", i) for i in range(1, n_rcv)]
    turned = [turn_call(block, w_dev, r_dev) for block in received]
    half = n_rcv // 2
    sizes = (n_rcv, w_dev, r_dev, bins)
    stacks = stacks_call(None, turned, sources, tuple(range(half)), *sizes)
    stacks = stacks_call(stacks, turned, sources, tuple(range(half, n_rcv)), *sizes)
    return stacks.reshape(n_src, r_dev, 2, bins)


def correlate(received, sources):
    rr = received[:, :, 0]
    ri = received[:, :, 1]
    sr = sources[:, :, 0]
    si = sources[:, :, 1]
    real = jnp.einsum("wsf,wrf->srf", sr, rr, preferred_element_type=jnp.float32)
    real = real + jnp.einsum("wsf,wrf->srf", si, ri, preferred_element_type=jnp.float32)
    imag = jnp.einsum("wsf,wrf->srf", sr, ri, preferred_element_type=jnp.float32)
    imag = imag - jnp.einsum("wsf,wrf->srf", si, rr, preferred_element_type=jnp.float32)
    return jnp.stack([real, imag], axis=2)


def body_any(traces, valid, src_station):
    w_dev, r_dev, samples = traces.shape
    n_win = lax.axis_size("win")
    n_rcv = lax.axis_size("rcv")
    bins = F // n_win
    table = jnp.asarray(band_table(samples, F, samples // 16))
    spectra = jnp.dot(
        traces.reshape(w_dev * r_dev, samples), table, preferred_element_type=jnp.float32
    )
    spectra = spectra.reshape(w_dev, r_dev, 2, F)
    power = jnp.sum(spectra * spectra, axis=(2, 3), keepdims=True) / F
    keep = valid.astype(jnp.float32)[:, None, None, None]
    white = (spectra * lax.rsqrt(power + 1e-06) * keep).astype(jnp.bfloat16)
    blocks = white.reshape(w_dev, r_dev, 2, n_win, bins).transpose(3, 0, 1, 2, 4)
    me = lax.axis_index("win")
    offset = lax.axis_index("rcv") * r_dev
    station_ids = offset + jnp.arange(r_dev, dtype=jnp.int32)
    selector = (src_station[:, None] == station_ids[None, :]).astype(jnp.bfloat16)
    received = []
    for j in range(n_win):
        block = lax.dynamic_index_in_dim(blocks, me ^ j, 0, keepdims=False)
        received.append(swap(block, "win", j) if j else block)
    received = jnp.concatenate(received, axis=0)
    rows = jnp.einsum("sr,wrcf->wscf", selector, received, preferred_element_type=jnp.float32)
    rows = lax.all_to_all(rows.astype(jnp.bfloat16), "rcv", 0, 0, tiled=True)
    rows = rows.reshape((n_rcv, -1) + rows.shape[1:])
    merged = jnp.sum(rows.astype(jnp.float32), axis=0).astype(jnp.bfloat16)
    sources = lax.all_gather(merged, "rcv", axis=0, tiled=True)
    return correlate(received, sources) * (1.0 / math.sqrt(w_dev * n_win))


def solution(mesh):
    sizes = (mesh.shape["win"], mesh.shape["rcv"])
    return jax.shard_map(
        body if sizes == (4, 4) else body_any,
        mesh=mesh,
        in_specs=(P("win", ("groups", "rcv"), None), P(("groups", "win")), P("groups")),
        out_specs=P(None, ("groups", "rcv"), None, "win"),
        check_vma=False,
    )
```

```python
import functools
import math

import jax
import jax.numpy as jnp
import numpy as np
from jax import lax
from jax.experimental import pallas as pl
from jax.experimental.pallas import tpu as pltpu
from jax.sharding import PartitionSpec as P

F = 512
SMEM = pltpu.MemorySpace.SMEM
VMEM = pltpu.MemorySpace.VMEM


def angles(samples, freqs, count):
    phase = samples[:, None] * freqs[None, :] % count
    return phase.astype(np.float64) * (2.0 * math.pi / count)


def band_table(count, bins, first):
    angle = angles(np.arange(count), first + np.arange(bins), count)
    return np.concatenate([np.cos(angle), -np.sin(angle)], axis=1).astype(jnp.bfloat16)


def quarter_tables(count, bins, first, n_win):
    j = np.arange(bins // 4)

    def columns(re, im):
        both = np.stack([re, im], axis=1).reshape(re.shape[0], 2, n_win, -1)
        return both.transpose(0, 2, 1, 3).reshape(re.shape[0], -1)

    tables = []
    for m in range(4):
        angle = angles(np.arange(count // 4), first + 4 * j + m, count)
        cos, sin = np.cos(angle), np.sin(angle)
        rows = [columns(cos, -sin)]
        if m == 1:
            rows.append(columns(-sin, -cos))
        if m == 3:
            rows.append(columns(sin, cos))
        tables.append(np.concatenate(rows, axis=0))
    return [np.concatenate(tables[:1] + tables[2:3], axis=0).astype(jnp.bfloat16),
            np.concatenate(tables[1:2] + tables[3:], axis=0).astype(jnp.bfloat16)]


def in_hbm(value):
    return pltpu.with_memory_space_constraint(value, pltpu.HBM)


def spectra_kernel(n_win, n_rcv, w_dev, r_dev, n_src, valid_hbm, src_hbm, x_hbm, even_hbm, odd_hbm, *refs):
    r_refs = refs[:n_win]
    q_refs = refs[n_win:n_win + n_rcv]
    x_ref, y_ref, white_ref, sel_ref, even_ref, odd_ref, valid_ref, src_ref, sems, x_sems = refs[n_win + n_rcv:]
    step = pl.program_id(0)
    steps, rows, samples = x_ref.shape
    w_step = rows // r_dev
    n_own = n_src // n_rcv
    quarter = samples // 4
    win = lax.axis_index("win")
    rcv = lax.axis_index("rcv")

    def small(k):
        pair = ((valid_hbm, valid_ref), (src_hbm, src_ref), (even_hbm, even_ref), (odd_hbm, odd_ref))[k]
        return pltpu.make_async_copy(*pair, sems.at[k])

    def piece_of(k, q):
        columns = pl.ds(q * quarter, quarter)
        return pltpu.make_async_copy(
            x_hbm.at[pl.ds(k * rows, rows), columns], x_ref.at[k, :, columns], x_sems.at[k, q]
        )

    @pl.when(step == 0)
    def _():
        for q in range(4):
            piece_of(0, q).start()
        for k in range(4):
            small(k).start()
        for k in range(1, steps):
            for q in range(4):
                piece_of(k, q).start()

    for q in range(4):
        piece_of(step, q).wait()
    b0, b1, b2, b3 = (x_ref[step, :, q * quarter:(q + 1) * quarter] for q in range(4))
    x0, x1, x2, x3 = (b.astype(jnp.float32) for b in (b0, b1, b2, b3))
    y_ref[:, :quarter] = ((x0 + x2) + (x1 + x3)).astype(jnp.bfloat16)
    y_ref[:, quarter:2 * quarter] = ((x0 + x2) - (x1 + x3)).astype(jnp.bfloat16)
    y_ref[:, 2 * quarter:3 * quarter] = b0 - b2
    y_ref[:, 3 * quarter:] = b1 - b3

    @pl.when(step == 0)
    def _():
        for k in range(3):
            small(k).wait()
        shape = (n_rcv * w_step * n_own, rows)
        out_row = lax.broadcasted_iota(jnp.int32, shape, 0)
        column = lax.broadcasted_iota(jnp.int32, shape, 1)
        wanted = jnp.zeros(shape, jnp.int32)
        for i in range(n_rcv):
            for k in range(n_own):
                mine = (out_row // (w_step * n_own) == i) & (out_row % n_own == k)
                station = src_ref[(rcv ^ i) * n_own + k] - rcv * r_dev
                wanted = jnp.where(mine, station, wanted)
        inside = (wanted >= 0) & (wanted < r_dev)
        hit = inside & (column == wanted + (out_row // n_own) % w_step * r_dev)
        sel_ref[...] = hit.astype(jnp.float32).astype(jnp.bfloat16)

    def product(lhs, table):
        return jnp.dot(lhs, table, preferred_element_type=jnp.float32)

    even = [
        product(y_ref[:, :quarter], even_ref[:quarter]),
        product(y_ref[:, quarter:2 * quarter], even_ref[quarter:]),
    ]

    @pl.when(step == 0)
    def _():
        small(3).wait()

    odd = [
        product(y_ref[:, 2 * quarter:], odd_ref[:2 * quarter]),
        product(y_ref[:, 2 * quarter:], odd_ref[2 * quarter:]),
    ]
    spectra = [even[0], odd[0], even[1], odd[1]]
    squares = sum(jnp.sum(s * s, axis=1, keepdims=True) for s in spectra)
    gain = lax.rsqrt(squares / F + 1e-06)
    row = lax.broadcasted_iota(jnp.int32, (rows, 1), 0)
    keep = jnp.zeros((rows, 1), jnp.float32)
    for t in range(w_step):
        own = (row >= t * r_dev) & (row < (t + 1) * r_dev)
        keep = jnp.where(own, valid_ref[step * w_step + t].astype(jnp.float32), keep)
    gain = gain * keep
    white = [s * gain for s in spectra]
    piece = white[0].shape[1] // n_win
    for d in range(n_win):
        columns = slice(d * piece, (d + 1) * piece)
        block = jnp.concatenate([part[:, columns] for part in white], axis=1)
        white_ref[d] = block.astype(jnp.bfloat16)
    for j in range(n_win):
        r_refs[j][...] = white_ref[win ^ j]
    count = w_step * n_own
    start = pl.multiple_of(step * count, count)
    for j in range(n_win):
        rows_of = product(sel_ref[...], white_ref[win ^ j]).astype(jnp.bfloat16)
        for i in range(n_rcv):
            q_refs[i][j, pl.ds(start, count), :] = rows_of[i * count:(i + 1) * count]


def spectra_call(traces, valid, src_station, n_win, n_rcv):
    w_dev, r_dev, samples = traces.shape
    n_src = src_station.shape[0]
    n_own = n_src // n_rcv
    steps = 4
    rows = w_dev * r_dev // steps
    lanes = 2 * F // n_win
    even, odd = (jnp.asarray(t) for t in quarter_tables(samples, F, samples // 16, n_win))
    block = jax.ShapeDtypeStruct((w_dev * r_dev, lanes), jnp.bfloat16)
    picked = jax.ShapeDtypeStruct((n_win, w_dev * n_own, lanes), jnp.bfloat16)
    flops = 2 * w_dev * r_dev * (samples // 4) * 6 * (F // 2)
    hbm = pl.BlockSpec(memory_space=pltpu.HBM)
    return pl.pallas_call(
        functools.partial(spectra_kernel, n_win, n_rcv, w_dev, r_dev, n_src),
        grid=(steps,),
        in_specs=[hbm] * 5,
        out_specs=[pl.BlockSpec((rows, lanes), lambda g: (g, 0))] * n_win
        + [pl.BlockSpec(picked.shape, lambda g: (0, 0, 0))] * n_rcv,
        out_shape=[block] * n_win + [picked] * n_rcv,
        scratch_shapes=[
            pltpu.VMEM((steps, rows, samples), jnp.bfloat16),
            pltpu.VMEM((rows, samples), jnp.bfloat16),
            pltpu.VMEM((n_win, rows, lanes), jnp.bfloat16),
            pltpu.VMEM((n_src * (w_dev // steps), rows), jnp.bfloat16),
            pltpu.VMEM(even.shape, jnp.bfloat16),
            pltpu.VMEM(odd.shape, jnp.bfloat16),
            pltpu.SMEM(valid.shape, jnp.int32),
            pltpu.SMEM(src_station.shape, jnp.int32),
            pltpu.SemaphoreType.DMA((4,)),
            pltpu.SemaphoreType.DMA((steps, 4)),
        ],
        compiler_params=pltpu.CompilerParams(vmem_limit_bytes=48 * 2**20),
        cost_estimate=pl.CostEstimate(
            flops=flops, bytes_accessed=w_dev * r_dev * samples * 2, transcendentals=0
        ),
        name="spectra",
    )(*(in_hbm(x) for x in (valid, src_station, traces.reshape(w_dev * r_dev, samples), even, odd)))


def bin_order(lanes):
    quarter = lanes // 8
    lane = lax.broadcasted_iota(jnp.int32, (lanes, lanes), 1)
    row = lax.broadcasted_iota(jnp.int32, (lanes, lanes), 0)
    part = (lane // quarter) % 2
    bin_of = 4 * (lane % quarter) + lane // (2 * quarter)
    hit = row == part * (lanes // 2) + bin_of
    return hit.astype(jnp.float32).astype(jnp.bfloat16)


def turn_kernel(w_dev, r_dev, x_ref, out_ref, rows_ref):
    lanes = x_ref.shape[1]
    bins = lanes // 2
    pad = out_ref.shape[2] // 2
    order = bin_order(lanes)
    for w in range(w_dev):
        turned = lax.dot_general(
            order, x_ref[w * r_dev:(w + 1) * r_dev], (((1,), (1,)), ((), ())),
            preferred_element_type=jnp.float32,
        )
        rows_ref[pl.ds(w, lanes, stride=w_dev), :r_dev] = turned
    rr = rows_ref[:bins * w_dev].reshape(bins, w_dev, pad)
    ri = rows_ref[bins * w_dev:].reshape(bins, w_dev, pad)
    out_ref[:, :, :pad] = jnp.concatenate([rr, ri], axis=1).astype(jnp.bfloat16)
    out_ref[:, :, pad:] = jnp.concatenate([ri, -rr], axis=1).astype(jnp.bfloat16)


def turn_call(block, w_dev, r_dev):
    lanes = block.shape[1]
    pad = 128
    return pl.pallas_call(
        functools.partial(turn_kernel, w_dev, r_dev),
        in_specs=[pl.BlockSpec(memory_space=VMEM)],
        out_specs=pl.BlockSpec(memory_space=VMEM),
        out_shape=jax.ShapeDtypeStruct((lanes // 2, 2 * w_dev, 2 * pad), jnp.bfloat16),
        scratch_shapes=[pltpu.VMEM((lanes * w_dev, pad), jnp.float32)],
        compiler_params=pltpu.CompilerParams(vmem_limit_bytes=16 * 2**20),
        cost_estimate=pl.CostEstimate(
            flops=2 * w_dev * lanes * lanes * pad, bytes_accessed=2 * 2**20, transcendentals=0
        ),
        name="turn",
    )(block)


def merge_kernel(*refs):
    picked = refs[:-5]
    outs = refs[-4:]
    for j, out_ref in enumerate(outs):
        total = picked[0][j].astype(jnp.float32)
        for q_ref in picked[1:]:
            total = total + q_ref[j].astype(jnp.float32)
        out_ref[...] = total.astype(jnp.bfloat16)


def merge_call(picked, after):
    n_win, rows, lanes = picked[0].shape
    vmem = pl.BlockSpec(memory_space=VMEM)
    return pl.pallas_call(
        merge_kernel,
        in_specs=[vmem] * len(picked) + [pl.BlockSpec(memory_space=pl.ANY)],
        out_specs=[vmem] * n_win,
        out_shape=[jax.ShapeDtypeStruct((rows, lanes), jnp.bfloat16)] * n_win,
        compiler_params=pltpu.CompilerParams(vmem_limit_bytes=4 * 2**20),
        cost_estimate=pl.CostEstimate(flops=2**18, bytes_accessed=2**19, transcendentals=0),
        name="merge",
    )(*picked, after)


def stacks_kernel(shares, n_win, w_dev, r_dev, n_own, bins, *refs):
    t_refs = refs[:n_win]
    s_refs = refs[n_win:n_win + len(shares)]
    out_hbm, srow_ref, left_ref, prod_ref, out_ref, sems = refs[-6:]
    lanes = 2 * bins
    windows = n_win * w_dev
    count = len(shares) * n_own
    pad = 128
    rcv = lax.axis_index("rcv")

    def product(lhs, rhs, dims=(((1,), (0,)), ((), ()))):
        return lax.dot_general(lhs, rhs, dims, preferred_element_type=jnp.float32)

    order = bin_order(lanes)
    both = order[:bins] + order[bins:]
    lane = lax.broadcasted_iota(jnp.int32, (w_dev, lanes), 1)
    real = (lane // (bins // 4)) % 2 == 0

    for k, s_ref in enumerate(s_refs):
        for j in range(n_win):
            block = s_ref[j].astype(jnp.float32)
            for h in range(lanes // pad):
                half = block[:, h * pad:(h + 1) * pad]
                srow_ref[h, pl.ds((k * n_win + j) * w_dev * n_own, w_dev * n_own), :] = half
    for s in range(count):
        first = s // n_own * windows * n_own + s % n_own
        values = jnp.concatenate(
            [srow_ref[h, pl.ds(first, windows, stride=n_own), :] for h in range(lanes // pad)],
            axis=1,
        )
        stacked = []
        for j in range(n_win):
            own = values[j * w_dev:(j + 1) * w_dev]
            stacked += [jnp.where(real, own, 0.0), jnp.where(real, 0.0, own)]
        stacked = jnp.concatenate(stacked, axis=0).astype(jnp.bfloat16)
        turned = product(both, stacked, (((1,), (1,)), ((), ())))
        left_ref[pl.ds(s, bins, stride=count), :2 * windows] = turned

    for f in range(bins):
        right = jnp.concatenate([t_ref[f] for t_ref in t_refs], axis=0)
        left = left_ref[pl.ds(f * count, count), :2 * windows].astype(jnp.bfloat16)
        result = product(left, right)
        for c in range(2):
            prod_ref[c, pl.ds(f, count, stride=bins), :] = result[:, c * pad:(c + 1) * pad]

    scale = 1.0 / math.sqrt(windows)
    copies = []
    for s in range(count):
        for c in range(2):
            turned = prod_ref[c, s * bins:(s + 1) * bins, :].T
            out_ref[s, pl.ds(c, r_dev, stride=2), :] = turned[:r_dev] * scale
        row = (rcv ^ shares[s // n_own]) * n_own + s % n_own
        copies.append(pltpu.make_async_copy(out_ref.at[s], out_hbm.at[row], sems.at[s]))
        copies[-1].start()
    for copy in copies:
        copy.wait()


def stacks_call(out, turned, sources, shares, n_rcv, w_dev, r_dev, bins):
    n_win = len(turned)
    n_own = sources[0].shape[1] // w_dev
    windows = n_win * w_dev
    count = len(shares) * n_own
    whole = pl.BlockSpec(memory_space=VMEM)
    args = list(turned) + [sources[i] for i in shares]
    specs = [whole] * len(args)
    aliases = {}
    if out is not None:
        aliases = {len(args): 0}
        args.append(out)
        specs.append(pl.BlockSpec(memory_space=pl.ANY))
    return pl.pallas_call(
        functools.partial(stacks_kernel, shares, n_win, w_dev, r_dev, n_own, bins),
        in_specs=specs,
        out_specs=pl.BlockSpec(memory_space=pltpu.HBM),
        out_shape=jax.ShapeDtypeStruct((n_rcv * n_own, 2 * r_dev, bins), jnp.float32),
        input_output_aliases=aliases,
        scratch_shapes=[
            pltpu.VMEM((2 * bins // 128, windows * count, 128), jnp.float32),
            pltpu.VMEM((bins * count, 128), jnp.float32),
            pltpu.VMEM((2, count * bins, 128), jnp.float32),
            pltpu.VMEM((count, 2 * r_dev, bins), jnp.float32),
            pltpu.SemaphoreType.DMA((count,)),
        ],
        compiler_params=pltpu.CompilerParams(vmem_limit_bytes=20 * 2**20),
        cost_estimate=pl.CostEstimate(
            flops=8 * windows * count * r_dev * bins, bytes_accessed=6 * 2**20, transcendentals=0
        ),
        name="stacks",
    )(*args)


def swap(value, axis, by):
    size = lax.axis_size(axis)
    return lax.ppermute(value, axis, [(i, i ^ by) for i in range(size)])


def body(traces, valid, src_station):
    w_dev, r_dev, samples = traces.shape
    n_src = src_station.shape[0]
    n_win = lax.axis_size("win")
    n_rcv = lax.axis_size("rcv")
    bins = F // n_win

    out = spectra_call(traces, valid, src_station, n_win, n_rcv)
    received, picked = out[:n_win], out[n_win:]

    picked = [picked[0]] + [swap(picked[i], "rcv", i) for i in range(1, n_rcv)]
    received = [received[0]] + [swap(received[j], "win", j) for j in range(1, n_win)]
    merged = merge_call(picked, received[2])
    blocks = [merged[0]] + [swap(merged[j], "win", j) for j in range(1, n_win)]
    blocks = jnp.stack(blocks, axis=0)
    sources = [blocks] + [swap(blocks, "rcv", i) for i in range(1, n_rcv)]
    turned = [turn_call(block, w_dev, r_dev) for block in received]
    half = n_rcv // 2
    sizes = (n_rcv, w_dev, r_dev, bins)
    stacks = stacks_call(None, turned, sources, tuple(range(half)), *sizes)
    stacks = stacks_call(stacks, turned, sources, tuple(range(half, n_rcv)), *sizes)
    return stacks.reshape(n_src, r_dev, 2, bins)


def correlate(received, sources):
    rr = received[:, :, 0]
    ri = received[:, :, 1]
    sr = sources[:, :, 0]
    si = sources[:, :, 1]
    real = jnp.einsum("wsf,wrf->srf", sr, rr, preferred_element_type=jnp.float32)
    real = real + jnp.einsum("wsf,wrf->srf", si, ri, preferred_element_type=jnp.float32)
    imag = jnp.einsum("wsf,wrf->srf", sr, ri, preferred_element_type=jnp.float32)
    imag = imag - jnp.einsum("wsf,wrf->srf", si, rr, preferred_element_type=jnp.float32)
    return jnp.stack([real, imag], axis=2)


def body_any(traces, valid, src_station):
    w_dev, r_dev, samples = traces.shape
    n_win = lax.axis_size("win")
    n_rcv = lax.axis_size("rcv")
    bins = F // n_win
    table = jnp.asarray(band_table(samples, F, samples // 16))
    spectra = jnp.dot(
        traces.reshape(w_dev * r_dev, samples), table, preferred_element_type=jnp.float32
    )
    spectra = spectra.reshape(w_dev, r_dev, 2, F)
    power = jnp.sum(spectra * spectra, axis=(2, 3), keepdims=True) / F
    keep = valid.astype(jnp.float32)[:, None, None, None]
    white = (spectra * lax.rsqrt(power + 1e-06) * keep).astype(jnp.bfloat16)
    blocks = white.reshape(w_dev, r_dev, 2, n_win, bins).transpose(3, 0, 1, 2, 4)
    me = lax.axis_index("win")
    offset = lax.axis_index("rcv") * r_dev
    station_ids = offset + jnp.arange(r_dev, dtype=jnp.int32)
    selector = (src_station[:, None] == station_ids[None, :]).astype(jnp.bfloat16)
    received = []
    for j in range(n_win):
        block = lax.dynamic_index_in_dim(blocks, me ^ j, 0, keepdims=False)
        received.append(swap(block, "win", j) if j else block)
    received = jnp.concatenate(received, axis=0)
    rows = jnp.einsum("sr,wrcf->wscf", selector, received, preferred_element_type=jnp.float32)
    rows = lax.all_to_all(rows.astype(jnp.bfloat16), "rcv", 0, 0, tiled=True)
    rows = rows.reshape((n_rcv, -1) + rows.shape[1:])
    merged = jnp.sum(rows.astype(jnp.float32), axis=0).astype(jnp.bfloat16)
    sources = lax.all_gather(merged, "rcv", axis=0, tiled=True)
    return correlate(received, sources) * (1.0 / math.sqrt(w_dev * n_win))


def solution(mesh):
    sizes = (mesh.shape["win"], mesh.shape["rcv"])
    return jax.shard_map(
        body if sizes == (4, 4) else body_any,
        mesh=mesh,
        in_specs=(P("win", ("groups", "rcv"), None), P(("groups", "win")), P("groups")),
        out_specs=P(None, ("groups", "rcv"), None, "win"),
        check_vma=False,
    )
```

```python
import functools
import math

import jax
import jax.numpy as jnp
import numpy as np
from jax import lax
from jax.experimental import pallas as pl
from jax.experimental.pallas import tpu as pltpu
from jax.sharding import PartitionSpec as P

F = 512
SMEM = pltpu.MemorySpace.SMEM
VMEM = pltpu.MemorySpace.VMEM


def angles(samples, freqs, count):
    phase = samples[:, None] * freqs[None, :] % count
    return phase.astype(np.float64) * (2.0 * math.pi / count)


def band_table(count, bins, first):
    angle = angles(np.arange(count), first + np.arange(bins), count)
    return np.concatenate([np.cos(angle), -np.sin(angle)], axis=1).astype(jnp.bfloat16)


FINE = 32


def angle_factors(count, bins, first, n_win):
    j = np.arange(bins // 4).reshape(n_win, 1, -1)
    turn = np.array([0.0, 0.5 * math.pi]).reshape(1, 2, 1)

    def factors(samples, shift):
        out = []
        for m in range(4):
            freqs = np.broadcast_to(first + 4 * j + m, (n_win, 2, bins // 4 // n_win))
            angle = angles(samples, freqs.reshape(-1), count)
            angle = angle + np.broadcast_to(shift, freqs.shape).reshape(1, -1)
            out.append(np.stack([np.cos(angle), np.sin(angle)]))
        return np.stack(out).astype(np.float32)

    return factors(np.arange(0, count // 4, FINE), 0.0 * turn), factors(np.arange(FINE), turn)


def make_tables(coarse_ref, fine_ref, even_ref, odd_ref):
    steps = coarse_ref.shape[2]
    quarter = steps * FINE
    for m in range(4):
        cos_b, sin_b = fine_ref[m, 0], fine_ref[m, 1]
        out_ref = odd_ref if m % 2 else even_ref
        base = (m // 2) * (2 * quarter if m % 2 else quarter)
        for a in range(steps):
            cos_a, sin_a = (coarse_ref[m, k, a:a + 1, :] for k in range(2))
            rows = slice(base + a * FINE, base + (a + 1) * FINE)
            out_ref[rows, :] = (cos_a * cos_b - sin_a * sin_b).astype(jnp.bfloat16)
            if m % 2:
                if m == 1:
                    cos_a, sin_a = -cos_a, -sin_a
                rows = slice(rows.start + quarter, rows.stop + quarter)
                out_ref[rows, :] = (cos_a * sin_b + sin_a * cos_b).astype(jnp.bfloat16)


def in_hbm(value):
    return pltpu.with_memory_space_constraint(value, pltpu.HBM)


def spectra_kernel(n_win, n_rcv, w_dev, r_dev, n_src, valid_hbm, src_hbm, x_hbm, coarse_hbm, fine_hbm, *refs):
    r_refs = refs[:n_win]
    q_refs = refs[n_win:n_win + n_rcv]
    (x_ref, y_ref, white_ref, sel_ref, even_ref, odd_ref, coarse_ref, fine_ref,
     valid_ref, src_ref, sems, x_sems) = refs[n_win + n_rcv:]
    step = pl.program_id(0)
    steps, rows, samples = x_ref.shape
    w_step = rows // r_dev
    n_own = n_src // n_rcv
    quarter = samples // 4
    win = lax.axis_index("win")
    rcv = lax.axis_index("rcv")

    def small(k):
        source = (coarse_hbm, fine_hbm, valid_hbm, src_hbm)[k]
        target = (coarse_ref, fine_ref, valid_ref, src_ref)[k]
        return pltpu.make_async_copy(source, target, sems.at[k])

    def piece_of(k, q):
        columns = pl.ds(q * quarter, quarter)
        return pltpu.make_async_copy(
            x_hbm.at[pl.ds(k * rows, rows), columns], x_ref.at[k, :, columns], x_sems.at[k, q]
        )

    @pl.when(step == 0)
    def _():
        for k in range(4):
            small(k).start()
        for k in range(steps):
            for q in range(4):
                piece_of(k, q).start()
        small(0).wait()
        small(1).wait()
        make_tables(coarse_ref, fine_ref, even_ref, odd_ref)

    for q in range(4):
        piece_of(step, q).wait()
    b0, b1, b2, b3 = (x_ref[step, :, q * quarter:(q + 1) * quarter] for q in range(4))
    x0, x1, x2, x3 = (b.astype(jnp.float32) for b in (b0, b1, b2, b3))
    y_ref[:, :quarter] = ((x0 + x2) + (x1 + x3)).astype(jnp.bfloat16)
    y_ref[:, quarter:2 * quarter] = ((x0 + x2) - (x1 + x3)).astype(jnp.bfloat16)
    y_ref[:, 2 * quarter:3 * quarter] = b0 - b2
    y_ref[:, 3 * quarter:] = b1 - b3

    @pl.when(step == 0)
    def _():
        small(2).wait()
        small(3).wait()
        shape = (n_rcv * w_step * n_own, rows)
        out_row = lax.broadcasted_iota(jnp.int32, shape, 0)
        column = lax.broadcasted_iota(jnp.int32, shape, 1)
        wanted = jnp.zeros(shape, jnp.int32)
        for i in range(n_rcv):
            for k in range(n_own):
                mine = (out_row // (w_step * n_own) == i) & (out_row % n_own == k)
                station = src_ref[(rcv ^ i) * n_own + k] - rcv * r_dev
                wanted = jnp.where(mine, station, wanted)
        inside = (wanted >= 0) & (wanted < r_dev)
        hit = inside & (column == wanted + (out_row // n_own) % w_step * r_dev)
        sel_ref[...] = hit.astype(jnp.float32).astype(jnp.bfloat16)

    def product(lhs, table):
        return jnp.dot(lhs, table, preferred_element_type=jnp.float32)

    spectra = [
        product(y_ref[:, :quarter], even_ref[:quarter]),
        product(y_ref[:, 2 * quarter:], odd_ref[:2 * quarter]),
        product(y_ref[:, quarter:2 * quarter], even_ref[quarter:]),
        product(y_ref[:, 2 * quarter:], odd_ref[2 * quarter:]),
    ]
    squares = sum(jnp.sum(s * s, axis=1, keepdims=True) for s in spectra)
    gain = lax.rsqrt(squares / F + 1e-06)
    row = lax.broadcasted_iota(jnp.int32, (rows, 1), 0)
    keep = jnp.zeros((rows, 1), jnp.float32)
    for t in range(w_step):
        own = (row >= t * r_dev) & (row < (t + 1) * r_dev)
        keep = jnp.where(own, valid_ref[step * w_step + t].astype(jnp.float32), keep)
    gain = gain * keep
    white = [s * gain for s in spectra]
    piece = white[0].shape[1] // n_win
    for d in range(n_win):
        columns = slice(d * piece, (d + 1) * piece)
        block = jnp.concatenate([part[:, columns] for part in white], axis=1)
        white_ref[d] = block.astype(jnp.bfloat16)
    for j in range(n_win):
        r_refs[j][...] = white_ref[win ^ j]
    count = w_step * n_own
    start = pl.multiple_of(step * count, count)
    for j in range(n_win):
        rows_of = product(sel_ref[...], white_ref[win ^ j]).astype(jnp.bfloat16)
        for i in range(n_rcv):
            q_refs[i][j, pl.ds(start, count), :] = rows_of[i * count:(i + 1) * count]


def spectra_call(traces, valid, src_station, n_win, n_rcv):
    w_dev, r_dev, samples = traces.shape
    n_src = src_station.shape[0]
    n_own = n_src // n_rcv
    steps = 4
    rows = w_dev * r_dev // steps
    lanes = 2 * F // n_win
    coarse, fine = (jnp.asarray(t) for t in angle_factors(samples, F, samples // 16, n_win))
    block = jax.ShapeDtypeStruct((w_dev * r_dev, lanes), jnp.bfloat16)
    picked = jax.ShapeDtypeStruct((n_win, w_dev * n_own, lanes), jnp.bfloat16)
    flops = 2 * w_dev * r_dev * (samples // 4) * 6 * (F // 2)
    hbm = pl.BlockSpec(memory_space=pltpu.HBM)
    return pl.pallas_call(
        functools.partial(spectra_kernel, n_win, n_rcv, w_dev, r_dev, n_src),
        grid=(steps,),
        in_specs=[hbm] * 5,
        out_specs=[pl.BlockSpec((rows, lanes), lambda g: (g, 0))] * n_win
        + [pl.BlockSpec(picked.shape, lambda g: (0, 0, 0))] * n_rcv,
        out_shape=[block] * n_win + [picked] * n_rcv,
        scratch_shapes=[
            pltpu.VMEM((steps, rows, samples), jnp.bfloat16),
            pltpu.VMEM((rows, samples), jnp.bfloat16),
            pltpu.VMEM((n_win, rows, lanes), jnp.bfloat16),
            pltpu.VMEM((n_src * (w_dev // steps), rows), jnp.bfloat16),
            pltpu.VMEM((samples // 2, F // 2), jnp.bfloat16),
            pltpu.VMEM((samples, F // 2), jnp.bfloat16),
            pltpu.VMEM(coarse.shape, jnp.float32),
            pltpu.VMEM(fine.shape, jnp.float32),
            pltpu.SMEM(valid.shape, jnp.int32),
            pltpu.SMEM(src_station.shape, jnp.int32),
            pltpu.SemaphoreType.DMA((4,)),
            pltpu.SemaphoreType.DMA((steps, 4)),
        ],
        compiler_params=pltpu.CompilerParams(vmem_limit_bytes=48 * 2**20),
        cost_estimate=pl.CostEstimate(
            flops=flops, bytes_accessed=w_dev * r_dev * samples * 2, transcendentals=0
        ),
        name="spectra",
    )(*(in_hbm(x) for x in (valid, src_station, traces.reshape(w_dev * r_dev, samples), coarse, fine)))


def bin_order(lanes):
    quarter = lanes // 8
    lane = lax.broadcasted_iota(jnp.int32, (lanes, lanes), 1)
    row = lax.broadcasted_iota(jnp.int32, (lanes, lanes), 0)
    part = (lane // quarter) % 2
    bin_of = 4 * (lane % quarter) + lane // (2 * quarter)
    hit = row == part * (lanes // 2) + bin_of
    return hit.astype(jnp.float32).astype(jnp.bfloat16)


def turn_kernel(w_dev, r_dev, x_ref, out_ref, rows_ref):
    lanes = x_ref.shape[1]
    bins = lanes // 2
    pad = out_ref.shape[2] // 2
    order = bin_order(lanes)
    for w in range(w_dev):
        turned = lax.dot_general(
            order, x_ref[w * r_dev:(w + 1) * r_dev], (((1,), (1,)), ((), ())),
            preferred_element_type=jnp.float32,
        )
        rows_ref[pl.ds(w, lanes, stride=w_dev), :r_dev] = turned
    rr = rows_ref[:bins * w_dev].reshape(bins, w_dev, pad)
    ri = rows_ref[bins * w_dev:].reshape(bins, w_dev, pad)
    out_ref[:, :, :pad] = jnp.concatenate([rr, ri], axis=1).astype(jnp.bfloat16)
    out_ref[:, :, pad:] = jnp.concatenate([ri, -rr], axis=1).astype(jnp.bfloat16)


def turn_call(block, w_dev, r_dev):
    lanes = block.shape[1]
    pad = 128
    return pl.pallas_call(
        functools.partial(turn_kernel, w_dev, r_dev),
        in_specs=[pl.BlockSpec(memory_space=VMEM)],
        out_specs=pl.BlockSpec(memory_space=VMEM),
        out_shape=jax.ShapeDtypeStruct((lanes // 2, 2 * w_dev, 2 * pad), jnp.bfloat16),
        scratch_shapes=[pltpu.VMEM((lanes * w_dev, pad), jnp.float32)],
        compiler_params=pltpu.CompilerParams(vmem_limit_bytes=16 * 2**20),
        cost_estimate=pl.CostEstimate(
            flops=2 * w_dev * lanes * lanes * pad, bytes_accessed=2 * 2**20, transcendentals=0
        ),
        name="turn",
    )(block)


def merge_kernel(*refs):
    picked = refs[:-5]
    outs = refs[-4:]
    for j, out_ref in enumerate(outs):
        total = picked[0][j].astype(jnp.float32)
        for q_ref in picked[1:]:
            total = total + q_ref[j].astype(jnp.float32)
        out_ref[...] = total.astype(jnp.bfloat16)


def merge_call(picked, after):
    n_win, rows, lanes = picked[0].shape
    vmem = pl.BlockSpec(memory_space=VMEM)
    return pl.pallas_call(
        merge_kernel,
        in_specs=[vmem] * len(picked) + [pl.BlockSpec(memory_space=pl.ANY)],
        out_specs=[vmem] * n_win,
        out_shape=[jax.ShapeDtypeStruct((rows, lanes), jnp.bfloat16)] * n_win,
        compiler_params=pltpu.CompilerParams(vmem_limit_bytes=4 * 2**20),
        cost_estimate=pl.CostEstimate(flops=2**18, bytes_accessed=2**19, transcendentals=0),
        name="merge",
    )(*picked, after)


def stacks_kernel(shares, n_win, w_dev, r_dev, n_own, bins, *refs):
    t_refs = refs[:n_win]
    s_refs = refs[n_win:n_win + len(shares)]
    out_hbm, srow_ref, left_ref, prod_ref, out_ref, sems = refs[-6:]
    lanes = 2 * bins
    windows = n_win * w_dev
    count = len(shares) * n_own
    pad = 128
    rcv = lax.axis_index("rcv")

    def product(lhs, rhs, dims=(((1,), (0,)), ((), ()))):
        return lax.dot_general(lhs, rhs, dims, preferred_element_type=jnp.float32)

    order = bin_order(lanes)
    both = order[:bins] + order[bins:]
    lane = lax.broadcasted_iota(jnp.int32, (w_dev, lanes), 1)
    real = (lane // (bins // 4)) % 2 == 0

    for k, s_ref in enumerate(s_refs):
        for j in range(n_win):
            block = s_ref[j].astype(jnp.float32)
            for h in range(lanes // pad):
                half = block[:, h * pad:(h + 1) * pad]
                srow_ref[h, pl.ds((k * n_win + j) * w_dev * n_own, w_dev * n_own), :] = half
    for s in range(count):
        first = s // n_own * windows * n_own + s % n_own
        values = jnp.concatenate(
            [srow_ref[h, pl.ds(first, windows, stride=n_own), :] for h in range(lanes // pad)],
            axis=1,
        )
        stacked = []
        for j in range(n_win):
            own = values[j * w_dev:(j + 1) * w_dev]
            stacked += [jnp.where(real, own, 0.0), jnp.where(real, 0.0, own)]
        stacked = jnp.concatenate(stacked, axis=0).astype(jnp.bfloat16)
        turned = product(both, stacked, (((1,), (1,)), ((), ())))
        left_ref[pl.ds(s, bins, stride=count), :2 * windows] = turned

    for f in range(bins):
        right = jnp.concatenate([t_ref[f] for t_ref in t_refs], axis=0)
        left = left_ref[pl.ds(f * count, count), :2 * windows].astype(jnp.bfloat16)
        result = product(left, right)
        for c in range(2):
            prod_ref[c, pl.ds(f, count, stride=bins), :] = result[:, c * pad:(c + 1) * pad]

    scale = 1.0 / math.sqrt(windows)
    copies = []
    for s in range(count):
        for c in range(2):
            turned = prod_ref[c, s * bins:(s + 1) * bins, :].T
            out_ref[s, pl.ds(c, r_dev, stride=2), :] = turned[:r_dev] * scale
        row = (rcv ^ shares[s // n_own]) * n_own + s % n_own
        copies.append(pltpu.make_async_copy(out_ref.at[s], out_hbm.at[row], sems.at[s]))
        copies[-1].start()
    for copy in copies:
        copy.wait()


def stacks_call(out, turned, sources, shares, n_rcv, w_dev, r_dev, bins):
    n_win = len(turned)
    n_own = sources[0].shape[1] // w_dev
    windows = n_win * w_dev
    count = len(shares) * n_own
    whole = pl.BlockSpec(memory_space=VMEM)
    args = list(turned) + [sources[i] for i in shares]
    specs = [whole] * len(args)
    aliases = {}
    if out is not None:
        aliases = {len(args): 0}
        args.append(out)
        specs.append(pl.BlockSpec(memory_space=pl.ANY))
    return pl.pallas_call(
        functools.partial(stacks_kernel, shares, n_win, w_dev, r_dev, n_own, bins),
        in_specs=specs,
        out_specs=pl.BlockSpec(memory_space=pltpu.HBM),
        out_shape=jax.ShapeDtypeStruct((n_rcv * n_own, 2 * r_dev, bins), jnp.float32),
        input_output_aliases=aliases,
        scratch_shapes=[
            pltpu.VMEM((2 * bins // 128, windows * count, 128), jnp.float32),
            pltpu.VMEM((bins * count, 128), jnp.float32),
            pltpu.VMEM((2, count * bins, 128), jnp.float32),
            pltpu.VMEM((count, 2 * r_dev, bins), jnp.float32),
            pltpu.SemaphoreType.DMA((count,)),
        ],
        compiler_params=pltpu.CompilerParams(vmem_limit_bytes=20 * 2**20),
        cost_estimate=pl.CostEstimate(
            flops=8 * windows * count * r_dev * bins, bytes_accessed=6 * 2**20, transcendentals=0
        ),
        name="stacks",
    )(*args)


def swap(value, axis, by):
    size = lax.axis_size(axis)
    return lax.ppermute(value, axis, [(i, i ^ by) for i in range(size)])


def body(traces, valid, src_station):
    w_dev, r_dev, samples = traces.shape
    n_src = src_station.shape[0]
    n_win = lax.axis_size("win")
    n_rcv = lax.axis_size("rcv")
    bins = F // n_win

    out = spectra_call(traces, valid, src_station, n_win, n_rcv)
    received, picked = out[:n_win], out[n_win:]

    picked = [picked[0]] + [swap(picked[i], "rcv", i) for i in range(1, n_rcv)]
    received = [received[0]] + [swap(received[j], "win", j) for j in range(1, n_win)]
    merged = merge_call(picked, received[2])
    blocks = [merged[0]] + [swap(merged[j], "win", j) for j in range(1, n_win)]
    blocks = jnp.stack(blocks, axis=0)
    sources = [blocks] + [swap(blocks, "rcv", i) for i in range(1, n_rcv)]
    turned = [turn_call(block, w_dev, r_dev) for block in received]
    half = n_rcv // 2
    sizes = (n_rcv, w_dev, r_dev, bins)
    stacks = stacks_call(None, turned, sources, tuple(range(half)), *sizes)
    stacks = stacks_call(stacks, turned, sources, tuple(range(half, n_rcv)), *sizes)
    return stacks.reshape(n_src, r_dev, 2, bins)


def correlate(received, sources):
    rr = received[:, :, 0]
    ri = received[:, :, 1]
    sr = sources[:, :, 0]
    si = sources[:, :, 1]
    real = jnp.einsum("wsf,wrf->srf", sr, rr, preferred_element_type=jnp.float32)
    real = real + jnp.einsum("wsf,wrf->srf", si, ri, preferred_element_type=jnp.float32)
    imag = jnp.einsum("wsf,wrf->srf", sr, ri, preferred_element_type=jnp.float32)
    imag = imag - jnp.einsum("wsf,wrf->srf", si, rr, preferred_element_type=jnp.float32)
    return jnp.stack([real, imag], axis=2)


def body_any(traces, valid, src_station):
    w_dev, r_dev, samples = traces.shape
    n_win = lax.axis_size("win")
    n_rcv = lax.axis_size("rcv")
    bins = F // n_win
    table = jnp.asarray(band_table(samples, F, samples // 16))
    spectra = jnp.dot(
        traces.reshape(w_dev * r_dev, samples), table, preferred_element_type=jnp.float32
    )
    spectra = spectra.reshape(w_dev, r_dev, 2, F)
    power = jnp.sum(spectra * spectra, axis=(2, 3), keepdims=True) / F
    keep = valid.astype(jnp.float32)[:, None, None, None]
    white = (spectra * lax.rsqrt(power + 1e-06) * keep).astype(jnp.bfloat16)
    blocks = white.reshape(w_dev, r_dev, 2, n_win, bins).transpose(3, 0, 1, 2, 4)
    me = lax.axis_index("win")
    offset = lax.axis_index("rcv") * r_dev
    station_ids = offset + jnp.arange(r_dev, dtype=jnp.int32)
    selector = (src_station[:, None] == station_ids[None, :]).astype(jnp.bfloat16)
    received = []
    for j in range(n_win):
        block = lax.dynamic_index_in_dim(blocks, me ^ j, 0, keepdims=False)
        received.append(swap(block, "win", j) if j else block)
    received = jnp.concatenate(received, axis=0)
    rows = jnp.einsum("sr,wrcf->wscf", selector, received, preferred_element_type=jnp.float32)
    rows = lax.all_to_all(rows.astype(jnp.bfloat16), "rcv", 0, 0, tiled=True)
    rows = rows.reshape((n_rcv, -1) + rows.shape[1:])
    merged = jnp.sum(rows.astype(jnp.float32), axis=0).astype(jnp.bfloat16)
    sources = lax.all_gather(merged, "rcv", axis=0, tiled=True)
    return correlate(received, sources) * (1.0 / math.sqrt(w_dev * n_win))


def solution(mesh):
    sizes = (mesh.shape["win"], mesh.shape["rcv"])
    return jax.shard_map(
        body if sizes == (4, 4) else body_any,
        mesh=mesh,
        in_specs=(P("win", ("groups", "rcv"), None), P(("groups", "win")), P("groups")),
        out_specs=P(None, ("groups", "rcv"), None, "win"),
        check_vma=False,
    )
```

```python
import functools
import math

import jax
import jax.numpy as jnp
import numpy as np
from jax import lax
from jax.experimental import pallas as pl
from jax.experimental.pallas import tpu as pltpu
from jax.sharding import PartitionSpec as P

F = 512
SMEM = pltpu.MemorySpace.SMEM
VMEM = pltpu.MemorySpace.VMEM


def angles(samples, freqs, count):
    phase = samples[:, None] * freqs[None, :] % count
    return phase.astype(np.float64) * (2.0 * math.pi / count)


def band_table(count, bins, first):
    angle = angles(np.arange(count), first + np.arange(bins), count)
    return np.concatenate([np.cos(angle), -np.sin(angle)], axis=1).astype(jnp.bfloat16)


FINE = 32


def angle_factors(count, bins, first, n_win):
    j = np.arange(bins // 4).reshape(n_win, 1, -1)
    turn = np.array([0.0, 0.5 * math.pi]).reshape(1, 2, 1)

    def factors(samples, shift):
        out = []
        for m in range(4):
            freqs = np.broadcast_to(first + 4 * j + m, (n_win, 2, bins // 4 // n_win))
            angle = angles(samples, freqs.reshape(-1), count)
            angle = angle + np.broadcast_to(shift, freqs.shape).reshape(1, -1)
            out.append(np.stack([np.cos(angle), np.sin(angle)]))
        return np.stack(out).astype(np.float32)

    return factors(np.arange(0, count // 4, FINE), 0.0 * turn), factors(np.arange(FINE), turn)


def make_tables(coarse_ref, fine_ref, even_ref, odd_ref):
    steps = coarse_ref.shape[2]
    quarter = steps * FINE
    for m in range(4):
        cos_b, sin_b = fine_ref[m, 0], fine_ref[m, 1]
        out_ref = odd_ref if m % 2 else even_ref
        base = (m // 2) * (2 * quarter if m % 2 else quarter)
        for a in range(steps):
            cos_a, sin_a = (coarse_ref[m, k, a:a + 1, :] for k in range(2))
            rows = slice(base + a * FINE, base + (a + 1) * FINE)
            out_ref[rows, :] = (cos_a * cos_b - sin_a * sin_b).astype(jnp.bfloat16)
            if m % 2:
                if m == 1:
                    cos_a, sin_a = -cos_a, -sin_a
                rows = slice(rows.start + quarter, rows.stop + quarter)
                out_ref[rows, :] = (cos_a * sin_b + sin_a * cos_b).astype(jnp.bfloat16)


def in_hbm(value):
    return pltpu.with_memory_space_constraint(value, pltpu.HBM)


def order_sources(src_ref, r_dev, n_own, order_ref, plan_ref):
    n_src = src_ref.shape[0]
    size = order_ref.shape
    down = lax.broadcasted_iota(jnp.int32, size, 0).astype(jnp.float32)
    along = lax.broadcasted_iota(jnp.int32, size, 1).astype(jnp.float32)
    none = jnp.full(size, float(2**20), jnp.float32)
    column, row = none, none
    for s in range(n_src):
        station = src_ref[s].astype(jnp.float32)
        column = jnp.where(down == s, station, column)
        row = jnp.where(along == s, station, row)
    rank_along = jnp.sum((column < row).astype(jnp.float32), axis=0, keepdims=True)
    rank_down = jnp.sum((row < column).astype(jnp.float32), axis=1, keepdims=True)
    sorted_down = jnp.sum(jnp.where(rank_along == down, row, 0.0), axis=1, keepdims=True)
    at_place = rank_down == along
    sorted_along = jnp.sum(jnp.where(at_place, column, 0.0), axis=0, keepdims=True)
    source_along = jnp.sum(jnp.where(at_place, down, 0.0), axis=0, keepdims=True)
    order_ref[...] = jnp.broadcast_to(sorted_down, size)
    place = along[:1]
    owner, share = jnp.zeros_like(place), jnp.zeros_like(place)
    for z in range(1, n_src // n_own):
        owner = owner + (sorted_along >= z * r_dev).astype(jnp.float32)
        share = share + (place >= z * n_own).astype(jnp.float32)
    far = jnp.where((place < n_src) & (jnp.abs(owner - share) > 1.5), 1.0, 0.0)
    far = jnp.max(far, axis=1, keepdims=True)
    plan = jnp.where(down[:8] == 0, source_along, far)
    plan_ref[...] = plan.astype(jnp.int32)


def spectra_kernel(n_win, n_rcv, w_dev, r_dev, n_src, valid_hbm, src_hbm, x_hbm, coarse_hbm, fine_hbm, *refs):
    r_refs = refs[:n_win]
    q_refs = refs[n_win:n_win + n_rcv]
    plan_ref = refs[n_win + n_rcv]
    (x_ref, y_ref, white_ref, sel_ref, order_ref, even_ref, odd_ref, coarse_ref, fine_ref,
     valid_ref, src_ref, sems, x_sems) = refs[n_win + n_rcv + 1:]
    step = pl.program_id(0)
    steps, rows, samples = x_ref.shape
    w_step = rows // r_dev
    n_own = n_src // n_rcv
    quarter = samples // 4
    win = lax.axis_index("win")
    rcv = lax.axis_index("rcv")

    def small(k):
        source = (coarse_hbm, fine_hbm, valid_hbm, src_hbm)[k]
        target = (coarse_ref, fine_ref, valid_ref, src_ref)[k]
        return pltpu.make_async_copy(source, target, sems.at[k])

    def piece_of(k, q):
        columns = pl.ds(q * quarter, quarter)
        return pltpu.make_async_copy(
            x_hbm.at[pl.ds(k * rows, rows), columns], x_ref.at[k, :, columns], x_sems.at[k, q]
        )

    @pl.when(step == 0)
    def _():
        for k in range(4):
            small(k).start()
        for k in range(steps):
            for q in range(4):
                piece_of(k, q).start()
        small(0).wait()
        small(1).wait()
        make_tables(coarse_ref, fine_ref, even_ref, odd_ref)

    for q in range(4):
        piece_of(step, q).wait()
    b0, b1, b2, b3 = (x_ref[step, :, q * quarter:(q + 1) * quarter] for q in range(4))
    x0, x1, x2, x3 = (b.astype(jnp.float32) for b in (b0, b1, b2, b3))
    y_ref[:, :quarter] = ((x0 + x2) + (x1 + x3)).astype(jnp.bfloat16)
    y_ref[:, quarter:2 * quarter] = ((x0 + x2) - (x1 + x3)).astype(jnp.bfloat16)
    y_ref[:, 2 * quarter:3 * quarter] = b0 - b2
    y_ref[:, 3 * quarter:] = b1 - b3

    @pl.when(step == 0)
    def _():
        small(2).wait()
        small(3).wait()
        order_sources(src_ref, r_dev, n_own, order_ref, plan_ref)
        stations = []
        for d in range(n_rcv):
            share = pl.multiple_of(((rcv + d) % n_rcv) * n_own, n_own)
            column = order_ref[pl.ds(share, n_own), 0:1]
            stations.append(jnp.concatenate([column] * w_step, axis=0))
        wanted = jnp.concatenate(stations, axis=0).astype(jnp.int32) - rcv * r_dev
        shape = (n_rcv * w_step * n_own, rows)
        out_row = lax.broadcasted_iota(jnp.int32, shape, 0)
        column = lax.broadcasted_iota(jnp.int32, shape, 1)
        inside = (wanted >= 0) & (wanted < r_dev)
        hit = inside & (column == wanted + (out_row // n_own) % w_step * r_dev)
        sel_ref[...] = hit.astype(jnp.float32).astype(jnp.bfloat16)

    def product(lhs, table):
        return jnp.dot(lhs, table, preferred_element_type=jnp.float32)

    spectra = [
        product(y_ref[:, :quarter], even_ref[:quarter]),
        product(y_ref[:, 2 * quarter:], odd_ref[:2 * quarter]),
        product(y_ref[:, quarter:2 * quarter], even_ref[quarter:]),
        product(y_ref[:, 2 * quarter:], odd_ref[2 * quarter:]),
    ]
    squares = sum(jnp.sum(s * s, axis=1, keepdims=True) for s in spectra)
    gain = lax.rsqrt(squares / F + 1e-06)
    row = lax.broadcasted_iota(jnp.int32, (rows, 1), 0)
    keep = jnp.zeros((rows, 1), jnp.float32)
    for t in range(w_step):
        own = (row >= t * r_dev) & (row < (t + 1) * r_dev)
        keep = jnp.where(own, valid_ref[step * w_step + t].astype(jnp.float32), keep)
    gain = gain * keep
    white = [s * gain for s in spectra]
    piece = white[0].shape[1] // n_win
    for d in range(n_win):
        columns = slice(d * piece, (d + 1) * piece)
        block = jnp.concatenate([part[:, columns] for part in white], axis=1)
        white_ref[d] = block.astype(jnp.bfloat16)
    for j in range(n_win):
        r_refs[j][...] = white_ref[win ^ j]
    count = w_step * n_own
    start = pl.multiple_of(step * count, count)
    for j in range(n_win):
        rows_of = product(sel_ref[...], white_ref[win ^ j]).astype(jnp.bfloat16)
        for i in range(n_rcv):
            q_refs[i][j, pl.ds(start, count), :] = rows_of[i * count:(i + 1) * count]


def spectra_call(traces, valid, src_station, n_win, n_rcv):
    w_dev, r_dev, samples = traces.shape
    n_src = src_station.shape[0]
    n_own = n_src // n_rcv
    steps = 4
    rows = w_dev * r_dev // steps
    lanes = 2 * F // n_win
    coarse, fine = (jnp.asarray(t) for t in angle_factors(samples, F, samples // 16, n_win))
    block = jax.ShapeDtypeStruct((w_dev * r_dev, lanes), jnp.bfloat16)
    picked = jax.ShapeDtypeStruct((n_win, w_dev * n_own, lanes), jnp.bfloat16)
    flops = 2 * w_dev * r_dev * (samples // 4) * 6 * (F // 2)
    hbm = pl.BlockSpec(memory_space=pltpu.HBM)
    return pl.pallas_call(
        functools.partial(spectra_kernel, n_win, n_rcv, w_dev, r_dev, n_src),
        grid=(steps,),
        in_specs=[hbm] * 5,
        out_specs=[pl.BlockSpec((rows, lanes), lambda g: (g, 0))] * n_win
        + [pl.BlockSpec(picked.shape, lambda g: (0, 0, 0))] * n_rcv
        + [pl.BlockSpec((8, 128), lambda g: (0, 0))],
        out_shape=[block] * n_win + [picked] * n_rcv + [jax.ShapeDtypeStruct((8, 128), jnp.int32)],
        scratch_shapes=[
            pltpu.VMEM((steps, rows, samples), jnp.bfloat16),
            pltpu.VMEM((rows, samples), jnp.bfloat16),
            pltpu.VMEM((n_win, rows, lanes), jnp.bfloat16),
            pltpu.VMEM((n_src * (w_dev // steps), rows), jnp.bfloat16),
            pltpu.VMEM((n_src, 128), jnp.float32),
            pltpu.VMEM((samples // 2, F // 2), jnp.bfloat16),
            pltpu.VMEM((samples, F // 2), jnp.bfloat16),
            pltpu.VMEM(coarse.shape, jnp.float32),
            pltpu.VMEM(fine.shape, jnp.float32),
            pltpu.SMEM(valid.shape, jnp.int32),
            pltpu.SMEM(src_station.shape, jnp.int32),
            pltpu.SemaphoreType.DMA((4,)),
            pltpu.SemaphoreType.DMA((steps, 4)),
        ],
        compiler_params=pltpu.CompilerParams(vmem_limit_bytes=48 * 2**20),
        cost_estimate=pl.CostEstimate(
            flops=flops, bytes_accessed=w_dev * r_dev * samples * 2, transcendentals=0
        ),
        name="spectra",
    )(*(in_hbm(x) for x in (valid, src_station, traces.reshape(w_dev * r_dev, samples), coarse, fine)))


def bin_order(lanes):
    quarter = lanes // 8
    lane = lax.broadcasted_iota(jnp.int32, (lanes, lanes), 1)
    row = lax.broadcasted_iota(jnp.int32, (lanes, lanes), 0)
    part = (lane // quarter) % 2
    bin_of = 4 * (lane % quarter) + lane // (2 * quarter)
    hit = row == part * (lanes // 2) + bin_of
    return hit.astype(jnp.float32).astype(jnp.bfloat16)


def turn_kernel(w_dev, r_dev, x_ref, out_ref, rows_ref):
    lanes = x_ref.shape[1]
    bins = lanes // 2
    pad = out_ref.shape[2] // 2
    order = bin_order(lanes)
    for w in range(w_dev):
        turned = lax.dot_general(
            order, x_ref[w * r_dev:(w + 1) * r_dev], (((1,), (1,)), ((), ())),
            preferred_element_type=jnp.float32,
        )
        rows_ref[pl.ds(w, lanes, stride=w_dev), :r_dev] = turned
    rr = rows_ref[:bins * w_dev].reshape(bins, w_dev, pad)
    ri = rows_ref[bins * w_dev:].reshape(bins, w_dev, pad)
    out_ref[:, :, :pad] = jnp.concatenate([rr, ri], axis=1).astype(jnp.bfloat16)
    out_ref[:, :, pad:] = jnp.concatenate([ri, -rr], axis=1).astype(jnp.bfloat16)


def turn_call(block, w_dev, r_dev):
    lanes = block.shape[1]
    pad = 128
    return pl.pallas_call(
        functools.partial(turn_kernel, w_dev, r_dev),
        in_specs=[pl.BlockSpec(memory_space=VMEM)],
        out_specs=pl.BlockSpec(memory_space=VMEM),
        out_shape=jax.ShapeDtypeStruct((lanes // 2, 2 * w_dev, 2 * pad), jnp.bfloat16),
        scratch_shapes=[pltpu.VMEM((lanes * w_dev, pad), jnp.float32)],
        compiler_params=pltpu.CompilerParams(vmem_limit_bytes=16 * 2**20),
        cost_estimate=pl.CostEstimate(
            flops=2 * w_dev * lanes * lanes * pad, bytes_accessed=2 * 2**20, transcendentals=0
        ),
        name="turn",
    )(block)


def merge_kernel(n_win, *refs):
    picked, outs = refs[:-n_win], refs[-n_win:]
    for j, out_ref in enumerate(outs):
        total = picked[0][j].astype(jnp.float32)
        for q_ref in picked[1:]:
            total = total + q_ref[j].astype(jnp.float32)
        out_ref[...] = total.astype(jnp.bfloat16)


def merge_call(*picked):
    n_win, rows, lanes = picked[0].shape
    vmem = pl.BlockSpec(memory_space=VMEM)
    return pl.pallas_call(
        functools.partial(merge_kernel, n_win),
        in_specs=[vmem] * len(picked),
        out_specs=[vmem] * n_win,
        out_shape=[jax.ShapeDtypeStruct((rows, lanes), jnp.bfloat16)] * n_win,
        compiler_params=pltpu.CompilerParams(vmem_limit_bytes=4 * 2**20),
        cost_estimate=pl.CostEstimate(flops=2**18, bytes_accessed=2**19, transcendentals=0),
        name="merge",
    )(*picked)


def join_kernel(*refs):
    blocks, out_ref = refs[:-2], refs[-1]
    for j, block_ref in enumerate(blocks):
        out_ref[j] = block_ref[...]


def join_call(blocks, after):
    rows, lanes = blocks[0].shape
    vmem = pl.BlockSpec(memory_space=VMEM)
    return pl.pallas_call(
        join_kernel,
        in_specs=[vmem] * len(blocks) + [pl.BlockSpec(memory_space=pl.ANY)],
        out_specs=vmem,
        out_shape=jax.ShapeDtypeStruct((len(blocks), rows, lanes), jnp.bfloat16),
        compiler_params=pltpu.CompilerParams(vmem_limit_bytes=4 * 2**20),
        cost_estimate=pl.CostEstimate(flops=2**18, bytes_accessed=2**19, transcendentals=0),
        name="join",
    )(*blocks, after)


def stacks_kernel(shares, n_win, w_dev, r_dev, n_own, bins, plan_ref, *refs):
    t_refs = refs[:n_win]
    s_refs = refs[n_win:n_win + len(shares)]
    out_hbm, srow_ref, left_ref, prod_ref, out_ref, sems = refs[-6:]
    lanes = 2 * bins
    windows = n_win * w_dev
    count = len(shares) * n_own
    pad = 128
    rcv = lax.axis_index("rcv")

    def product(lhs, rhs, dims=(((1,), (0,)), ((), ()))):
        return lax.dot_general(lhs, rhs, dims, preferred_element_type=jnp.float32)

    order = bin_order(lanes)
    both = order[:bins] + order[bins:]
    lane = lax.broadcasted_iota(jnp.int32, (w_dev, lanes), 1)
    real = (lane // (bins // 4)) % 2 == 0

    for k, s_ref in enumerate(s_refs):
        for j in range(n_win):
            block = s_ref[j].astype(jnp.float32)
            for h in range(lanes // pad):
                half = block[:, h * pad:(h + 1) * pad]
                srow_ref[h, pl.ds((k * n_win + j) * w_dev * n_own, w_dev * n_own), :] = half
    for s in range(count):
        first = s // n_own * windows * n_own + s % n_own
        values = jnp.concatenate(
            [srow_ref[h, pl.ds(first, windows, stride=n_own), :] for h in range(lanes // pad)],
            axis=1,
        )
        stacked = []
        for j in range(n_win):
            own = values[j * w_dev:(j + 1) * w_dev]
            stacked += [jnp.where(real, own, 0.0), jnp.where(real, 0.0, own)]
        stacked = jnp.concatenate(stacked, axis=0).astype(jnp.bfloat16)
        turned = product(both, stacked, (((1,), (1,)), ((), ())))
        left_ref[pl.ds(s, bins, stride=count), :2 * windows] = turned

    for f in range(bins):
        right = jnp.concatenate([t_ref[f] for t_ref in t_refs], axis=0)
        left = left_ref[pl.ds(f * count, count), :2 * windows].astype(jnp.bfloat16)
        result = product(left, right)
        for c in range(2):
            prod_ref[c, pl.ds(f, count, stride=bins), :] = result[:, c * pad:(c + 1) * pad]

    scale = 1.0 / math.sqrt(windows)
    copies = []
    for s in range(count):
        for c in range(2):
            turned = prod_ref[c, s * bins:(s + 1) * bins, :].T
            out_ref[s, pl.ds(c, r_dev, stride=2), :] = turned[:r_dev] * scale
        row = plan_ref[0, (rcv ^ shares[s // n_own]) * n_own + s % n_own]
        copies.append(pltpu.make_async_copy(out_ref.at[s], out_hbm.at[row], sems.at[s]))
        copies[-1].start()
    for copy in copies:
        copy.wait()


def stacks_call(out, plan, turned, sources, shares, n_rcv, w_dev, r_dev, bins):
    n_win = len(turned)
    n_own = sources[0].shape[1] // w_dev
    windows = n_win * w_dev
    count = len(shares) * n_own
    whole = pl.BlockSpec(memory_space=VMEM)
    args = [plan] + list(turned) + [sources[i] for i in shares]
    specs = [pl.BlockSpec(memory_space=SMEM)] + [whole] * (len(args) - 1)
    aliases = {}
    if out is not None:
        aliases = {len(args): 0}
        args.append(out)
        specs.append(pl.BlockSpec(memory_space=pl.ANY))
    return pl.pallas_call(
        functools.partial(stacks_kernel, shares, n_win, w_dev, r_dev, n_own, bins),
        in_specs=specs,
        out_specs=pl.BlockSpec(memory_space=pltpu.HBM),
        out_shape=jax.ShapeDtypeStruct((n_rcv * n_own, 2 * r_dev, bins), jnp.float32),
        input_output_aliases=aliases,
        scratch_shapes=[
            pltpu.VMEM((2 * bins // 128, windows * count, 128), jnp.float32),
            pltpu.VMEM((bins * count, 128), jnp.float32),
            pltpu.VMEM((2, count * bins, 128), jnp.float32),
            pltpu.VMEM((count, 2 * r_dev, bins), jnp.float32),
            pltpu.SemaphoreType.DMA((count,)),
        ],
        compiler_params=pltpu.CompilerParams(vmem_limit_bytes=20 * 2**20),
        cost_estimate=pl.CostEstimate(
            flops=8 * windows * count * r_dev * bins, bytes_accessed=6 * 2**20, transcendentals=0
        ),
        name="stacks",
    )(*args)


def swap(value, axis, by):
    size = lax.axis_size(axis)
    return lax.ppermute(value, axis, [(i, i ^ by) for i in range(size)])


def exchange_far(picked):
    n_rcv = len(picked)
    total = picked[0]
    for d in range(1, n_rcv):
        pairs = [(z, (z + d) % n_rcv) for z in range(n_rcv)]
        pairs = [(a, b) for a, b in pairs if abs(a - b) > 1]
        total = total + lax.ppermute(picked[d], "rcv", pairs)
    return total


def body(traces, valid, src_station):
    w_dev, r_dev, samples = traces.shape
    n_src = src_station.shape[0]
    n_win = lax.axis_size("win")
    n_rcv = lax.axis_size("rcv")
    bins = F // n_win

    out = spectra_call(traces, valid, src_station, n_win, n_rcv)
    received, picked, plan = out[:n_win], out[n_win:n_win + n_rcv], out[-1]

    right = lax.ppermute(picked[1], "rcv", [(z, z + 1) for z in range(n_rcv - 1)])
    left = lax.ppermute(picked[-1], "rcv", [(z + 1, z) for z in range(n_rcv - 1)])
    own = lax.cond(plan[1, 0] > 0, exchange_far, lambda q: q[0], picked)
    received = [received[0]] + [swap(received[j], "win", j) for j in range(1, n_win)]
    merged = merge_call(own, right, left)
    blocks = [merged[0]] + [swap(merged[j], "win", j) for j in range(1, n_win)]
    blocks = join_call(blocks, received[2])
    sources = [blocks] + [swap(blocks, "rcv", i) for i in range(1, n_rcv)]
    turned = [turn_call(block, w_dev, r_dev) for block in received]
    half = n_rcv // 2
    sizes = (n_rcv, w_dev, r_dev, bins)
    stacks = stacks_call(None, plan, turned, sources, tuple(range(half)), *sizes)
    stacks = stacks_call(stacks, plan, turned, sources, tuple(range(half, n_rcv)), *sizes)
    return stacks.reshape(n_src, r_dev, 2, bins)


def correlate(received, sources):
    rr = received[:, :, 0]
    ri = received[:, :, 1]
    sr = sources[:, :, 0]
    si = sources[:, :, 1]
    real = jnp.einsum("wsf,wrf->srf", sr, rr, preferred_element_type=jnp.float32)
    real = real + jnp.einsum("wsf,wrf->srf", si, ri, preferred_element_type=jnp.float32)
    imag = jnp.einsum("wsf,wrf->srf", sr, ri, preferred_element_type=jnp.float32)
    imag = imag - jnp.einsum("wsf,wrf->srf", si, rr, preferred_element_type=jnp.float32)
    return jnp.stack([real, imag], axis=2)


def body_any(traces, valid, src_station):
    w_dev, r_dev, samples = traces.shape
    n_win = lax.axis_size("win")
    n_rcv = lax.axis_size("rcv")
    bins = F // n_win
    table = jnp.asarray(band_table(samples, F, samples // 16))
    spectra = jnp.dot(
        traces.reshape(w_dev * r_dev, samples), table, preferred_element_type=jnp.float32
    )
    spectra = spectra.reshape(w_dev, r_dev, 2, F)
    power = jnp.sum(spectra * spectra, axis=(2, 3), keepdims=True) / F
    keep = valid.astype(jnp.float32)[:, None, None, None]
    white = (spectra * lax.rsqrt(power + 1e-06) * keep).astype(jnp.bfloat16)
    blocks = white.reshape(w_dev, r_dev, 2, n_win, bins).transpose(3, 0, 1, 2, 4)
    me = lax.axis_index("win")
    offset = lax.axis_index("rcv") * r_dev
    station_ids = offset + jnp.arange(r_dev, dtype=jnp.int32)
    selector = (src_station[:, None] == station_ids[None, :]).astype(jnp.bfloat16)
    received = []
    for j in range(n_win):
        block = lax.dynamic_index_in_dim(blocks, me ^ j, 0, keepdims=False)
        received.append(swap(block, "win", j) if j else block)
    received = jnp.concatenate(received, axis=0)
    rows = jnp.einsum("sr,wrcf->wscf", selector, received, preferred_element_type=jnp.float32)
    rows = lax.all_to_all(rows.astype(jnp.bfloat16), "rcv", 0, 0, tiled=True)
    rows = rows.reshape((n_rcv, -1) + rows.shape[1:])
    merged = jnp.sum(rows.astype(jnp.float32), axis=0).astype(jnp.bfloat16)
    sources = lax.all_gather(merged, "rcv", axis=0, tiled=True)
    return correlate(received, sources) * (1.0 / math.sqrt(w_dev * n_win))


def solution(mesh):
    sizes = (mesh.shape["win"], mesh.shape["rcv"])
    return jax.shard_map(
        body if sizes == (4, 4) else body_any,
        mesh=mesh,
        in_specs=(P("win", ("groups", "rcv"), None), P(("groups", "win")), P("groups")),
        out_specs=P(None, ("groups", "rcv"), None, "win"),
        check_vma=False,
    )
```

```python
import functools
import math

import jax
import jax.numpy as jnp
import numpy as np
from jax import lax
from jax.experimental import pallas as pl
from jax.experimental.pallas import tpu as pltpu
from jax.sharding import PartitionSpec as P

F = 512
SMEM = pltpu.MemorySpace.SMEM
VMEM = pltpu.MemorySpace.VMEM


def angles(samples, freqs, count):
    phase = samples[:, None] * freqs[None, :] % count
    return phase.astype(np.float64) * (2.0 * math.pi / count)


def band_table(count, bins, first):
    angle = angles(np.arange(count), first + np.arange(bins), count)
    return np.concatenate([np.cos(angle), -np.sin(angle)], axis=1).astype(jnp.bfloat16)


FINE = 32


def angle_factors(count, bins, first, n_win):
    j = np.arange(bins // 4).reshape(n_win, 1, -1)
    turn = np.array([0.0, 0.5 * math.pi]).reshape(1, 2, 1)

    def factors(samples, shift):
        out = []
        for m in range(4):
            freqs = np.broadcast_to(first + 4 * j + m, (n_win, 2, bins // 4 // n_win))
            angle = angles(samples, freqs.reshape(-1), count)
            angle = angle + np.broadcast_to(shift, freqs.shape).reshape(1, -1)
            out.append(np.stack([np.cos(angle), np.sin(angle)]))
        return np.stack(out).astype(np.float32)

    return factors(np.arange(0, count // 4, FINE), 0.0 * turn), factors(np.arange(FINE), turn)


def make_tables(coarse_ref, fine_ref, even_ref, odd_ref):
    steps = coarse_ref.shape[2]
    quarter = steps * FINE
    for m in range(4):
        cos_b, sin_b = fine_ref[m, 0], fine_ref[m, 1]
        out_ref = odd_ref if m % 2 else even_ref
        base = (m // 2) * (2 * quarter if m % 2 else quarter)
        for a in range(steps):
            cos_a, sin_a = (coarse_ref[m, k, a:a + 1, :] for k in range(2))
            rows = slice(base + a * FINE, base + (a + 1) * FINE)
            out_ref[rows, :] = (cos_a * cos_b - sin_a * sin_b).astype(jnp.bfloat16)
            if m % 2:
                if m == 1:
                    cos_a, sin_a = -cos_a, -sin_a
                rows = slice(rows.start + quarter, rows.stop + quarter)
                out_ref[rows, :] = (cos_a * sin_b + sin_a * cos_b).astype(jnp.bfloat16)


def in_hbm(value):
    return pltpu.with_memory_space_constraint(value, pltpu.HBM)


def order_sources(src_ref, r_dev, n_own, order_ref, plan_ref, flag_ref):
    n_src = src_ref.shape[0]
    size = order_ref.shape
    down = lax.broadcasted_iota(jnp.int32, size, 0).astype(jnp.float32)
    along = lax.broadcasted_iota(jnp.int32, size, 1).astype(jnp.float32)
    none = jnp.full(size, float(2**20), jnp.float32)
    column, row = none, none
    for s in range(n_src):
        station = src_ref[s].astype(jnp.float32)
        column = jnp.where(down == s, station, column)
        row = jnp.where(along == s, station, row)
    rank_along = jnp.sum((column < row).astype(jnp.float32), axis=0, keepdims=True)
    rank_down = jnp.sum((row < column).astype(jnp.float32), axis=1, keepdims=True)
    sorted_down = jnp.sum(jnp.where(rank_along == down, row, 0.0), axis=1, keepdims=True)
    at_place = rank_down == along
    sorted_along = jnp.sum(jnp.where(at_place, column, 0.0), axis=0, keepdims=True)
    source_along = jnp.sum(jnp.where(at_place, down, 0.0), axis=0, keepdims=True)
    order_ref[...] = jnp.broadcast_to(sorted_down, size)
    place = along[:1]
    owner, share = jnp.zeros_like(place), jnp.zeros_like(place)
    for z in range(1, n_src // n_own):
        owner = owner + (sorted_along >= z * r_dev).astype(jnp.float32)
        share = share + (place >= z * n_own).astype(jnp.float32)
    far = jnp.where((place < n_src) & (jnp.abs(owner - share) > 1.5), 1.0, 0.0)
    plan_ref[...] = jnp.broadcast_to(source_along, plan_ref.shape).astype(jnp.int32)
    flag_ref[0] = jnp.max(far).astype(jnp.int32)


def spectra_kernel(
    n_win, n_rcv, r_dev, split, valid_hbm, src_hbm, x_hbm, coarse_hbm, fine_hbm, *refs
):
    r_refs = refs[:n_win + 1]
    q_refs = refs[n_win + 1:n_win + 1 + n_rcv]
    (plan_ref, flag_ref, x_ref, y_ref, white_ref, sel_ref, order_ref, even_ref, odd_ref,
     coarse_ref, fine_ref, valid_ref, src_ref, sems, x_sems) = refs[n_win + 1 + n_rcv:]
    chunks, rows, samples = x_ref.shape
    w_step = rows // r_dev
    n_own = src_ref.shape[0] // n_rcv
    quarter = samples // 4
    win = lax.axis_index("win")
    rcv = lax.axis_index("rcv")

    def small(k):
        source = (coarse_hbm, fine_hbm, src_hbm, valid_hbm)[k]
        target = (coarse_ref, fine_ref, src_ref, valid_ref)[k]
        return pltpu.make_async_copy(source, target, sems.at[k])

    def chunk(k):
        return pltpu.make_async_copy(x_hbm.at[pl.ds(k * rows, rows)], x_ref.at[k], x_sems.at[k])

    for k in range(4):
        small(k).start()
    for k in range(chunks):
        chunk(k).start()
    small(0).wait()
    small(1).wait()
    make_tables(coarse_ref, fine_ref, even_ref, odd_ref)
    small(2).wait()
    order_sources(src_ref, r_dev, n_own, order_ref, plan_ref, flag_ref)
    stations = []
    for d in range(n_rcv):
        share = pl.multiple_of(((rcv + d) % n_rcv) * n_own, n_own)
        stations += [order_ref[pl.ds(share, n_own), 0:1]] * w_step
    wanted = jnp.concatenate(stations, axis=0).astype(jnp.int32) - rcv * r_dev
    shape = (n_rcv * w_step * n_own, rows)
    out_row = lax.broadcasted_iota(jnp.int32, shape, 0)
    column = lax.broadcasted_iota(jnp.int32, shape, 1)
    inside = (wanted >= 0) & (wanted < r_dev)
    hit = inside & (column == wanted + (out_row // n_own) % w_step * r_dev)
    sel_ref[...] = hit.astype(jnp.float32).astype(jnp.bfloat16)
    small(3).wait()

    def product(lhs, table):
        return jnp.dot(lhs, table, preferred_element_type=jnp.float32)

    def add_quarters(k, first, last):
        part = slice(first, last)
        b0, b1, b2, b3 = (x_ref[k, part, q * quarter:(q + 1) * quarter] for q in range(4))
        x0, x1, x2, x3 = (b.astype(jnp.float32) for b in (b0, b1, b2, b3))
        y_ref[k, part, :quarter] = ((x0 + x2) + (x1 + x3)).astype(jnp.bfloat16)
        y_ref[k, part, quarter:2 * quarter] = ((x0 + x2) - (x1 + x3)).astype(jnp.bfloat16)
        y_ref[k, part, 2 * quarter:3 * quarter] = b0 - b2
        y_ref[k, part, 3 * quarter:] = b1 - b3

    parts = 4
    size = rows // parts
    chunk(0).wait()
    add_quarters(0, 0, rows)
    row = lax.broadcasted_iota(jnp.int32, (rows, 1), 0)
    for k in range(chunks):
        more = k + 1 < chunks
        if more:
            chunk(k + 1).wait()
        spectra = []
        for m in range(4):
            if m % 2:
                table = odd_ref[(m // 2) * 2 * quarter:(m // 2 + 1) * 2 * quarter]
                spectra.append(product(y_ref[k, :, 2 * quarter:], table))
            else:
                half = slice((m // 2) * quarter, (m // 2 + 1) * quarter)
                spectra.append(product(y_ref[k, :, half], even_ref[half]))
            if more:
                add_quarters(k + 1, m * size, (m + 1) * size)
        squares = sum(jnp.sum(s * s, axis=1, keepdims=True) for s in spectra)
        gain = lax.rsqrt(squares / F + 1e-06)
        keep = jnp.zeros((rows, 1), jnp.float32)
        for t in range(w_step):
            own = (row >= t * r_dev) & (row < (t + 1) * r_dev)
            keep = jnp.where(own, valid_ref[k * w_step + t].astype(jnp.float32), keep)
        gain = gain * keep
        white = [s * gain for s in spectra]
        piece = white[0].shape[1] // n_win
        for d in range(n_win):
            columns = slice(d * piece, (d + 1) * piece)
            block = jnp.concatenate([part[:, columns] for part in white], axis=1)
            white_ref[k, d] = block.astype(jnp.bfloat16)
        count = w_step * n_own
        for j in range(n_win):
            block = white_ref[k, win ^ j]
            first, target = k * rows, r_refs[j]
            if j == split and k >= chunks // 2:
                first, target = first - chunks // 2 * rows, r_refs[n_win]
            target[first:first + rows, :] = block
            picked = product(sel_ref[...], block).astype(jnp.bfloat16)
            for d in range(n_rcv):
                q_refs[d][j, k * count:(k + 1) * count, :] = picked[d * count:(d + 1) * count]


def spectra_call(traces, valid, src_station, n_win, n_rcv, split):
    w_dev, r_dev, samples = traces.shape
    n_src = src_station.shape[0]
    n_own = n_src // n_rcv
    chunks = 4
    every = w_dev * r_dev
    rows = every // chunks
    lanes = 2 * F // n_win
    coarse, fine = (jnp.asarray(t) for t in angle_factors(samples, F, samples // 16, n_win))
    heights = [every // 2 if j == split else every for j in range(n_win)] + [every // 2]
    shapes = [jax.ShapeDtypeStruct((height, lanes), jnp.bfloat16) for height in heights]
    shapes += [jax.ShapeDtypeStruct((n_win, w_dev * n_own, lanes), jnp.bfloat16)] * n_rcv
    shapes += [jax.ShapeDtypeStruct((8, 128), jnp.int32), jax.ShapeDtypeStruct((1,), jnp.int32)]
    vmem = pl.BlockSpec(memory_space=VMEM)
    out = pl.pallas_call(
        functools.partial(spectra_kernel, n_win, n_rcv, r_dev, split),
        in_specs=[pl.BlockSpec(memory_space=pltpu.HBM)] * 5,
        out_specs=[vmem] * (len(shapes) - 1) + [pl.BlockSpec(memory_space=SMEM)],
        out_shape=shapes,
        scratch_shapes=[
            pltpu.VMEM((chunks, rows, samples), jnp.bfloat16),
            pltpu.VMEM((chunks, rows, samples), jnp.bfloat16),
            pltpu.VMEM((chunks, n_win, rows, lanes), jnp.bfloat16),
            pltpu.VMEM((n_src * (w_dev // chunks), rows), jnp.bfloat16),
            pltpu.VMEM((n_src, 128), jnp.float32),
            pltpu.VMEM((samples // 2, F // 2), jnp.bfloat16),
            pltpu.VMEM((samples, F // 2), jnp.bfloat16),
            pltpu.VMEM(coarse.shape, jnp.float32),
            pltpu.VMEM(fine.shape, jnp.float32),
            pltpu.SMEM(valid.shape, jnp.int32),
            pltpu.SMEM(src_station.shape, jnp.int32),
            pltpu.SemaphoreType.DMA((4,)),
            pltpu.SemaphoreType.DMA((chunks,)),
        ],
        compiler_params=pltpu.CompilerParams(vmem_limit_bytes=36 * 2**20),
        cost_estimate=pl.CostEstimate(
            flops=2 * every * (samples // 4) * 6 * (F // 2), bytes_accessed=every * samples * 2,
            transcendentals=0,
        ),
        name="spectra",
    )(*(in_hbm(x) for x in (valid, src_station, traces.reshape(every, samples), coarse, fine)))
    blocks = [[block] for block in out[:n_win]]
    blocks[split].append(out[n_win])
    return blocks, out[n_win + 1:n_win + 1 + n_rcv], out[-2], out[-1]


def bin_order(lanes):
    quarter = lanes // 8
    lane = lax.broadcasted_iota(jnp.int32, (lanes, lanes), 1)
    row = lax.broadcasted_iota(jnp.int32, (lanes, lanes), 0)
    part = (lane // quarter) % 2
    bin_of = 4 * (lane % quarter) + lane // (2 * quarter)
    hit = row == part * (lanes // 2) + bin_of
    return hit.astype(jnp.float32).astype(jnp.bfloat16)


def turn_kernel(r_dev, *refs):
    x_refs, (out_ref, rows_ref) = refs[:-2], refs[-2:]
    lanes = x_refs[0].shape[1]
    bins = lanes // 2
    w_dev = out_ref.shape[1] // 2
    pad = out_ref.shape[2] // 2
    order = bin_order(lanes)
    windows = [(x, w) for x in x_refs for w in range(x.shape[0] // r_dev)]
    for k, (x_ref, w) in enumerate(windows):
        turned = lax.dot_general(
            order, x_ref[w * r_dev:(w + 1) * r_dev], (((1,), (1,)), ((), ())),
            preferred_element_type=jnp.float32,
        )
        rows_ref[pl.ds(k, lanes, stride=w_dev), :r_dev] = turned
    rr = rows_ref[:bins * w_dev].reshape(bins, w_dev, pad)
    ri = rows_ref[bins * w_dev:].reshape(bins, w_dev, pad)
    out_ref[:, :, :pad] = jnp.concatenate([rr, ri], axis=1).astype(jnp.bfloat16)
    out_ref[:, :, pad:] = jnp.concatenate([ri, -rr], axis=1).astype(jnp.bfloat16)


def turn_call(parts, w_dev, r_dev):
    lanes = parts[0].shape[1]
    pad = 128
    vmem = pl.BlockSpec(memory_space=VMEM)
    return pl.pallas_call(
        functools.partial(turn_kernel, r_dev),
        in_specs=[vmem] * len(parts),
        out_specs=vmem,
        out_shape=jax.ShapeDtypeStruct((lanes // 2, 2 * w_dev, 2 * pad), jnp.bfloat16),
        scratch_shapes=[pltpu.VMEM((lanes * w_dev, pad), jnp.float32)],
        compiler_params=pltpu.CompilerParams(vmem_limit_bytes=16 * 2**20),
        cost_estimate=pl.CostEstimate(
            flops=2 * w_dev * lanes * lanes * pad, bytes_accessed=2 * 2**20, transcendentals=0
        ),
        name="turn",
    )(*parts)


def merge_kernel(n_win, *refs):
    picked, outs = refs[:-n_win], refs[-n_win:]
    for j, out_ref in enumerate(outs):
        total = picked[0][j].astype(jnp.float32)
        for q_ref in picked[1:]:
            total = total + q_ref[j].astype(jnp.float32)
        out_ref[...] = total.astype(jnp.bfloat16)


def merge_call(*picked):
    n_win, rows, lanes = picked[0].shape
    vmem = pl.BlockSpec(memory_space=VMEM)
    return pl.pallas_call(
        functools.partial(merge_kernel, n_win),
        in_specs=[vmem] * len(picked),
        out_specs=[vmem] * n_win,
        out_shape=[jax.ShapeDtypeStruct((rows, lanes), jnp.bfloat16)] * n_win,
        compiler_params=pltpu.CompilerParams(vmem_limit_bytes=4 * 2**20),
        cost_estimate=pl.CostEstimate(flops=2**18, bytes_accessed=2**19, transcendentals=0),
        name="merge",
    )(*picked)


def join_kernel(n_win, *refs):
    out_ref = refs[-1]
    for j in range(n_win):
        out_ref[j] = refs[j][...]


def join_call(blocks, after, later):
    rows, lanes = blocks[0].shape
    n_win = len(blocks)
    vmem, anywhere = pl.BlockSpec(memory_space=VMEM), pl.BlockSpec(memory_space=pl.ANY)
    out = pl.pallas_call(
        functools.partial(join_kernel, n_win),
        in_specs=[vmem] * n_win + [anywhere] * (1 + len(later)),
        out_specs=[anywhere] * len(later) + [vmem],
        out_shape=[jax.ShapeDtypeStruct(x.shape, x.dtype) for x in later]
        + [jax.ShapeDtypeStruct((n_win, rows, lanes), jnp.bfloat16)],
        input_output_aliases={n_win + 1 + k: k for k in range(len(later))},
        compiler_params=pltpu.CompilerParams(vmem_limit_bytes=4 * 2**20),
        cost_estimate=pl.CostEstimate(flops=2**18, bytes_accessed=2**19, transcendentals=0),
        name="join",
    )(*blocks, after, *later)
    return out[-1], out[:-1]


def stacks_kernel(shares, n_win, w_dev, r_dev, n_own, bins, plan_ref, *refs):
    t_refs = refs[:n_win]
    s_refs = refs[n_win:n_win + len(shares)]
    out_hbm, srow_ref, left_ref, prod_ref, out_ref, sems = refs[-6:]
    lanes = 2 * bins
    windows = n_win * w_dev
    count = len(shares) * n_own
    pad = 128
    rcv = lax.axis_index("rcv")

    def product(lhs, rhs, dims=(((1,), (0,)), ((), ()))):
        return lax.dot_general(lhs, rhs, dims, preferred_element_type=jnp.float32)

    order = bin_order(lanes)
    both = order[:bins] + order[bins:]
    lane = lax.broadcasted_iota(jnp.int32, (w_dev, lanes), 1)
    real = (lane // (bins // 4)) % 2 == 0

    for k, s_ref in enumerate(s_refs):
        for j in range(n_win):
            block = s_ref[j].astype(jnp.float32)
            for h in range(lanes // pad):
                half = block[:, h * pad:(h + 1) * pad]
                srow_ref[h, pl.ds((k * n_win + j) * w_dev * n_own, w_dev * n_own), :] = half
    for s in range(count):
        first = s // n_own * windows * n_own + s % n_own
        values = jnp.concatenate(
            [srow_ref[h, pl.ds(first, windows, stride=n_own), :] for h in range(lanes // pad)],
            axis=1,
        )
        stacked = []
        for j in range(n_win):
            own = values[j * w_dev:(j + 1) * w_dev]
            stacked += [jnp.where(real, own, 0.0), jnp.where(real, 0.0, own)]
        stacked = jnp.concatenate(stacked, axis=0).astype(jnp.bfloat16)
        turned = product(both, stacked, (((1,), (1,)), ((), ())))
        left_ref[pl.ds(s, bins, stride=count), :2 * windows] = turned

    for f in range(bins):
        right = jnp.concatenate([t_ref[f] for t_ref in t_refs], axis=0)
        left = left_ref[pl.ds(f * count, count), :2 * windows].astype(jnp.bfloat16)
        result = product(left, right)
        for c in range(2):
            prod_ref[c, pl.ds(f, count, stride=bins), :] = result[:, c * pad:(c + 1) * pad]

    scale = 1.0 / math.sqrt(windows)
    copies = []
    for s in range(count):
        for c in range(2):
            turned = prod_ref[c, s * bins:(s + 1) * bins, :].T
            out_ref[s, pl.ds(c, r_dev, stride=2), :] = turned[:r_dev] * scale
        row = plan_ref[0, (rcv ^ shares[s // n_own]) * n_own + s % n_own]
        copies.append(pltpu.make_async_copy(out_ref.at[s], out_hbm.at[row], sems.at[s]))
        copies[-1].start()
    for copy in copies:
        copy.wait()


def stacks_call(out, plan, turned, sources, shares, n_rcv, w_dev, r_dev, bins):
    n_win = len(turned)
    n_own = sources[0].shape[1] // w_dev
    windows = n_win * w_dev
    count = len(shares) * n_own
    whole = pl.BlockSpec(memory_space=VMEM)
    args = [plan] + list(turned) + [sources[i] for i in shares]
    specs = [pl.BlockSpec(memory_space=SMEM)] + [whole] * (len(args) - 1)
    aliases = {}
    if out is not None:
        aliases = {len(args): 0}
        args.append(out)
        specs.append(pl.BlockSpec(memory_space=pl.ANY))
    return pl.pallas_call(
        functools.partial(stacks_kernel, shares, n_win, w_dev, r_dev, n_own, bins),
        in_specs=specs,
        out_specs=pl.BlockSpec(memory_space=pltpu.HBM),
        out_shape=jax.ShapeDtypeStruct((n_rcv * n_own, 2 * r_dev, bins), jnp.float32),
        input_output_aliases=aliases,
        scratch_shapes=[
            pltpu.VMEM((2 * bins // 128, windows * count, 128), jnp.float32),
            pltpu.VMEM((bins * count, 128), jnp.float32),
            pltpu.VMEM((2, count * bins, 128), jnp.float32),
            pltpu.VMEM((count, 2 * r_dev, bins), jnp.float32),
            pltpu.SemaphoreType.DMA((count,)),
        ],
        compiler_params=pltpu.CompilerParams(vmem_limit_bytes=20 * 2**20),
        cost_estimate=pl.CostEstimate(
            flops=8 * windows * count * r_dev * bins, bytes_accessed=6 * 2**20, transcendentals=0
        ),
        name="stacks",
    )(*args)


def swap(value, axis, by):
    size = lax.axis_size(axis)
    return lax.ppermute(value, axis, [(i, i ^ by) for i in range(size)])


def merge_near(picked, right, left):
    return merge_call(picked[0], right, left)


def merge_all(picked, right, left):
    n_rcv = len(picked)
    far = []
    for d in range(1, n_rcv):
        pairs = [(z, (z + d) % n_rcv) for z in range(n_rcv)]
        pairs = [(a, b) for a, b in pairs if abs(a - b) > 1]
        far.append(lax.ppermute(picked[d], "rcv", pairs))
    return merge_call(picked[0], right, left, *far)


def body(traces, valid, src_station):
    w_dev, r_dev, samples = traces.shape
    n_src = src_station.shape[0]
    n_win = lax.axis_size("win")
    n_rcv = lax.axis_size("rcv")
    bins = F // n_win
    split = n_win // 2

    blocks, picked, plan, flag = spectra_call(traces, valid, src_station, n_win, n_rcv, split)

    right = lax.ppermute(picked[1], "rcv", [(z, z + 1) for z in range(n_rcv - 1)])
    left = lax.ppermute(picked[-1], "rcv", [(z + 1, z) for z in range(n_rcv - 1)])
    merged = lax.cond(flag.reshape(()) > 0, merge_all, merge_near, picked, right, left)
    merged = [merged[0]] + [swap(merged[j], "win", j) for j in range(1, n_win)]

    early = [(0, 0)] + [(j, 0) for j in range(1, split + 1)]
    late = [(j, k) for j in range(1, n_win) for k in range(len(blocks[j])) if (j, k) not in early]
    received = {(0, 0): blocks[0][0]}
    received.update({(j, 0): swap(blocks[j][0], "win", j) for j in range(1, split + 1)})
    joined, later = join_call(merged, received[split, 0], [blocks[j][k] for j, k in late])
    received.update({(j, k): swap(x, "win", j) for (j, k), x in zip(late, later)})
    sources = [joined] + [swap(joined, "rcv", i) for i in range(1, n_rcv)]

    turned = [
        turn_call([received[j, k] for k in range(len(blocks[j]))], w_dev, r_dev)
        for j in range(n_win)
    ]
    half = n_rcv // 2
    sizes = (n_rcv, w_dev, r_dev, bins)
    stacks = stacks_call(None, plan, turned, sources, tuple(range(half)), *sizes)
    stacks = stacks_call(stacks, plan, turned, sources, tuple(range(half, n_rcv)), *sizes)
    return stacks.reshape(n_src, r_dev, 2, bins)


def correlate(received, sources):
    rr = received[:, :, 0]
    ri = received[:, :, 1]
    sr = sources[:, :, 0]
    si = sources[:, :, 1]
    real = jnp.einsum("wsf,wrf->srf", sr, rr, preferred_element_type=jnp.float32)
    real = real + jnp.einsum("wsf,wrf->srf", si, ri, preferred_element_type=jnp.float32)
    imag = jnp.einsum("wsf,wrf->srf", sr, ri, preferred_element_type=jnp.float32)
    imag = imag - jnp.einsum("wsf,wrf->srf", si, rr, preferred_element_type=jnp.float32)
    return jnp.stack([real, imag], axis=2)


def body_any(traces, valid, src_station):
    w_dev, r_dev, samples = traces.shape
    n_win = lax.axis_size("win")
    n_rcv = lax.axis_size("rcv")
    bins = F // n_win
    table = jnp.asarray(band_table(samples, F, samples // 16))
    spectra = jnp.dot(
        traces.reshape(w_dev * r_dev, samples), table, preferred_element_type=jnp.float32
    )
    spectra = spectra.reshape(w_dev, r_dev, 2, F)
    power = jnp.sum(spectra * spectra, axis=(2, 3), keepdims=True) / F
    keep = valid.astype(jnp.float32)[:, None, None, None]
    white = (spectra * lax.rsqrt(power + 1e-06) * keep).astype(jnp.bfloat16)
    blocks = white.reshape(w_dev, r_dev, 2, n_win, bins).transpose(3, 0, 1, 2, 4)
    me = lax.axis_index("win")
    offset = lax.axis_index("rcv") * r_dev
    station_ids = offset + jnp.arange(r_dev, dtype=jnp.int32)
    selector = (src_station[:, None] == station_ids[None, :]).astype(jnp.bfloat16)
    received = []
    for j in range(n_win):
        block = lax.dynamic_index_in_dim(blocks, me ^ j, 0, keepdims=False)
        received.append(swap(block, "win", j) if j else block)
    received = jnp.concatenate(received, axis=0)
    rows = jnp.einsum("sr,wrcf->wscf", selector, received, preferred_element_type=jnp.float32)
    rows = lax.all_to_all(rows.astype(jnp.bfloat16), "rcv", 0, 0, tiled=True)
    rows = rows.reshape((n_rcv, -1) + rows.shape[1:])
    merged = jnp.sum(rows.astype(jnp.float32), axis=0).astype(jnp.bfloat16)
    sources = lax.all_gather(merged, "rcv", axis=0, tiled=True)
    return correlate(received, sources) * (1.0 / math.sqrt(w_dev * n_win))


def solution(mesh):
    sizes = (mesh.shape["win"], mesh.shape["rcv"])
    return jax.shard_map(
        body if sizes == (4, 4) else body_any,
        mesh=mesh,
        in_specs=(P("win", ("groups", "rcv"), None), P(("groups", "win")), P("groups")),
        out_specs=P(None, ("groups", "rcv"), None, "win"),
        check_vma=False,
    )
```

```python
import functools
import math

import jax
import jax.numpy as jnp
import numpy as np
from jax import lax
from jax.experimental import pallas as pl
from jax.experimental.pallas import tpu as pltpu
from jax.sharding import PartitionSpec as P

F = 512
SMEM = pltpu.MemorySpace.SMEM
VMEM = pltpu.MemorySpace.VMEM


def angles(samples, freqs, count):
    phase = samples[:, None] * freqs[None, :] % count
    return phase.astype(np.float64) * (2.0 * math.pi / count)


def band_table(count, bins, first):
    angle = angles(np.arange(count), first + np.arange(bins), count)
    return np.concatenate([np.cos(angle), -np.sin(angle)], axis=1).astype(jnp.bfloat16)


FINE = 32


def angle_factors(count, bins, first, n_win):
    j = np.arange(bins // 4).reshape(n_win, 1, -1)
    turn = np.array([0.0, 0.5 * math.pi]).reshape(1, 2, 1)

    def factors(samples, shift):
        out = []
        for m in range(4):
            freqs = np.broadcast_to(first + 4 * j + m, (n_win, 2, bins // 4 // n_win))
            angle = angles(samples, freqs.reshape(-1), count)
            angle = angle + np.broadcast_to(shift, freqs.shape).reshape(1, -1)
            out.append(np.stack([np.cos(angle), np.sin(angle)]))
        return np.stack(out).astype(np.float32)

    return factors(np.arange(0, count // 4, FINE), 0.0 * turn), factors(np.arange(FINE), turn)


def make_tables(coarse_ref, fine_ref, even_ref, odd_ref):
    steps = coarse_ref.shape[2]
    quarter = steps * FINE
    for m in range(4):
        cos_b, sin_b = fine_ref[m, 0], fine_ref[m, 1]
        out_ref = odd_ref if m % 2 else even_ref
        base = (m // 2) * (2 * quarter if m % 2 else quarter)
        for a in range(steps):
            cos_a, sin_a = (coarse_ref[m, k, a:a + 1, :] for k in range(2))
            rows = slice(base + a * FINE, base + (a + 1) * FINE)
            out_ref[rows, :] = (cos_a * cos_b - sin_a * sin_b).astype(jnp.bfloat16)
            if m % 2:
                if m == 1:
                    cos_a, sin_a = -cos_a, -sin_a
                rows = slice(rows.start + quarter, rows.stop + quarter)
                out_ref[rows, :] = (cos_a * sin_b + sin_a * cos_b).astype(jnp.bfloat16)


def in_hbm(value):
    return pltpu.with_memory_space_constraint(value, pltpu.HBM)


def order_sources(src_ref, r_dev, n_own, order_ref, plan_ref, flag_ref):
    n_src = src_ref.shape[0]
    size = order_ref.shape
    down = lax.broadcasted_iota(jnp.int32, size, 0).astype(jnp.float32)
    along = lax.broadcasted_iota(jnp.int32, size, 1).astype(jnp.float32)
    none = jnp.full(size, float(2**20), jnp.float32)
    column, row = none, none
    for s in range(n_src):
        station = src_ref[s].astype(jnp.float32)
        column = jnp.where(down == s, station, column)
        row = jnp.where(along == s, station, row)
    rank_along = jnp.sum((column < row).astype(jnp.float32), axis=0, keepdims=True)
    rank_down = jnp.sum((row < column).astype(jnp.float32), axis=1, keepdims=True)
    sorted_down = jnp.sum(jnp.where(rank_along == down, row, 0.0), axis=1, keepdims=True)
    at_place = rank_down == along
    sorted_along = jnp.sum(jnp.where(at_place, column, 0.0), axis=0, keepdims=True)
    source_along = jnp.sum(jnp.where(at_place, down, 0.0), axis=0, keepdims=True)
    order_ref[...] = jnp.broadcast_to(sorted_down, size)
    place = along[:1]
    owner, share = jnp.zeros_like(place), jnp.zeros_like(place)
    for z in range(1, n_src // n_own):
        owner = owner + (sorted_along >= z * r_dev).astype(jnp.float32)
        share = share + (place >= z * n_own).astype(jnp.float32)
    far = jnp.where((place < n_src) & (jnp.abs(owner - share) > 1.5), 1.0, 0.0)
    plan_ref[...] = jnp.broadcast_to(source_along, plan_ref.shape).astype(jnp.int32)
    flag_ref[0] = jnp.max(far).astype(jnp.int32)


def spectra_kernel(
    n_win, n_rcv, r_dev, valid_hbm, src_hbm, x_hbm, coarse_hbm, fine_hbm, *refs
):
    r_refs = refs[:n_win]
    q_refs = refs[n_win:n_win + n_rcv]
    (plan_ref, flag_ref, x_ref, y_ref, white_ref, sel_ref, order_ref, even_ref, odd_ref,
     coarse_ref, fine_ref, valid_ref, src_ref, sems, x_sems) = refs[n_win + n_rcv:]
    chunks, rows, samples = x_ref.shape
    w_step = rows // r_dev
    n_own = src_ref.shape[0] // n_rcv
    quarter = samples // 4
    win = lax.axis_index("win")
    rcv = lax.axis_index("rcv")

    def small(k):
        source = (coarse_hbm, fine_hbm, src_hbm, valid_hbm)[k]
        target = (coarse_ref, fine_ref, src_ref, valid_ref)[k]
        return pltpu.make_async_copy(source, target, sems.at[k])

    def chunk(k):
        return pltpu.make_async_copy(x_hbm.at[pl.ds(k * rows, rows)], x_ref.at[k], x_sems.at[k])

    for k in range(4):
        small(k).start()
    for k in range(chunks):
        chunk(k).start()
    small(0).wait()
    small(1).wait()
    make_tables(coarse_ref, fine_ref, even_ref, odd_ref)
    small(2).wait()
    order_sources(src_ref, r_dev, n_own, order_ref, plan_ref, flag_ref)
    stations = []
    for d in range(n_rcv):
        share = pl.multiple_of((rcv ^ d) * n_own, n_own)
        stations += [order_ref[pl.ds(share, n_own), 0:1]] * w_step
    wanted = jnp.concatenate(stations, axis=0).astype(jnp.int32) - rcv * r_dev
    shape = (n_rcv * w_step * n_own, rows)
    out_row = lax.broadcasted_iota(jnp.int32, shape, 0)
    column = lax.broadcasted_iota(jnp.int32, shape, 1)
    inside = (wanted >= 0) & (wanted < r_dev)
    hit = inside & (column == wanted + (out_row // n_own) % w_step * r_dev)
    sel_ref[...] = hit.astype(jnp.float32).astype(jnp.bfloat16)
    small(3).wait()

    def product(lhs, table):
        return jnp.dot(lhs, table, preferred_element_type=jnp.float32)

    def add_quarters(k, first, last):
        part = slice(first, last)
        b0, b1, b2, b3 = (x_ref[k, part, q * quarter:(q + 1) * quarter] for q in range(4))
        x0, x1, x2, x3 = (b.astype(jnp.float32) for b in (b0, b1, b2, b3))
        y_ref[k, part, :quarter] = ((x0 + x2) + (x1 + x3)).astype(jnp.bfloat16)
        y_ref[k, part, quarter:2 * quarter] = ((x0 + x2) - (x1 + x3)).astype(jnp.bfloat16)
        y_ref[k, part, 2 * quarter:3 * quarter] = b0 - b2
        y_ref[k, part, 3 * quarter:] = b1 - b3

    parts = 4
    size = rows // parts
    chunk(0).wait()
    add_quarters(0, 0, rows)
    row = lax.broadcasted_iota(jnp.int32, (rows, 1), 0)
    for k in range(chunks):
        more = k + 1 < chunks
        if more:
            chunk(k + 1).wait()
        spectra = []
        for m in range(4):
            if m % 2:
                table = odd_ref[(m // 2) * 2 * quarter:(m // 2 + 1) * 2 * quarter]
                spectra.append(product(y_ref[k, :, 2 * quarter:], table))
            else:
                half = slice((m // 2) * quarter, (m // 2 + 1) * quarter)
                spectra.append(product(y_ref[k, :, half], even_ref[half]))
            if more:
                add_quarters(k + 1, m * size, (m + 1) * size)
        squares = sum(jnp.sum(s * s, axis=1, keepdims=True) for s in spectra)
        gain = lax.rsqrt(squares / F + 1e-06)
        keep = jnp.zeros((rows, 1), jnp.float32)
        for t in range(w_step):
            own = (row >= t * r_dev) & (row < (t + 1) * r_dev)
            keep = jnp.where(own, valid_ref[k * w_step + t].astype(jnp.float32), keep)
        gain = gain * keep
        white = [s * gain for s in spectra]
        piece = white[0].shape[1] // n_win
        for d in range(n_win):
            columns = slice(d * piece, (d + 1) * piece)
            block = jnp.concatenate([part[:, columns] for part in white], axis=1)
            white_ref[k, d] = block.astype(jnp.bfloat16)
        count = w_step * n_own
        for j in range(n_win):
            block = white_ref[k, win ^ j]
            r_refs[j][k * rows:(k + 1) * rows, :] = block
            picked = product(sel_ref[...], block).astype(jnp.bfloat16)
            for d in range(n_rcv):
                q_refs[d][j, k * count:(k + 1) * count, :] = picked[d * count:(d + 1) * count]


def spectra_call(traces, valid, src_station, n_win, n_rcv):
    w_dev, r_dev, samples = traces.shape
    n_src = src_station.shape[0]
    n_own = n_src // n_rcv
    chunks = 4
    every = w_dev * r_dev
    rows = every // chunks
    lanes = 2 * F // n_win
    coarse, fine = (jnp.asarray(t) for t in angle_factors(samples, F, samples // 16, n_win))
    shapes = [jax.ShapeDtypeStruct((every, lanes), jnp.bfloat16)] * n_win
    shapes += [jax.ShapeDtypeStruct((n_win, w_dev * n_own, lanes), jnp.bfloat16)] * n_rcv
    shapes += [jax.ShapeDtypeStruct((8, 128), jnp.int32), jax.ShapeDtypeStruct((1,), jnp.int32)]
    vmem = pl.BlockSpec(memory_space=VMEM)
    out = pl.pallas_call(
        functools.partial(spectra_kernel, n_win, n_rcv, r_dev),
        in_specs=[pl.BlockSpec(memory_space=pltpu.HBM)] * 5,
        out_specs=[vmem] * (len(shapes) - 1) + [pl.BlockSpec(memory_space=SMEM)],
        out_shape=shapes,
        scratch_shapes=[
            pltpu.VMEM((chunks, rows, samples), jnp.bfloat16),
            pltpu.VMEM((chunks, rows, samples), jnp.bfloat16),
            pltpu.VMEM((chunks, n_win, rows, lanes), jnp.bfloat16),
            pltpu.VMEM((n_src * (w_dev // chunks), rows), jnp.bfloat16),
            pltpu.VMEM((n_src, 128), jnp.float32),
            pltpu.VMEM((samples // 2, F // 2), jnp.bfloat16),
            pltpu.VMEM((samples, F // 2), jnp.bfloat16),
            pltpu.VMEM(coarse.shape, jnp.float32),
            pltpu.VMEM(fine.shape, jnp.float32),
            pltpu.SMEM(valid.shape, jnp.int32),
            pltpu.SMEM(src_station.shape, jnp.int32),
            pltpu.SemaphoreType.DMA((4,)),
            pltpu.SemaphoreType.DMA((chunks,)),
        ],
        compiler_params=pltpu.CompilerParams(vmem_limit_bytes=36 * 2**20),
        cost_estimate=pl.CostEstimate(
            flops=2 * every * (samples // 4) * 6 * (F // 2), bytes_accessed=every * samples * 2,
            transcendentals=0,
        ),
        name="spectra",
    )(*(in_hbm(x) for x in (valid, src_station, traces.reshape(every, samples), coarse, fine)))
    return out[:n_win], out[n_win:n_win + n_rcv], out[-2], out[-1]


def bin_order(lanes):
    quarter = lanes // 8
    lane = lax.broadcasted_iota(jnp.int32, (lanes, lanes), 1)
    row = lax.broadcasted_iota(jnp.int32, (lanes, lanes), 0)
    part = (lane // quarter) % 2
    bin_of = 4 * (lane % quarter) + lane // (2 * quarter)
    hit = row == part * (lanes // 2) + bin_of
    return hit.astype(jnp.float32).astype(jnp.bfloat16)


def turn_kernel(r_dev, *refs):
    x_refs, (out_ref, rows_ref) = refs[:-2], refs[-2:]
    lanes = x_refs[0].shape[1]
    bins = lanes // 2
    w_dev = out_ref.shape[1] // 2
    pad = out_ref.shape[2] // 2
    order = bin_order(lanes)
    windows = [(x, w) for x in x_refs for w in range(x.shape[0] // r_dev)]
    for k, (x_ref, w) in enumerate(windows):
        turned = lax.dot_general(
            order, x_ref[w * r_dev:(w + 1) * r_dev], (((1,), (1,)), ((), ())),
            preferred_element_type=jnp.float32,
        )
        rows_ref[pl.ds(k, lanes, stride=w_dev), :r_dev] = turned
    rr = rows_ref[:bins * w_dev].reshape(bins, w_dev, pad)
    ri = rows_ref[bins * w_dev:].reshape(bins, w_dev, pad)
    out_ref[:, :, :pad] = jnp.concatenate([rr, ri], axis=1).astype(jnp.bfloat16)
    out_ref[:, :, pad:] = jnp.concatenate([ri, -rr], axis=1).astype(jnp.bfloat16)


def turn_call(parts, w_dev, r_dev):
    lanes = parts[0].shape[1]
    pad = 128
    vmem = pl.BlockSpec(memory_space=VMEM)
    return pl.pallas_call(
        functools.partial(turn_kernel, r_dev),
        in_specs=[vmem] * len(parts),
        out_specs=vmem,
        out_shape=jax.ShapeDtypeStruct((lanes // 2, 2 * w_dev, 2 * pad), jnp.bfloat16),
        scratch_shapes=[pltpu.VMEM((lanes * w_dev, pad), jnp.float32)],
        compiler_params=pltpu.CompilerParams(vmem_limit_bytes=16 * 2**20),
        cost_estimate=pl.CostEstimate(
            flops=2 * w_dev * lanes * lanes * pad, bytes_accessed=2 * 2**20, transcendentals=0
        ),
        name="turn",
    )(*parts)


def merge_kernel(n_win, *refs):
    picked, outs = refs[:-n_win], refs[-n_win:]
    for j, out_ref in enumerate(outs):
        total = picked[0][j].astype(jnp.float32)
        for q_ref in picked[1:]:
            total = total + q_ref[j].astype(jnp.float32)
        out_ref[...] = total.astype(jnp.bfloat16)


def merge_call(*picked):
    n_win, rows, lanes = picked[0].shape
    vmem = pl.BlockSpec(memory_space=VMEM)
    return pl.pallas_call(
        functools.partial(merge_kernel, n_win),
        in_specs=[vmem] * len(picked),
        out_specs=[vmem] * n_win,
        out_shape=[jax.ShapeDtypeStruct((rows, lanes), jnp.bfloat16)] * n_win,
        compiler_params=pltpu.CompilerParams(vmem_limit_bytes=4 * 2**20),
        cost_estimate=pl.CostEstimate(flops=2**18, bytes_accessed=2**19, transcendentals=0),
        name="merge",
    )(*picked)


def join_kernel(n_win, *refs):
    out_ref = refs[-1]
    for j in range(n_win):
        out_ref[j] = refs[j][...]


def join_call(blocks, later):
    rows, lanes = blocks[0].shape
    n_win = len(blocks)
    vmem, anywhere = pl.BlockSpec(memory_space=VMEM), pl.BlockSpec(memory_space=pl.ANY)
    out = pl.pallas_call(
        functools.partial(join_kernel, n_win),
        in_specs=[vmem] * n_win + [anywhere] * len(later),
        out_specs=[anywhere] * len(later) + [vmem],
        out_shape=[jax.ShapeDtypeStruct(x.shape, x.dtype) for x in later]
        + [jax.ShapeDtypeStruct((n_win, rows, lanes), jnp.bfloat16)],
        input_output_aliases={n_win + k: k for k in range(len(later))},
        compiler_params=pltpu.CompilerParams(vmem_limit_bytes=4 * 2**20),
        cost_estimate=pl.CostEstimate(flops=2**18, bytes_accessed=2**19, transcendentals=0),
        name="join",
    )(*blocks, *later)
    return out[-1], out[:-1]


def stacks_kernel(shares, n_win, w_dev, r_dev, n_own, bins, plan_hbm, *refs):
    t_refs = refs[:n_win]
    s_refs = refs[n_win:n_win + len(shares)]
    out_hbm, srow_ref, left_ref, prod_ref, out_ref, plan_ref, sems, plan_sem = refs[-8:]
    plan_copy = pltpu.make_async_copy(plan_hbm, plan_ref, plan_sem)
    plan_copy.start()
    lanes = 2 * bins
    windows = n_win * w_dev
    count = len(shares) * n_own
    pad = 128
    rcv = lax.axis_index("rcv")

    def product(lhs, rhs, dims=(((1,), (0,)), ((), ()))):
        return lax.dot_general(lhs, rhs, dims, preferred_element_type=jnp.float32)

    order = bin_order(lanes)
    both = order[:bins] + order[bins:]
    lane = lax.broadcasted_iota(jnp.int32, (w_dev, lanes), 1)
    real = (lane // (bins // 4)) % 2 == 0

    for k, s_ref in enumerate(s_refs):
        for j in range(n_win):
            block = s_ref[j].astype(jnp.float32)
            for h in range(lanes // pad):
                half = block[:, h * pad:(h + 1) * pad]
                srow_ref[h, pl.ds((k * n_win + j) * w_dev * n_own, w_dev * n_own), :] = half
    for s in range(count):
        first = s // n_own * windows * n_own + s % n_own
        values = jnp.concatenate(
            [srow_ref[h, pl.ds(first, windows, stride=n_own), :] for h in range(lanes // pad)],
            axis=1,
        )
        stacked = []
        for j in range(n_win):
            own = values[j * w_dev:(j + 1) * w_dev]
            stacked += [jnp.where(real, own, 0.0), jnp.where(real, 0.0, own)]
        stacked = jnp.concatenate(stacked, axis=0).astype(jnp.bfloat16)
        turned = product(both, stacked, (((1,), (1,)), ((), ())))
        left_ref[pl.ds(s, bins, stride=count), :2 * windows] = turned

    for f in range(bins):
        right = jnp.concatenate([t_ref[f] for t_ref in t_refs], axis=0)
        left = left_ref[pl.ds(f * count, count), :2 * windows].astype(jnp.bfloat16)
        result = product(left, right)
        for c in range(2):
            prod_ref[c, pl.ds(f, count, stride=bins), :] = result[:, c * pad:(c + 1) * pad]

    scale = 1.0 / math.sqrt(windows)
    plan_copy.wait()
    copies = []
    for s in range(count):
        for c in range(2):
            turned = prod_ref[c, s * bins:(s + 1) * bins, :].T
            out_ref[s, pl.ds(c, r_dev, stride=2), :] = turned[:r_dev] * scale
        row = plan_ref[0, (rcv ^ shares[s // n_own]) * n_own + s % n_own]
        copies.append(pltpu.make_async_copy(out_ref.at[s], out_hbm.at[row], sems.at[s]))
        copies[-1].start()
    for copy in copies:
        copy.wait()


def stacks_call(out, plan, turned, sources, shares, n_rcv, w_dev, r_dev, bins):
    n_win = len(turned)
    n_own = sources[0].shape[1] // w_dev
    windows = n_win * w_dev
    count = len(shares) * n_own
    whole = pl.BlockSpec(memory_space=VMEM)
    args = [plan] + list(turned) + [sources[i] for i in shares]
    specs = [pl.BlockSpec(memory_space=pl.ANY)] + [whole] * (len(args) - 1)
    aliases = {}
    if out is not None:
        aliases = {len(args): 0}
        args.append(out)
        specs.append(pl.BlockSpec(memory_space=pl.ANY))
    return pl.pallas_call(
        functools.partial(stacks_kernel, shares, n_win, w_dev, r_dev, n_own, bins),
        in_specs=specs,
        out_specs=pl.BlockSpec(memory_space=pltpu.HBM),
        out_shape=jax.ShapeDtypeStruct((n_rcv * n_own, 2 * r_dev, bins), jnp.float32),
        input_output_aliases=aliases,
        scratch_shapes=[
            pltpu.VMEM((2 * bins // 128, windows * count, 128), jnp.float32),
            pltpu.VMEM((bins * count, 128), jnp.float32),
            pltpu.VMEM((2, count * bins, 128), jnp.float32),
            pltpu.VMEM((count, 2 * r_dev, bins), jnp.float32),
            pltpu.SMEM(plan.shape, jnp.int32),
            pltpu.SemaphoreType.DMA((count,)),
            pltpu.SemaphoreType.DMA,
        ],
        compiler_params=pltpu.CompilerParams(vmem_limit_bytes=20 * 2**20),
        cost_estimate=pl.CostEstimate(
            flops=8 * windows * count * r_dev * bins, bytes_accessed=6 * 2**20, transcendentals=0
        ),
        name="stacks",
    )(*args)


def swap(value, axis, by):
    size = lax.axis_size(axis)
    return lax.ppermute(value, axis, [(i, i ^ by) for i in range(size)])


def near_and_far(n_rcv, by):
    pairs = [(z, z ^ by) for z in range(n_rcv)]
    return [p for p in pairs if abs(p[0] - p[1]) == 1], [p for p in pairs if abs(p[0] - p[1]) > 1]


def merge_near(picked, near):
    return merge_call(picked[0], *near)


def merge_all(picked, near):
    far = []
    for i in range(1, len(picked)):
        pairs = near_and_far(len(picked), i)[1]
        if pairs:
            far.append(lax.ppermute(picked[i], "rcv", pairs))
    return merge_call(picked[0], *near, *far)


def body(traces, valid, src_station):
    w_dev, r_dev, samples = traces.shape
    n_src = src_station.shape[0]
    n_win = lax.axis_size("win")
    n_rcv = lax.axis_size("rcv")
    bins = F // n_win
    early = n_win // 2

    blocks, picked, plan, flag = spectra_call(traces, valid, src_station, n_win, n_rcv)

    near = []
    for i in range(1, n_rcv):
        pairs = near_and_far(n_rcv, i)[0]
        if pairs:
            near.append(lax.ppermute(picked[i], "rcv", pairs))
    merged = lax.cond(flag.reshape(()) > 0, merge_all, merge_near, picked, near)

    merged = [merged[0]] + [swap(merged[j], "win", j) for j in range(1, n_win)]
    late = [j for j in range(1, n_win) if j != early]
    joined, later = join_call(merged, [blocks[j] for j in late])
    received = {0: blocks[0], early: swap(blocks[early], "win", early)}
    received.update({j: swap(block, "win", j) for j, block in zip(late, later)})
    sources = [joined] + [swap(joined, "rcv", i) for i in range(1, n_rcv)]

    turned = [turn_call([received[j]], w_dev, r_dev) for j in range(n_win)]
    half = n_rcv // 2
    sizes = (n_rcv, w_dev, r_dev, bins)
    stacks = stacks_call(None, plan, turned, sources, tuple(range(half)), *sizes)
    stacks = stacks_call(stacks, plan, turned, sources, tuple(range(half, n_rcv)), *sizes)
    return stacks.reshape(n_src, r_dev, 2, bins)


def correlate(received, sources):
    rr = received[:, :, 0]
    ri = received[:, :, 1]
    sr = sources[:, :, 0]
    si = sources[:, :, 1]
    real = jnp.einsum("wsf,wrf->srf", sr, rr, preferred_element_type=jnp.float32)
    real = real + jnp.einsum("wsf,wrf->srf", si, ri, preferred_element_type=jnp.float32)
    imag = jnp.einsum("wsf,wrf->srf", sr, ri, preferred_element_type=jnp.float32)
    imag = imag - jnp.einsum("wsf,wrf->srf", si, rr, preferred_element_type=jnp.float32)
    return jnp.stack([real, imag], axis=2)


def body_any(traces, valid, src_station):
    w_dev, r_dev, samples = traces.shape
    n_win = lax.axis_size("win")
    n_rcv = lax.axis_size("rcv")
    bins = F // n_win
    table = jnp.asarray(band_table(samples, F, samples // 16))
    spectra = jnp.dot(
        traces.reshape(w_dev * r_dev, samples), table, preferred_element_type=jnp.float32
    )
    spectra = spectra.reshape(w_dev, r_dev, 2, F)
    power = jnp.sum(spectra * spectra, axis=(2, 3), keepdims=True) / F
    keep = valid.astype(jnp.float32)[:, None, None, None]
    white = (spectra * lax.rsqrt(power + 1e-06) * keep).astype(jnp.bfloat16)
    blocks = white.reshape(w_dev, r_dev, 2, n_win, bins).transpose(3, 0, 1, 2, 4)
    me = lax.axis_index("win")
    offset = lax.axis_index("rcv") * r_dev
    station_ids = offset + jnp.arange(r_dev, dtype=jnp.int32)
    selector = (src_station[:, None] == station_ids[None, :]).astype(jnp.bfloat16)
    received = []
    for j in range(n_win):
        block = lax.dynamic_index_in_dim(blocks, me ^ j, 0, keepdims=False)
        received.append(swap(block, "win", j) if j else block)
    received = jnp.concatenate(received, axis=0)
    rows = jnp.einsum("sr,wrcf->wscf", selector, received, preferred_element_type=jnp.float32)
    rows = lax.all_to_all(rows.astype(jnp.bfloat16), "rcv", 0, 0, tiled=True)
    rows = rows.reshape((n_rcv, -1) + rows.shape[1:])
    merged = jnp.sum(rows.astype(jnp.float32), axis=0).astype(jnp.bfloat16)
    sources = lax.all_gather(merged, "rcv", axis=0, tiled=True)
    return correlate(received, sources) * (1.0 / math.sqrt(w_dev * n_win))


def solution(mesh):
    sizes = (mesh.shape["win"], mesh.shape["rcv"])
    return jax.shard_map(
        body if sizes == (4, 4) else body_any,
        mesh=mesh,
        in_specs=(P("win", ("groups", "rcv"), None), P(("groups", "win")), P("groups")),
        out_specs=P(None, ("groups", "rcv"), None, "win"),
        check_vma=False,
    )
```

```python
import functools
import math

import jax
import jax.numpy as jnp
import numpy as np
from jax import lax
from jax.experimental import pallas as pl
from jax.experimental.pallas import tpu as pltpu
from jax.sharding import PartitionSpec as P

F = 512
SMEM = pltpu.MemorySpace.SMEM
VMEM = pltpu.MemorySpace.VMEM


def angles(samples, freqs, count):
    phase = samples[:, None] * freqs[None, :] % count
    return phase.astype(np.float64) * (2.0 * math.pi / count)


def band_table(count, bins, first):
    angle = angles(np.arange(count), first + np.arange(bins), count)
    return np.concatenate([np.cos(angle), -np.sin(angle)], axis=1).astype(jnp.bfloat16)


FINE = 32


def angle_factors(count, bins, first, n_win):
    j = np.arange(bins // 4).reshape(n_win, 1, -1)
    turn = np.array([0.0, 0.5 * math.pi]).reshape(1, 2, 1)

    def factors(samples, shift):
        out = []
        for m in range(4):
            freqs = np.broadcast_to(first + 4 * j + m, (n_win, 2, bins // 4 // n_win))
            angle = angles(samples, freqs.reshape(-1), count)
            angle = angle + np.broadcast_to(shift, freqs.shape).reshape(1, -1)
            out.append(np.stack([np.cos(angle), np.sin(angle)]))
        return np.stack(out).astype(np.float32)

    return factors(np.arange(0, count // 4, FINE), 0.0 * turn), factors(np.arange(FINE), turn)


def make_tables(coarse_ref, fine_ref, table_ref):
    for m in range(table_ref.shape[0]):
        cos_b, sin_b = fine_ref[m, 0], fine_ref[m, 1]
        for a in range(coarse_ref.shape[2]):
            cos_a, sin_a = (coarse_ref[m, k, a:a + 1, :] for k in range(2))
            rows = slice(a * FINE, (a + 1) * FINE)
            table_ref[m, rows, :] = (cos_a * cos_b - sin_a * sin_b).astype(jnp.bfloat16)


def in_hbm(value):
    return pltpu.with_memory_space_constraint(value, pltpu.HBM)


def order_sources(src_ref, r_dev, n_own, order_ref, plan_ref, flag_ref):
    n_src = src_ref.shape[0]
    size = order_ref.shape
    down = lax.broadcasted_iota(jnp.int32, size, 0).astype(jnp.float32)
    along = lax.broadcasted_iota(jnp.int32, size, 1).astype(jnp.float32)
    none = jnp.full(size, float(2**20), jnp.float32)
    column, row = none, none
    for s in range(n_src):
        station = src_ref[s].astype(jnp.float32)
        column = jnp.where(down == s, station, column)
        row = jnp.where(along == s, station, row)
    rank_along = jnp.sum((column < row).astype(jnp.float32), axis=0, keepdims=True)
    rank_down = jnp.sum((row < column).astype(jnp.float32), axis=1, keepdims=True)
    sorted_down = jnp.sum(jnp.where(rank_along == down, row, 0.0), axis=1, keepdims=True)
    at_place = rank_down == along
    sorted_along = jnp.sum(jnp.where(at_place, column, 0.0), axis=0, keepdims=True)
    source_along = jnp.sum(jnp.where(at_place, down, 0.0), axis=0, keepdims=True)
    order_ref[...] = jnp.broadcast_to(sorted_down, size)
    place = along[:1]
    owner, share = jnp.zeros_like(place), jnp.zeros_like(place)
    for z in range(1, n_src // n_own):
        owner = owner + (sorted_along >= z * r_dev).astype(jnp.float32)
        share = share + (place >= z * n_own).astype(jnp.float32)
    far = jnp.where((place < n_src) & (jnp.abs(owner - share) > 1.5), 1.0, 0.0)
    plan_ref[...] = jnp.broadcast_to(source_along, plan_ref.shape).astype(jnp.int32)
    flag_ref[0] = jnp.max(far).astype(jnp.int32)


def spectra_kernel(
    n_win, n_rcv, r_dev, valid_hbm, src_hbm, x_hbm, coarse_hbm, fine_hbm, *refs
):
    r_refs = refs[:n_win]
    q_refs = refs[n_win:n_win + n_rcv]
    (plan_ref, flag_ref, x_ref, even_ref, odd_ref, white_ref, sel_ref, order_ref, table_ref,
     coarse_ref, fine_ref, valid_ref, src_ref, sems, x_sems) = refs[n_win + n_rcv:]
    chunks, rows, samples = x_ref.shape
    w_step = rows // r_dev
    n_own = src_ref.shape[0] // n_rcv
    quarter = samples // 4
    win = lax.axis_index("win")
    rcv = lax.axis_index("rcv")

    def small(k):
        source = (coarse_hbm, fine_hbm, src_hbm, valid_hbm)[k]
        target = (coarse_ref, fine_ref, src_ref, valid_ref)[k]
        return pltpu.make_async_copy(source, target, sems.at[k])

    def chunk(k):
        return pltpu.make_async_copy(x_hbm.at[pl.ds(k * rows, rows)], x_ref.at[k], x_sems.at[k])

    for k in range(4):
        small(k).start()
    for k in range(chunks):
        chunk(k).start()
    small(0).wait()
    small(1).wait()
    make_tables(coarse_ref, fine_ref, table_ref)
    small(2).wait()
    order_sources(src_ref, r_dev, n_own, order_ref, plan_ref, flag_ref)
    stations = []
    for d in range(n_rcv):
        share = pl.multiple_of((rcv ^ d) * n_own, n_own)
        stations += [order_ref[pl.ds(share, n_own), 0:1]] * w_step
    wanted = jnp.concatenate(stations, axis=0).astype(jnp.int32) - rcv * r_dev
    shape = (n_rcv * w_step * n_own, rows)
    out_row = lax.broadcasted_iota(jnp.int32, shape, 0)
    column = lax.broadcasted_iota(jnp.int32, shape, 1)
    inside = (wanted >= 0) & (wanted < r_dev)
    hit = inside & (column == wanted + (out_row // n_own) % w_step * r_dev)
    sel_ref[...] = hit.astype(jnp.float32).astype(jnp.bfloat16)
    small(3).wait()

    def product(lhs, table):
        return jnp.dot(lhs, table, preferred_element_type=jnp.float32)

    def add_quarters(k, first, last):
        part = slice(first, last)
        b0, b1, b2, b3 = (x_ref[k, part, q * quarter:(q + 1) * quarter] for q in range(4))
        x0, x1, x2, x3 = (b.astype(jnp.float32) for b in (b0, b1, b2, b3))
        even_ref[k, 0, part] = ((x0 + x2) + (x1 + x3)).astype(jnp.bfloat16)
        even_ref[k, 1, part] = ((x0 + x2) - (x1 + x3)).astype(jnp.bfloat16)
        odd_ref[k, part] = b0 - b2
        odd_ref[k, rows + first:rows + last] = b1 - b3

    lanes = table_ref.shape[2]
    lane = lax.broadcasted_iota(jnp.int32, (rows, lanes), 1)
    piece = lanes // n_win
    real = lane % piece < piece // 2

    def odd_spectra(k, m):
        both = product(odd_ref[k], table_ref[m])
        second = both[rows:]
        back, forth = pltpu.roll(second, lanes - piece // 2, 1), pltpu.roll(second, piece // 2, 1)
        turned = jnp.where(real, back, -forth)
        return both[:rows] + turned if m == 1 else both[:rows] - turned

    parts = 4
    size = rows // parts
    chunk(0).wait()
    add_quarters(0, 0, rows)
    row = lax.broadcasted_iota(jnp.int32, (rows, 1), 0)
    for k in range(chunks):
        more = k + 1 < chunks
        if more:
            chunk(k + 1).wait()
        spectra = []
        for m in range(4):
            if m % 2:
                spectra.append(odd_spectra(k, m))
            else:
                spectra.append(product(even_ref[k, m // 2], table_ref[m]))
            if more:
                add_quarters(k + 1, m * size, (m + 1) * size)
        squares = sum(jnp.sum(s * s, axis=1, keepdims=True) for s in spectra)
        gain = lax.rsqrt(squares / F + 1e-06)
        keep = jnp.zeros((rows, 1), jnp.float32)
        for t in range(w_step):
            own = (row >= t * r_dev) & (row < (t + 1) * r_dev)
            keep = jnp.where(own, valid_ref[k * w_step + t].astype(jnp.float32), keep)
        gain = gain * keep
        white = [s * gain for s in spectra]
        for d in range(n_win):
            columns = slice(d * piece, (d + 1) * piece)
            block = jnp.concatenate([part[:, columns] for part in white], axis=1)
            white_ref[k, d] = block.astype(jnp.bfloat16)
        count = w_step * n_own
        for j in range(n_win):
            block = white_ref[k, win ^ j]
            r_refs[j][k * rows:(k + 1) * rows, :] = block
            picked = product(sel_ref[...], block).astype(jnp.bfloat16)
            for d in range(n_rcv):
                q_refs[d][j, k * count:(k + 1) * count, :] = picked[d * count:(d + 1) * count]


def spectra_call(traces, valid, src_station, n_win, n_rcv):
    w_dev, r_dev, samples = traces.shape
    n_src = src_station.shape[0]
    n_own = n_src // n_rcv
    chunks = 4
    every = w_dev * r_dev
    rows = every // chunks
    lanes = 2 * F // n_win
    coarse, fine = (jnp.asarray(t) for t in angle_factors(samples, F, samples // 16, n_win))
    shapes = [jax.ShapeDtypeStruct((every, lanes), jnp.bfloat16)] * n_win
    shapes += [jax.ShapeDtypeStruct((n_win, w_dev * n_own, lanes), jnp.bfloat16)] * n_rcv
    shapes += [jax.ShapeDtypeStruct((8, 128), jnp.int32), jax.ShapeDtypeStruct((1,), jnp.int32)]
    vmem = pl.BlockSpec(memory_space=VMEM)
    out = pl.pallas_call(
        functools.partial(spectra_kernel, n_win, n_rcv, r_dev),
        in_specs=[pl.BlockSpec(memory_space=pltpu.HBM)] * 5,
        out_specs=[vmem] * (len(shapes) - 1) + [pl.BlockSpec(memory_space=SMEM)],
        out_shape=shapes,
        scratch_shapes=[
            pltpu.VMEM((chunks, rows, samples), jnp.bfloat16),
            pltpu.VMEM((chunks, 2, rows, samples // 4), jnp.bfloat16),
            pltpu.VMEM((chunks, 2 * rows, samples // 4), jnp.bfloat16),
            pltpu.VMEM((chunks, n_win, rows, lanes), jnp.bfloat16),
            pltpu.VMEM((n_src * (w_dev // chunks), rows), jnp.bfloat16),
            pltpu.VMEM((n_src, 128), jnp.float32),
            pltpu.VMEM((4, samples // 4, F // 2), jnp.bfloat16),
            pltpu.VMEM(coarse.shape, jnp.float32),
            pltpu.VMEM(fine.shape, jnp.float32),
            pltpu.SMEM(valid.shape, jnp.int32),
            pltpu.SMEM(src_station.shape, jnp.int32),
            pltpu.SemaphoreType.DMA((4,)),
            pltpu.SemaphoreType.DMA((chunks,)),
        ],
        compiler_params=pltpu.CompilerParams(vmem_limit_bytes=36 * 2**20),
        cost_estimate=pl.CostEstimate(
            flops=2 * every * (samples // 4) * 6 * (F // 2), bytes_accessed=every * samples * 2,
            transcendentals=0,
        ),
        name="spectra",
    )(*(in_hbm(x) for x in (valid, src_station, traces.reshape(every, samples), coarse, fine)))
    return out[:n_win], out[n_win:n_win + n_rcv], out[-2], out[-1]


def bin_order(lanes):
    quarter = lanes // 8
    lane = lax.broadcasted_iota(jnp.int32, (lanes, lanes), 1)
    row = lax.broadcasted_iota(jnp.int32, (lanes, lanes), 0)
    part = (lane // quarter) % 2
    bin_of = 4 * (lane % quarter) + lane // (2 * quarter)
    hit = row == part * (lanes // 2) + bin_of
    return hit.astype(jnp.float32).astype(jnp.bfloat16)


def turn_kernel(r_dev, *refs):
    x_refs, (out_ref, rows_ref) = refs[:-2], refs[-2:]
    lanes = x_refs[0].shape[1]
    bins = lanes // 2
    w_dev = out_ref.shape[1] // 2
    pad = out_ref.shape[2] // 2
    order = bin_order(lanes)
    windows = [(x, w) for x in x_refs for w in range(x.shape[0] // r_dev)]
    for k, (x_ref, w) in enumerate(windows):
        turned = lax.dot_general(
            order, x_ref[w * r_dev:(w + 1) * r_dev], (((1,), (1,)), ((), ())),
            preferred_element_type=jnp.float32,
        )
        rows_ref[pl.ds(k, lanes, stride=w_dev), :r_dev] = turned
    rr = rows_ref[:bins * w_dev].reshape(bins, w_dev, pad)
    ri = rows_ref[bins * w_dev:].reshape(bins, w_dev, pad)
    out_ref[:, :, :pad] = jnp.concatenate([rr, ri], axis=1).astype(jnp.bfloat16)
    out_ref[:, :, pad:] = jnp.concatenate([ri, -rr], axis=1).astype(jnp.bfloat16)


def turn_call(parts, w_dev, r_dev):
    lanes = parts[0].shape[1]
    pad = 128
    vmem = pl.BlockSpec(memory_space=VMEM)
    return pl.pallas_call(
        functools.partial(turn_kernel, r_dev),
        in_specs=[vmem] * len(parts),
        out_specs=vmem,
        out_shape=jax.ShapeDtypeStruct((lanes // 2, 2 * w_dev, 2 * pad), jnp.bfloat16),
        scratch_shapes=[pltpu.VMEM((lanes * w_dev, pad), jnp.float32)],
        compiler_params=pltpu.CompilerParams(vmem_limit_bytes=16 * 2**20),
        cost_estimate=pl.CostEstimate(
            flops=2 * w_dev * lanes * lanes * pad, bytes_accessed=2 * 2**20, transcendentals=0
        ),
        name="turn",
    )(*parts)


def merge_kernel(n_win, *refs):
    picked, outs = refs[:-n_win], refs[-n_win:]
    for j, out_ref in enumerate(outs):
        total = picked[0][j].astype(jnp.float32)
        for q_ref in picked[1:]:
            total = total + q_ref[j].astype(jnp.float32)
        out_ref[...] = total.astype(jnp.bfloat16)


def merge_call(*picked):
    n_win, rows, lanes = picked[0].shape
    vmem = pl.BlockSpec(memory_space=VMEM)
    return pl.pallas_call(
        functools.partial(merge_kernel, n_win),
        in_specs=[vmem] * len(picked),
        out_specs=[vmem] * n_win,
        out_shape=[jax.ShapeDtypeStruct((rows, lanes), jnp.bfloat16)] * n_win,
        compiler_params=pltpu.CompilerParams(vmem_limit_bytes=4 * 2**20),
        cost_estimate=pl.CostEstimate(flops=2**18, bytes_accessed=2**19, transcendentals=0),
        name="merge",
    )(*picked)


def join_kernel(n_win, *refs):
    out_ref = refs[-1]
    for j in range(n_win):
        out_ref[j] = refs[j][...]


def join_call(blocks, after, later):
    rows, lanes = blocks[0].shape
    n_win = len(blocks)
    vmem, anywhere = pl.BlockSpec(memory_space=VMEM), pl.BlockSpec(memory_space=pl.ANY)
    out = pl.pallas_call(
        functools.partial(join_kernel, n_win),
        in_specs=[vmem] * n_win + [anywhere] * (1 + len(later)),
        out_specs=[anywhere] * len(later) + [vmem],
        out_shape=[jax.ShapeDtypeStruct(x.shape, x.dtype) for x in later]
        + [jax.ShapeDtypeStruct((n_win, rows, lanes), jnp.bfloat16)],
        input_output_aliases={n_win + 1 + k: k for k in range(len(later))},
        compiler_params=pltpu.CompilerParams(vmem_limit_bytes=4 * 2**20),
        cost_estimate=pl.CostEstimate(flops=2**18, bytes_accessed=2**19, transcendentals=0),
        name="join",
    )(*blocks, after, *later)
    return out[-1], out[:-1]


def stacks_kernel(shares, n_win, w_dev, r_dev, n_own, bins, plan_hbm, *refs):
    t_refs = refs[:n_win]
    s_refs = refs[n_win:n_win + len(shares)]
    out_hbm, srow_ref, left_ref, prod_ref, out_ref, plan_ref, sems, plan_sem = refs[-8:]
    plan_copy = pltpu.make_async_copy(plan_hbm, plan_ref, plan_sem)
    plan_copy.start()
    lanes = 2 * bins
    windows = n_win * w_dev
    count = len(shares) * n_own
    pad = 128
    rcv = lax.axis_index("rcv")

    def product(lhs, rhs, dims=(((1,), (0,)), ((), ()))):
        return lax.dot_general(lhs, rhs, dims, preferred_element_type=jnp.float32)

    order = bin_order(lanes)
    both = order[:bins] + order[bins:]
    lane = lax.broadcasted_iota(jnp.int32, (w_dev, lanes), 1)
    real = (lane // (bins // 4)) % 2 == 0

    for k, s_ref in enumerate(s_refs):
        for j in range(n_win):
            block = s_ref[j].astype(jnp.float32)
            for h in range(lanes // pad):
                half = block[:, h * pad:(h + 1) * pad]
                srow_ref[h, pl.ds((k * n_win + j) * w_dev * n_own, w_dev * n_own), :] = half
    for s in range(count):
        first = s // n_own * windows * n_own + s % n_own
        values = jnp.concatenate(
            [srow_ref[h, pl.ds(first, windows, stride=n_own), :] for h in range(lanes // pad)],
            axis=1,
        )
        stacked = []
        for j in range(n_win):
            own = values[j * w_dev:(j + 1) * w_dev]
            stacked += [jnp.where(real, own, 0.0), jnp.where(real, 0.0, own)]
        stacked = jnp.concatenate(stacked, axis=0).astype(jnp.bfloat16)
        turned = product(both, stacked, (((1,), (1,)), ((), ())))
        left_ref[pl.ds(s, bins, stride=count), :2 * windows] = turned

    for f in range(bins):
        right = jnp.concatenate([t_ref[f] for t_ref in t_refs], axis=0)
        left = left_ref[pl.ds(f * count, count), :2 * windows].astype(jnp.bfloat16)
        result = product(left, right)
        for c in range(2):
            prod_ref[c, pl.ds(f, count, stride=bins), :] = result[:, c * pad:(c + 1) * pad]

    scale = 1.0 / math.sqrt(windows)
    plan_copy.wait()
    copies = []
    for s in range(count):
        for c in range(2):
            turned = prod_ref[c, s * bins:(s + 1) * bins, :].T
            out_ref[s, pl.ds(c, r_dev, stride=2), :] = turned[:r_dev] * scale
        row = plan_ref[0, (rcv ^ shares[s // n_own]) * n_own + s % n_own]
        copies.append(pltpu.make_async_copy(out_ref.at[s], out_hbm.at[row], sems.at[s]))
        copies[-1].start()
    for copy in copies:
        copy.wait()


def stacks_call(out, plan, turned, sources, shares, n_rcv, w_dev, r_dev, bins):
    n_win = len(turned)
    n_own = sources[0].shape[1] // w_dev
    windows = n_win * w_dev
    count = len(shares) * n_own
    whole = pl.BlockSpec(memory_space=VMEM)
    args = [plan] + list(turned) + [sources[i] for i in shares]
    specs = [pl.BlockSpec(memory_space=pl.ANY)] + [whole] * (len(args) - 1)
    aliases = {}
    if out is not None:
        aliases = {len(args): 0}
        args.append(out)
        specs.append(pl.BlockSpec(memory_space=pl.ANY))
    return pl.pallas_call(
        functools.partial(stacks_kernel, shares, n_win, w_dev, r_dev, n_own, bins),
        in_specs=specs,
        out_specs=pl.BlockSpec(memory_space=pltpu.HBM),
        out_shape=jax.ShapeDtypeStruct((n_rcv * n_own, 2 * r_dev, bins), jnp.float32),
        input_output_aliases=aliases,
        scratch_shapes=[
            pltpu.VMEM((2 * bins // 128, windows * count, 128), jnp.float32),
            pltpu.VMEM((bins * count, 128), jnp.float32),
            pltpu.VMEM((2, count * bins, 128), jnp.float32),
            pltpu.VMEM((count, 2 * r_dev, bins), jnp.float32),
            pltpu.SMEM(plan.shape, jnp.int32),
            pltpu.SemaphoreType.DMA((count,)),
            pltpu.SemaphoreType.DMA,
        ],
        compiler_params=pltpu.CompilerParams(vmem_limit_bytes=20 * 2**20),
        cost_estimate=pl.CostEstimate(
            flops=8 * windows * count * r_dev * bins, bytes_accessed=6 * 2**20, transcendentals=0
        ),
        name="stacks",
    )(*args)


def swap(value, axis, by):
    size = lax.axis_size(axis)
    return lax.ppermute(value, axis, [(i, i ^ by) for i in range(size)])


def near_and_far(n_rcv, by):
    pairs = [(z, z ^ by) for z in range(n_rcv)]
    return [p for p in pairs if abs(p[0] - p[1]) == 1], [p for p in pairs if abs(p[0] - p[1]) > 1]


def merge_near(picked, near):
    return merge_call(picked[0], *near)


def merge_all(picked, near):
    far = []
    for i in range(1, len(picked)):
        pairs = near_and_far(len(picked), i)[1]
        if pairs:
            far.append(lax.ppermute(picked[i], "rcv", pairs))
    return merge_call(picked[0], *near, *far)


def body(traces, valid, src_station):
    w_dev, r_dev, samples = traces.shape
    n_src = src_station.shape[0]
    n_win = lax.axis_size("win")
    n_rcv = lax.axis_size("rcv")
    bins = F // n_win
    early = n_win // 2

    blocks, picked, plan, flag = spectra_call(traces, valid, src_station, n_win, n_rcv)

    near = []
    for i in range(1, n_rcv):
        pairs = near_and_far(n_rcv, i)[0]
        if pairs:
            near.append(lax.ppermute(picked[i], "rcv", pairs))
    merged = lax.cond(flag.reshape(()) > 0, merge_all, merge_near, picked, near)

    merged = [merged[0]] + [swap(merged[j], "win", j) for j in range(1, n_win)]
    late = [j for j in range(1, n_win) if j != early]
    received = {0: blocks[0], early: swap(blocks[early], "win", early)}
    joined, later = join_call(merged, received[early], [blocks[j] for j in late])
    received.update({j: swap(block, "win", j) for j, block in zip(late, later)})
    sources = [joined] + [swap(joined, "rcv", i) for i in range(1, n_rcv)]

    turned = [turn_call([received[j]], w_dev, r_dev) for j in range(n_win)]
    half = n_rcv // 2
    sizes = (n_rcv, w_dev, r_dev, bins)
    stacks = stacks_call(None, plan, turned, sources, tuple(range(half)), *sizes)
    stacks = stacks_call(stacks, plan, turned, sources, tuple(range(half, n_rcv)), *sizes)
    return stacks.reshape(n_src, r_dev, 2, bins)


def correlate(received, sources):
    rr = received[:, :, 0]
    ri = received[:, :, 1]
    sr = sources[:, :, 0]
    si = sources[:, :, 1]
    real = jnp.einsum("wsf,wrf->srf", sr, rr, preferred_element_type=jnp.float32)
    real = real + jnp.einsum("wsf,wrf->srf", si, ri, preferred_element_type=jnp.float32)
    imag = jnp.einsum("wsf,wrf->srf", sr, ri, preferred_element_type=jnp.float32)
    imag = imag - jnp.einsum("wsf,wrf->srf", si, rr, preferred_element_type=jnp.float32)
    return jnp.stack([real, imag], axis=2)


def body_any(traces, valid, src_station):
    w_dev, r_dev, samples = traces.shape
    n_win = lax.axis_size("win")
    n_rcv = lax.axis_size("rcv")
    bins = F // n_win
    table = jnp.asarray(band_table(samples, F, samples // 16))
    spectra = jnp.dot(
        traces.reshape(w_dev * r_dev, samples), table, preferred_element_type=jnp.float32
    )
    spectra = spectra.reshape(w_dev, r_dev, 2, F)
    power = jnp.sum(spectra * spectra, axis=(2, 3), keepdims=True) / F
    keep = valid.astype(jnp.float32)[:, None, None, None]
    white = (spectra * lax.rsqrt(power + 1e-06) * keep).astype(jnp.bfloat16)
    blocks = white.reshape(w_dev, r_dev, 2, n_win, bins).transpose(3, 0, 1, 2, 4)
    me = lax.axis_index("win")
    offset = lax.axis_index("rcv") * r_dev
    station_ids = offset + jnp.arange(r_dev, dtype=jnp.int32)
    selector = (src_station[:, None] == station_ids[None, :]).astype(jnp.bfloat16)
    received = []
    for j in range(n_win):
        block = lax.dynamic_index_in_dim(blocks, me ^ j, 0, keepdims=False)
        received.append(swap(block, "win", j) if j else block)
    received = jnp.concatenate(received, axis=0)
    rows = jnp.einsum("sr,wrcf->wscf", selector, received, preferred_element_type=jnp.float32)
    rows = lax.all_to_all(rows.astype(jnp.bfloat16), "rcv", 0, 0, tiled=True)
    rows = rows.reshape((n_rcv, -1) + rows.shape[1:])
    merged = jnp.sum(rows.astype(jnp.float32), axis=0).astype(jnp.bfloat16)
    sources = lax.all_gather(merged, "rcv", axis=0, tiled=True)
    return correlate(received, sources) * (1.0 / math.sqrt(w_dev * n_win))


def solution(mesh):
    sizes = (mesh.shape["win"], mesh.shape["rcv"])
    return jax.shard_map(
        body if sizes == (4, 4) else body_any,
        mesh=mesh,
        in_specs=(P("win", ("groups", "rcv"), None), P(("groups", "win")), P("groups")),
        out_specs=P(None, ("groups", "rcv"), None, "win"),
        check_vma=False,
    )
```

```python
import functools
import math

import jax
import jax.numpy as jnp
import numpy as np
from jax import lax
from jax.experimental import pallas as pl
from jax.experimental.pallas import tpu as pltpu
from jax.sharding import PartitionSpec as P

F = 512
SMEM = pltpu.MemorySpace.SMEM
VMEM = pltpu.MemorySpace.VMEM


def angles(samples, freqs, count):
    phase = samples[:, None] * freqs[None, :] % count
    return phase.astype(np.float64) * (2.0 * math.pi / count)


def band_table(count, bins, first):
    angle = angles(np.arange(count), first + np.arange(bins), count)
    return np.concatenate([np.cos(angle), -np.sin(angle)], axis=1).astype(jnp.bfloat16)


BLOCK = 32


def table_seeds(count, bins, first, n_win):
    j = np.arange(bins // 4)
    turn = np.array([0.0, 0.5 * math.pi]).reshape(1, 2, 1)
    seeds, twice = [], []
    for m in range(4):
        freqs = np.broadcast_to((first + 4 * j + m).reshape(n_win, 1, -1), (n_win, 2, j.size // n_win))
        angle = angles(np.arange(2 * BLOCK), freqs.reshape(-1), count)
        angle = angle + np.broadcast_to(turn, freqs.shape).reshape(1, -1)
        seeds.append(np.cos(angle).reshape(2, BLOCK, -1))
        step = angles(np.full(8, BLOCK), freqs.reshape(-1), count)
        twice.append(2.0 * np.cos(step))
    return np.stack(seeds).astype(np.float32), np.stack(twice).astype(np.float32)


def make_tables(seed_ref, twice_ref, table_ref):
    for first in (0, 2):
        state = {}
        for m in (first, first + 1):
            twice = jnp.concatenate([twice_ref[m]] * (BLOCK // 8), axis=0)
            state[m] = (seed_ref[m, 0], seed_ref[m, 1], twice)
        for a in range(table_ref.shape[1] // BLOCK):
            for m, (here, after, twice) in state.items():
                table_ref[m, a * BLOCK:(a + 1) * BLOCK, :] = here.astype(jnp.bfloat16)
                state[m] = (after, twice * after - here, twice)


def in_hbm(value):
    return pltpu.with_memory_space_constraint(value, pltpu.HBM)


def order_sources(src_ref, r_dev, n_own, order_ref, plan_ref, flag_ref):
    n_src = src_ref.shape[0]
    size = order_ref.shape
    down = lax.broadcasted_iota(jnp.int32, size, 0).astype(jnp.float32)
    along = lax.broadcasted_iota(jnp.int32, size, 1).astype(jnp.float32)
    none = jnp.full(size, float(2**20), jnp.float32)
    column, row = none, none
    for s in range(n_src):
        station = src_ref[s].astype(jnp.float32)
        column = jnp.where(down == s, station, column)
        row = jnp.where(along == s, station, row)
    rank_along = jnp.sum((column < row).astype(jnp.float32), axis=0, keepdims=True)
    rank_down = jnp.sum((row < column).astype(jnp.float32), axis=1, keepdims=True)
    sorted_down = jnp.sum(jnp.where(rank_along == down, row, 0.0), axis=1, keepdims=True)
    at_place = rank_down == along
    sorted_along = jnp.sum(jnp.where(at_place, column, 0.0), axis=0, keepdims=True)
    source_along = jnp.sum(jnp.where(at_place, down, 0.0), axis=0, keepdims=True)
    order_ref[...] = jnp.broadcast_to(sorted_down, size)
    place = along[:1]
    owner, share = jnp.zeros_like(place), jnp.zeros_like(place)
    for z in range(1, n_src // n_own):
        owner = owner + (sorted_along >= z * r_dev).astype(jnp.float32)
        share = share + (place >= z * n_own).astype(jnp.float32)
    far = jnp.where((place < n_src) & (jnp.abs(owner - share) > 1.5), 1.0, 0.0)
    plan_ref[...] = jnp.broadcast_to(source_along, plan_ref.shape).astype(jnp.int32)
    flag_ref[0] = jnp.max(far).astype(jnp.int32)


def spectra_kernel(
    n_win, n_rcv, r_dev, valid_hbm, src_hbm, x_hbm, seed_hbm, twice_hbm, *refs
):
    r_refs = refs[:n_win]
    q_refs = refs[n_win:n_win + n_rcv]
    (plan_ref, flag_ref, x_ref, even_ref, odd_ref, white_ref, sel_ref, order_ref, table_ref,
     seed_ref, twice_ref, valid_ref, src_ref, sems, x_sems) = refs[n_win + n_rcv:]
    chunks, rows, samples = x_ref.shape
    w_step = rows // r_dev
    n_own = src_ref.shape[0] // n_rcv
    quarter = samples // 4
    win = lax.axis_index("win")
    rcv = lax.axis_index("rcv")

    def small(k):
        source = (seed_hbm, twice_hbm, src_hbm, valid_hbm)[k]
        target = (seed_ref, twice_ref, src_ref, valid_ref)[k]
        return pltpu.make_async_copy(source, target, sems.at[k])

    def chunk(k):
        return pltpu.make_async_copy(x_hbm.at[pl.ds(k * rows, rows)], x_ref.at[k], x_sems.at[k])

    for k in range(4):
        small(k).start()
    for k in range(chunks):
        chunk(k).start()
    small(0).wait()
    small(1).wait()
    make_tables(seed_ref, twice_ref, table_ref)
    small(2).wait()
    order_sources(src_ref, r_dev, n_own, order_ref, plan_ref, flag_ref)
    stations = []
    for d in range(n_rcv):
        share = pl.multiple_of((rcv ^ d) * n_own, n_own)
        stations += [order_ref[pl.ds(share, n_own), 0:1]] * w_step
    wanted = jnp.concatenate(stations, axis=0).astype(jnp.int32) - rcv * r_dev
    shape = (n_rcv * w_step * n_own, rows)
    out_row = lax.broadcasted_iota(jnp.int32, shape, 0)
    column = lax.broadcasted_iota(jnp.int32, shape, 1)
    inside = (wanted >= 0) & (wanted < r_dev)
    hit = inside & (column == wanted + (out_row // n_own) % w_step * r_dev)
    sel_ref[...] = hit.astype(jnp.float32).astype(jnp.bfloat16)
    small(3).wait()

    def product(lhs, table):
        return jnp.dot(lhs, table, preferred_element_type=jnp.float32)

    def add_quarters(k, first, last):
        part = slice(first, last)
        b0, b1, b2, b3 = (x_ref[k, part, q * quarter:(q + 1) * quarter] for q in range(4))
        x0, x1, x2, x3 = (b.astype(jnp.float32) for b in (b0, b1, b2, b3))
        even_ref[k, 0, part] = ((x0 + x2) + (x1 + x3)).astype(jnp.bfloat16)
        even_ref[k, 1, part] = ((x0 + x2) - (x1 + x3)).astype(jnp.bfloat16)
        odd_ref[k, part] = b0 - b2
        odd_ref[k, rows + first:rows + last] = b1 - b3

    lanes = table_ref.shape[2]
    lane = lax.broadcasted_iota(jnp.int32, (rows, lanes), 1)
    piece = lanes // n_win
    real = lane % piece < piece // 2

    def odd_spectra(k, m):
        both = product(odd_ref[k], table_ref[m])
        second = both[rows:]
        back, forth = pltpu.roll(second, lanes - piece // 2, 1), pltpu.roll(second, piece // 2, 1)
        turned = jnp.where(real, back, -forth)
        return both[:rows] + turned if m == 1 else both[:rows] - turned

    parts = 4
    size = rows // parts
    chunk(0).wait()
    add_quarters(0, 0, rows)
    row = lax.broadcasted_iota(jnp.int32, (rows, 1), 0)
    for k in range(chunks):
        more = k + 1 < chunks
        if more:
            chunk(k + 1).wait()
        spectra = []
        for m in range(4):
            if m % 2:
                spectra.append(odd_spectra(k, m))
            else:
                spectra.append(product(even_ref[k, m // 2], table_ref[m]))
            if more:
                add_quarters(k + 1, m * size, (m + 1) * size)
        squares = sum(jnp.sum(s * s, axis=1, keepdims=True) for s in spectra)
        gain = lax.rsqrt(squares / F + 1e-06)
        keep = jnp.zeros((rows, 1), jnp.float32)
        for t in range(w_step):
            own = (row >= t * r_dev) & (row < (t + 1) * r_dev)
            keep = jnp.where(own, valid_ref[k * w_step + t].astype(jnp.float32), keep)
        gain = gain * keep
        white = [s * gain for s in spectra]
        for d in range(n_win):
            columns = slice(d * piece, (d + 1) * piece)
            block = jnp.concatenate([part[:, columns] for part in white], axis=1)
            white_ref[k, d] = block.astype(jnp.bfloat16)
        count = w_step * n_own
        for j in range(n_win):
            block = white_ref[k, win ^ j]
            r_refs[j][k * rows:(k + 1) * rows, :] = block
            picked = product(sel_ref[...], block).astype(jnp.bfloat16)
            for d in range(n_rcv):
                q_refs[d][j, k * count:(k + 1) * count, :] = picked[d * count:(d + 1) * count]


def spectra_call(traces, valid, src_station, n_win, n_rcv):
    w_dev, r_dev, samples = traces.shape
    n_src = src_station.shape[0]
    n_own = n_src // n_rcv
    chunks = 4
    every = w_dev * r_dev
    rows = every // chunks
    lanes = 2 * F // n_win
    seed, twice = (jnp.asarray(t) for t in table_seeds(samples, F, samples // 16, n_win))
    shapes = [jax.ShapeDtypeStruct((every, lanes), jnp.bfloat16)] * n_win
    shapes += [jax.ShapeDtypeStruct((n_win, w_dev * n_own, lanes), jnp.bfloat16)] * n_rcv
    shapes += [jax.ShapeDtypeStruct((8, 128), jnp.int32), jax.ShapeDtypeStruct((1,), jnp.int32)]
    vmem = pl.BlockSpec(memory_space=VMEM)
    out = pl.pallas_call(
        functools.partial(spectra_kernel, n_win, n_rcv, r_dev),
        in_specs=[pl.BlockSpec(memory_space=pltpu.HBM)] * 5,
        out_specs=[vmem] * (len(shapes) - 1) + [pl.BlockSpec(memory_space=SMEM)],
        out_shape=shapes,
        scratch_shapes=[
            pltpu.VMEM((chunks, rows, samples), jnp.bfloat16),
            pltpu.VMEM((chunks, 2, rows, samples // 4), jnp.bfloat16),
            pltpu.VMEM((chunks, 2 * rows, samples // 4), jnp.bfloat16),
            pltpu.VMEM((chunks, n_win, rows, lanes), jnp.bfloat16),
            pltpu.VMEM((n_src * (w_dev // chunks), rows), jnp.bfloat16),
            pltpu.VMEM((n_src, 128), jnp.float32),
            pltpu.VMEM((4, samples // 4, F // 2), jnp.bfloat16),
            pltpu.VMEM(seed.shape, jnp.float32),
            pltpu.VMEM(twice.shape, jnp.float32),
            pltpu.SMEM(valid.shape, jnp.int32),
            pltpu.SMEM(src_station.shape, jnp.int32),
            pltpu.SemaphoreType.DMA((4,)),
            pltpu.SemaphoreType.DMA((chunks,)),
        ],
        compiler_params=pltpu.CompilerParams(vmem_limit_bytes=36 * 2**20),
        cost_estimate=pl.CostEstimate(
            flops=2 * every * (samples // 4) * 6 * (F // 2), bytes_accessed=every * samples * 2,
            transcendentals=0,
        ),
        name="spectra",
    )(*(in_hbm(x) for x in (valid, src_station, traces.reshape(every, samples), seed, twice)))
    return out[:n_win], out[n_win:n_win + n_rcv], out[-2], out[-1]


def bin_order(lanes):
    quarter = lanes // 8
    lane = lax.broadcasted_iota(jnp.int32, (lanes, lanes), 1)
    row = lax.broadcasted_iota(jnp.int32, (lanes, lanes), 0)
    part = (lane // quarter) % 2
    bin_of = 4 * (lane % quarter) + lane // (2 * quarter)
    hit = row == part * (lanes // 2) + bin_of
    return hit.astype(jnp.float32).astype(jnp.bfloat16)


def turn_kernel(r_dev, *refs):
    x_refs, (out_ref, rows_ref) = refs[:-2], refs[-2:]
    lanes = x_refs[0].shape[1]
    bins = lanes // 2
    w_dev = out_ref.shape[1] // 2
    pad = out_ref.shape[2] // 2
    order = bin_order(lanes)
    windows = [(x, w) for x in x_refs for w in range(x.shape[0] // r_dev)]
    for k, (x_ref, w) in enumerate(windows):
        turned = lax.dot_general(
            order, x_ref[w * r_dev:(w + 1) * r_dev], (((1,), (1,)), ((), ())),
            preferred_element_type=jnp.float32,
        )
        rows_ref[pl.ds(k, lanes, stride=w_dev), :r_dev] = turned
    rr = rows_ref[:bins * w_dev].reshape(bins, w_dev, pad)
    ri = rows_ref[bins * w_dev:].reshape(bins, w_dev, pad)
    out_ref[:, :, :pad] = jnp.concatenate([rr, ri], axis=1).astype(jnp.bfloat16)
    out_ref[:, :, pad:] = jnp.concatenate([ri, -rr], axis=1).astype(jnp.bfloat16)


def turn_call(parts, w_dev, r_dev):
    lanes = parts[0].shape[1]
    pad = 128
    vmem = pl.BlockSpec(memory_space=VMEM)
    return pl.pallas_call(
        functools.partial(turn_kernel, r_dev),
        in_specs=[vmem] * len(parts),
        out_specs=vmem,
        out_shape=jax.ShapeDtypeStruct((lanes // 2, 2 * w_dev, 2 * pad), jnp.bfloat16),
        scratch_shapes=[pltpu.VMEM((lanes * w_dev, pad), jnp.float32)],
        compiler_params=pltpu.CompilerParams(vmem_limit_bytes=16 * 2**20),
        cost_estimate=pl.CostEstimate(
            flops=2 * w_dev * lanes * lanes * pad, bytes_accessed=2 * 2**20, transcendentals=0
        ),
        name="turn",
    )(*parts)


def merge_kernel(n_win, *refs):
    picked, outs = refs[:-n_win], refs[-n_win:]
    for j, out_ref in enumerate(outs):
        total = picked[0][j].astype(jnp.float32)
        for q_ref in picked[1:]:
            total = total + q_ref[j].astype(jnp.float32)
        out_ref[...] = total.astype(jnp.bfloat16)


def merge_call(*picked):
    n_win, rows, lanes = picked[0].shape
    vmem = pl.BlockSpec(memory_space=VMEM)
    return pl.pallas_call(
        functools.partial(merge_kernel, n_win),
        in_specs=[vmem] * len(picked),
        out_specs=[vmem] * n_win,
        out_shape=[jax.ShapeDtypeStruct((rows, lanes), jnp.bfloat16)] * n_win,
        compiler_params=pltpu.CompilerParams(vmem_limit_bytes=4 * 2**20),
        cost_estimate=pl.CostEstimate(flops=2**18, bytes_accessed=2**19, transcendentals=0),
        name="merge",
    )(*picked)


def join_kernel(count, *refs):
    out_ref = refs[-1]
    for k in range(count):
        out_ref[k] = refs[k][...]


def join_call(blocks, after=(), later=()):
    rows, lanes = blocks[0].shape
    count = len(blocks)
    first = count + len(after)
    vmem, anywhere = pl.BlockSpec(memory_space=VMEM), pl.BlockSpec(memory_space=pl.ANY)
    out = pl.pallas_call(
        functools.partial(join_kernel, count),
        in_specs=[vmem] * count + [anywhere] * (len(after) + len(later)),
        out_specs=[anywhere] * len(later) + [vmem],
        out_shape=[jax.ShapeDtypeStruct(x.shape, x.dtype) for x in later]
        + [jax.ShapeDtypeStruct((count, rows, lanes), jnp.bfloat16)],
        input_output_aliases={first + k: k for k in range(len(later))},
        compiler_params=pltpu.CompilerParams(vmem_limit_bytes=4 * 2**20),
        cost_estimate=pl.CostEstimate(flops=2**18, bytes_accessed=2**19, transcendentals=0),
        name="join",
    )(*blocks, *after, *later)
    return out[-1], out[:-1]


def stacks_kernel(shares, n_parts, n_win, w_dev, r_dev, n_own, bins, plan_hbm, *refs):
    t_refs = refs[:n_win]
    s_refs = refs[n_win:n_win + n_parts * len(shares)]
    out_hbm, srow_ref, left_ref, prod_ref, out_ref, plan_ref, sems, plan_sem = refs[-8:]
    plan_copy = pltpu.make_async_copy(plan_hbm, plan_ref, plan_sem)
    plan_copy.start()
    lanes = 2 * bins
    windows = n_win * w_dev
    count = len(shares) * n_own
    pad = 128
    rcv = lax.axis_index("rcv")

    def product(lhs, rhs, dims=(((1,), (0,)), ((), ()))):
        return lax.dot_general(lhs, rhs, dims, preferred_element_type=jnp.float32)

    order = bin_order(lanes)
    both = order[:bins] + order[bins:]
    lane = lax.broadcasted_iota(jnp.int32, (w_dev, lanes), 1)
    real = (lane // (bins // 4)) % 2 == 0

    for k in range(len(shares)):
        for j in range(n_win):
            part, place = divmod(j, n_win // n_parts)
            block = s_refs[k * n_parts + part][place].astype(jnp.float32)
            for h in range(lanes // pad):
                half = block[:, h * pad:(h + 1) * pad]
                srow_ref[h, pl.ds((k * n_win + j) * w_dev * n_own, w_dev * n_own), :] = half
    for s in range(count):
        first = s // n_own * windows * n_own + s % n_own
        values = jnp.concatenate(
            [srow_ref[h, pl.ds(first, windows, stride=n_own), :] for h in range(lanes // pad)],
            axis=1,
        )
        stacked = []
        for j in range(n_win):
            own = values[j * w_dev:(j + 1) * w_dev]
            stacked += [jnp.where(real, own, 0.0), jnp.where(real, 0.0, own)]
        stacked = jnp.concatenate(stacked, axis=0).astype(jnp.bfloat16)
        turned = product(both, stacked, (((1,), (1,)), ((), ())))
        left_ref[pl.ds(s, bins, stride=count), :2 * windows] = turned

    for f in range(bins):
        right = jnp.concatenate([t_ref[f] for t_ref in t_refs], axis=0)
        left = left_ref[pl.ds(f * count, count), :2 * windows].astype(jnp.bfloat16)
        result = product(left, right)
        for c in range(2):
            prod_ref[c, pl.ds(f, count, stride=bins), :] = result[:, c * pad:(c + 1) * pad]

    scale = 1.0 / math.sqrt(windows)
    plan_copy.wait()
    copies = []
    for s in range(count):
        for c in range(2):
            turned = prod_ref[c, s * bins:(s + 1) * bins, :].T
            out_ref[s, pl.ds(c, r_dev, stride=2), :] = turned[:r_dev] * scale
        row = plan_ref[0, (rcv ^ shares[s // n_own]) * n_own + s % n_own]
        copies.append(pltpu.make_async_copy(out_ref.at[s], out_hbm.at[row], sems.at[s]))
        copies[-1].start()
    for copy in copies:
        copy.wait()


def stacks_call(out, plan, turned, sources, shares, n_rcv, w_dev, r_dev, bins):
    n_win = len(turned)
    n_parts = len(sources[0])
    n_own = sources[0][0].shape[1] // w_dev
    windows = n_win * w_dev
    count = len(shares) * n_own
    whole = pl.BlockSpec(memory_space=VMEM)
    args = [plan] + list(turned) + [part for i in shares for part in sources[i]]
    specs = [pl.BlockSpec(memory_space=pl.ANY)] + [whole] * (len(args) - 1)
    aliases = {}
    if out is not None:
        aliases = {len(args): 0}
        args.append(out)
        specs.append(pl.BlockSpec(memory_space=pl.ANY))
    return pl.pallas_call(
        functools.partial(stacks_kernel, shares, n_parts, n_win, w_dev, r_dev, n_own, bins),
        in_specs=specs,
        out_specs=pl.BlockSpec(memory_space=pltpu.HBM),
        out_shape=jax.ShapeDtypeStruct((n_rcv * n_own, 2 * r_dev, bins), jnp.float32),
        input_output_aliases=aliases,
        scratch_shapes=[
            pltpu.VMEM((2 * bins // 128, windows * count, 128), jnp.float32),
            pltpu.VMEM((bins * count, 128), jnp.float32),
            pltpu.VMEM((2, count * bins, 128), jnp.float32),
            pltpu.VMEM((count, 2 * r_dev, bins), jnp.float32),
            pltpu.SMEM(plan.shape, jnp.int32),
            pltpu.SemaphoreType.DMA((count,)),
            pltpu.SemaphoreType.DMA,
        ],
        compiler_params=pltpu.CompilerParams(vmem_limit_bytes=20 * 2**20),
        cost_estimate=pl.CostEstimate(
            flops=8 * windows * count * r_dev * bins, bytes_accessed=6 * 2**20, transcendentals=0
        ),
        name="stacks",
    )(*args)


def swap(value, axis, by):
    size = lax.axis_size(axis)
    return lax.ppermute(value, axis, [(i, i ^ by) for i in range(size)])


def near_and_far(n_rcv, by):
    pairs = [(z, z ^ by) for z in range(n_rcv)]
    return [p for p in pairs if abs(p[0] - p[1]) == 1], [p for p in pairs if abs(p[0] - p[1]) > 1]


def merge_near(picked, near):
    return merge_call(picked[0], *near)


def merge_all(picked, near):
    far = []
    for i in range(1, len(picked)):
        pairs = near_and_far(len(picked), i)[1]
        if pairs:
            far.append(lax.ppermute(picked[i], "rcv", pairs))
    return merge_call(picked[0], *near, *far)


def body(traces, valid, src_station):
    w_dev, r_dev, samples = traces.shape
    n_src = src_station.shape[0]
    n_win = lax.axis_size("win")
    n_rcv = lax.axis_size("rcv")
    bins = F // n_win
    early = n_win // 2

    blocks, picked, plan, flag = spectra_call(traces, valid, src_station, n_win, n_rcv)

    near = []
    for i in range(1, n_rcv):
        pairs = near_and_far(n_rcv, i)[0]
        if pairs:
            near.append(lax.ppermute(picked[i], "rcv", pairs))
    merged = lax.cond(flag.reshape(()) > 0, merge_all, merge_near, picked, near)

    merged = [merged[0]] + [swap(merged[j], "win", j) for j in range(1, n_win)]
    late = [j for j in range(1, n_win) if j != early]
    received = {0: blocks[0], early: swap(blocks[early], "win", early)}
    joined, later = join_call(merged, [received[early]], [blocks[j] for j in late])
    received.update({j: swap(block, "win", j) for j, block in zip(late, later)})
    sources = [[joined]] + [[swap(joined, "rcv", i)] for i in range(1, n_rcv)]

    turned = [turn_call([received[j]], w_dev, r_dev) for j in range(n_win)]
    half = n_rcv // 2
    sizes = (n_rcv, w_dev, r_dev, bins)
    stacks = stacks_call(None, plan, turned, sources, tuple(range(half)), *sizes)
    stacks = stacks_call(stacks, plan, turned, sources, tuple(range(half, n_rcv)), *sizes)
    return stacks.reshape(n_src, r_dev, 2, bins)


def correlate(received, sources):
    rr = received[:, :, 0]
    ri = received[:, :, 1]
    sr = sources[:, :, 0]
    si = sources[:, :, 1]
    real = jnp.einsum("wsf,wrf->srf", sr, rr, preferred_element_type=jnp.float32)
    real = real + jnp.einsum("wsf,wrf->srf", si, ri, preferred_element_type=jnp.float32)
    imag = jnp.einsum("wsf,wrf->srf", sr, ri, preferred_element_type=jnp.float32)
    imag = imag - jnp.einsum("wsf,wrf->srf", si, rr, preferred_element_type=jnp.float32)
    return jnp.stack([real, imag], axis=2)


def body_any(traces, valid, src_station):
    w_dev, r_dev, samples = traces.shape
    n_win = lax.axis_size("win")
    n_rcv = lax.axis_size("rcv")
    bins = F // n_win
    table = jnp.asarray(band_table(samples, F, samples // 16))
    spectra = jnp.dot(
        traces.reshape(w_dev * r_dev, samples), table, preferred_element_type=jnp.float32
    )
    spectra = spectra.reshape(w_dev, r_dev, 2, F)
    power = jnp.sum(spectra * spectra, axis=(2, 3), keepdims=True) / F
    keep = valid.astype(jnp.float32)[:, None, None, None]
    white = (spectra * lax.rsqrt(power + 1e-06) * keep).astype(jnp.bfloat16)
    blocks = white.reshape(w_dev, r_dev, 2, n_win, bins).transpose(3, 0, 1, 2, 4)
    me = lax.axis_index("win")
    offset = lax.axis_index("rcv") * r_dev
    station_ids = offset + jnp.arange(r_dev, dtype=jnp.int32)
    selector = (src_station[:, None] == station_ids[None, :]).astype(jnp.bfloat16)
    received = []
    for j in range(n_win):
        block = lax.dynamic_index_in_dim(blocks, me ^ j, 0, keepdims=False)
        received.append(swap(block, "win", j) if j else block)
    received = jnp.concatenate(received, axis=0)
    rows = jnp.einsum("sr,wrcf->wscf", selector, received, preferred_element_type=jnp.float32)
    rows = lax.all_to_all(rows.astype(jnp.bfloat16), "rcv", 0, 0, tiled=True)
    rows = rows.reshape((n_rcv, -1) + rows.shape[1:])
    merged = jnp.sum(rows.astype(jnp.float32), axis=0).astype(jnp.bfloat16)
    sources = lax.all_gather(merged, "rcv", axis=0, tiled=True)
    return correlate(received, sources) * (1.0 / math.sqrt(w_dev * n_win))


def solution(mesh):
    sizes = (mesh.shape["win"], mesh.shape["rcv"])
    return jax.shard_map(
        body if sizes == (4, 4) else body_any,
        mesh=mesh,
        in_specs=(P("win", ("groups", "rcv"), None), P(("groups", "win")), P("groups")),
        out_specs=P(None, ("groups", "rcv"), None, "win"),
        check_vma=False,
    )
```

```python
import functools
import math

import jax
import jax.numpy as jnp
import numpy as np
from jax import lax
from jax.experimental import pallas as pl
from jax.experimental.pallas import tpu as pltpu
from jax.sharding import PartitionSpec as P

F = 512
SMEM = pltpu.MemorySpace.SMEM
VMEM = pltpu.MemorySpace.VMEM


def angles(samples, freqs, count):
    phase = samples[:, None] * freqs[None, :] % count
    return phase.astype(np.float64) * (2.0 * math.pi / count)


def band_table(count, bins, first):
    angle = angles(np.arange(count), first + np.arange(bins), count)
    return np.concatenate([np.cos(angle), -np.sin(angle)], axis=1).astype(jnp.bfloat16)


BLOCK = 32


def table_seeds(count, bins, first, n_win):
    j = np.arange(bins // 4)
    turn = np.array([0.0, 0.5 * math.pi]).reshape(1, 2, 1)
    seeds, twice = [], []
    for m in range(4):
        freqs = np.broadcast_to((first + 4 * j + m).reshape(n_win, 1, -1), (n_win, 2, j.size // n_win))
        angle = angles(np.arange(2 * BLOCK), freqs.reshape(-1), count)
        angle = angle + np.broadcast_to(turn, freqs.shape).reshape(1, -1)
        seeds.append(np.cos(angle).reshape(2, BLOCK, -1))
        step = angles(np.full(8, BLOCK), freqs.reshape(-1), count)
        twice.append(2.0 * np.cos(step))
    return np.stack(seeds).astype(np.float32), np.stack(twice).astype(np.float32)


def make_tables(seed_ref, twice_ref, table_ref):
    for first in (0, 2):
        state = {}
        for m in (first, first + 1):
            twice = jnp.concatenate([twice_ref[m]] * (BLOCK // 8), axis=0)
            state[m] = (seed_ref[m, 0], seed_ref[m, 1], twice)
        for a in range(table_ref.shape[1] // BLOCK):
            for m, (here, after, twice) in state.items():
                table_ref[m, a * BLOCK:(a + 1) * BLOCK, :] = here.astype(jnp.bfloat16)
                state[m] = (after, twice * after - here, twice)


def in_hbm(value):
    return pltpu.with_memory_space_constraint(value, pltpu.HBM)


def order_sources(src_ref, r_dev, n_own, order_ref, plan_ref, flag_ref):
    n_src = src_ref.shape[0]
    size = order_ref.shape
    down = lax.broadcasted_iota(jnp.int32, size, 0).astype(jnp.float32)
    along = lax.broadcasted_iota(jnp.int32, size, 1).astype(jnp.float32)
    none = jnp.full(size, float(2**20), jnp.float32)
    column, row = none, none
    for s in range(n_src):
        station = src_ref[s].astype(jnp.float32)
        column = jnp.where(down == s, station, column)
        row = jnp.where(along == s, station, row)
    rank_along = jnp.sum((column < row).astype(jnp.float32), axis=0, keepdims=True)
    rank_down = jnp.sum((row < column).astype(jnp.float32), axis=1, keepdims=True)
    sorted_down = jnp.sum(jnp.where(rank_along == down, row, 0.0), axis=1, keepdims=True)
    at_place = rank_down == along
    sorted_along = jnp.sum(jnp.where(at_place, column, 0.0), axis=0, keepdims=True)
    source_along = jnp.sum(jnp.where(at_place, down, 0.0), axis=0, keepdims=True)
    order_ref[...] = jnp.broadcast_to(sorted_down, size)
    place = along[:1]
    owner, share = jnp.zeros_like(place), jnp.zeros_like(place)
    for z in range(1, n_src // n_own):
        owner = owner + (sorted_along >= z * r_dev).astype(jnp.float32)
        share = share + (place >= z * n_own).astype(jnp.float32)
    far = jnp.where((place < n_src) & (jnp.abs(owner - share) > 1.5), 1.0, 0.0)
    plan_ref[...] = jnp.broadcast_to(source_along, plan_ref.shape).astype(jnp.int32)
    flag_ref[0] = jnp.max(far).astype(jnp.int32)


def spectra_kernel(
    n_win, n_rcv, r_dev, valid_hbm, src_hbm, x_hbm, seed_hbm, twice_hbm, *refs
):
    r_refs = refs[:n_win]
    q_refs = refs[n_win:n_win + n_rcv]
    (plan_ref, flag_ref, x_ref, even_ref, odd_ref, white_ref, sel_ref, order_ref, table_ref,
     seed_ref, twice_ref, valid_ref, src_ref, sems, x_sems) = refs[n_win + n_rcv:]
    chunks, rows, samples = x_ref.shape
    w_step = rows // r_dev
    n_own = src_ref.shape[0] // n_rcv
    quarter = samples // 4
    win = lax.axis_index("win")
    rcv = lax.axis_index("rcv")

    def small(k):
        source = (seed_hbm, twice_hbm, src_hbm, valid_hbm)[k]
        target = (seed_ref, twice_ref, src_ref, valid_ref)[k]
        return pltpu.make_async_copy(source, target, sems.at[k])

    def chunk(k):
        return pltpu.make_async_copy(x_hbm.at[pl.ds(k * rows, rows)], x_ref.at[k], x_sems.at[k])

    for k in range(4):
        small(k).start()
    for k in range(chunks):
        chunk(k).start()
    small(0).wait()
    small(1).wait()
    make_tables(seed_ref, twice_ref, table_ref)
    small(2).wait()
    order_sources(src_ref, r_dev, n_own, order_ref, plan_ref, flag_ref)
    stations = []
    for d in range(n_rcv):
        share = pl.multiple_of((rcv ^ d) * n_own, n_own)
        stations += [order_ref[pl.ds(share, n_own), 0:1]] * w_step
    wanted = jnp.concatenate(stations, axis=0).astype(jnp.int32) - rcv * r_dev
    shape = (n_rcv * w_step * n_own, rows)
    out_row = lax.broadcasted_iota(jnp.int32, shape, 0)
    column = lax.broadcasted_iota(jnp.int32, shape, 1)
    inside = (wanted >= 0) & (wanted < r_dev)
    hit = inside & (column == wanted + (out_row // n_own) % w_step * r_dev)
    sel_ref[...] = hit.astype(jnp.float32).astype(jnp.bfloat16)
    small(3).wait()

    def product(lhs, table):
        return jnp.dot(lhs, table, preferred_element_type=jnp.float32)

    def add_quarters(k, first, last):
        part = slice(first, last)
        b0, b1, b2, b3 = (x_ref[k, part, q * quarter:(q + 1) * quarter] for q in range(4))
        x0, x1, x2, x3 = (b.astype(jnp.float32) for b in (b0, b1, b2, b3))
        even_ref[k, 0, part] = ((x0 + x2) + (x1 + x3)).astype(jnp.bfloat16)
        even_ref[k, 1, part] = ((x0 + x2) - (x1 + x3)).astype(jnp.bfloat16)
        odd_ref[k, part] = b0 - b2
        odd_ref[k, rows + first:rows + last] = b1 - b3

    lanes = table_ref.shape[2]
    lane = lax.broadcasted_iota(jnp.int32, (rows, lanes), 1)
    piece = lanes // n_win
    real = lane % piece < piece // 2

    def odd_spectra(k, m):
        both = product(odd_ref[k], table_ref[m])
        second = both[rows:]
        back, forth = pltpu.roll(second, lanes - piece // 2, 1), pltpu.roll(second, piece // 2, 1)
        turned = jnp.where(real, back, -forth)
        return both[:rows] + turned if m == 1 else both[:rows] - turned

    parts = 4
    size = rows // parts
    chunk(0).wait()
    add_quarters(0, 0, rows)
    row = lax.broadcasted_iota(jnp.int32, (rows, 1), 0)
    for k in range(chunks):
        more = k + 1 < chunks
        if more:
            chunk(k + 1).wait()
        spectra = []
        for m in range(4):
            if m % 2:
                spectra.append(odd_spectra(k, m))
            else:
                spectra.append(product(even_ref[k, m // 2], table_ref[m]))
            if more:
                add_quarters(k + 1, m * size, (m + 1) * size)
        squares = sum(jnp.sum(s * s, axis=1, keepdims=True) for s in spectra)
        gain = lax.rsqrt(squares / F + 1e-06)
        keep = jnp.zeros((rows, 1), jnp.float32)
        for t in range(w_step):
            own = (row >= t * r_dev) & (row < (t + 1) * r_dev)
            keep = jnp.where(own, valid_ref[k * w_step + t].astype(jnp.float32), keep)
        gain = gain * keep
        white = [s * gain for s in spectra]
        for d in range(n_win):
            columns = slice(d * piece, (d + 1) * piece)
            block = jnp.concatenate([part[:, columns] for part in white], axis=1)
            white_ref[k, d] = block.astype(jnp.bfloat16)
        count = w_step * n_own
        for j in range(n_win):
            block = white_ref[k, win ^ j]
            r_refs[j][k * rows:(k + 1) * rows, :] = block
            picked = product(sel_ref[...], block).astype(jnp.bfloat16)
            for d in range(n_rcv):
                q_refs[d][j, k * count:(k + 1) * count, :] = picked[d * count:(d + 1) * count]


def spectra_call(traces, valid, src_station, n_win, n_rcv):
    w_dev, r_dev, samples = traces.shape
    n_src = src_station.shape[0]
    n_own = n_src // n_rcv
    chunks = 2
    every = w_dev * r_dev
    rows = every // chunks
    lanes = 2 * F // n_win
    seed, twice = (jnp.asarray(t) for t in table_seeds(samples, F, samples // 16, n_win))
    shapes = [jax.ShapeDtypeStruct((every, lanes), jnp.bfloat16)] * n_win
    shapes += [jax.ShapeDtypeStruct((n_win, w_dev * n_own, lanes), jnp.bfloat16)] * n_rcv
    shapes += [jax.ShapeDtypeStruct((8, 128), jnp.int32), jax.ShapeDtypeStruct((1,), jnp.int32)]
    vmem = pl.BlockSpec(memory_space=VMEM)
    out = pl.pallas_call(
        functools.partial(spectra_kernel, n_win, n_rcv, r_dev),
        in_specs=[pl.BlockSpec(memory_space=pltpu.HBM)] * 5,
        out_specs=[vmem] * (len(shapes) - 1) + [pl.BlockSpec(memory_space=SMEM)],
        out_shape=shapes,
        scratch_shapes=[
            pltpu.VMEM((chunks, rows, samples), jnp.bfloat16),
            pltpu.VMEM((chunks, 2, rows, samples // 4), jnp.bfloat16),
            pltpu.VMEM((chunks, 2 * rows, samples // 4), jnp.bfloat16),
            pltpu.VMEM((chunks, n_win, rows, lanes), jnp.bfloat16),
            pltpu.VMEM((n_src * (w_dev // chunks), rows), jnp.bfloat16),
            pltpu.VMEM((n_src, 128), jnp.float32),
            pltpu.VMEM((4, samples // 4, F // 2), jnp.bfloat16),
            pltpu.VMEM(seed.shape, jnp.float32),
            pltpu.VMEM(twice.shape, jnp.float32),
            pltpu.SMEM(valid.shape, jnp.int32),
            pltpu.SMEM(src_station.shape, jnp.int32),
            pltpu.SemaphoreType.DMA((4,)),
            pltpu.SemaphoreType.DMA((chunks,)),
        ],
        compiler_params=pltpu.CompilerParams(vmem_limit_bytes=36 * 2**20),
        cost_estimate=pl.CostEstimate(
            flops=2 * every * (samples // 4) * 6 * (F // 2), bytes_accessed=every * samples * 2,
            transcendentals=0,
        ),
        name="spectra",
    )(*(in_hbm(x) for x in (valid, src_station, traces.reshape(every, samples), seed, twice)))
    return out[:n_win], out[n_win:n_win + n_rcv], out[-2], out[-1]


def bin_order(lanes):
    quarter = lanes // 8
    lane = lax.broadcasted_iota(jnp.int32, (lanes, lanes), 1)
    row = lax.broadcasted_iota(jnp.int32, (lanes, lanes), 0)
    part = (lane // quarter) % 2
    bin_of = 4 * (lane % quarter) + lane // (2 * quarter)
    hit = row == part * (lanes // 2) + bin_of
    return hit.astype(jnp.float32).astype(jnp.bfloat16)


def turn_kernel(r_dev, *refs):
    x_refs, (out_ref, rows_ref) = refs[:-2], refs[-2:]
    lanes = x_refs[0].shape[1]
    bins = lanes // 2
    w_dev = out_ref.shape[1] // 2
    pad = out_ref.shape[2] // 2
    order = bin_order(lanes)
    windows = [(x, w) for x in x_refs for w in range(x.shape[0] // r_dev)]
    for k, (x_ref, w) in enumerate(windows):
        turned = lax.dot_general(
            order, x_ref[w * r_dev:(w + 1) * r_dev], (((1,), (1,)), ((), ())),
            preferred_element_type=jnp.float32,
        )
        rows_ref[pl.ds(k, lanes, stride=w_dev), :r_dev] = turned
    rr = rows_ref[:bins * w_dev].reshape(bins, w_dev, pad)
    ri = rows_ref[bins * w_dev:].reshape(bins, w_dev, pad)
    out_ref[:, :, :pad] = jnp.concatenate([rr, ri], axis=1).astype(jnp.bfloat16)
    out_ref[:, :, pad:] = jnp.concatenate([ri, -rr], axis=1).astype(jnp.bfloat16)


def turn_call(parts, w_dev, r_dev):
    lanes = parts[0].shape[1]
    pad = 128
    vmem = pl.BlockSpec(memory_space=VMEM)
    return pl.pallas_call(
        functools.partial(turn_kernel, r_dev),
        in_specs=[vmem] * len(parts),
        out_specs=vmem,
        out_shape=jax.ShapeDtypeStruct((lanes // 2, 2 * w_dev, 2 * pad), jnp.bfloat16),
        scratch_shapes=[pltpu.VMEM((lanes * w_dev, pad), jnp.float32)],
        compiler_params=pltpu.CompilerParams(vmem_limit_bytes=16 * 2**20),
        cost_estimate=pl.CostEstimate(
            flops=2 * w_dev * lanes * lanes * pad, bytes_accessed=2 * 2**20, transcendentals=0
        ),
        name="turn",
    )(*parts)


def merge_kernel(n_win, *refs):
    picked, outs = refs[:-n_win], refs[-n_win:]
    for j, out_ref in enumerate(outs):
        total = picked[0][j].astype(jnp.float32)
        for q_ref in picked[1:]:
            total = total + q_ref[j].astype(jnp.float32)
        out_ref[...] = total.astype(jnp.bfloat16)


def merge_call(*picked):
    n_win, rows, lanes = picked[0].shape
    vmem = pl.BlockSpec(memory_space=VMEM)
    return pl.pallas_call(
        functools.partial(merge_kernel, n_win),
        in_specs=[vmem] * len(picked),
        out_specs=[vmem] * n_win,
        out_shape=[jax.ShapeDtypeStruct((rows, lanes), jnp.bfloat16)] * n_win,
        compiler_params=pltpu.CompilerParams(vmem_limit_bytes=4 * 2**20),
        cost_estimate=pl.CostEstimate(flops=2**18, bytes_accessed=2**19, transcendentals=0),
        name="merge",
    )(*picked)


def join_kernel(count, *refs):
    out_ref = refs[-1]
    for k in range(count):
        out_ref[k] = refs[k][...]


def join_call(blocks, after=(), later=()):
    rows, lanes = blocks[0].shape
    count = len(blocks)
    first = count + len(after)
    vmem, anywhere = pl.BlockSpec(memory_space=VMEM), pl.BlockSpec(memory_space=pl.ANY)
    out = pl.pallas_call(
        functools.partial(join_kernel, count),
        in_specs=[vmem] * count + [anywhere] * (len(after) + len(later)),
        out_specs=[anywhere] * len(later) + [vmem],
        out_shape=[jax.ShapeDtypeStruct(x.shape, x.dtype) for x in later]
        + [jax.ShapeDtypeStruct((count, rows, lanes), jnp.bfloat16)],
        input_output_aliases={first + k: k for k in range(len(later))},
        compiler_params=pltpu.CompilerParams(vmem_limit_bytes=4 * 2**20),
        cost_estimate=pl.CostEstimate(flops=2**18, bytes_accessed=2**19, transcendentals=0),
        name="join",
    )(*blocks, *after, *later)
    return out[-1], out[:-1]


def stacks_kernel(shares, n_parts, n_win, w_dev, r_dev, n_own, bins, plan_hbm, *refs):
    t_refs = refs[:n_win]
    s_refs = refs[n_win:n_win + n_parts * len(shares)]
    out_hbm, srow_ref, left_ref, prod_ref, out_ref, plan_ref, sems, plan_sem = refs[-8:]
    plan_copy = pltpu.make_async_copy(plan_hbm, plan_ref, plan_sem)
    plan_copy.start()
    lanes = 2 * bins
    windows = n_win * w_dev
    count = len(shares) * n_own
    pad = 128
    rcv = lax.axis_index("rcv")

    def product(lhs, rhs, dims=(((1,), (0,)), ((), ()))):
        return lax.dot_general(lhs, rhs, dims, preferred_element_type=jnp.float32)

    order = bin_order(lanes)
    both = order[:bins] + order[bins:]
    lane = lax.broadcasted_iota(jnp.int32, (w_dev, lanes), 1)
    real = (lane // (bins // 4)) % 2 == 0

    for k in range(len(shares)):
        for j in range(n_win):
            part, place = divmod(j, n_win // n_parts)
            block = s_refs[k * n_parts + part][place].astype(jnp.float32)
            for h in range(lanes // pad):
                half = block[:, h * pad:(h + 1) * pad]
                srow_ref[h, pl.ds((k * n_win + j) * w_dev * n_own, w_dev * n_own), :] = half
    for s in range(count):
        first = s // n_own * windows * n_own + s % n_own
        values = jnp.concatenate(
            [srow_ref[h, pl.ds(first, windows, stride=n_own), :] for h in range(lanes // pad)],
            axis=1,
        )
        stacked = []
        for j in range(n_win):
            own = values[j * w_dev:(j + 1) * w_dev]
            stacked += [jnp.where(real, own, 0.0), jnp.where(real, 0.0, own)]
        stacked = jnp.concatenate(stacked, axis=0).astype(jnp.bfloat16)
        turned = product(both, stacked, (((1,), (1,)), ((), ())))
        left_ref[pl.ds(s, bins, stride=count), :2 * windows] = turned

    for f in range(bins):
        right = jnp.concatenate([t_ref[f] for t_ref in t_refs], axis=0)
        left = left_ref[pl.ds(f * count, count), :2 * windows].astype(jnp.bfloat16)
        result = product(left, right)
        for c in range(2):
            prod_ref[c, pl.ds(f, count, stride=bins), :] = result[:, c * pad:(c + 1) * pad]

    scale = 1.0 / math.sqrt(windows)
    plan_copy.wait()
    copies = []
    for s in range(count):
        for c in range(2):
            turned = prod_ref[c, s * bins:(s + 1) * bins, :].T
            out_ref[s, pl.ds(c, r_dev, stride=2), :] = turned[:r_dev] * scale
        row = plan_ref[0, (rcv ^ shares[s // n_own]) * n_own + s % n_own]
        copies.append(pltpu.make_async_copy(out_ref.at[s], out_hbm.at[row], sems.at[s]))
        copies[-1].start()
    for copy in copies:
        copy.wait()


def stacks_call(out, plan, turned, sources, shares, n_rcv, w_dev, r_dev, bins):
    n_win = len(turned)
    n_parts = len(sources[0])
    n_own = sources[0][0].shape[1] // w_dev
    windows = n_win * w_dev
    count = len(shares) * n_own
    whole = pl.BlockSpec(memory_space=VMEM)
    args = [plan] + list(turned) + [part for i in shares for part in sources[i]]
    specs = [pl.BlockSpec(memory_space=pl.ANY)] + [whole] * (len(args) - 1)
    aliases = {}
    if out is not None:
        aliases = {len(args): 0}
        args.append(out)
        specs.append(pl.BlockSpec(memory_space=pl.ANY))
    return pl.pallas_call(
        functools.partial(stacks_kernel, shares, n_parts, n_win, w_dev, r_dev, n_own, bins),
        in_specs=specs,
        out_specs=pl.BlockSpec(memory_space=pltpu.HBM),
        out_shape=jax.ShapeDtypeStruct((n_rcv * n_own, 2 * r_dev, bins), jnp.float32),
        input_output_aliases=aliases,
        scratch_shapes=[
            pltpu.VMEM((2 * bins // 128, windows * count, 128), jnp.float32),
            pltpu.VMEM((bins * count, 128), jnp.float32),
            pltpu.VMEM((2, count * bins, 128), jnp.float32),
            pltpu.VMEM((count, 2 * r_dev, bins), jnp.float32),
            pltpu.SMEM(plan.shape, jnp.int32),
            pltpu.SemaphoreType.DMA((count,)),
            pltpu.SemaphoreType.DMA,
        ],
        compiler_params=pltpu.CompilerParams(vmem_limit_bytes=20 * 2**20),
        cost_estimate=pl.CostEstimate(
            flops=8 * windows * count * r_dev * bins, bytes_accessed=6 * 2**20, transcendentals=0
        ),
        name="stacks",
    )(*args)


def swap(value, axis, by):
    size = lax.axis_size(axis)
    return lax.ppermute(value, axis, [(i, i ^ by) for i in range(size)])


def near_and_far(n_rcv, by):
    pairs = [(z, z ^ by) for z in range(n_rcv)]
    return [p for p in pairs if abs(p[0] - p[1]) == 1], [p for p in pairs if abs(p[0] - p[1]) > 1]


def merge_near(picked, near):
    return merge_call(picked[0], *near)


def merge_all(picked, near):
    far = []
    for i in range(1, len(picked)):
        pairs = near_and_far(len(picked), i)[1]
        if pairs:
            far.append(lax.ppermute(picked[i], "rcv", pairs))
    return merge_call(picked[0], *near, *far)


def body(traces, valid, src_station):
    w_dev, r_dev, samples = traces.shape
    n_src = src_station.shape[0]
    n_win = lax.axis_size("win")
    n_rcv = lax.axis_size("rcv")
    bins = F // n_win
    early = n_win // 2

    blocks, picked, plan, flag = spectra_call(traces, valid, src_station, n_win, n_rcv)

    near = {}
    for i in range(1, n_rcv):
        pairs = near_and_far(n_rcv, i)[0]
        if pairs:
            near[i] = lax.ppermute(picked[i], "rcv", pairs)
    picked = [picked[0] + near.pop(n_rcv - 1)] + list(picked[1:])
    near = list(near.values())
    merged = lax.cond(flag.reshape(()) > 0, merge_all, merge_near, picked, near)

    merged = [merged[0]] + [swap(merged[j], "win", j) for j in range(1, n_win)]
    late = [j for j in range(1, n_win) if j != early]
    received = {0: blocks[0], early: swap(blocks[early], "win", early)}
    joined, later = join_call(merged, [received[early]], [blocks[j] for j in late])
    received.update({j: swap(block, "win", j) for j, block in zip(late, later)})
    sources = [[joined]] + [[swap(joined, "rcv", i)] for i in range(1, n_rcv)]

    turned = [turn_call([received[j]], w_dev, r_dev) for j in range(n_win)]
    half = n_rcv // 2
    sizes = (n_rcv, w_dev, r_dev, bins)
    stacks = stacks_call(None, plan, turned, sources, tuple(range(half)), *sizes)
    stacks = stacks_call(stacks, plan, turned, sources, tuple(range(half, n_rcv)), *sizes)
    return stacks.reshape(n_src, r_dev, 2, bins)


def correlate(received, sources):
    rr = received[:, :, 0]
    ri = received[:, :, 1]
    sr = sources[:, :, 0]
    si = sources[:, :, 1]
    real = jnp.einsum("wsf,wrf->srf", sr, rr, preferred_element_type=jnp.float32)
    real = real + jnp.einsum("wsf,wrf->srf", si, ri, preferred_element_type=jnp.float32)
    imag = jnp.einsum("wsf,wrf->srf", sr, ri, preferred_element_type=jnp.float32)
    imag = imag - jnp.einsum("wsf,wrf->srf", si, rr, preferred_element_type=jnp.float32)
    return jnp.stack([real, imag], axis=2)


def body_any(traces, valid, src_station):
    w_dev, r_dev, samples = traces.shape
    n_win = lax.axis_size("win")
    n_rcv = lax.axis_size("rcv")
    bins = F // n_win
    table = jnp.asarray(band_table(samples, F, samples // 16))
    spectra = jnp.dot(
        traces.reshape(w_dev * r_dev, samples), table, preferred_element_type=jnp.float32
    )
    spectra = spectra.reshape(w_dev, r_dev, 2, F)
    power = jnp.sum(spectra * spectra, axis=(2, 3), keepdims=True) / F
    keep = valid.astype(jnp.float32)[:, None, None, None]
    white = (spectra * lax.rsqrt(power + 1e-06) * keep).astype(jnp.bfloat16)
    blocks = white.reshape(w_dev, r_dev, 2, n_win, bins).transpose(3, 0, 1, 2, 4)
    me = lax.axis_index("win")
    offset = lax.axis_index("rcv") * r_dev
    station_ids = offset + jnp.arange(r_dev, dtype=jnp.int32)
    selector = (src_station[:, None] == station_ids[None, :]).astype(jnp.bfloat16)
    received = []
    for j in range(n_win):
        block = lax.dynamic_index_in_dim(blocks, me ^ j, 0, keepdims=False)
        received.append(swap(block, "win", j) if j else block)
    received = jnp.concatenate(received, axis=0)
    rows = jnp.einsum("sr,wrcf->wscf", selector, received, preferred_element_type=jnp.float32)
    rows = lax.all_to_all(rows.astype(jnp.bfloat16), "rcv", 0, 0, tiled=True)
    rows = rows.reshape((n_rcv, -1) + rows.shape[1:])
    merged = jnp.sum(rows.astype(jnp.float32), axis=0).astype(jnp.bfloat16)
    sources = lax.all_gather(merged, "rcv", axis=0, tiled=True)
    return correlate(received, sources) * (1.0 / math.sqrt(w_dev * n_win))


def solution(mesh):
    sizes = (mesh.shape["win"], mesh.shape["rcv"])
    return jax.shard_map(
        body if sizes == (4, 4) else body_any,
        mesh=mesh,
        in_specs=(P("win", ("groups", "rcv"), None), P(("groups", "win")), P("groups")),
        out_specs=P(None, ("groups", "rcv"), None, "win"),
        check_vma=False,
    )
```

```python
import functools
import math

import jax
import jax.numpy as jnp
import numpy as np
from jax import lax
from jax.experimental import pallas as pl
from jax.experimental.pallas import tpu as pltpu
from jax.sharding import PartitionSpec as P

F = 512
SMEM = pltpu.MemorySpace.SMEM
VMEM = pltpu.MemorySpace.VMEM


def angles(samples, freqs, count):
    phase = samples[:, None] * freqs[None, :] % count
    return phase.astype(np.float64) * (2.0 * math.pi / count)


def band_table(count, bins, first):
    angle = angles(np.arange(count), first + np.arange(bins), count)
    return np.concatenate([np.cos(angle), -np.sin(angle)], axis=1).astype(jnp.bfloat16)


BLOCK = 32


def table_seeds(count, bins, first, n_win):
    j = np.arange(bins // 4)
    turn = np.array([0.0, 0.5 * math.pi]).reshape(1, 2, 1)
    seeds, twice = [], []
    for m in range(4):
        freqs = np.broadcast_to((first + 4 * j + m).reshape(n_win, 1, -1), (n_win, 2, j.size // n_win))
        angle = angles(np.arange(2 * BLOCK), freqs.reshape(-1), count)
        angle = angle + np.broadcast_to(turn, freqs.shape).reshape(1, -1)
        seeds.append(np.cos(angle).reshape(2, BLOCK, -1))
        step = angles(np.full(8, BLOCK), freqs.reshape(-1), count)
        twice.append(2.0 * np.cos(step))
    return np.stack(seeds).astype(np.float32), np.stack(twice).astype(np.float32)


def make_tables(seed_ref, twice_ref, table_ref):
    for first in (0, 2):
        state = {}
        for m in (first, first + 1):
            twice = jnp.concatenate([twice_ref[m]] * (BLOCK // 8), axis=0)
            state[m] = (seed_ref[m, 0], seed_ref[m, 1], twice)
        for a in range(table_ref.shape[1] // BLOCK):
            for m, (here, after, twice) in state.items():
                table_ref[m, a * BLOCK:(a + 1) * BLOCK, :] = here.astype(jnp.bfloat16)
                state[m] = (after, twice * after - here, twice)


def in_hbm(value):
    return pltpu.with_memory_space_constraint(value, pltpu.HBM)


def order_sources(src_ref, r_dev, n_own, order_ref, plan_ref, flag_ref):
    n_src = src_ref.shape[0]
    size = order_ref.shape
    down = lax.broadcasted_iota(jnp.int32, size, 0).astype(jnp.float32)
    along = lax.broadcasted_iota(jnp.int32, size, 1).astype(jnp.float32)
    none = jnp.full(size, float(2**20), jnp.float32)
    column, row = none, none
    for s in range(n_src):
        station = src_ref[s].astype(jnp.float32)
        column = jnp.where(down == s, station, column)
        row = jnp.where(along == s, station, row)
    rank_along = jnp.sum((column < row).astype(jnp.float32), axis=0, keepdims=True)
    rank_down = jnp.sum((row < column).astype(jnp.float32), axis=1, keepdims=True)
    sorted_down = jnp.sum(jnp.where(rank_along == down, row, 0.0), axis=1, keepdims=True)
    at_place = rank_down == along
    sorted_along = jnp.sum(jnp.where(at_place, column, 0.0), axis=0, keepdims=True)
    source_along = jnp.sum(jnp.where(at_place, down, 0.0), axis=0, keepdims=True)
    order_ref[...] = jnp.broadcast_to(sorted_down, size)
    place = along[:1]
    owner, share = jnp.zeros_like(place), jnp.zeros_like(place)
    for z in range(1, n_src // n_own):
        owner = owner + (sorted_along >= z * r_dev).astype(jnp.float32)
        share = share + (place >= z * n_own).astype(jnp.float32)
    far = jnp.where((place < n_src) & (jnp.abs(owner - share) > 1.5), 1.0, 0.0)
    plan_ref[...] = jnp.broadcast_to(source_along, plan_ref.shape).astype(jnp.int32)
    flag_ref[0] = jnp.max(far).astype(jnp.int32)


def spectra_kernel(
    n_win, n_rcv, r_dev, valid_hbm, src_hbm, x_hbm, seed_hbm, twice_hbm, *refs
):
    r_refs = refs[:n_win]
    q_refs = refs[n_win:n_win + n_rcv]
    (plan_ref, flag_ref, x_ref, even_ref, odd_ref, white_ref, sel_ref, order_ref, table_ref,
     seed_ref, twice_ref, valid_ref, src_ref, sems, x_sems) = refs[n_win + n_rcv:]
    chunks, rows, samples = x_ref.shape
    w_step = rows // r_dev
    n_own = src_ref.shape[0] // n_rcv
    quarter = samples // 4
    win = lax.axis_index("win")
    rcv = lax.axis_index("rcv")

    def small(k):
        source = (seed_hbm, twice_hbm, src_hbm, valid_hbm)[k]
        target = (seed_ref, twice_ref, src_ref, valid_ref)[k]
        return pltpu.make_async_copy(source, target, sems.at[k])

    def chunk(k):
        return pltpu.make_async_copy(x_hbm.at[pl.ds(k * rows, rows)], x_ref.at[k], x_sems.at[k])

    for k in range(4):
        small(k).start()
    for k in range(chunks):
        chunk(k).start()
    small(0).wait()
    small(1).wait()
    make_tables(seed_ref, twice_ref, table_ref)
    small(2).wait()
    order_sources(src_ref, r_dev, n_own, order_ref, plan_ref, flag_ref)
    stations = []
    for d in range(n_rcv):
        share = pl.multiple_of((rcv ^ d) * n_own, n_own)
        stations += [order_ref[pl.ds(share, n_own), 0:1]] * w_step
    wanted = jnp.concatenate(stations, axis=0).astype(jnp.int32) - rcv * r_dev
    shape = (n_rcv * w_step * n_own, rows)
    out_row = lax.broadcasted_iota(jnp.int32, shape, 0)
    column = lax.broadcasted_iota(jnp.int32, shape, 1)
    inside = (wanted >= 0) & (wanted < r_dev)
    hit = inside & (column == wanted + (out_row // n_own) % w_step * r_dev)
    sel_ref[...] = hit.astype(jnp.float32).astype(jnp.bfloat16)
    small(3).wait()

    def product(lhs, table):
        return jnp.dot(lhs, table, preferred_element_type=jnp.float32)

    def add_quarters(k, first, last):
        part = slice(first, last)
        b0, b1, b2, b3 = (x_ref[k, part, q * quarter:(q + 1) * quarter] for q in range(4))
        x0, x1, x2, x3 = (b.astype(jnp.float32) for b in (b0, b1, b2, b3))
        even_ref[k, 0, part] = ((x0 + x2) + (x1 + x3)).astype(jnp.bfloat16)
        even_ref[k, 1, part] = ((x0 + x2) - (x1 + x3)).astype(jnp.bfloat16)
        odd_ref[k, part] = b0 - b2
        odd_ref[k, rows + first:rows + last] = b1 - b3

    lanes = table_ref.shape[2]
    lane = lax.broadcasted_iota(jnp.int32, (rows, lanes), 1)
    piece = lanes // n_win
    real = lane % piece < piece // 2

    def odd_spectra(k, m):
        both = product(odd_ref[k], table_ref[m])
        second = both[rows:]
        back, forth = pltpu.roll(second, lanes - piece // 2, 1), pltpu.roll(second, piece // 2, 1)
        turned = jnp.where(real, back, -forth)
        return both[:rows] + turned if m == 1 else both[:rows] - turned

    parts = 4
    size = rows // parts
    chunk(0).wait()
    add_quarters(0, 0, rows)
    row = lax.broadcasted_iota(jnp.int32, (rows, 1), 0)
    for k in range(chunks):
        more = k + 1 < chunks
        if more:
            chunk(k + 1).wait()
        spectra = []
        for m in range(4):
            if m % 2:
                spectra.append(odd_spectra(k, m))
            else:
                spectra.append(product(even_ref[k, m // 2], table_ref[m]))
            if more:
                add_quarters(k + 1, m * size, (m + 1) * size)
        squares = sum(jnp.sum(s * s, axis=1, keepdims=True) for s in spectra)
        gain = lax.rsqrt(squares / F + 1e-06)
        keep = jnp.zeros((rows, 1), jnp.float32)
        for t in range(w_step):
            own = (row >= t * r_dev) & (row < (t + 1) * r_dev)
            keep = jnp.where(own, valid_ref[k * w_step + t].astype(jnp.float32), keep)
        gain = gain * keep
        white = [s * gain for s in spectra]
        for d in range(n_win):
            columns = slice(d * piece, (d + 1) * piece)
            block = jnp.concatenate([part[:, columns] for part in white], axis=1)
            white_ref[k, d] = block.astype(jnp.bfloat16)
        count = w_step * n_own
        for j in range(n_win):
            block = white_ref[k, win ^ j]
            r_refs[j][k * rows:(k + 1) * rows, :] = block
            picked = product(sel_ref[...], block).astype(jnp.bfloat16)
            for d in range(n_rcv):
                q_refs[d][j, k * count:(k + 1) * count, :] = picked[d * count:(d + 1) * count]


def spectra_call(traces, valid, src_station, n_win, n_rcv):
    w_dev, r_dev, samples = traces.shape
    n_src = src_station.shape[0]
    n_own = n_src // n_rcv
    chunks = 2
    every = w_dev * r_dev
    rows = every // chunks
    lanes = 2 * F // n_win
    seed, twice = (jnp.asarray(t) for t in table_seeds(samples, F, samples // 16, n_win))
    shapes = [jax.ShapeDtypeStruct((every, lanes), jnp.bfloat16)] * n_win
    shapes += [jax.ShapeDtypeStruct((n_win, w_dev * n_own, lanes), jnp.bfloat16)] * n_rcv
    shapes += [jax.ShapeDtypeStruct((8, 128), jnp.int32), jax.ShapeDtypeStruct((1,), jnp.int32)]
    vmem = pl.BlockSpec(memory_space=VMEM)
    out = pl.pallas_call(
        functools.partial(spectra_kernel, n_win, n_rcv, r_dev),
        in_specs=[pl.BlockSpec(memory_space=pltpu.HBM)] * 5,
        out_specs=[vmem] * (len(shapes) - 1) + [pl.BlockSpec(memory_space=SMEM)],
        out_shape=shapes,
        scratch_shapes=[
            pltpu.VMEM((chunks, rows, samples), jnp.bfloat16),
            pltpu.VMEM((chunks, 2, rows, samples // 4), jnp.bfloat16),
            pltpu.VMEM((chunks, 2 * rows, samples // 4), jnp.bfloat16),
            pltpu.VMEM((chunks, n_win, rows, lanes), jnp.bfloat16),
            pltpu.VMEM((n_src * (w_dev // chunks), rows), jnp.bfloat16),
            pltpu.VMEM((n_src, 128), jnp.float32),
            pltpu.VMEM((4, samples // 4, F // 2), jnp.bfloat16),
            pltpu.VMEM(seed.shape, jnp.float32),
            pltpu.VMEM(twice.shape, jnp.float32),
            pltpu.SMEM(valid.shape, jnp.int32),
            pltpu.SMEM(src_station.shape, jnp.int32),
            pltpu.SemaphoreType.DMA((4,)),
            pltpu.SemaphoreType.DMA((chunks,)),
        ],
        compiler_params=pltpu.CompilerParams(vmem_limit_bytes=36 * 2**20),
        cost_estimate=pl.CostEstimate(
            flops=2 * every * (samples // 4) * 6 * (F // 2), bytes_accessed=every * samples * 2,
            transcendentals=0,
        ),
        name="spectra",
    )(*(in_hbm(x) for x in (valid, src_station, traces.reshape(every, samples), seed, twice)))
    return out[:n_win], out[n_win:n_win + n_rcv], out[-2], out[-1]


def bin_order(lanes):
    quarter = lanes // 8
    lane = lax.broadcasted_iota(jnp.int32, (lanes, lanes), 1)
    row = lax.broadcasted_iota(jnp.int32, (lanes, lanes), 0)
    part = (lane // quarter) % 2
    bin_of = 4 * (lane % quarter) + lane // (2 * quarter)
    hit = row == part * (lanes // 2) + bin_of
    return hit.astype(jnp.float32).astype(jnp.bfloat16)


def turn_kernel(r_dev, *refs):
    x_refs, (out_ref, rows_ref) = refs[:-2], refs[-2:]
    lanes = x_refs[0].shape[1]
    bins = lanes // 2
    w_dev = out_ref.shape[1] // 2
    pad = out_ref.shape[2] // 2
    order = bin_order(lanes)
    windows = [(x, w) for x in x_refs for w in range(x.shape[0] // r_dev)]
    for k, (x_ref, w) in enumerate(windows):
        turned = lax.dot_general(
            order, x_ref[w * r_dev:(w + 1) * r_dev], (((1,), (1,)), ((), ())),
            preferred_element_type=jnp.float32,
        )
        rows_ref[pl.ds(k, lanes, stride=w_dev), :r_dev] = turned
    rr = rows_ref[:bins * w_dev].reshape(bins, w_dev, pad)
    ri = rows_ref[bins * w_dev:].reshape(bins, w_dev, pad)
    out_ref[:, :, :pad] = jnp.concatenate([rr, ri], axis=1).astype(jnp.bfloat16)
    out_ref[:, :, pad:] = jnp.concatenate([ri, -rr], axis=1).astype(jnp.bfloat16)


def turn_call(parts, w_dev, r_dev):
    lanes = parts[0].shape[1]
    pad = 128
    vmem = pl.BlockSpec(memory_space=VMEM)
    return pl.pallas_call(
        functools.partial(turn_kernel, r_dev),
        in_specs=[vmem] * len(parts),
        out_specs=vmem,
        out_shape=jax.ShapeDtypeStruct((lanes // 2, 2 * w_dev, 2 * pad), jnp.bfloat16),
        scratch_shapes=[pltpu.VMEM((lanes * w_dev, pad), jnp.float32)],
        compiler_params=pltpu.CompilerParams(vmem_limit_bytes=16 * 2**20),
        cost_estimate=pl.CostEstimate(
            flops=2 * w_dev * lanes * lanes * pad, bytes_accessed=2 * 2**20, transcendentals=0
        ),
        name="turn",
    )(*parts)


def merge_kernel(n_win, *refs):
    picked, outs = refs[:-n_win], refs[-n_win:]
    for j, out_ref in enumerate(outs):
        total = picked[0][j].astype(jnp.float32)
        for q_ref in picked[1:]:
            total = total + q_ref[j].astype(jnp.float32)
        out_ref[...] = total.astype(jnp.bfloat16)


def merge_call(*picked):
    n_win, rows, lanes = picked[0].shape
    vmem = pl.BlockSpec(memory_space=VMEM)
    return pl.pallas_call(
        functools.partial(merge_kernel, n_win),
        in_specs=[vmem] * len(picked),
        out_specs=[vmem] * n_win,
        out_shape=[jax.ShapeDtypeStruct((rows, lanes), jnp.bfloat16)] * n_win,
        compiler_params=pltpu.CompilerParams(vmem_limit_bytes=4 * 2**20),
        cost_estimate=pl.CostEstimate(flops=2**18, bytes_accessed=2**19, transcendentals=0),
        name="merge",
    )(*picked)


def join_kernel(count, *refs):
    out_ref = refs[-1]
    for k in range(count):
        out_ref[k] = refs[k][...]


def join_call(blocks, after=(), later=()):
    rows, lanes = blocks[0].shape
    count = len(blocks)
    first = count + len(after)
    vmem, anywhere = pl.BlockSpec(memory_space=VMEM), pl.BlockSpec(memory_space=pl.ANY)
    out = pl.pallas_call(
        functools.partial(join_kernel, count),
        in_specs=[vmem] * count + [anywhere] * (len(after) + len(later)),
        out_specs=[anywhere] * len(later) + [vmem],
        out_shape=[jax.ShapeDtypeStruct(x.shape, x.dtype) for x in later]
        + [jax.ShapeDtypeStruct((count, rows, lanes), jnp.bfloat16)],
        input_output_aliases={first + k: k for k in range(len(later))},
        compiler_params=pltpu.CompilerParams(vmem_limit_bytes=4 * 2**20),
        cost_estimate=pl.CostEstimate(flops=2**18, bytes_accessed=2**19, transcendentals=0),
        name="join",
    )(*blocks, *after, *later)
    return out[-1], out[:-1]


def stacks_kernel(shares, n_parts, n_win, w_dev, r_dev, n_own, bins, plan_hbm, *refs):
    t_refs = refs[:n_win]
    s_refs = refs[n_win:n_win + n_parts * len(shares)]
    out_hbm, srow_ref, left_ref, prod_ref, out_ref, plan_ref, sems, plan_sem = refs[-8:]
    plan_copy = pltpu.make_async_copy(plan_hbm, plan_ref, plan_sem)
    plan_copy.start()
    lanes = 2 * bins
    windows = n_win * w_dev
    count = len(shares) * n_own
    pad = 128
    rcv = lax.axis_index("rcv")

    def product(lhs, rhs, dims=(((1,), (0,)), ((), ()))):
        return lax.dot_general(lhs, rhs, dims, preferred_element_type=jnp.float32)

    order = bin_order(lanes)
    both = order[:bins] + order[bins:]
    lane = lax.broadcasted_iota(jnp.int32, (w_dev, lanes), 1)
    real = (lane // (bins // 4)) % 2 == 0

    depth = 2 * windows
    group = lanes // depth
    lane = lax.broadcasted_iota(jnp.int32, (bins, lanes), 1)
    row = lax.broadcasted_iota(jnp.int32, (bins, lanes), 0)
    in_place = lane // depth == row % group
    for k in range(len(shares)):
        for j in range(n_win):
            part, place = divmod(j, n_win // n_parts)
            block = s_refs[k * n_parts + part][place].astype(jnp.float32)
            for h in range(lanes // pad):
                half = block[:, h * pad:(h + 1) * pad]
                srow_ref[h, pl.ds((k * n_win + j) * w_dev * n_own, w_dev * n_own), :] = half
    for s in range(count):
        first = s // n_own * windows * n_own + s % n_own
        values = jnp.concatenate(
            [srow_ref[h, pl.ds(first, windows, stride=n_own), :] for h in range(lanes // pad)],
            axis=1,
        )
        stacked = []
        for j in range(n_win):
            own = values[j * w_dev:(j + 1) * w_dev]
            stacked += [jnp.where(real, own, 0.0), jnp.where(real, 0.0, own)]
        stacked = jnp.concatenate(stacked, axis=0).astype(jnp.bfloat16)
        stacked = jnp.concatenate([stacked] * group, axis=0)
        turned = product(both, stacked, (((1,), (1,)), ((), ())))
        turned = jnp.where(in_place, turned, 0.0)
        for h in range(lanes // pad):
            half = turned[:, h * pad:(h + 1) * pad]
            left_ref[h, pl.ds(s, bins, stride=count), :] = half

    for first in range(0, bins, group):
        members = range(first, first + group)
        right = jnp.concatenate([t_ref[f] for f in members for t_ref in t_refs], axis=0)
        rows = pl.ds(first * count, group * count)
        left = jnp.concatenate([left_ref[h, rows, :] for h in range(lanes // pad)], axis=1)
        result = product(left.astype(jnp.bfloat16), right)
        for k, f in enumerate(members):
            for c in range(2):
                block = result[k * count:(k + 1) * count, c * pad:(c + 1) * pad]
                prod_ref[c, pl.ds(f, count, stride=bins), :] = block

    scale = 1.0 / math.sqrt(windows)
    plan_copy.wait()
    copies = []
    for s in range(count):
        for c in range(2):
            turned = prod_ref[c, s * bins:(s + 1) * bins, :].T
            out_ref[s, pl.ds(c, r_dev, stride=2), :] = turned[:r_dev] * scale
        row = plan_ref[0, (rcv ^ shares[s // n_own]) * n_own + s % n_own]
        copies.append(pltpu.make_async_copy(out_ref.at[s], out_hbm.at[row], sems.at[s]))
        copies[-1].start()
    for copy in copies:
        copy.wait()


def stacks_call(out, plan, turned, sources, shares, n_rcv, w_dev, r_dev, bins):
    n_win = len(turned)
    n_parts = len(sources[0])
    n_own = sources[0][0].shape[1] // w_dev
    windows = n_win * w_dev
    count = len(shares) * n_own
    whole = pl.BlockSpec(memory_space=VMEM)
    args = [plan] + list(turned) + [part for i in shares for part in sources[i]]
    specs = [pl.BlockSpec(memory_space=pl.ANY)] + [whole] * (len(args) - 1)
    aliases = {}
    if out is not None:
        aliases = {len(args): 0}
        args.append(out)
        specs.append(pl.BlockSpec(memory_space=pl.ANY))
    return pl.pallas_call(
        functools.partial(stacks_kernel, shares, n_parts, n_win, w_dev, r_dev, n_own, bins),
        in_specs=specs,
        out_specs=pl.BlockSpec(memory_space=pltpu.HBM),
        out_shape=jax.ShapeDtypeStruct((n_rcv * n_own, 2 * r_dev, bins), jnp.float32),
        input_output_aliases=aliases,
        scratch_shapes=[
            pltpu.VMEM((2 * bins // 128, windows * count, 128), jnp.float32),
            pltpu.VMEM((2 * bins // 128, bins * count, 128), jnp.float32),
            pltpu.VMEM((2, count * bins, 128), jnp.float32),
            pltpu.VMEM((count, 2 * r_dev, bins), jnp.float32),
            pltpu.SMEM(plan.shape, jnp.int32),
            pltpu.SemaphoreType.DMA((count,)),
            pltpu.SemaphoreType.DMA,
        ],
        compiler_params=pltpu.CompilerParams(vmem_limit_bytes=20 * 2**20),
        cost_estimate=pl.CostEstimate(
            flops=8 * windows * count * r_dev * bins, bytes_accessed=6 * 2**20, transcendentals=0
        ),
        name="stacks",
    )(*args)


def swap(value, axis, by):
    size = lax.axis_size(axis)
    return lax.ppermute(value, axis, [(i, i ^ by) for i in range(size)])


def near_and_far(n_rcv, by):
    pairs = [(z, z ^ by) for z in range(n_rcv)]
    return [p for p in pairs if abs(p[0] - p[1]) == 1], [p for p in pairs if abs(p[0] - p[1]) > 1]


def merge_near(picked, near):
    return merge_call(picked[0], *near)


def merge_all(picked, near):
    far = []
    for i in range(1, len(picked)):
        pairs = near_and_far(len(picked), i)[1]
        if pairs:
            far.append(lax.ppermute(picked[i], "rcv", pairs))
    return merge_call(picked[0], *near, *far)


def body(traces, valid, src_station):
    w_dev, r_dev, samples = traces.shape
    n_src = src_station.shape[0]
    n_win = lax.axis_size("win")
    n_rcv = lax.axis_size("rcv")
    bins = F // n_win
    early = n_win // 2

    blocks, picked, plan, flag = spectra_call(traces, valid, src_station, n_win, n_rcv)

    near = {}
    for i in range(1, n_rcv):
        pairs = near_and_far(n_rcv, i)[0]
        if pairs:
            near[i] = lax.ppermute(picked[i], "rcv", pairs)
    picked = [picked[0] + near.pop(n_rcv - 1)] + list(picked[1:])
    near = list(near.values())
    merged = lax.cond(flag.reshape(()) > 0, merge_all, merge_near, picked, near)

    merged = [merged[0]] + [swap(merged[j], "win", j) for j in range(1, n_win)]
    late = [j for j in range(1, n_win) if j != early]
    received = {0: blocks[0], early: swap(blocks[early], "win", early)}
    joined, later = join_call(merged, [received[early]], [blocks[j] for j in late])
    received.update({j: swap(block, "win", j) for j, block in zip(late, later)})
    sources = [[joined]] + [[swap(joined, "rcv", i)] for i in range(1, n_rcv)]

    turned = [turn_call([received[j]], w_dev, r_dev) for j in range(n_win)]
    half = n_rcv // 2
    sizes = (n_rcv, w_dev, r_dev, bins)
    stacks = stacks_call(None, plan, turned, sources, tuple(range(half)), *sizes)
    stacks = stacks_call(stacks, plan, turned, sources, tuple(range(half, n_rcv)), *sizes)
    return stacks.reshape(n_src, r_dev, 2, bins)


def correlate(received, sources):
    rr = received[:, :, 0]
    ri = received[:, :, 1]
    sr = sources[:, :, 0]
    si = sources[:, :, 1]
    real = jnp.einsum("wsf,wrf->srf", sr, rr, preferred_element_type=jnp.float32)
    real = real + jnp.einsum("wsf,wrf->srf", si, ri, preferred_element_type=jnp.float32)
    imag = jnp.einsum("wsf,wrf->srf", sr, ri, preferred_element_type=jnp.float32)
    imag = imag - jnp.einsum("wsf,wrf->srf", si, rr, preferred_element_type=jnp.float32)
    return jnp.stack([real, imag], axis=2)


def body_any(traces, valid, src_station):
    w_dev, r_dev, samples = traces.shape
    n_win = lax.axis_size("win")
    n_rcv = lax.axis_size("rcv")
    bins = F // n_win
    table = jnp.asarray(band_table(samples, F, samples // 16))
    spectra = jnp.dot(
        traces.reshape(w_dev * r_dev, samples), table, preferred_element_type=jnp.float32
    )
    spectra = spectra.reshape(w_dev, r_dev, 2, F)
    power = jnp.sum(spectra * spectra, axis=(2, 3), keepdims=True) / F
    keep = valid.astype(jnp.float32)[:, None, None, None]
    white = (spectra * lax.rsqrt(power + 1e-06) * keep).astype(jnp.bfloat16)
    blocks = white.reshape(w_dev, r_dev, 2, n_win, bins).transpose(3, 0, 1, 2, 4)
    me = lax.axis_index("win")
    offset = lax.axis_index("rcv") * r_dev
    station_ids = offset + jnp.arange(r_dev, dtype=jnp.int32)
    selector = (src_station[:, None] == station_ids[None, :]).astype(jnp.bfloat16)
    received = []
    for j in range(n_win):
        block = lax.dynamic_index_in_dim(blocks, me ^ j, 0, keepdims=False)
        received.append(swap(block, "win", j) if j else block)
    received = jnp.concatenate(received, axis=0)
    rows = jnp.einsum("sr,wrcf->wscf", selector, received, preferred_element_type=jnp.float32)
    rows = lax.all_to_all(rows.astype(jnp.bfloat16), "rcv", 0, 0, tiled=True)
    rows = rows.reshape((n_rcv, -1) + rows.shape[1:])
    merged = jnp.sum(rows.astype(jnp.float32), axis=0).astype(jnp.bfloat16)
    sources = lax.all_gather(merged, "rcv", axis=0, tiled=True)
    return correlate(received, sources) * (1.0 / math.sqrt(w_dev * n_win))


def solution(mesh):
    sizes = (mesh.shape["win"], mesh.shape["rcv"])
    return jax.shard_map(
        body if sizes == (4, 4) else body_any,
        mesh=mesh,
        in_specs=(P("win", ("groups", "rcv"), None), P(("groups", "win")), P("groups")),
        out_specs=P(None, ("groups", "rcv"), None, "win"),
        check_vma=False,
    )
```

```python
import functools
import math

import jax
import jax.numpy as jnp
import numpy as np
from jax import lax
from jax.experimental import pallas as pl
from jax.experimental.pallas import tpu as pltpu
from jax.sharding import PartitionSpec as P

F = 512
SMEM = pltpu.MemorySpace.SMEM
VMEM = pltpu.MemorySpace.VMEM


def angles(samples, freqs, count):
    phase = samples[:, None] * freqs[None, :] % count
    return phase.astype(np.float64) * (2.0 * math.pi / count)


def band_table(count, bins, first):
    angle = angles(np.arange(count), first + np.arange(bins), count)
    return np.concatenate([np.cos(angle), -np.sin(angle)], axis=1).astype(jnp.bfloat16)


BLOCK = 32


def table_seeds(count, bins, first, n_win):
    j = np.arange(bins // 4)
    turn = np.array([0.0, 0.5 * math.pi]).reshape(1, 2, 1)
    seeds, twice = [], []
    for m in range(4):
        freqs = np.broadcast_to((first + 4 * j + m).reshape(n_win, 1, -1), (n_win, 2, j.size // n_win))
        angle = angles(np.arange(2 * BLOCK), freqs.reshape(-1), count)
        angle = angle + np.broadcast_to(turn, freqs.shape).reshape(1, -1)
        seeds.append(np.cos(angle).reshape(2, BLOCK, -1))
        step = angles(np.full(8, BLOCK), freqs.reshape(-1), count)
        twice.append(2.0 * np.cos(step))
    return np.stack(seeds).astype(np.float32), np.stack(twice).astype(np.float32)


def make_tables(seed_ref, twice_ref, table_ref):
    for first in (0, 2):
        state = {}
        for m in (first, first + 1):
            twice = jnp.concatenate([twice_ref[m]] * (BLOCK // 8), axis=0)
            state[m] = (seed_ref[m, 0], seed_ref[m, 1], twice)
        for a in range(table_ref.shape[1] // BLOCK):
            for m, (here, after, twice) in state.items():
                table_ref[m, a * BLOCK:(a + 1) * BLOCK, :] = here.astype(jnp.bfloat16)
                state[m] = (after, twice * after - here, twice)


def in_hbm(value):
    return pltpu.with_memory_space_constraint(value, pltpu.HBM)


def order_sources(src_ref, r_dev, n_own, order_ref, plan_ref, flag_ref):
    n_src = src_ref.shape[0]
    size = order_ref.shape
    down = lax.broadcasted_iota(jnp.int32, size, 0).astype(jnp.float32)
    along = lax.broadcasted_iota(jnp.int32, size, 1).astype(jnp.float32)
    none = jnp.full(size, float(2**20), jnp.float32)
    column, row = none, none
    for s in range(n_src):
        station = src_ref[s].astype(jnp.float32)
        column = jnp.where(down == s, station, column)
        row = jnp.where(along == s, station, row)
    rank_along = jnp.sum((column < row).astype(jnp.float32), axis=0, keepdims=True)
    rank_down = jnp.sum((row < column).astype(jnp.float32), axis=1, keepdims=True)
    sorted_down = jnp.sum(jnp.where(rank_along == down, row, 0.0), axis=1, keepdims=True)
    at_place = rank_down == along
    sorted_along = jnp.sum(jnp.where(at_place, column, 0.0), axis=0, keepdims=True)
    source_along = jnp.sum(jnp.where(at_place, down, 0.0), axis=0, keepdims=True)
    order_ref[...] = jnp.broadcast_to(sorted_down, size)
    place = along[:1]
    owner, share = jnp.zeros_like(place), jnp.zeros_like(place)
    for z in range(1, n_src // n_own):
        owner = owner + (sorted_along >= z * r_dev).astype(jnp.float32)
        share = share + (place >= z * n_own).astype(jnp.float32)
    far = jnp.where((place < n_src) & (jnp.abs(owner - share) > 1.5), 1.0, 0.0)
    plan_ref[...] = jnp.broadcast_to(source_along, plan_ref.shape).astype(jnp.int32)
    flag_ref[0] = jnp.max(far).astype(jnp.int32)


def spectra_kernel(
    n_win, n_rcv, r_dev, valid_hbm, src_hbm, x_hbm, seed_hbm, twice_hbm, *refs
):
    r_refs = refs[:n_win]
    q_refs = refs[n_win:n_win + n_rcv]
    (plan_ref, flag_ref, x_ref, even_ref, odd_ref, white_ref, sel_ref, order_ref, table_ref,
     seed_ref, twice_ref, valid_ref, src_ref, sems, x_sems) = refs[n_win + n_rcv:]
    chunks, rows, samples = x_ref.shape
    w_step = rows // r_dev
    n_own = src_ref.shape[0] // n_rcv
    quarter = samples // 4
    win = lax.axis_index("win")
    rcv = lax.axis_index("rcv")

    def small(k):
        source = (seed_hbm, twice_hbm, src_hbm, valid_hbm)[k]
        target = (seed_ref, twice_ref, src_ref, valid_ref)[k]
        return pltpu.make_async_copy(source, target, sems.at[k])

    def chunk(k):
        return pltpu.make_async_copy(x_hbm.at[pl.ds(k * rows, rows)], x_ref.at[k], x_sems.at[k])

    for k in range(4):
        small(k).start()
    for k in range(chunks):
        chunk(k).start()
    small(0).wait()
    small(1).wait()
    make_tables(seed_ref, twice_ref, table_ref)
    small(2).wait()
    order_sources(src_ref, r_dev, n_own, order_ref, plan_ref, flag_ref)
    stations = []
    for d in range(n_rcv):
        share = pl.multiple_of((rcv ^ d) * n_own, n_own)
        stations += [order_ref[pl.ds(share, n_own), 0:1]] * w_step
    wanted = jnp.concatenate(stations, axis=0).astype(jnp.int32) - rcv * r_dev
    shape = (n_rcv * w_step * n_own, rows)
    out_row = lax.broadcasted_iota(jnp.int32, shape, 0)
    column = lax.broadcasted_iota(jnp.int32, shape, 1)
    inside = (wanted >= 0) & (wanted < r_dev)
    hit = inside & (column == wanted + (out_row // n_own) % w_step * r_dev)
    sel_ref[...] = hit.astype(jnp.float32).astype(jnp.bfloat16)
    small(3).wait()

    def product(lhs, table):
        return jnp.dot(lhs, table, preferred_element_type=jnp.float32)

    def add_quarters(k, first, last):
        part = slice(first, last)
        b0, b1, b2, b3 = (x_ref[k, part, q * quarter:(q + 1) * quarter] for q in range(4))
        x0, x1, x2, x3 = (b.astype(jnp.float32) for b in (b0, b1, b2, b3))
        even_ref[k, 0, part] = ((x0 + x2) + (x1 + x3)).astype(jnp.bfloat16)
        even_ref[k, 1, part] = ((x0 + x2) - (x1 + x3)).astype(jnp.bfloat16)
        odd_ref[k, part] = b0 - b2
        odd_ref[k, rows + first:rows + last] = b1 - b3

    lanes = table_ref.shape[2]
    lane = lax.broadcasted_iota(jnp.int32, (rows, lanes), 1)
    piece = lanes // n_win
    real = lane % piece < piece // 2

    def odd_spectra(k, m):
        both = product(odd_ref[k], table_ref[m])
        second = both[rows:]
        back, forth = pltpu.roll(second, lanes - piece // 2, 1), pltpu.roll(second, piece // 2, 1)
        turned = jnp.where(real, back, -forth)
        return both[:rows] + turned if m == 1 else both[:rows] - turned

    parts = 4
    size = rows // parts
    chunk(0).wait()
    add_quarters(0, 0, rows)
    row = lax.broadcasted_iota(jnp.int32, (rows, 1), 0)
    for k in range(chunks):
        more = k + 1 < chunks
        if more:
            chunk(k + 1).wait()
        spectra = []
        for m in range(4):
            if m % 2:
                spectra.append(odd_spectra(k, m))
            else:
                spectra.append(product(even_ref[k, m // 2], table_ref[m]))
            if more:
                add_quarters(k + 1, m * size, (m + 1) * size)
        squares = sum(jnp.sum(s * s, axis=1, keepdims=True) for s in spectra)
        gain = lax.rsqrt(squares / F + 1e-06)
        keep = jnp.zeros((rows, 1), jnp.float32)
        for t in range(w_step):
            own = (row >= t * r_dev) & (row < (t + 1) * r_dev)
            keep = jnp.where(own, valid_ref[k * w_step + t].astype(jnp.float32), keep)
        gain = gain * keep
        white = [s * gain for s in spectra]
        for d in range(n_win):
            columns = slice(d * piece, (d + 1) * piece)
            block = jnp.concatenate([part[:, columns] for part in white], axis=1)
            white_ref[k, d] = block.astype(jnp.bfloat16)
        count = w_step * n_own
        for j in range(n_win):
            block = white_ref[k, win ^ j]
            r_refs[j][k * rows:(k + 1) * rows, :] = block
            picked = product(sel_ref[...], block).astype(jnp.bfloat16)
            for d in range(n_rcv):
                q_refs[d][j, k * count:(k + 1) * count, :] = picked[d * count:(d + 1) * count]


def spectra_call(traces, valid, src_station, n_win, n_rcv):
    w_dev, r_dev, samples = traces.shape
    n_src = src_station.shape[0]
    n_own = n_src // n_rcv
    chunks = 2
    every = w_dev * r_dev
    rows = every // chunks
    lanes = 2 * F // n_win
    seed, twice = (jnp.asarray(t) for t in table_seeds(samples, F, samples // 16, n_win))
    shapes = [jax.ShapeDtypeStruct((every, lanes), jnp.bfloat16)] * n_win
    shapes += [jax.ShapeDtypeStruct((n_win, w_dev * n_own, lanes), jnp.bfloat16)] * n_rcv
    shapes += [jax.ShapeDtypeStruct((8, 128), jnp.int32), jax.ShapeDtypeStruct((1,), jnp.int32)]
    vmem = pl.BlockSpec(memory_space=VMEM)
    out = pl.pallas_call(
        functools.partial(spectra_kernel, n_win, n_rcv, r_dev),
        in_specs=[pl.BlockSpec(memory_space=pltpu.HBM)] * 5,
        out_specs=[vmem] * (len(shapes) - 1) + [pl.BlockSpec(memory_space=SMEM)],
        out_shape=shapes,
        scratch_shapes=[
            pltpu.VMEM((chunks, rows, samples), jnp.bfloat16),
            pltpu.VMEM((chunks, 2, rows, samples // 4), jnp.bfloat16),
            pltpu.VMEM((chunks, 2 * rows, samples // 4), jnp.bfloat16),
            pltpu.VMEM((chunks, n_win, rows, lanes), jnp.bfloat16),
            pltpu.VMEM((n_src * (w_dev // chunks), rows), jnp.bfloat16),
            pltpu.VMEM((n_src, 128), jnp.float32),
            pltpu.VMEM((4, samples // 4, F // 2), jnp.bfloat16),
            pltpu.VMEM(seed.shape, jnp.float32),
            pltpu.VMEM(twice.shape, jnp.float32),
            pltpu.SMEM(valid.shape, jnp.int32),
            pltpu.SMEM(src_station.shape, jnp.int32),
            pltpu.SemaphoreType.DMA((4,)),
            pltpu.SemaphoreType.DMA((chunks,)),
        ],
        compiler_params=pltpu.CompilerParams(vmem_limit_bytes=36 * 2**20),
        cost_estimate=pl.CostEstimate(
            flops=2 * every * (samples // 4) * 6 * (F // 2), bytes_accessed=every * samples * 2,
            transcendentals=0,
        ),
        name="spectra",
    )(*(in_hbm(x) for x in (valid, src_station, traces.reshape(every, samples), seed, twice)))
    return out[:n_win], out[n_win:n_win + n_rcv], out[-2], out[-1]


def bin_order(lanes):
    quarter = lanes // 8
    lane = lax.broadcasted_iota(jnp.int32, (lanes, lanes), 1)
    row = lax.broadcasted_iota(jnp.int32, (lanes, lanes), 0)
    part = (lane // quarter) % 2
    bin_of = 4 * (lane % quarter) + lane // (2 * quarter)
    hit = row == part * (lanes // 2) + bin_of
    return hit.astype(jnp.float32).astype(jnp.bfloat16)


def turn_kernel(r_dev, *refs):
    x_refs, (out_ref, rows_ref) = refs[:-2], refs[-2:]
    lanes = x_refs[0].shape[1]
    bins = lanes // 2
    w_dev = out_ref.shape[1] // 2
    pad = out_ref.shape[2] // 2
    order = bin_order(lanes)
    windows = [(x, w) for x in x_refs for w in range(x.shape[0] // r_dev)]
    for k, (x_ref, w) in enumerate(windows):
        turned = lax.dot_general(
            order, x_ref[w * r_dev:(w + 1) * r_dev], (((1,), (1,)), ((), ())),
            preferred_element_type=jnp.float32,
        )
        rows_ref[pl.ds(k, lanes, stride=w_dev), :r_dev] = turned
    rr = rows_ref[:bins * w_dev].reshape(bins, w_dev, pad)
    ri = rows_ref[bins * w_dev:].reshape(bins, w_dev, pad)
    out_ref[:, :, :pad] = jnp.concatenate([rr, ri], axis=1).astype(jnp.bfloat16)
    out_ref[:, :, pad:] = jnp.concatenate([ri, -rr], axis=1).astype(jnp.bfloat16)


def turn_call(parts, w_dev, r_dev):
    lanes = parts[0].shape[1]
    pad = 128
    vmem = pl.BlockSpec(memory_space=VMEM)
    return pl.pallas_call(
        functools.partial(turn_kernel, r_dev),
        in_specs=[vmem] * len(parts),
        out_specs=vmem,
        out_shape=jax.ShapeDtypeStruct((lanes // 2, 2 * w_dev, 2 * pad), jnp.bfloat16),
        scratch_shapes=[pltpu.VMEM((lanes * w_dev, pad), jnp.float32)],
        compiler_params=pltpu.CompilerParams(vmem_limit_bytes=16 * 2**20),
        cost_estimate=pl.CostEstimate(
            flops=2 * w_dev * lanes * lanes * pad, bytes_accessed=2 * 2**20, transcendentals=0
        ),
        name="turn",
    )(*parts)


def merge_kernel(n_win, *refs):
    picked, outs = refs[:-n_win], refs[-n_win:]
    for j, out_ref in enumerate(outs):
        total = picked[0][j].astype(jnp.float32)
        for q_ref in picked[1:]:
            total = total + q_ref[j].astype(jnp.float32)
        out_ref[...] = total.astype(jnp.bfloat16)


def merge_call(*picked):
    n_win, rows, lanes = picked[0].shape
    vmem = pl.BlockSpec(memory_space=VMEM)
    return pl.pallas_call(
        functools.partial(merge_kernel, n_win),
        in_specs=[vmem] * len(picked),
        out_specs=[vmem] * n_win,
        out_shape=[jax.ShapeDtypeStruct((rows, lanes), jnp.bfloat16)] * n_win,
        compiler_params=pltpu.CompilerParams(vmem_limit_bytes=4 * 2**20),
        cost_estimate=pl.CostEstimate(flops=2**18, bytes_accessed=2**19, transcendentals=0),
        name="merge",
    )(*picked)


def lefts_kernel(n_win, w_dev, n_own, *refs):
    out_ref, srow_ref, rows_ref = refs[-3:]
    rows, lanes = refs[0].shape
    bins = lanes // 2
    windows = n_win * w_dev
    pad = rows_ref.shape[1]
    for j in range(n_win):
        block = refs[j][...].astype(jnp.float32)
        for h in range(lanes // pad):
            srow_ref[h, j * rows:(j + 1) * rows, :] = block[:, h * pad:(h + 1) * pad]

    lane = lax.broadcasted_iota(jnp.int32, (bins, lanes), 1)
    row = lax.broadcasted_iota(jnp.int32, (bins, lanes), 0)
    quarter = lanes // 8
    bin_of = 4 * (lane % quarter) + lane // (2 * quarter)
    pick = bin_of == 2 * (row % (bins // 2)) + row // (bins // 2)
    pick = pick.astype(jnp.float32).astype(jnp.bfloat16)
    real = (lane[:w_dev] // quarter) % 2 == 0
    low = lax.broadcasted_iota(jnp.int32, (bins // 2, pad), 1) < pad // 2
    for s in range(n_own):
        values = jnp.concatenate(
            [srow_ref[h, pl.ds(s, windows, stride=n_own), :] for h in range(lanes // pad)], axis=1
        )
        stacked = []
        for j in range(n_win):
            own = values[j * w_dev:(j + 1) * w_dev]
            stacked += [jnp.where(real, own, 0.0), jnp.where(real, 0.0, own)]
        stacked = jnp.concatenate(stacked * 2, axis=0).astype(jnp.bfloat16)
        turned = lax.dot_general(
            pick, stacked, (((1,), (1,)), ((), ())), preferred_element_type=jnp.float32
        )
        pairs = jnp.where(low, turned[:bins // 2], turned[bins // 2:])
        rows_ref[pl.ds(s, bins // 2, stride=n_own), :] = pairs
    out_ref[...] = rows_ref[...].reshape(out_ref.shape).astype(jnp.bfloat16)


def lefts_call(blocks, after, later, w_dev):
    rows, lanes = blocks[0].shape
    n_win = len(blocks)
    n_own = rows // w_dev
    pad = 128
    first = n_win + len(after)
    vmem, anywhere = pl.BlockSpec(memory_space=VMEM), pl.BlockSpec(memory_space=pl.ANY)
    out = pl.pallas_call(
        functools.partial(lefts_kernel, n_win, w_dev, n_own),
        in_specs=[vmem] * n_win + [anywhere] * (len(after) + len(later)),
        out_specs=[anywhere] * len(later) + [vmem],
        out_shape=[jax.ShapeDtypeStruct(x.shape, x.dtype) for x in later]
        + [jax.ShapeDtypeStruct((lanes // 8, 2 * n_own, pad), jnp.bfloat16)],
        input_output_aliases={first + k: k for k in range(len(later))},
        scratch_shapes=[
            pltpu.VMEM((lanes // pad, n_win * rows, pad), jnp.float32),
            pltpu.VMEM((lanes // 4 * n_own, pad), jnp.float32),
        ],
        compiler_params=pltpu.CompilerParams(vmem_limit_bytes=6 * 2**20),
        cost_estimate=pl.CostEstimate(flops=2**26, bytes_accessed=2**19, transcendentals=0),
        name="lefts",
    )(*blocks, *after, *later)
    return out[-1], out[:-1]


def stacks_kernel(shares, n_win, w_dev, r_dev, n_own, bins, plan_hbm, *refs):
    t_refs = refs[:n_win]
    s_refs = refs[n_win:n_win + len(shares)]
    out_hbm, prod_ref, out_ref, plan_ref, sems, plan_sem = refs[-6:]
    plan_copy = pltpu.make_async_copy(plan_hbm, plan_ref, plan_sem)
    plan_copy.start()
    windows = n_win * w_dev
    count = len(shares) * n_own
    pad = 128
    rcv = lax.axis_index("rcv")

    low = lax.broadcasted_iota(jnp.int32, (count, pad), 1) < pad // 2
    for group in range(bins // 4):
        values = [s_ref[group].astype(jnp.float32) for s_ref in s_refs]
        for p in range(2):
            rows = jnp.concatenate([v[p * n_own:(p + 1) * n_own] for v in values], axis=0)
            left = jnp.concatenate([jnp.where(low, rows, 0.0), jnp.where(low, 0.0, rows)], axis=0)
            first = 4 * group + 2 * p
            right = [t_ref[f] for f in (first, first + 1) for t_ref in t_refs]
            result = jnp.dot(
                left.astype(jnp.bfloat16), jnp.concatenate(right, axis=0),
                preferred_element_type=jnp.float32,
            )
            for k in range(2):
                for c in range(2):
                    block = result[k * count:(k + 1) * count, c * pad:(c + 1) * pad]
                    prod_ref[c, pl.ds(first + k, count, stride=bins), :] = block

    scale = 1.0 / math.sqrt(windows)
    plan_copy.wait()
    copies = []
    for s in range(count):
        for c in range(2):
            turned = prod_ref[c, s * bins:(s + 1) * bins, :].T
            out_ref[s, pl.ds(c, r_dev, stride=2), :] = turned[:r_dev] * scale
        row = plan_ref[0, (rcv ^ shares[s // n_own]) * n_own + s % n_own]
        copies.append(pltpu.make_async_copy(out_ref.at[s], out_hbm.at[row], sems.at[s]))
        copies[-1].start()
    for copy in copies:
        copy.wait()


def stacks_call(out, plan, turned, sources, shares, n_rcv, w_dev, r_dev, bins):
    n_win = len(turned)
    n_own = sources[0].shape[1] // 2
    windows = n_win * w_dev
    count = len(shares) * n_own
    whole = pl.BlockSpec(memory_space=VMEM)
    args = [plan] + list(turned) + [sources[i] for i in shares]
    specs = [pl.BlockSpec(memory_space=pl.ANY)] + [whole] * (len(args) - 1)
    aliases = {}
    if out is not None:
        aliases = {len(args): 0}
        args.append(out)
        specs.append(pl.BlockSpec(memory_space=pl.ANY))
    return pl.pallas_call(
        functools.partial(stacks_kernel, shares, n_win, w_dev, r_dev, n_own, bins),
        in_specs=specs,
        out_specs=pl.BlockSpec(memory_space=pltpu.HBM),
        out_shape=jax.ShapeDtypeStruct((n_rcv * n_own, 2 * r_dev, bins), jnp.float32),
        input_output_aliases=aliases,
        scratch_shapes=[
            pltpu.VMEM((2, count * bins, 128), jnp.float32),
            pltpu.VMEM((count, 2 * r_dev, bins), jnp.float32),
            pltpu.SMEM(plan.shape, jnp.int32),
            pltpu.SemaphoreType.DMA((count,)),
            pltpu.SemaphoreType.DMA,
        ],
        compiler_params=pltpu.CompilerParams(vmem_limit_bytes=20 * 2**20),
        cost_estimate=pl.CostEstimate(
            flops=8 * windows * count * r_dev * bins, bytes_accessed=6 * 2**20, transcendentals=0
        ),
        name="stacks",
    )(*args)


def swap(value, axis, by):
    size = lax.axis_size(axis)
    return lax.ppermute(value, axis, [(i, i ^ by) for i in range(size)])


def near_and_far(n_rcv, by):
    pairs = [(z, z ^ by) for z in range(n_rcv)]
    return [p for p in pairs if abs(p[0] - p[1]) == 1], [p for p in pairs if abs(p[0] - p[1]) > 1]


def merge_near(picked, near):
    return merge_call(picked[0], *near)


def merge_all(picked, near):
    far = []
    for i in range(1, len(picked)):
        pairs = near_and_far(len(picked), i)[1]
        if pairs:
            far.append(lax.ppermute(picked[i], "rcv", pairs))
    return merge_call(picked[0], *near, *far)


def body(traces, valid, src_station):
    w_dev, r_dev, samples = traces.shape
    n_src = src_station.shape[0]
    n_win = lax.axis_size("win")
    n_rcv = lax.axis_size("rcv")
    bins = F // n_win
    early = n_win // 2

    blocks, picked, plan, flag = spectra_call(traces, valid, src_station, n_win, n_rcv)

    near = {}
    for i in range(1, n_rcv):
        pairs = near_and_far(n_rcv, i)[0]
        if pairs:
            near[i] = lax.ppermute(picked[i], "rcv", pairs)
    picked = [picked[0] + near.pop(n_rcv - 1)] + list(picked[1:])
    near = list(near.values())
    merged = lax.cond(flag.reshape(()) > 0, merge_all, merge_near, picked, near)

    merged = [merged[0]] + [swap(merged[j], "win", j) for j in range(1, n_win)]
    late = [j for j in range(1, n_win) if j != early]
    received = {0: blocks[0], early: swap(blocks[early], "win", early)}
    lefts, later = lefts_call(merged, [received[early]], [blocks[j] for j in late], w_dev)
    received.update({j: swap(block, "win", j) for j, block in zip(late, later)})
    sources = [lefts] + [swap(lefts, "rcv", i) for i in range(1, n_rcv)]

    turned = [turn_call([received[j]], w_dev, r_dev) for j in range(n_win)]
    half = n_rcv // 2
    sizes = (n_rcv, w_dev, r_dev, bins)
    stacks = stacks_call(None, plan, turned, sources, tuple(range(half)), *sizes)
    stacks = stacks_call(stacks, plan, turned, sources, tuple(range(half, n_rcv)), *sizes)
    return stacks.reshape(n_src, r_dev, 2, bins)


def correlate(received, sources):
    rr = received[:, :, 0]
    ri = received[:, :, 1]
    sr = sources[:, :, 0]
    si = sources[:, :, 1]
    real = jnp.einsum("wsf,wrf->srf", sr, rr, preferred_element_type=jnp.float32)
    real = real + jnp.einsum("wsf,wrf->srf", si, ri, preferred_element_type=jnp.float32)
    imag = jnp.einsum("wsf,wrf->srf", sr, ri, preferred_element_type=jnp.float32)
    imag = imag - jnp.einsum("wsf,wrf->srf", si, rr, preferred_element_type=jnp.float32)
    return jnp.stack([real, imag], axis=2)


def body_any(traces, valid, src_station):
    w_dev, r_dev, samples = traces.shape
    n_win = lax.axis_size("win")
    n_rcv = lax.axis_size("rcv")
    bins = F // n_win
    table = jnp.asarray(band_table(samples, F, samples // 16))
    spectra = jnp.dot(
        traces.reshape(w_dev * r_dev, samples), table, preferred_element_type=jnp.float32
    )
    spectra = spectra.reshape(w_dev, r_dev, 2, F)
    power = jnp.sum(spectra * spectra, axis=(2, 3), keepdims=True) / F
    keep = valid.astype(jnp.float32)[:, None, None, None]
    white = (spectra * lax.rsqrt(power + 1e-06) * keep).astype(jnp.bfloat16)
    blocks = white.reshape(w_dev, r_dev, 2, n_win, bins).transpose(3, 0, 1, 2, 4)
    me = lax.axis_index("win")
    offset = lax.axis_index("rcv") * r_dev
    station_ids = offset + jnp.arange(r_dev, dtype=jnp.int32)
    selector = (src_station[:, None] == station_ids[None, :]).astype(jnp.bfloat16)
    received = []
    for j in range(n_win):
        block = lax.dynamic_index_in_dim(blocks, me ^ j, 0, keepdims=False)
        received.append(swap(block, "win", j) if j else block)
    received = jnp.concatenate(received, axis=0)
    rows = jnp.einsum("sr,wrcf->wscf", selector, received, preferred_element_type=jnp.float32)
    rows = lax.all_to_all(rows.astype(jnp.bfloat16), "rcv", 0, 0, tiled=True)
    rows = rows.reshape((n_rcv, -1) + rows.shape[1:])
    merged = jnp.sum(rows.astype(jnp.float32), axis=0).astype(jnp.bfloat16)
    sources = lax.all_gather(merged, "rcv", axis=0, tiled=True)
    return correlate(received, sources) * (1.0 / math.sqrt(w_dev * n_win))


def solution(mesh):
    sizes = (mesh.shape["win"], mesh.shape["rcv"])
    return jax.shard_map(
        body if sizes == (4, 4) else body_any,
        mesh=mesh,
        in_specs=(P("win", ("groups", "rcv"), None), P(("groups", "win")), P("groups")),
        out_specs=P(None, ("groups", "rcv"), None, "win"),
        check_vma=False,
    )
```

```python
import functools
import math

import jax
import jax.numpy as jnp
import numpy as np
from jax import lax
from jax.experimental import pallas as pl
from jax.experimental.pallas import tpu as pltpu
from jax.sharding import PartitionSpec as P

F = 512
SMEM = pltpu.MemorySpace.SMEM
VMEM = pltpu.MemorySpace.VMEM


def angles(samples, freqs, count):
    phase = samples[:, None] * freqs[None, :] % count
    return phase.astype(np.float64) * (2.0 * math.pi / count)


def band_table(count, bins, first):
    angle = angles(np.arange(count), first + np.arange(bins), count)
    return np.concatenate([np.cos(angle), -np.sin(angle)], axis=1).astype(jnp.bfloat16)


BLOCK = 32


def table_seeds(count, bins, first, n_win):
    j = np.arange(bins // 4)
    turn = np.array([0.0, 0.5 * math.pi]).reshape(1, 2, 1)
    seeds, twice = [], []
    for m in range(4):
        freqs = np.broadcast_to((first + 4 * j + m).reshape(n_win, 1, -1), (n_win, 2, j.size // n_win))
        angle = angles(np.arange(2 * BLOCK), freqs.reshape(-1), count)
        angle = angle + np.broadcast_to(turn, freqs.shape).reshape(1, -1)
        seeds.append(np.cos(angle).reshape(2, BLOCK, -1))
        step = angles(np.full(8, BLOCK), freqs.reshape(-1), count)
        twice.append(2.0 * np.cos(step))
    return np.stack(seeds).astype(np.float32), np.stack(twice).astype(np.float32)


def make_tables(seed_ref, twice_ref, table_ref):
    for first in (0, 2):
        state = {}
        for m in (first, first + 1):
            twice = jnp.concatenate([twice_ref[m]] * (BLOCK // 8), axis=0)
            state[m] = (seed_ref[m, 0], seed_ref[m, 1], twice)
        for a in range(table_ref.shape[1] // BLOCK):
            for m, (here, after, twice) in state.items():
                table_ref[m, a * BLOCK:(a + 1) * BLOCK, :] = here.astype(jnp.bfloat16)
                state[m] = (after, twice * after - here, twice)


def in_hbm(value):
    return pltpu.with_memory_space_constraint(value, pltpu.HBM)


def order_sources(src_ref, r_dev, n_own, order_ref, plan_ref, flag_ref):
    n_src = src_ref.shape[0]
    size = order_ref.shape
    down = lax.broadcasted_iota(jnp.int32, size, 0).astype(jnp.float32)
    along = lax.broadcasted_iota(jnp.int32, size, 1).astype(jnp.float32)
    none = jnp.full(size, float(2**20), jnp.float32)
    column, row = none, none
    for s in range(n_src):
        station = src_ref[s].astype(jnp.float32)
        column = jnp.where(down == s, station, column)
        row = jnp.where(along == s, station, row)
    rank_along = jnp.sum((column < row).astype(jnp.float32), axis=0, keepdims=True)
    rank_down = jnp.sum((row < column).astype(jnp.float32), axis=1, keepdims=True)
    sorted_down = jnp.sum(jnp.where(rank_along == down, row, 0.0), axis=1, keepdims=True)
    at_place = rank_down == along
    sorted_along = jnp.sum(jnp.where(at_place, column, 0.0), axis=0, keepdims=True)
    source_along = jnp.sum(jnp.where(at_place, down, 0.0), axis=0, keepdims=True)
    order_ref[...] = jnp.broadcast_to(sorted_down, size)
    place = along[:1]
    owner, share = jnp.zeros_like(place), jnp.zeros_like(place)
    for z in range(1, n_src // n_own):
        owner = owner + (sorted_along >= z * r_dev).astype(jnp.float32)
        share = share + (place >= z * n_own).astype(jnp.float32)
    far = jnp.where((place < n_src) & (jnp.abs(owner - share) > 1.5), 1.0, 0.0)
    plan_ref[...] = jnp.broadcast_to(source_along, plan_ref.shape).astype(jnp.int32)
    flag_ref[0] = jnp.max(far).astype(jnp.int32)


def spectra_kernel(
    n_win, n_rcv, r_dev, valid_hbm, src_hbm, x_hbm, seed_hbm, twice_hbm, *refs
):
    r_refs = refs[:n_win]
    q_refs = refs[n_win:n_win + n_rcv]
    (plan_ref, flag_ref, x_ref, even_ref, odd_ref, white_ref, sel_ref, order_ref, table_ref,
     seed_ref, twice_ref, valid_ref, src_ref, sems, x_sems) = refs[n_win + n_rcv:]
    chunks, rows, samples = x_ref.shape
    w_step = rows // r_dev
    n_own = src_ref.shape[0] // n_rcv
    quarter = samples // 4
    win = lax.axis_index("win")
    rcv = lax.axis_index("rcv")

    def small(k):
        source = (seed_hbm, twice_hbm, src_hbm, valid_hbm)[k]
        target = (seed_ref, twice_ref, src_ref, valid_ref)[k]
        return pltpu.make_async_copy(source, target, sems.at[k])

    def chunk(k):
        return pltpu.make_async_copy(x_hbm.at[pl.ds(k * rows, rows)], x_ref.at[k], x_sems.at[k])

    for k in range(4):
        small(k).start()
    for k in range(chunks):
        chunk(k).start()
    small(0).wait()
    small(1).wait()
    make_tables(seed_ref, twice_ref, table_ref)
    small(2).wait()
    order_sources(src_ref, r_dev, n_own, order_ref, plan_ref, flag_ref)
    stations = []
    for d in range(n_rcv):
        share = pl.multiple_of((rcv ^ d) * n_own, n_own)
        stations += [order_ref[pl.ds(share, n_own), 0:1]] * w_step
    wanted = jnp.concatenate(stations, axis=0).astype(jnp.int32) - rcv * r_dev
    shape = (n_rcv * w_step * n_own, rows)
    out_row = lax.broadcasted_iota(jnp.int32, shape, 0)
    column = lax.broadcasted_iota(jnp.int32, shape, 1)
    inside = (wanted >= 0) & (wanted < r_dev)
    hit = inside & (column == wanted + (out_row // n_own) % w_step * r_dev)
    sel_ref[...] = hit.astype(jnp.float32).astype(jnp.bfloat16)
    small(3).wait()

    def product(lhs, table):
        return jnp.dot(lhs, table, preferred_element_type=jnp.float32)

    def add_quarters(k, first, last):
        part = slice(first, last)
        b0, b1, b2, b3 = (x_ref[k, part, q * quarter:(q + 1) * quarter] for q in range(4))
        x0, x1, x2, x3 = (b.astype(jnp.float32) for b in (b0, b1, b2, b3))
        even_ref[k, 0, part] = ((x0 + x2) + (x1 + x3)).astype(jnp.bfloat16)
        even_ref[k, 1, part] = ((x0 + x2) - (x1 + x3)).astype(jnp.bfloat16)
        odd_ref[k, part] = b0 - b2
        odd_ref[k, rows + first:rows + last] = b1 - b3

    lanes = table_ref.shape[2]
    lane = lax.broadcasted_iota(jnp.int32, (rows, lanes), 1)
    piece = lanes // n_win
    real = lane % piece < piece // 2

    def odd_spectra(k, m):
        both = product(odd_ref[k], table_ref[m])
        second = both[rows:]
        back, forth = pltpu.roll(second, lanes - piece // 2, 1), pltpu.roll(second, piece // 2, 1)
        turned = jnp.where(real, back, -forth)
        return both[:rows] + turned if m == 1 else both[:rows] - turned

    parts = 4
    size = rows // parts
    chunk(0).wait()
    add_quarters(0, 0, rows)
    row = lax.broadcasted_iota(jnp.int32, (rows, 1), 0)
    for k in range(chunks):
        more = k + 1 < chunks
        if more:
            chunk(k + 1).wait()
        spectra = []
        for m in range(4):
            if m % 2:
                spectra.append(odd_spectra(k, m))
            else:
                spectra.append(product(even_ref[k, m // 2], table_ref[m]))
            if more:
                add_quarters(k + 1, m * size, (m + 1) * size)
        squares = sum(jnp.sum(s * s, axis=1, keepdims=True) for s in spectra)
        gain = lax.rsqrt(squares / F + 1e-06)
        keep = jnp.zeros((rows, 1), jnp.float32)
        for t in range(w_step):
            own = (row >= t * r_dev) & (row < (t + 1) * r_dev)
            keep = jnp.where(own, valid_ref[k * w_step + t].astype(jnp.float32), keep)
        gain = gain * keep
        white = [s * gain for s in spectra]
        for d in range(n_win):
            columns = slice(d * piece, (d + 1) * piece)
            block = jnp.concatenate([part[:, columns] for part in white], axis=1)
            white_ref[k, d] = block.astype(jnp.bfloat16)
        count = w_step * n_own
        for j in range(n_win):
            block = white_ref[k, win ^ j]
            r_refs[j][k * rows:(k + 1) * rows, :] = block
            picked = product(sel_ref[...], block).astype(jnp.bfloat16)
            for d in range(n_rcv):
                q_refs[d][j, k * count:(k + 1) * count, :] = picked[d * count:(d + 1) * count]


def spectra_call(traces, valid, src_station, n_win, n_rcv):
    w_dev, r_dev, samples = traces.shape
    n_src = src_station.shape[0]
    n_own = n_src // n_rcv
    chunks = 2
    every = w_dev * r_dev
    rows = every // chunks
    lanes = 2 * F // n_win
    seed, twice = (jnp.asarray(t) for t in table_seeds(samples, F, samples // 16, n_win))
    shapes = [jax.ShapeDtypeStruct((every, lanes), jnp.bfloat16)] * n_win
    shapes += [jax.ShapeDtypeStruct((n_win, w_dev * n_own, lanes), jnp.bfloat16)] * n_rcv
    shapes += [jax.ShapeDtypeStruct((8, 128), jnp.int32), jax.ShapeDtypeStruct((1,), jnp.int32)]
    vmem = pl.BlockSpec(memory_space=VMEM)
    out = pl.pallas_call(
        functools.partial(spectra_kernel, n_win, n_rcv, r_dev),
        in_specs=[pl.BlockSpec(memory_space=pltpu.HBM)] * 5,
        out_specs=[vmem] * (len(shapes) - 1) + [pl.BlockSpec(memory_space=SMEM)],
        out_shape=shapes,
        scratch_shapes=[
            pltpu.VMEM((chunks, rows, samples), jnp.bfloat16),
            pltpu.VMEM((chunks, 2, rows, samples // 4), jnp.bfloat16),
            pltpu.VMEM((chunks, 2 * rows, samples // 4), jnp.bfloat16),
            pltpu.VMEM((chunks, n_win, rows, lanes), jnp.bfloat16),
            pltpu.VMEM((n_src * (w_dev // chunks), rows), jnp.bfloat16),
            pltpu.VMEM((n_src, 128), jnp.float32),
            pltpu.VMEM((4, samples // 4, F // 2), jnp.bfloat16),
            pltpu.VMEM(seed.shape, jnp.float32),
            pltpu.VMEM(twice.shape, jnp.float32),
            pltpu.SMEM(valid.shape, jnp.int32),
            pltpu.SMEM(src_station.shape, jnp.int32),
            pltpu.SemaphoreType.DMA((4,)),
            pltpu.SemaphoreType.DMA((chunks,)),
        ],
        compiler_params=pltpu.CompilerParams(vmem_limit_bytes=36 * 2**20),
        cost_estimate=pl.CostEstimate(
            flops=2 * every * (samples // 4) * 6 * (F // 2), bytes_accessed=every * samples * 2,
            transcendentals=0,
        ),
        name="spectra",
    )(*(in_hbm(x) for x in (valid, src_station, traces.reshape(every, samples), seed, twice)))
    return out[:n_win], out[n_win:n_win + n_rcv], out[-2], out[-1]


def bin_order(lanes):
    quarter = lanes // 8
    lane = lax.broadcasted_iota(jnp.int32, (lanes, lanes), 1)
    row = lax.broadcasted_iota(jnp.int32, (lanes, lanes), 0)
    part = (lane // quarter) % 2
    bin_of = 4 * (lane % quarter) + lane // (2 * quarter)
    hit = row == part * (lanes // 2) + bin_of
    return hit.astype(jnp.float32).astype(jnp.bfloat16)


def turn_kernel(r_dev, *refs):
    x_refs, (out_ref, rows_ref) = refs[:-2], refs[-2:]
    lanes = x_refs[0].shape[1]
    bins = lanes // 2
    w_dev = out_ref.shape[1] // 2
    pad = out_ref.shape[2] // 2
    order = bin_order(lanes)
    windows = [(x, w) for x in x_refs for w in range(x.shape[0] // r_dev)]
    none = jnp.zeros((pad - r_dev, lanes), jnp.bfloat16)
    for k, (x_ref, w) in enumerate(windows):
        block = jnp.concatenate([x_ref[w * r_dev:(w + 1) * r_dev], none], axis=0)
        turned = lax.dot_general(
            order, block, (((1,), (1,)), ((), ())), preferred_element_type=jnp.float32
        )
        rows_ref[pl.ds(k, lanes, stride=w_dev), :] = turned
    rr = rows_ref[:bins * w_dev].reshape(bins, w_dev, pad)
    ri = rows_ref[bins * w_dev:].reshape(bins, w_dev, pad)
    out_ref[:, :, :pad] = jnp.concatenate([rr, ri], axis=1).astype(jnp.bfloat16)
    out_ref[:, :, pad:] = jnp.concatenate([ri, -rr], axis=1).astype(jnp.bfloat16)


def turn_call(parts, w_dev, r_dev):
    lanes = parts[0].shape[1]
    pad = 128
    vmem = pl.BlockSpec(memory_space=VMEM)
    return pl.pallas_call(
        functools.partial(turn_kernel, r_dev),
        in_specs=[vmem] * len(parts),
        out_specs=vmem,
        out_shape=jax.ShapeDtypeStruct((lanes // 2, 2 * w_dev, 2 * pad), jnp.bfloat16),
        scratch_shapes=[pltpu.VMEM((lanes * w_dev, pad), jnp.float32)],
        compiler_params=pltpu.CompilerParams(vmem_limit_bytes=16 * 2**20),
        cost_estimate=pl.CostEstimate(
            flops=2 * w_dev * lanes * lanes * pad, bytes_accessed=2 * 2**20, transcendentals=0
        ),
        name="turn",
    )(*parts)


def merge_kernel(n_win, *refs):
    picked, outs = refs[:-n_win], refs[-n_win:]
    for j, out_ref in enumerate(outs):
        total = picked[0][j].astype(jnp.float32)
        for q_ref in picked[1:]:
            total = total + q_ref[j].astype(jnp.float32)
        out_ref[...] = total.astype(jnp.bfloat16)


def merge_call(*picked):
    n_win, rows, lanes = picked[0].shape
    vmem = pl.BlockSpec(memory_space=VMEM)
    return pl.pallas_call(
        functools.partial(merge_kernel, n_win),
        in_specs=[vmem] * len(picked),
        out_specs=[vmem] * n_win,
        out_shape=[jax.ShapeDtypeStruct((rows, lanes), jnp.bfloat16)] * n_win,
        compiler_params=pltpu.CompilerParams(vmem_limit_bytes=4 * 2**20),
        cost_estimate=pl.CostEstimate(flops=2**18, bytes_accessed=2**19, transcendentals=0),
        name="merge",
    )(*picked)


def lefts_kernel(n_win, w_dev, n_own, *refs):
    out_ref, srow_ref, rows_ref = refs[-3:]
    rows, lanes = refs[0].shape
    bins = lanes // 2
    windows = n_win * w_dev
    pad = rows_ref.shape[1]
    for j in range(n_win):
        block = refs[j][...].astype(jnp.float32)
        for h in range(lanes // pad):
            srow_ref[h, j * rows:(j + 1) * rows, :] = block[:, h * pad:(h + 1) * pad]

    lane = lax.broadcasted_iota(jnp.int32, (bins, lanes), 1)
    row = lax.broadcasted_iota(jnp.int32, (bins, lanes), 0)
    quarter = lanes // 8
    bin_of = 4 * (lane % quarter) + lane // (2 * quarter)
    pick = bin_of == 2 * (row % (bins // 2)) + row // (bins // 2)
    pick = pick.astype(jnp.float32).astype(jnp.bfloat16)
    real = (lane[:w_dev] // quarter) % 2 == 0
    low = lax.broadcasted_iota(jnp.int32, (bins // 2, pad), 1) < pad // 2
    for s in range(n_own):
        values = jnp.concatenate(
            [srow_ref[h, pl.ds(s, windows, stride=n_own), :] for h in range(lanes // pad)], axis=1
        )
        stacked = []
        for j in range(n_win):
            own = values[j * w_dev:(j + 1) * w_dev]
            stacked += [jnp.where(real, own, 0.0), jnp.where(real, 0.0, own)]
        stacked = jnp.concatenate(stacked * 2, axis=0).astype(jnp.bfloat16)
        turned = lax.dot_general(
            pick, stacked, (((1,), (1,)), ((), ())), preferred_element_type=jnp.float32
        )
        pairs = jnp.where(low, turned[:bins // 2], turned[bins // 2:])
        rows_ref[pl.ds(s, bins // 2, stride=n_own), :] = pairs
    out_ref[...] = rows_ref[...].reshape(out_ref.shape).astype(jnp.bfloat16)


def lefts_call(blocks, after, later, w_dev):
    rows, lanes = blocks[0].shape
    n_win = len(blocks)
    n_own = rows // w_dev
    pad = 128
    first = n_win + len(after)
    vmem, anywhere = pl.BlockSpec(memory_space=VMEM), pl.BlockSpec(memory_space=pl.ANY)
    out = pl.pallas_call(
        functools.partial(lefts_kernel, n_win, w_dev, n_own),
        in_specs=[vmem] * n_win + [anywhere] * (len(after) + len(later)),
        out_specs=[anywhere] * len(later) + [vmem],
        out_shape=[jax.ShapeDtypeStruct(x.shape, x.dtype) for x in later]
        + [jax.ShapeDtypeStruct((lanes // 8, 2 * n_own, pad), jnp.bfloat16)],
        input_output_aliases={first + k: k for k in range(len(later))},
        scratch_shapes=[
            pltpu.VMEM((lanes // pad, n_win * rows, pad), jnp.float32),
            pltpu.VMEM((lanes // 4 * n_own, pad), jnp.float32),
        ],
        compiler_params=pltpu.CompilerParams(vmem_limit_bytes=6 * 2**20),
        cost_estimate=pl.CostEstimate(flops=2**26, bytes_accessed=2**19, transcendentals=0),
        name="lefts",
    )(*blocks, *after, *later)
    return out[-1], out[:-1]


def stacks_kernel(shares, n_win, w_dev, r_dev, n_own, bins, plan_hbm, *refs):
    t_refs = refs[:n_win]
    s_refs = refs[n_win:n_win + len(shares)]
    out_hbm, prod_ref, out_ref, plan_ref, sems, plan_sem = refs[-6:]
    plan_copy = pltpu.make_async_copy(plan_hbm, plan_ref, plan_sem)
    plan_copy.start()
    windows = n_win * w_dev
    count = len(shares) * n_own
    pad = 128
    rcv = lax.axis_index("rcv")

    low = lax.broadcasted_iota(jnp.int32, (count, pad), 1) < pad // 2
    for group in range(bins // 4):
        values = [s_ref[group].astype(jnp.float32) for s_ref in s_refs]
        for p in range(2):
            rows = jnp.concatenate([v[p * n_own:(p + 1) * n_own] for v in values], axis=0)
            left = jnp.concatenate([jnp.where(low, rows, 0.0), jnp.where(low, 0.0, rows)], axis=0)
            first = 4 * group + 2 * p
            right = [t_ref[f] for f in (first, first + 1) for t_ref in t_refs]
            result = jnp.dot(
                left.astype(jnp.bfloat16), jnp.concatenate(right, axis=0),
                preferred_element_type=jnp.float32,
            )
            for k in range(2):
                for c in range(2):
                    block = result[k * count:(k + 1) * count, c * pad:(c + 1) * pad]
                    prod_ref[c, pl.ds(first + k, count, stride=bins), :] = block

    scale = 1.0 / math.sqrt(windows)
    plan_copy.wait()
    copies = []
    column = lax.broadcasted_iota(jnp.int32, (r_dev, 2 * pad), 1)
    row = lax.broadcasted_iota(jnp.int32, (r_dev, 2 * pad), 0)
    twice = (column % pad == row).astype(jnp.float32).astype(jnp.bfloat16)
    for s in range(count):
        both = jnp.concatenate([prod_ref[c, s * bins:(s + 1) * bins, :] for c in range(2)], axis=0)
        high = both.astype(jnp.bfloat16)
        rest = (both - high.astype(jnp.float32)).astype(jnp.bfloat16)
        turned = lax.dot_general(
            twice, jnp.concatenate([high, rest], axis=1), (((1,), (1,)), ((), ())),
            preferred_element_type=jnp.float32,
        )
        for c in range(2):
            half = turned[:, c * bins:(c + 1) * bins] * scale
            out_ref[s, pl.ds(c, r_dev, stride=2), :] = half
        row = plan_ref[0, (rcv ^ shares[s // n_own]) * n_own + s % n_own]
        copies.append(pltpu.make_async_copy(out_ref.at[s], out_hbm.at[row], sems.at[s]))
        copies[-1].start()
    for copy in copies:
        copy.wait()


def stacks_call(out, plan, turned, sources, shares, n_rcv, w_dev, r_dev, bins):
    n_win = len(turned)
    n_own = sources[0].shape[1] // 2
    windows = n_win * w_dev
    count = len(shares) * n_own
    whole = pl.BlockSpec(memory_space=VMEM)
    args = [plan] + list(turned) + [sources[i] for i in shares]
    specs = [pl.BlockSpec(memory_space=pl.ANY)] + [whole] * (len(args) - 1)
    aliases = {}
    if out is not None:
        aliases = {len(args): 0}
        args.append(out)
        specs.append(pl.BlockSpec(memory_space=pl.ANY))
    return pl.pallas_call(
        functools.partial(stacks_kernel, shares, n_win, w_dev, r_dev, n_own, bins),
        in_specs=specs,
        out_specs=pl.BlockSpec(memory_space=pltpu.HBM),
        out_shape=jax.ShapeDtypeStruct((n_rcv * n_own, 2 * r_dev, bins), jnp.float32),
        input_output_aliases=aliases,
        scratch_shapes=[
            pltpu.VMEM((2, count * bins, 128), jnp.float32),
            pltpu.VMEM((count, 2 * r_dev, bins), jnp.float32),
            pltpu.SMEM(plan.shape, jnp.int32),
            pltpu.SemaphoreType.DMA((count,)),
            pltpu.SemaphoreType.DMA,
        ],
        compiler_params=pltpu.CompilerParams(vmem_limit_bytes=20 * 2**20),
        cost_estimate=pl.CostEstimate(
            flops=8 * windows * count * r_dev * bins, bytes_accessed=6 * 2**20, transcendentals=0
        ),
        name="stacks",
    )(*args)


def swap(value, axis, by):
    size = lax.axis_size(axis)
    return lax.ppermute(value, axis, [(i, i ^ by) for i in range(size)])


def near_and_far(n_rcv, by):
    pairs = [(z, z ^ by) for z in range(n_rcv)]
    return [p for p in pairs if abs(p[0] - p[1]) == 1], [p for p in pairs if abs(p[0] - p[1]) > 1]


def merge_near(picked, near):
    return merge_call(picked[0], *near)


def merge_all(picked, near):
    far = []
    for i in range(1, len(picked)):
        pairs = near_and_far(len(picked), i)[1]
        if pairs:
            far.append(lax.ppermute(picked[i], "rcv", pairs))
    return merge_call(picked[0], *near, *far)


def body(traces, valid, src_station):
    w_dev, r_dev, samples = traces.shape
    n_src = src_station.shape[0]
    n_win = lax.axis_size("win")
    n_rcv = lax.axis_size("rcv")
    bins = F // n_win
    early = n_win // 2

    blocks, picked, plan, flag = spectra_call(traces, valid, src_station, n_win, n_rcv)

    near = {}
    for i in range(1, n_rcv):
        pairs = near_and_far(n_rcv, i)[0]
        if pairs:
            near[i] = lax.ppermute(picked[i], "rcv", pairs)
    picked = [picked[0] + near.pop(n_rcv - 1)] + list(picked[1:])
    near = list(near.values())
    merged = lax.cond(flag.reshape(()) > 0, merge_all, merge_near, picked, near)

    merged = [merged[0]] + [swap(merged[j], "win", j) for j in range(1, n_win)]
    late = [j for j in range(1, n_win) if j != early]
    received = {0: blocks[0], early: swap(blocks[early], "win", early)}
    lefts, later = lefts_call(merged, [received[early]], [blocks[j] for j in late], w_dev)
    received.update({j: swap(block, "win", j) for j, block in zip(late, later)})
    sources = [lefts] + [swap(lefts, "rcv", i) for i in range(1, n_rcv)]

    turned = [turn_call([received[j]], w_dev, r_dev) for j in range(n_win)]
    half = n_rcv // 2
    sizes = (n_rcv, w_dev, r_dev, bins)
    stacks = stacks_call(None, plan, turned, sources, tuple(range(half)), *sizes)
    stacks = stacks_call(stacks, plan, turned, sources, tuple(range(half, n_rcv)), *sizes)
    return stacks.reshape(n_src, r_dev, 2, bins)


def correlate(received, sources):
    rr = received[:, :, 0]
    ri = received[:, :, 1]
    sr = sources[:, :, 0]
    si = sources[:, :, 1]
    real = jnp.einsum("wsf,wrf->srf", sr, rr, preferred_element_type=jnp.float32)
    real = real + jnp.einsum("wsf,wrf->srf", si, ri, preferred_element_type=jnp.float32)
    imag = jnp.einsum("wsf,wrf->srf", sr, ri, preferred_element_type=jnp.float32)
    imag = imag - jnp.einsum("wsf,wrf->srf", si, rr, preferred_element_type=jnp.float32)
    return jnp.stack([real, imag], axis=2)


def body_any(traces, valid, src_station):
    w_dev, r_dev, samples = traces.shape
    n_win = lax.axis_size("win")
    n_rcv = lax.axis_size("rcv")
    bins = F // n_win
    table = jnp.asarray(band_table(samples, F, samples // 16))
    spectra = jnp.dot(
        traces.reshape(w_dev * r_dev, samples), table, preferred_element_type=jnp.float32
    )
    spectra = spectra.reshape(w_dev, r_dev, 2, F)
    power = jnp.sum(spectra * spectra, axis=(2, 3), keepdims=True) / F
    keep = valid.astype(jnp.float32)[:, None, None, None]
    white = (spectra * lax.rsqrt(power + 1e-06) * keep).astype(jnp.bfloat16)
    blocks = white.reshape(w_dev, r_dev, 2, n_win, bins).transpose(3, 0, 1, 2, 4)
    me = lax.axis_index("win")
    offset = lax.axis_index("rcv") * r_dev
    station_ids = offset + jnp.arange(r_dev, dtype=jnp.int32)
    selector = (src_station[:, None] == station_ids[None, :]).astype(jnp.bfloat16)
    received = []
    for j in range(n_win):
        block = lax.dynamic_index_in_dim(blocks, me ^ j, 0, keepdims=False)
        received.append(swap(block, "win", j) if j else block)
    received = jnp.concatenate(received, axis=0)
    rows = jnp.einsum("sr,wrcf->wscf", selector, received, preferred_element_type=jnp.float32)
    rows = lax.all_to_all(rows.astype(jnp.bfloat16), "rcv", 0, 0, tiled=True)
    rows = rows.reshape((n_rcv, -1) + rows.shape[1:])
    merged = jnp.sum(rows.astype(jnp.float32), axis=0).astype(jnp.bfloat16)
    sources = lax.all_gather(merged, "rcv", axis=0, tiled=True)
    return correlate(received, sources) * (1.0 / math.sqrt(w_dev * n_win))


def solution(mesh):
    sizes = (mesh.shape["win"], mesh.shape["rcv"])
    return jax.shard_map(
        body if sizes == (4, 4) else body_any,
        mesh=mesh,
        in_specs=(P("win", ("groups", "rcv"), None), P(("groups", "win")), P("groups")),
        out_specs=P(None, ("groups", "rcv"), None, "win"),
        check_vma=False,
    )
```

```python
import functools
import math

import jax
import jax.numpy as jnp
import numpy as np
from jax import lax
from jax.experimental import pallas as pl
from jax.experimental.pallas import tpu as pltpu
from jax.sharding import PartitionSpec as P

F = 512
SMEM = pltpu.MemorySpace.SMEM
VMEM = pltpu.MemorySpace.VMEM


def angles(samples, freqs, count):
    phase = samples[:, None] * freqs[None, :] % count
    return phase.astype(np.float64) * (2.0 * math.pi / count)


def band_table(count, bins, first):
    angle = angles(np.arange(count), first + np.arange(bins), count)
    return np.concatenate([np.cos(angle), -np.sin(angle)], axis=1).astype(jnp.bfloat16)


BLOCK = 32


def table_seeds(count, bins, first, n_win):
    j = np.arange(bins // 4)
    turn = np.array([0.0, 0.5 * math.pi]).reshape(1, 2, 1)
    seeds, twice = [], []
    for m in range(4):
        freqs = np.broadcast_to((first + 4 * j + m).reshape(n_win, 1, -1), (n_win, 2, j.size // n_win))
        angle = angles(np.arange(2 * BLOCK), freqs.reshape(-1), count)
        angle = angle + np.broadcast_to(turn, freqs.shape).reshape(1, -1)
        seeds.append(np.cos(angle).reshape(2, BLOCK, -1))
        step = angles(np.full(8, BLOCK), freqs.reshape(-1), count)
        twice.append(2.0 * np.cos(step))
    return np.stack(seeds).astype(np.float32), np.stack(twice).astype(np.float32)


def make_tables(seed_ref, twice_ref, table_ref):
    for first in (0, 2):
        state = {}
        for m in (first, first + 1):
            twice = jnp.concatenate([twice_ref[m]] * (BLOCK // 8), axis=0)
            state[m] = (seed_ref[m, 0], seed_ref[m, 1], twice)
        for a in range(table_ref.shape[1] // BLOCK):
            for m, (here, after, twice) in state.items():
                table_ref[m, a * BLOCK:(a + 1) * BLOCK, :] = here.astype(jnp.bfloat16)
                state[m] = (after, twice * after - here, twice)


def in_hbm(value):
    return pltpu.with_memory_space_constraint(value, pltpu.HBM)


def order_sources(src_ref, r_dev, n_own, order_ref, plan_ref, flag_ref):
    n_src = src_ref.shape[0]
    size = order_ref.shape
    down = lax.broadcasted_iota(jnp.int32, size, 0).astype(jnp.float32)
    along = lax.broadcasted_iota(jnp.int32, size, 1).astype(jnp.float32)
    none = jnp.full(size, float(2**20), jnp.float32)
    column, row = none, none
    for s in range(n_src):
        station = src_ref[s].astype(jnp.float32)
        column = jnp.where(down == s, station, column)
        row = jnp.where(along == s, station, row)
    rank_along = jnp.sum((column < row).astype(jnp.float32), axis=0, keepdims=True)
    rank_down = jnp.sum((row < column).astype(jnp.float32), axis=1, keepdims=True)
    sorted_down = jnp.sum(jnp.where(rank_along == down, row, 0.0), axis=1, keepdims=True)
    at_place = rank_down == along
    sorted_along = jnp.sum(jnp.where(at_place, column, 0.0), axis=0, keepdims=True)
    source_along = jnp.sum(jnp.where(at_place, down, 0.0), axis=0, keepdims=True)
    order_ref[...] = jnp.broadcast_to(sorted_down, size)
    place = along[:1]
    owner, share = jnp.zeros_like(place), jnp.zeros_like(place)
    for z in range(1, n_src // n_own):
        owner = owner + (sorted_along >= z * r_dev).astype(jnp.float32)
        share = share + (place >= z * n_own).astype(jnp.float32)
    far = jnp.where((place < n_src) & (jnp.abs(owner - share) > 1.5), 1.0, 0.0)
    plan_ref[...] = jnp.broadcast_to(source_along, plan_ref.shape).astype(jnp.int32)
    flag_ref[0] = jnp.max(far).astype(jnp.int32)


def spectra_kernel(
    n_win, n_rcv, r_dev, valid_hbm, src_hbm, x_hbm, seed_hbm, twice_hbm, *refs
):
    r_refs = refs[:n_win]
    q_refs = refs[n_win:n_win + n_rcv]
    (plan_ref, flag_ref, x_ref, even_ref, odd_ref, white_ref, sel_ref, order_ref, table_ref,
     seed_ref, twice_ref, valid_ref, src_ref, sems, x_sems) = refs[n_win + n_rcv:]
    chunks, rows, samples = x_ref.shape
    w_step = rows // r_dev
    n_own = src_ref.shape[0] // n_rcv
    quarter = samples // 4
    win = lax.axis_index("win")
    rcv = lax.axis_index("rcv")

    def small(k):
        source = (seed_hbm, twice_hbm, src_hbm, valid_hbm)[k]
        target = (seed_ref, twice_ref, src_ref, valid_ref)[k]
        return pltpu.make_async_copy(source, target, sems.at[k])

    def chunk(k):
        return pltpu.make_async_copy(x_hbm.at[pl.ds(k * rows, rows)], x_ref.at[k], x_sems.at[k])

    for k in range(4):
        small(k).start()
    for k in range(chunks):
        chunk(k).start()
    small(0).wait()
    small(1).wait()
    make_tables(seed_ref, twice_ref, table_ref)
    small(2).wait()
    order_sources(src_ref, r_dev, n_own, order_ref, plan_ref, flag_ref)
    stations = []
    for d in range(n_rcv):
        share = pl.multiple_of((rcv ^ d) * n_own, n_own)
        stations += [order_ref[pl.ds(share, n_own), 0:1]] * w_step
    wanted = jnp.concatenate(stations, axis=0).astype(jnp.int32) - rcv * r_dev
    shape = (n_rcv * w_step * n_own, rows)
    out_row = lax.broadcasted_iota(jnp.int32, shape, 0)
    column = lax.broadcasted_iota(jnp.int32, shape, 1)
    inside = (wanted >= 0) & (wanted < r_dev)
    hit = inside & (column == wanted + (out_row // n_own) % w_step * r_dev)
    sel_ref[...] = hit.astype(jnp.float32).astype(jnp.bfloat16)
    small(3).wait()

    def product(lhs, table):
        return jnp.dot(lhs, table, preferred_element_type=jnp.float32)

    def add_quarters(k, first, last):
        part = slice(first, last)
        b0, b1, b2, b3 = (x_ref[k, part, q * quarter:(q + 1) * quarter] for q in range(4))
        x0, x1, x2, x3 = (b.astype(jnp.float32) for b in (b0, b1, b2, b3))
        even_ref[k, 0, part] = ((x0 + x2) + (x1 + x3)).astype(jnp.bfloat16)
        even_ref[k, 1, part] = ((x0 + x2) - (x1 + x3)).astype(jnp.bfloat16)
        odd_ref[k, part] = b0 - b2
        odd_ref[k, rows + first:rows + last] = b1 - b3

    lanes = table_ref.shape[2]
    lane = lax.broadcasted_iota(jnp.int32, (rows, lanes), 1)
    piece = lanes // n_win
    real = lane % piece < piece // 2

    def odd_spectra(k, m):
        both = product(odd_ref[k], table_ref[m])
        second = both[rows:]
        back, forth = pltpu.roll(second, lanes - piece // 2, 1), pltpu.roll(second, piece // 2, 1)
        turned = jnp.where(real, back, -forth)
        return both[:rows] + turned if m == 1 else both[:rows] - turned

    parts = 4
    size = rows // parts
    chunk(0).wait()
    add_quarters(0, 0, rows)
    row = lax.broadcasted_iota(jnp.int32, (rows, 1), 0)
    for k in range(chunks):
        more = k + 1 < chunks
        if more:
            chunk(k + 1).wait()
        spectra = []
        for m in range(4):
            if m % 2:
                spectra.append(odd_spectra(k, m))
            else:
                spectra.append(product(even_ref[k, m // 2], table_ref[m]))
            if more:
                add_quarters(k + 1, m * size, (m + 1) * size)
        squares = sum(jnp.sum(s * s, axis=1, keepdims=True) for s in spectra)
        gain = lax.rsqrt(squares / F + 1e-06)
        keep = jnp.zeros((rows, 1), jnp.float32)
        for t in range(w_step):
            own = (row >= t * r_dev) & (row < (t + 1) * r_dev)
            keep = jnp.where(own, valid_ref[k * w_step + t].astype(jnp.float32), keep)
        gain = gain * keep
        white = [s * gain for s in spectra]
        for d in range(n_win):
            columns = slice(d * piece, (d + 1) * piece)
            block = jnp.concatenate([part[:, columns] for part in white], axis=1)
            white_ref[k, d] = block.astype(jnp.bfloat16)
        count = w_step * n_own
        for j in range(n_win):
            block = white_ref[k, win ^ j]
            r_refs[j][k * rows:(k + 1) * rows, :] = block
            picked = product(sel_ref[...], block).astype(jnp.bfloat16)
            for d in range(n_rcv):
                q_refs[d][j, k * count:(k + 1) * count, :] = picked[d * count:(d + 1) * count]


def spectra_call(traces, valid, src_station, n_win, n_rcv):
    w_dev, r_dev, samples = traces.shape
    n_src = src_station.shape[0]
    n_own = n_src // n_rcv
    chunks = 2
    every = w_dev * r_dev
    rows = every // chunks
    lanes = 2 * F // n_win
    seed, twice = (jnp.asarray(t) for t in table_seeds(samples, F, samples // 16, n_win))
    shapes = [jax.ShapeDtypeStruct((every, lanes), jnp.bfloat16)] * n_win
    shapes += [jax.ShapeDtypeStruct((n_win, w_dev * n_own, lanes), jnp.bfloat16)] * n_rcv
    shapes += [jax.ShapeDtypeStruct((8, 128), jnp.int32), jax.ShapeDtypeStruct((1,), jnp.int32)]
    vmem = pl.BlockSpec(memory_space=VMEM)
    out = pl.pallas_call(
        functools.partial(spectra_kernel, n_win, n_rcv, r_dev),
        in_specs=[pl.BlockSpec(memory_space=pltpu.HBM)] * 5,
        out_specs=[vmem] * (len(shapes) - 1) + [pl.BlockSpec(memory_space=SMEM)],
        out_shape=shapes,
        scratch_shapes=[
            pltpu.VMEM((chunks, rows, samples), jnp.bfloat16),
            pltpu.VMEM((chunks, 2, rows, samples // 4), jnp.bfloat16),
            pltpu.VMEM((chunks, 2 * rows, samples // 4), jnp.bfloat16),
            pltpu.VMEM((chunks, n_win, rows, lanes), jnp.bfloat16),
            pltpu.VMEM((n_src * (w_dev // chunks), rows), jnp.bfloat16),
            pltpu.VMEM((n_src, 128), jnp.float32),
            pltpu.VMEM((4, samples // 4, F // 2), jnp.bfloat16),
            pltpu.VMEM(seed.shape, jnp.float32),
            pltpu.VMEM(twice.shape, jnp.float32),
            pltpu.SMEM(valid.shape, jnp.int32),
            pltpu.SMEM(src_station.shape, jnp.int32),
            pltpu.SemaphoreType.DMA((4,)),
            pltpu.SemaphoreType.DMA((chunks,)),
        ],
        compiler_params=pltpu.CompilerParams(vmem_limit_bytes=36 * 2**20),
        cost_estimate=pl.CostEstimate(
            flops=2 * every * (samples // 4) * 6 * (F // 2), bytes_accessed=every * samples * 2,
            transcendentals=0,
        ),
        name="spectra",
    )(*(in_hbm(x) for x in (valid, src_station, traces.reshape(every, samples), seed, twice)))
    return out[:n_win], out[n_win:n_win + n_rcv], out[-2], out[-1]


def bin_order(lanes):
    quarter = lanes // 8
    lane = lax.broadcasted_iota(jnp.int32, (lanes, lanes), 1)
    row = lax.broadcasted_iota(jnp.int32, (lanes, lanes), 0)
    part = (lane // quarter) % 2
    bin_of = 4 * (lane % quarter) + lane // (2 * quarter)
    hit = row == part * (lanes // 2) + bin_of
    return hit.astype(jnp.float32).astype(jnp.bfloat16)


def turn_kernel(r_dev, *refs):
    x_refs, (out_ref, rows_ref) = refs[:-2], refs[-2:]
    lanes = x_refs[0].shape[1]
    bins = lanes // 2
    w_dev = out_ref.shape[1] // 2
    pad = out_ref.shape[2] // 2
    order = bin_order(lanes)
    windows = [(x, w) for x in x_refs for w in range(x.shape[0] // r_dev)]
    for k, (x_ref, w) in enumerate(windows):
        turned = lax.dot_general(
            order, x_ref[w * r_dev:(w + 1) * r_dev], (((1,), (1,)), ((), ())),
            preferred_element_type=jnp.float32,
        )
        rows_ref[pl.ds(k, lanes, stride=w_dev), :r_dev] = turned
    rr = rows_ref[:bins * w_dev].reshape(bins, w_dev, pad)
    ri = rows_ref[bins * w_dev:].reshape(bins, w_dev, pad)
    out_ref[:, :, :pad] = jnp.concatenate([rr, ri], axis=1).astype(jnp.bfloat16)
    out_ref[:, :, pad:] = jnp.concatenate([ri, -rr], axis=1).astype(jnp.bfloat16)


def turn_call(parts, w_dev, r_dev):
    lanes = parts[0].shape[1]
    pad = 128
    vmem = pl.BlockSpec(memory_space=VMEM)
    return pl.pallas_call(
        functools.partial(turn_kernel, r_dev),
        in_specs=[vmem] * len(parts),
        out_specs=vmem,
        out_shape=jax.ShapeDtypeStruct((lanes // 2, 2 * w_dev, 2 * pad), jnp.bfloat16),
        scratch_shapes=[pltpu.VMEM((lanes * w_dev, pad), jnp.float32)],
        compiler_params=pltpu.CompilerParams(vmem_limit_bytes=16 * 2**20),
        cost_estimate=pl.CostEstimate(
            flops=2 * w_dev * lanes * lanes * pad, bytes_accessed=2 * 2**20, transcendentals=0
        ),
        name="turn",
    )(*parts)


def merge_kernel(n_win, *refs):
    picked, outs = refs[:-n_win], refs[-n_win:]
    for j, out_ref in enumerate(outs):
        total = picked[0][j].astype(jnp.float32)
        for q_ref in picked[1:]:
            total = total + q_ref[j].astype(jnp.float32)
        out_ref[...] = total.astype(jnp.bfloat16)


def merge_call(*picked):
    n_win, rows, lanes = picked[0].shape
    vmem = pl.BlockSpec(memory_space=VMEM)
    return pl.pallas_call(
        functools.partial(merge_kernel, n_win),
        in_specs=[vmem] * len(picked),
        out_specs=[vmem] * n_win,
        out_shape=[jax.ShapeDtypeStruct((rows, lanes), jnp.bfloat16)] * n_win,
        compiler_params=pltpu.CompilerParams(vmem_limit_bytes=4 * 2**20),
        cost_estimate=pl.CostEstimate(flops=2**18, bytes_accessed=2**19, transcendentals=0),
        name="merge",
    )(*picked)


def lefts_kernel(n_win, w_dev, n_own, *refs):
    out_ref, srow_ref, rows_ref = refs[-3:]
    rows, lanes = refs[0].shape
    bins = lanes // 2
    windows = n_win * w_dev
    pad = rows_ref.shape[1]
    for j in range(n_win):
        block = refs[j][...].astype(jnp.float32)
        for h in range(lanes // pad):
            srow_ref[h, j * rows:(j + 1) * rows, :] = block[:, h * pad:(h + 1) * pad]

    lane = lax.broadcasted_iota(jnp.int32, (bins, lanes), 1)
    row = lax.broadcasted_iota(jnp.int32, (bins, lanes), 0)
    quarter = lanes // 8
    bin_of = 4 * (lane % quarter) + lane // (2 * quarter)
    pick = bin_of == 2 * (row % (bins // 2)) + row // (bins // 2)
    pick = pick.astype(jnp.float32).astype(jnp.bfloat16)
    real = (lane[:w_dev] // quarter) % 2 == 0
    low = lax.broadcasted_iota(jnp.int32, (bins // 2, pad), 1) < pad // 2
    for s in range(n_own):
        values = jnp.concatenate(
            [srow_ref[h, pl.ds(s, windows, stride=n_own), :] for h in range(lanes // pad)], axis=1
        )
        stacked = []
        for j in range(n_win):
            own = values[j * w_dev:(j + 1) * w_dev]
            stacked += [jnp.where(real, own, 0.0), jnp.where(real, 0.0, own)]
        stacked = jnp.concatenate(stacked * 2, axis=0).astype(jnp.bfloat16)
        turned = lax.dot_general(
            pick, stacked, (((1,), (1,)), ((), ())), preferred_element_type=jnp.float32
        )
        pairs = jnp.where(low, turned[:bins // 2], turned[bins // 2:])
        rows_ref[pl.ds(s, bins // 2, stride=n_own), :] = pairs
    out_ref[...] = rows_ref[...].reshape(out_ref.shape).astype(jnp.bfloat16)


def lefts_call(blocks, after, later, w_dev):
    rows, lanes = blocks[0].shape
    n_win = len(blocks)
    n_own = rows // w_dev
    pad = 128
    first = n_win + len(after)
    vmem, anywhere = pl.BlockSpec(memory_space=VMEM), pl.BlockSpec(memory_space=pl.ANY)
    out = pl.pallas_call(
        functools.partial(lefts_kernel, n_win, w_dev, n_own),
        in_specs=[vmem] * n_win + [anywhere] * (len(after) + len(later)),
        out_specs=[anywhere] * len(later) + [vmem],
        out_shape=[jax.ShapeDtypeStruct(x.shape, x.dtype) for x in later]
        + [jax.ShapeDtypeStruct((lanes // 8, 2 * n_own, pad), jnp.bfloat16)],
        input_output_aliases={first + k: k for k in range(len(later))},
        scratch_shapes=[
            pltpu.VMEM((lanes // pad, n_win * rows, pad), jnp.float32),
            pltpu.VMEM((lanes // 4 * n_own, pad), jnp.float32),
        ],
        compiler_params=pltpu.CompilerParams(vmem_limit_bytes=6 * 2**20),
        cost_estimate=pl.CostEstimate(flops=2**26, bytes_accessed=2**19, transcendentals=0),
        name="lefts",
    )(*blocks, *after, *later)
    return out[-1], out[:-1]


def stacks_kernel(shares, n_win, w_dev, r_dev, n_own, bins, plan_hbm, *refs):
    t_refs = refs[:n_win]
    s_refs = refs[n_win:n_win + len(shares)]
    out_hbm, prod_ref, out_ref, plan_ref, sems, plan_sem = refs[-6:]
    plan_copy = pltpu.make_async_copy(plan_hbm, plan_ref, plan_sem)
    plan_copy.start()
    windows = n_win * w_dev
    count = len(shares) * n_own
    pitch = prod_ref.shape[1] // bins
    pad = 128
    rcv = lax.axis_index("rcv")

    low = lax.broadcasted_iota(jnp.int32, (count, pad), 1) < pad // 2
    for group in range(bins // 4):
        values = [s_ref[group].astype(jnp.float32) for s_ref in s_refs]
        for p in range(2):
            rows = jnp.concatenate([v[p * n_own:(p + 1) * n_own] for v in values], axis=0)
            left = jnp.concatenate([jnp.where(low, rows, 0.0), jnp.where(low, 0.0, rows)], axis=0)
            first = 4 * group + 2 * p
            right = [t_ref[f] for f in (first, first + 1) for t_ref in t_refs]
            result = jnp.dot(
                left.astype(jnp.bfloat16), jnp.concatenate(right, axis=0),
                preferred_element_type=jnp.float32,
            )
            for k in range(2):
                for c in range(2):
                    block = result[k * count:(k + 1) * count, c * pad:(c + 1) * pad]
                    prod_ref[c, pl.ds((first + k) * pitch, count), :] = block

    scale = 1.0 / math.sqrt(windows)
    plan_copy.wait()
    copies = []
    for s in range(count):
        for c in range(2):
            turned = prod_ref[c, pl.ds(s, bins, stride=pitch), :].T
            out_ref[s, pl.ds(c, r_dev, stride=2), :] = turned[:r_dev] * scale
        row = plan_ref[0, (rcv ^ shares[s // n_own]) * n_own + s % n_own]
        copies.append(pltpu.make_async_copy(out_ref.at[s], out_hbm.at[row], sems.at[s]))
        copies[-1].start()
    for copy in copies:
        copy.wait()


def stacks_call(out, plan, turned, sources, shares, n_rcv, w_dev, r_dev, bins):
    n_win = len(turned)
    n_own = sources[0].shape[1] // 2
    windows = n_win * w_dev
    count = len(shares) * n_own
    whole = pl.BlockSpec(memory_space=VMEM)
    args = [plan] + list(turned) + [sources[i] for i in shares]
    specs = [pl.BlockSpec(memory_space=pl.ANY)] + [whole] * (len(args) - 1)
    aliases = {}
    if out is not None:
        aliases = {len(args): 0}
        args.append(out)
        specs.append(pl.BlockSpec(memory_space=pl.ANY))
    return pl.pallas_call(
        functools.partial(stacks_kernel, shares, n_win, w_dev, r_dev, n_own, bins),
        in_specs=specs,
        out_specs=pl.BlockSpec(memory_space=pltpu.HBM),
        out_shape=jax.ShapeDtypeStruct((n_rcv * n_own, 2 * r_dev, bins), jnp.float32),
        input_output_aliases=aliases,
        scratch_shapes=[
            pltpu.VMEM((2, (count + 8) * bins, 128), jnp.float32),
            pltpu.VMEM((count, 2 * r_dev, bins), jnp.float32),
            pltpu.SMEM(plan.shape, jnp.int32),
            pltpu.SemaphoreType.DMA((count,)),
            pltpu.SemaphoreType.DMA,
        ],
        compiler_params=pltpu.CompilerParams(vmem_limit_bytes=20 * 2**20),
        cost_estimate=pl.CostEstimate(
            flops=8 * windows * count * r_dev * bins, bytes_accessed=6 * 2**20, transcendentals=0
        ),
        name="stacks",
    )(*args)


def swap(value, axis, by):
    size = lax.axis_size(axis)
    return lax.ppermute(value, axis, [(i, i ^ by) for i in range(size)])


def near_and_far(n_rcv, by):
    pairs = [(z, z ^ by) for z in range(n_rcv)]
    return [p for p in pairs if abs(p[0] - p[1]) == 1], [p for p in pairs if abs(p[0] - p[1]) > 1]


def merge_near(picked, near):
    return merge_call(picked[0], *near)


def merge_all(picked, near):
    far = []
    for i in range(1, len(picked)):
        pairs = near_and_far(len(picked), i)[1]
        if pairs:
            far.append(lax.ppermute(picked[i], "rcv", pairs))
    return merge_call(picked[0], *near, *far)


def body(traces, valid, src_station):
    w_dev, r_dev, samples = traces.shape
    n_src = src_station.shape[0]
    n_win = lax.axis_size("win")
    n_rcv = lax.axis_size("rcv")
    bins = F // n_win
    early = n_win // 2

    blocks, picked, plan, flag = spectra_call(traces, valid, src_station, n_win, n_rcv)

    near = {}
    for i in range(1, n_rcv):
        pairs = near_and_far(n_rcv, i)[0]
        if pairs:
            near[i] = lax.ppermute(picked[i], "rcv", pairs)
    picked = [picked[0] + near.pop(n_rcv - 1)] + list(picked[1:])
    near = list(near.values())
    merged = lax.cond(flag.reshape(()) > 0, merge_all, merge_near, picked, near)

    merged = [merged[0]] + [swap(merged[j], "win", j) for j in range(1, n_win)]
    late = [j for j in range(1, n_win) if j != early]
    received = {0: blocks[0], early: swap(blocks[early], "win", early)}
    lefts, later = lefts_call(merged, [received[early]], [blocks[j] for j in late], w_dev)
    received.update({j: swap(block, "win", j) for j, block in zip(late, later)})
    sources = [lefts] + [swap(lefts, "rcv", i) for i in range(1, n_rcv)]

    turned = [turn_call([received[j]], w_dev, r_dev) for j in range(n_win)]
    half = n_rcv // 2
    sizes = (n_rcv, w_dev, r_dev, bins)
    stacks = stacks_call(None, plan, turned, sources, tuple(range(half)), *sizes)
    stacks = stacks_call(stacks, plan, turned, sources, tuple(range(half, n_rcv)), *sizes)
    return stacks.reshape(n_src, r_dev, 2, bins)


def correlate(received, sources):
    rr = received[:, :, 0]
    ri = received[:, :, 1]
    sr = sources[:, :, 0]
    si = sources[:, :, 1]
    real = jnp.einsum("wsf,wrf->srf", sr, rr, preferred_element_type=jnp.float32)
    real = real + jnp.einsum("wsf,wrf->srf", si, ri, preferred_element_type=jnp.float32)
    imag = jnp.einsum("wsf,wrf->srf", sr, ri, preferred_element_type=jnp.float32)
    imag = imag - jnp.einsum("wsf,wrf->srf", si, rr, preferred_element_type=jnp.float32)
    return jnp.stack([real, imag], axis=2)


def body_any(traces, valid, src_station):
    w_dev, r_dev, samples = traces.shape
    n_win = lax.axis_size("win")
    n_rcv = lax.axis_size("rcv")
    bins = F // n_win
    table = jnp.asarray(band_table(samples, F, samples // 16))
    spectra = jnp.dot(
        traces.reshape(w_dev * r_dev, samples), table, preferred_element_type=jnp.float32
    )
    spectra = spectra.reshape(w_dev, r_dev, 2, F)
    power = jnp.sum(spectra * spectra, axis=(2, 3), keepdims=True) / F
    keep = valid.astype(jnp.float32)[:, None, None, None]
    white = (spectra * lax.rsqrt(power + 1e-06) * keep).astype(jnp.bfloat16)
    blocks = white.reshape(w_dev, r_dev, 2, n_win, bins).transpose(3, 0, 1, 2, 4)
    me = lax.axis_index("win")
    offset = lax.axis_index("rcv") * r_dev
    station_ids = offset + jnp.arange(r_dev, dtype=jnp.int32)
    selector = (src_station[:, None] == station_ids[None, :]).astype(jnp.bfloat16)
    received = []
    for j in range(n_win):
        block = lax.dynamic_index_in_dim(blocks, me ^ j, 0, keepdims=False)
        received.append(swap(block, "win", j) if j else block)
    received = jnp.concatenate(received, axis=0)
    rows = jnp.einsum("sr,wrcf->wscf", selector, received, preferred_element_type=jnp.float32)
    rows = lax.all_to_all(rows.astype(jnp.bfloat16), "rcv", 0, 0, tiled=True)
    rows = rows.reshape((n_rcv, -1) + rows.shape[1:])
    merged = jnp.sum(rows.astype(jnp.float32), axis=0).astype(jnp.bfloat16)
    sources = lax.all_gather(merged, "rcv", axis=0, tiled=True)
    return correlate(received, sources) * (1.0 / math.sqrt(w_dev * n_win))


def solution(mesh):
    sizes = (mesh.shape["win"], mesh.shape["rcv"])
    return jax.shard_map(
        body if sizes == (4, 4) else body_any,
        mesh=mesh,
        in_specs=(P("win", ("groups", "rcv"), None), P(("groups", "win")), P("groups")),
        out_specs=P(None, ("groups", "rcv"), None, "win"),
        check_vma=False,
    )
```

```python
import functools
import math

import jax
import jax.numpy as jnp
import numpy as np
from jax import lax
from jax.experimental import pallas as pl
from jax.experimental.pallas import tpu as pltpu
from jax.sharding import PartitionSpec as P

F = 512
SMEM = pltpu.MemorySpace.SMEM
VMEM = pltpu.MemorySpace.VMEM


def angles(samples, freqs, count):
    phase = samples[:, None] * freqs[None, :] % count
    return phase.astype(np.float64) * (2.0 * math.pi / count)


def band_table(count, bins, first):
    angle = angles(np.arange(count), first + np.arange(bins), count)
    return np.concatenate([np.cos(angle), -np.sin(angle)], axis=1).astype(jnp.bfloat16)


BLOCK = 32


def table_seeds(count, bins, first, n_win):
    j = np.arange(bins // 4)
    turn = np.array([0.0, 0.5 * math.pi]).reshape(1, 2, 1)
    seeds, twice = [], []
    for m in range(4):
        freqs = np.broadcast_to((first + 4 * j + m).reshape(n_win, 1, -1), (n_win, 2, j.size // n_win))
        angle = angles(np.arange(2 * BLOCK), freqs.reshape(-1), count)
        angle = angle + np.broadcast_to(turn, freqs.shape).reshape(1, -1)
        seeds.append(np.cos(angle).reshape(2, BLOCK, -1))
        step = angles(np.full(8, BLOCK), freqs.reshape(-1), count)
        twice.append(2.0 * np.cos(step))
    return np.stack(seeds).astype(np.float32), np.stack(twice).astype(np.float32)


def make_tables(seed_ref, twice_ref, table_ref):
    for first in (0, 2):
        state = {}
        for m in (first, first + 1):
            twice = jnp.concatenate([twice_ref[m]] * (BLOCK // 8), axis=0)
            state[m] = (seed_ref[m, 0], seed_ref[m, 1], twice)
        for a in range(table_ref.shape[1] // BLOCK):
            for m, (here, after, twice) in state.items():
                table_ref[m, a * BLOCK:(a + 1) * BLOCK, :] = here.astype(jnp.bfloat16)
                state[m] = (after, twice * after - here, twice)


def in_hbm(value):
    return pltpu.with_memory_space_constraint(value, pltpu.HBM)


def order_sources(src_ref, r_dev, n_own, order_ref, plan_ref, flag_ref):
    n_src = src_ref.shape[0]
    size = order_ref.shape
    down = lax.broadcasted_iota(jnp.int32, size, 0).astype(jnp.float32)
    along = lax.broadcasted_iota(jnp.int32, size, 1).astype(jnp.float32)
    none = jnp.full(size, float(2**20), jnp.float32)
    column, row = none, none
    for s in range(n_src):
        station = src_ref[s].astype(jnp.float32)
        column = jnp.where(down == s, station, column)
        row = jnp.where(along == s, station, row)
    rank_along = jnp.sum((column < row).astype(jnp.float32), axis=0, keepdims=True)
    rank_down = jnp.sum((row < column).astype(jnp.float32), axis=1, keepdims=True)
    sorted_down = jnp.sum(jnp.where(rank_along == down, row, 0.0), axis=1, keepdims=True)
    at_place = rank_down == along
    sorted_along = jnp.sum(jnp.where(at_place, column, 0.0), axis=0, keepdims=True)
    source_along = jnp.sum(jnp.where(at_place, down, 0.0), axis=0, keepdims=True)
    order_ref[...] = jnp.broadcast_to(sorted_down, size)
    place = along[:1]
    owner, share = jnp.zeros_like(place), jnp.zeros_like(place)
    for z in range(1, n_src // n_own):
        owner = owner + (sorted_along >= z * r_dev).astype(jnp.float32)
        share = share + (place >= z * n_own).astype(jnp.float32)
    far = jnp.where((place < n_src) & (jnp.abs(owner - share) > 1.5), 1.0, 0.0)
    plan_ref[...] = jnp.broadcast_to(source_along, plan_ref.shape).astype(jnp.int32)
    flag_ref[0] = jnp.max(far).astype(jnp.int32)


def spectra_kernel(
    n_win, n_rcv, r_dev, valid_hbm, src_hbm, x_hbm, seed_hbm, twice_hbm, *refs
):
    r_refs = refs[:n_win]
    q_refs = refs[n_win:n_win + n_rcv]
    (plan_ref, flag_ref, x_ref, even_ref, odd_ref, white_ref, sel_ref, order_ref, table_ref,
     seed_ref, twice_ref, valid_ref, src_ref, sems, x_sems) = refs[n_win + n_rcv:]
    chunks, rows, samples = x_ref.shape
    w_step = rows // r_dev
    n_own = src_ref.shape[0] // n_rcv
    quarter = samples // 4
    win = lax.axis_index("win")
    rcv = lax.axis_index("rcv")

    def small(k):
        source = (seed_hbm, twice_hbm, src_hbm, valid_hbm)[k]
        target = (seed_ref, twice_ref, src_ref, valid_ref)[k]
        return pltpu.make_async_copy(source, target, sems.at[k])

    def chunk(k):
        return pltpu.make_async_copy(x_hbm.at[pl.ds(k * rows, rows)], x_ref.at[k], x_sems.at[k])

    for k in range(4):
        small(k).start()
    for k in range(chunks):
        chunk(k).start()
    small(0).wait()
    small(1).wait()
    make_tables(seed_ref, twice_ref, table_ref)
    small(2).wait()
    order_sources(src_ref, r_dev, n_own, order_ref, plan_ref, flag_ref)
    stations = []
    for d in range(n_rcv):
        share = pl.multiple_of((rcv ^ d) * n_own, n_own)
        stations += [order_ref[pl.ds(share, n_own), 0:1]] * w_step
    wanted = jnp.concatenate(stations, axis=0).astype(jnp.int32) - rcv * r_dev
    shape = (n_rcv * w_step * n_own, rows)
    out_row = lax.broadcasted_iota(jnp.int32, shape, 0)
    column = lax.broadcasted_iota(jnp.int32, shape, 1)
    inside = (wanted >= 0) & (wanted < r_dev)
    hit = inside & (column == wanted + (out_row // n_own) % w_step * r_dev)
    sel_ref[...] = hit.astype(jnp.float32).astype(jnp.bfloat16)
    small(3).wait()

    def product(lhs, table):
        return jnp.dot(lhs, table, preferred_element_type=jnp.float32)

    def add_quarters(k, first, last):
        part = slice(first, last)
        b0, b1, b2, b3 = (x_ref[k, part, q * quarter:(q + 1) * quarter] for q in range(4))
        x0, x1, x2, x3 = (b.astype(jnp.float32) for b in (b0, b1, b2, b3))
        even_ref[k, 0, part] = ((x0 + x2) + (x1 + x3)).astype(jnp.bfloat16)
        even_ref[k, 1, part] = ((x0 + x2) - (x1 + x3)).astype(jnp.bfloat16)
        odd_ref[k, part] = b0 - b2
        odd_ref[k, rows + first:rows + last] = b1 - b3

    lanes = table_ref.shape[2]
    lane = lax.broadcasted_iota(jnp.int32, (rows, lanes), 1)
    piece = lanes // n_win
    real = lane % piece < piece // 2

    def odd_spectra(k, m):
        both = product(odd_ref[k], table_ref[m])
        second = both[rows:]
        back, forth = pltpu.roll(second, lanes - piece // 2, 1), pltpu.roll(second, piece // 2, 1)
        turned = jnp.where(real, back, -forth)
        return both[:rows] + turned if m == 1 else both[:rows] - turned

    parts = 4
    size = rows // parts
    chunk(0).wait()
    add_quarters(0, 0, rows)
    row = lax.broadcasted_iota(jnp.int32, (rows, 1), 0)
    for k in range(chunks):
        more = k + 1 < chunks
        if more:
            chunk(k + 1).wait()
        spectra = []
        for m in range(4):
            if m % 2:
                spectra.append(odd_spectra(k, m))
            else:
                spectra.append(product(even_ref[k, m // 2], table_ref[m]))
            if more:
                add_quarters(k + 1, m * size, (m + 1) * size)
        squares = sum(jnp.sum(s * s, axis=1, keepdims=True) for s in spectra)
        gain = lax.rsqrt(squares / F + 1e-06)
        keep = jnp.zeros((rows, 1), jnp.float32)
        for t in range(w_step):
            own = (row >= t * r_dev) & (row < (t + 1) * r_dev)
            keep = jnp.where(own, valid_ref[k * w_step + t].astype(jnp.float32), keep)
        gain = gain * keep
        white = [s * gain for s in spectra]
        for d in range(n_win):
            columns = slice(d * piece, (d + 1) * piece)
            block = jnp.concatenate([part[:, columns] for part in white], axis=1)
            white_ref[k, d] = block.astype(jnp.bfloat16)
        count = w_step * n_own
        for j in range(n_win):
            block = white_ref[k, win ^ j]
            r_refs[j][k * rows:(k + 1) * rows, :] = block
            picked = product(sel_ref[...], block).astype(jnp.bfloat16)
            for d in range(n_rcv):
                q_refs[d][j, k * count:(k + 1) * count, :] = picked[d * count:(d + 1) * count]


def spectra_call(traces, valid, src_station, n_win, n_rcv):
    w_dev, r_dev, samples = traces.shape
    n_src = src_station.shape[0]
    n_own = n_src // n_rcv
    chunks = 2
    every = w_dev * r_dev
    rows = every // chunks
    lanes = 2 * F // n_win
    seed, twice = (jnp.asarray(t) for t in table_seeds(samples, F, samples // 16, n_win))
    shapes = [jax.ShapeDtypeStruct((every, lanes), jnp.bfloat16)] * n_win
    shapes += [jax.ShapeDtypeStruct((n_win, w_dev * n_own, lanes), jnp.bfloat16)] * n_rcv
    shapes += [jax.ShapeDtypeStruct((8, 128), jnp.int32), jax.ShapeDtypeStruct((1,), jnp.int32)]
    vmem = pl.BlockSpec(memory_space=VMEM)
    out = pl.pallas_call(
        functools.partial(spectra_kernel, n_win, n_rcv, r_dev),
        in_specs=[pl.BlockSpec(memory_space=pltpu.HBM)] * 5,
        out_specs=[vmem] * (len(shapes) - 1) + [pl.BlockSpec(memory_space=SMEM)],
        out_shape=shapes,
        scratch_shapes=[
            pltpu.VMEM((chunks, rows, samples), jnp.bfloat16),
            pltpu.VMEM((chunks, 2, rows, samples // 4), jnp.bfloat16),
            pltpu.VMEM((chunks, 2 * rows, samples // 4), jnp.bfloat16),
            pltpu.VMEM((chunks, n_win, rows, lanes), jnp.bfloat16),
            pltpu.VMEM((n_src * (w_dev // chunks), rows), jnp.bfloat16),
            pltpu.VMEM((n_src, 128), jnp.float32),
            pltpu.VMEM((4, samples // 4, F // 2), jnp.bfloat16),
            pltpu.VMEM(seed.shape, jnp.float32),
            pltpu.VMEM(twice.shape, jnp.float32),
            pltpu.SMEM(valid.shape, jnp.int32),
            pltpu.SMEM(src_station.shape, jnp.int32),
            pltpu.SemaphoreType.DMA((4,)),
            pltpu.SemaphoreType.DMA((chunks,)),
        ],
        compiler_params=pltpu.CompilerParams(vmem_limit_bytes=36 * 2**20),
        cost_estimate=pl.CostEstimate(
            flops=2 * every * (samples // 4) * 6 * (F // 2), bytes_accessed=every * samples * 2,
            transcendentals=0,
        ),
        name="spectra",
    )(*(in_hbm(x) for x in (valid, src_station, traces.reshape(every, samples), seed, twice)))
    return out[:n_win], out[n_win:n_win + n_rcv], out[-2], out[-1]


def bin_order(lanes):
    quarter = lanes // 8
    lane = lax.broadcasted_iota(jnp.int32, (lanes, lanes), 1)
    row = lax.broadcasted_iota(jnp.int32, (lanes, lanes), 0)
    part = (lane // quarter) % 2
    bin_of = 4 * (lane % quarter) + lane // (2 * quarter)
    hit = row == part * (lanes // 2) + bin_of
    return hit.astype(jnp.float32).astype(jnp.bfloat16)


def turn_kernel(r_dev, *refs):
    x_refs, (out_ref, rows_ref) = refs[:-2], refs[-2:]
    lanes = x_refs[0].shape[1]
    bins = lanes // 2
    w_dev = out_ref.shape[1] // 2
    pad = out_ref.shape[2] // 2
    order = bin_order(lanes)
    windows = [(x, w) for x in x_refs for w in range(x.shape[0] // r_dev)]
    for k, (x_ref, w) in enumerate(windows):
        turned = lax.dot_general(
            order, x_ref[w * r_dev:(w + 1) * r_dev], (((1,), (1,)), ((), ())),
            preferred_element_type=jnp.float32,
        )
        rows_ref[pl.ds(k, lanes, stride=w_dev), :r_dev] = turned
    rr = rows_ref[:bins * w_dev].reshape(bins, w_dev, pad)
    ri = rows_ref[bins * w_dev:].reshape(bins, w_dev, pad)
    out_ref[:, :, :pad] = jnp.concatenate([rr, ri], axis=1).astype(jnp.bfloat16)
    out_ref[:, :, pad:] = jnp.concatenate([ri, -rr], axis=1).astype(jnp.bfloat16)


def turn_call(parts, w_dev, r_dev):
    lanes = parts[0].shape[1]
    pad = 128
    vmem = pl.BlockSpec(memory_space=VMEM)
    return pl.pallas_call(
        functools.partial(turn_kernel, r_dev),
        in_specs=[vmem] * len(parts),
        out_specs=vmem,
        out_shape=jax.ShapeDtypeStruct((lanes // 2, 2 * w_dev, 2 * pad), jnp.bfloat16),
        scratch_shapes=[pltpu.VMEM((lanes * w_dev, pad), jnp.float32)],
        compiler_params=pltpu.CompilerParams(vmem_limit_bytes=16 * 2**20),
        cost_estimate=pl.CostEstimate(
            flops=2 * w_dev * lanes * lanes * pad, bytes_accessed=2 * 2**20, transcendentals=0
        ),
        name="turn",
    )(*parts)


def merge_kernel(n_win, *refs):
    picked, outs = refs[:-n_win], refs[-n_win:]
    for j, out_ref in enumerate(outs):
        total = picked[0][j].astype(jnp.float32)
        for q_ref in picked[1:]:
            total = total + q_ref[j].astype(jnp.float32)
        out_ref[...] = total.astype(jnp.bfloat16)


def merge_call(*picked):
    n_win, rows, lanes = picked[0].shape
    vmem = pl.BlockSpec(memory_space=VMEM)
    return pl.pallas_call(
        functools.partial(merge_kernel, n_win),
        in_specs=[vmem] * len(picked),
        out_specs=[vmem] * n_win,
        out_shape=[jax.ShapeDtypeStruct((rows, lanes), jnp.bfloat16)] * n_win,
        compiler_params=pltpu.CompilerParams(vmem_limit_bytes=4 * 2**20),
        cost_estimate=pl.CostEstimate(flops=2**18, bytes_accessed=2**19, transcendentals=0),
        name="merge",
    )(*picked)


def lefts_kernel(n_win, w_dev, n_own, *refs):
    out_ref, srow_ref, rows_ref = refs[-3:]
    rows, lanes = refs[0].shape
    bins = lanes // 2
    windows = n_win * w_dev
    pad = rows_ref.shape[1]
    for j in range(n_win):
        block = refs[j][...].astype(jnp.float32)
        for h in range(lanes // pad):
            srow_ref[h, j * rows:(j + 1) * rows, :] = block[:, h * pad:(h + 1) * pad]

    lane = lax.broadcasted_iota(jnp.int32, (bins, lanes), 1)
    row = lax.broadcasted_iota(jnp.int32, (bins, lanes), 0)
    quarter = lanes // 8
    bin_of = 4 * (lane % quarter) + lane // (2 * quarter)
    pick = bin_of == 2 * (row % (bins // 2)) + row // (bins // 2)
    pick = pick.astype(jnp.float32).astype(jnp.bfloat16)
    real = (lane[:w_dev] // quarter) % 2 == 0
    low = lax.broadcasted_iota(jnp.int32, (bins // 2, pad), 1) < pad // 2
    for s in range(n_own):
        values = jnp.concatenate(
            [srow_ref[h, pl.ds(s, windows, stride=n_own), :] for h in range(lanes // pad)], axis=1
        )
        stacked = []
        for j in range(n_win):
            own = values[j * w_dev:(j + 1) * w_dev]
            stacked += [jnp.where(real, own, 0.0), jnp.where(real, 0.0, own)]
        stacked = jnp.concatenate(stacked * 2, axis=0).astype(jnp.bfloat16)
        turned = lax.dot_general(
            pick, stacked, (((1,), (1,)), ((), ())), preferred_element_type=jnp.float32
        )
        pairs = jnp.where(low, turned[:bins // 2], turned[bins // 2:])
        rows_ref[pl.ds(s, bins // 2, stride=n_own), :] = pairs
    out_ref[...] = rows_ref[...].reshape(out_ref.shape).astype(jnp.bfloat16)


def lefts_call(blocks, after, later, w_dev):
    rows, lanes = blocks[0].shape
    n_win = len(blocks)
    n_own = rows // w_dev
    pad = 128
    first = n_win + len(after)
    vmem, anywhere = pl.BlockSpec(memory_space=VMEM), pl.BlockSpec(memory_space=pl.ANY)
    out = pl.pallas_call(
        functools.partial(lefts_kernel, n_win, w_dev, n_own),
        in_specs=[vmem] * n_win + [anywhere] * (len(after) + len(later)),
        out_specs=[anywhere] * len(later) + [vmem],
        out_shape=[jax.ShapeDtypeStruct(x.shape, x.dtype) for x in later]
        + [jax.ShapeDtypeStruct((lanes // 8, 2 * n_own, pad), jnp.bfloat16)],
        input_output_aliases={first + k: k for k in range(len(later))},
        scratch_shapes=[
            pltpu.VMEM((lanes // pad, n_win * rows, pad), jnp.float32),
            pltpu.VMEM((lanes // 4 * n_own, pad), jnp.float32),
        ],
        compiler_params=pltpu.CompilerParams(vmem_limit_bytes=6 * 2**20),
        cost_estimate=pl.CostEstimate(flops=2**26, bytes_accessed=2**19, transcendentals=0),
        name="lefts",
    )(*blocks, *after, *later)
    return out[-1], out[:-1]


def stacks_kernel(shares, n_win, w_dev, r_dev, n_own, bins, plan_hbm, *refs):
    t_refs = refs[:n_win]
    s_refs = refs[n_win:n_win + len(shares)]
    out_hbm, prod_ref, out_ref, plan_ref, sems, plan_sem = refs[-6:]
    plan_copy = pltpu.make_async_copy(plan_hbm, plan_ref, plan_sem)
    plan_copy.start()
    windows = n_win * w_dev
    count = len(shares) * n_own
    pitch = prod_ref.shape[1] // bins
    pad = 128
    rcv = lax.axis_index("rcv")

    low = lax.broadcasted_iota(jnp.int32, (count, pad), 1) < pad // 2
    for group in range(bins // 4):
        values = [s_ref[group].astype(jnp.float32) for s_ref in s_refs]
        for p in range(2):
            rows = jnp.concatenate([v[p * n_own:(p + 1) * n_own] for v in values], axis=0)
            left = jnp.concatenate([jnp.where(low, rows, 0.0), jnp.where(low, 0.0, rows)], axis=0)
            first = 4 * group + 2 * p
            right = [t_ref[f] for f in (first, first + 1) for t_ref in t_refs]
            result = jnp.dot(
                left.astype(jnp.bfloat16), jnp.concatenate(right, axis=0),
                preferred_element_type=jnp.float32,
            )
            for k in range(2):
                for c in range(2):
                    block = result[k * count:(k + 1) * count, c * pad:(c + 1) * pad]
                    prod_ref[c, pl.ds((first + k) * pitch, count), :] = block

    scale = 1.0 / math.sqrt(windows)
    plan_copy.wait()
    copies = []
    for s in range(count):
        for c in range(2):
            turned = prod_ref[c, pl.ds(s, bins, stride=pitch), :].T
            out_ref[s, pl.ds(c, r_dev, stride=2), :] = turned[:r_dev] * scale
        row = plan_ref[0, (rcv ^ shares[s // n_own]) * n_own + s % n_own]
        copies.append(pltpu.make_async_copy(out_ref.at[s], out_hbm.at[row], sems.at[s]))
        copies[-1].start()
    for copy in copies:
        copy.wait()


def stacks_call(out, plan, turned, sources, shares, n_rcv, w_dev, r_dev, bins):
    n_win = len(turned)
    n_own = sources[0].shape[1] // 2
    windows = n_win * w_dev
    count = len(shares) * n_own
    whole = pl.BlockSpec(memory_space=VMEM)
    args = [plan] + list(turned) + [sources[i] for i in shares]
    specs = [pl.BlockSpec(memory_space=pl.ANY)] + [whole] * (len(args) - 1)
    aliases = {}
    if out is not None:
        aliases = {len(args): 0}
        args.append(out)
        specs.append(pl.BlockSpec(memory_space=pl.ANY))
    return pl.pallas_call(
        functools.partial(stacks_kernel, shares, n_win, w_dev, r_dev, n_own, bins),
        in_specs=specs,
        out_specs=pl.BlockSpec(memory_space=pltpu.HBM),
        out_shape=jax.ShapeDtypeStruct((n_rcv * n_own, 2 * r_dev, bins), jnp.float32),
        input_output_aliases=aliases,
        scratch_shapes=[
            pltpu.VMEM((2, (count + 8) * bins, 128), jnp.float32),
            pltpu.VMEM((count, 2 * r_dev, bins), jnp.float32),
            pltpu.SMEM(plan.shape, jnp.int32),
            pltpu.SemaphoreType.DMA((count,)),
            pltpu.SemaphoreType.DMA,
        ],
        compiler_params=pltpu.CompilerParams(vmem_limit_bytes=20 * 2**20),
        cost_estimate=pl.CostEstimate(
            flops=8 * windows * count * r_dev * bins, bytes_accessed=6 * 2**20, transcendentals=0
        ),
        name="stacks",
    )(*args)


def swap(value, axis, by):
    size = lax.axis_size(axis)
    return lax.ppermute(value, axis, [(i, i ^ by) for i in range(size)])


def near_and_far(n_rcv, by):
    pairs = [(z, z ^ by) for z in range(n_rcv)]
    return [p for p in pairs if abs(p[0] - p[1]) == 1], [p for p in pairs if abs(p[0] - p[1]) > 1]


def merge_near(picked, near):
    return merge_call(picked[0], *near)


def merge_all(picked, near):
    far = []
    for i in range(1, len(picked)):
        pairs = near_and_far(len(picked), i)[1]
        if pairs:
            far.append(lax.ppermute(picked[i], "rcv", pairs))
    return merge_call(picked[0], *near, *far)


def body(traces, valid, src_station):
    w_dev, r_dev, samples = traces.shape
    n_src = src_station.shape[0]
    n_win = lax.axis_size("win")
    n_rcv = lax.axis_size("rcv")
    bins = F // n_win
    early = n_win // 2

    blocks, picked, plan, flag = spectra_call(traces, valid, src_station, n_win, n_rcv)

    near = {}
    for i in range(1, n_rcv):
        pairs = near_and_far(n_rcv, i)[0]
        if pairs:
            near[i] = lax.ppermute(picked[i], "rcv", pairs)
    picked = [picked[0] + near.pop(n_rcv - 1)] + list(picked[1:])
    near = list(near.values())
    merged = lax.cond(flag.reshape(()) > 0, merge_all, merge_near, picked, near)

    merged = [merged[0]] + [swap(merged[j], "win", j) for j in range(1, n_win)]
    late = [j for j in range(1, n_win) if j != early]
    received = {0: blocks[0], early: swap(blocks[early], "win", early)}
    lefts, later = lefts_call(merged, [received[early]], [blocks[j] for j in late], w_dev)
    received.update({j: swap(block, "win", j) for j, block in zip(late, later)})
    sources = [lefts, swap(lefts, "rcv", 1), swap(lefts, "rcv", 2)]
    sources.append(swap(sources[2], "rcv", 1))


    turned = [turn_call([received[j]], w_dev, r_dev) for j in range(n_win)]
    half = n_rcv // 2
    sizes = (n_rcv, w_dev, r_dev, bins)
    stacks = stacks_call(None, plan, turned, sources, tuple(range(half)), *sizes)
    stacks = stacks_call(stacks, plan, turned, sources, tuple(range(half, n_rcv)), *sizes)
    return stacks.reshape(n_src, r_dev, 2, bins)


def correlate(received, sources):
    rr = received[:, :, 0]
    ri = received[:, :, 1]
    sr = sources[:, :, 0]
    si = sources[:, :, 1]
    real = jnp.einsum("wsf,wrf->srf", sr, rr, preferred_element_type=jnp.float32)
    real = real + jnp.einsum("wsf,wrf->srf", si, ri, preferred_element_type=jnp.float32)
    imag = jnp.einsum("wsf,wrf->srf", sr, ri, preferred_element_type=jnp.float32)
    imag = imag - jnp.einsum("wsf,wrf->srf", si, rr, preferred_element_type=jnp.float32)
    return jnp.stack([real, imag], axis=2)


def body_any(traces, valid, src_station):
    w_dev, r_dev, samples = traces.shape
    n_win = lax.axis_size("win")
    n_rcv = lax.axis_size("rcv")
    bins = F // n_win
    table = jnp.asarray(band_table(samples, F, samples // 16))
    spectra = jnp.dot(
        traces.reshape(w_dev * r_dev, samples), table, preferred_element_type=jnp.float32
    )
    spectra = spectra.reshape(w_dev, r_dev, 2, F)
    power = jnp.sum(spectra * spectra, axis=(2, 3), keepdims=True) / F
    keep = valid.astype(jnp.float32)[:, None, None, None]
    white = (spectra * lax.rsqrt(power + 1e-06) * keep).astype(jnp.bfloat16)
    blocks = white.reshape(w_dev, r_dev, 2, n_win, bins).transpose(3, 0, 1, 2, 4)
    me = lax.axis_index("win")
    offset = lax.axis_index("rcv") * r_dev
    station_ids = offset + jnp.arange(r_dev, dtype=jnp.int32)
    selector = (src_station[:, None] == station_ids[None, :]).astype(jnp.bfloat16)
    received = []
    for j in range(n_win):
        block = lax.dynamic_index_in_dim(blocks, me ^ j, 0, keepdims=False)
        received.append(swap(block, "win", j) if j else block)
    received = jnp.concatenate(received, axis=0)
    rows = jnp.einsum("sr,wrcf->wscf", selector, received, preferred_element_type=jnp.float32)
    rows = lax.all_to_all(rows.astype(jnp.bfloat16), "rcv", 0, 0, tiled=True)
    rows = rows.reshape((n_rcv, -1) + rows.shape[1:])
    merged = jnp.sum(rows.astype(jnp.float32), axis=0).astype(jnp.bfloat16)
    sources = lax.all_gather(merged, "rcv", axis=0, tiled=True)
    return correlate(received, sources) * (1.0 / math.sqrt(w_dev * n_win))


def solution(mesh):
    sizes = (mesh.shape["win"], mesh.shape["rcv"])
    return jax.shard_map(
        body if sizes == (4, 4) else body_any,
        mesh=mesh,
        in_specs=(P("win", ("groups", "rcv"), None), P(("groups", "win")), P("groups")),
        out_specs=P(None, ("groups", "rcv"), None, "win"),
        check_vma=False,
    )
```

```python
import functools
import math

import jax
import jax.numpy as jnp
import numpy as np
from jax import lax
from jax.experimental import pallas as pl
from jax.experimental.pallas import tpu as pltpu
from jax.sharding import PartitionSpec as P

F = 512
SMEM = pltpu.MemorySpace.SMEM
VMEM = pltpu.MemorySpace.VMEM


def angles(samples, freqs, count):
    phase = samples[:, None] * freqs[None, :] % count
    return phase.astype(np.float64) * (2.0 * math.pi / count)


def band_table(count, bins, first):
    angle = angles(np.arange(count), first + np.arange(bins), count)
    return np.concatenate([np.cos(angle), -np.sin(angle)], axis=1).astype(jnp.bfloat16)


BLOCK = 32


def table_seeds(count, bins, first, n_win):
    j = np.arange(bins // 4)
    turn = np.array([0.0, 0.5 * math.pi]).reshape(1, 2, 1)
    seeds, twice = [], []
    for m in range(4):
        freqs = np.broadcast_to((first + 4 * j + m).reshape(n_win, 1, -1), (n_win, 2, j.size // n_win))
        angle = angles(np.arange(2 * BLOCK), freqs.reshape(-1), count)
        angle = angle + np.broadcast_to(turn, freqs.shape).reshape(1, -1)
        seeds.append(np.cos(angle).reshape(2, BLOCK, -1))
        step = angles(np.full(8, BLOCK), freqs.reshape(-1), count)
        twice.append(2.0 * np.cos(step))
    return np.stack(seeds).astype(np.float32), np.stack(twice).astype(np.float32)


def make_tables(seed_ref, twice_ref, table_ref):
    for first in (0, 2):
        state = {}
        for m in (first, first + 1):
            twice = jnp.concatenate([twice_ref[m]] * (BLOCK // 8), axis=0)
            state[m] = (seed_ref[m, 0], seed_ref[m, 1], twice)
        for a in range(table_ref.shape[1] // BLOCK):
            for m, (here, after, twice) in state.items():
                table_ref[m, a * BLOCK:(a + 1) * BLOCK, :] = here.astype(jnp.bfloat16)
                state[m] = (after, twice * after - here, twice)


def in_hbm(value):
    return pltpu.with_memory_space_constraint(value, pltpu.HBM)


def order_sources(src_ref, r_dev, n_own, order_ref, plan_ref, flag_ref):
    n_src = src_ref.shape[0]
    size = order_ref.shape
    down = lax.broadcasted_iota(jnp.int32, size, 0).astype(jnp.float32)
    along = lax.broadcasted_iota(jnp.int32, size, 1).astype(jnp.float32)
    none = jnp.full(size, float(2**20), jnp.float32)
    column, row = none, none
    for s in range(n_src):
        station = src_ref[s].astype(jnp.float32)
        column = jnp.where(down == s, station, column)
        row = jnp.where(along == s, station, row)
    rank_along = jnp.sum((column < row).astype(jnp.float32), axis=0, keepdims=True)
    rank_down = jnp.sum((row < column).astype(jnp.float32), axis=1, keepdims=True)
    sorted_down = jnp.sum(jnp.where(rank_along == down, row, 0.0), axis=1, keepdims=True)
    at_place = rank_down == along
    sorted_along = jnp.sum(jnp.where(at_place, column, 0.0), axis=0, keepdims=True)
    source_along = jnp.sum(jnp.where(at_place, down, 0.0), axis=0, keepdims=True)
    order_ref[...] = jnp.broadcast_to(sorted_down, size)
    place = along[:1]
    owner, share = jnp.zeros_like(place), jnp.zeros_like(place)
    for z in range(1, n_src // n_own):
        owner = owner + (sorted_along >= z * r_dev).astype(jnp.float32)
        share = share + (place >= z * n_own).astype(jnp.float32)
    far = jnp.where((place < n_src) & (jnp.abs(owner - share) > 1.5), 1.0, 0.0)
    plan_ref[...] = jnp.broadcast_to(source_along, plan_ref.shape).astype(jnp.int32)
    flag_ref[0] = jnp.max(far).astype(jnp.int32)


def spectra_kernel(
    n_win, n_rcv, r_dev, valid_hbm, src_hbm, x_hbm, seed_hbm, twice_hbm, *refs
):
    r_refs = refs[:n_win]
    q_refs = refs[n_win:n_win + n_rcv]
    (plan_ref, flag_ref, x_ref, even_ref, odd_ref, white_ref, sel_ref, order_ref, table_ref,
     seed_ref, twice_ref, valid_ref, src_ref, sems, x_sems) = refs[n_win + n_rcv:]
    chunks, rows, samples = x_ref.shape
    w_step = rows // r_dev
    n_own = src_ref.shape[0] // n_rcv
    quarter = samples // 4
    win = lax.axis_index("win")
    rcv = lax.axis_index("rcv")

    def small(k):
        source = (seed_hbm, twice_hbm, src_hbm, valid_hbm)[k]
        target = (seed_ref, twice_ref, src_ref, valid_ref)[k]
        return pltpu.make_async_copy(source, target, sems.at[k])

    def chunk(k):
        return pltpu.make_async_copy(x_hbm.at[pl.ds(k * rows, rows)], x_ref.at[k], x_sems.at[k])

    for k in range(4):
        small(k).start()
    for k in range(chunks):
        chunk(k).start()
    small(0).wait()
    small(1).wait()
    make_tables(seed_ref, twice_ref, table_ref)
    small(2).wait()
    order_sources(src_ref, r_dev, n_own, order_ref, plan_ref, flag_ref)
    stations = []
    for d in range(n_rcv):
        share = pl.multiple_of((rcv ^ d) * n_own, n_own)
        stations += [order_ref[pl.ds(share, n_own), 0:1]] * w_step
    wanted = jnp.concatenate(stations, axis=0).astype(jnp.int32) - rcv * r_dev
    shape = (n_rcv * w_step * n_own, rows)
    out_row = lax.broadcasted_iota(jnp.int32, shape, 0)
    column = lax.broadcasted_iota(jnp.int32, shape, 1)
    inside = (wanted >= 0) & (wanted < r_dev)
    hit = inside & (column == wanted + (out_row // n_own) % w_step * r_dev)
    sel_ref[...] = hit.astype(jnp.float32).astype(jnp.bfloat16)
    small(3).wait()

    def product(lhs, table):
        return jnp.dot(lhs, table, preferred_element_type=jnp.float32)

    def add_quarters(k, first, last):
        part = slice(first, last)
        b0, b1, b2, b3 = (x_ref[k, part, q * quarter:(q + 1) * quarter] for q in range(4))
        x0, x1, x2, x3 = (b.astype(jnp.float32) for b in (b0, b1, b2, b3))
        even_ref[k, 0, part] = ((x0 + x2) + (x1 + x3)).astype(jnp.bfloat16)
        even_ref[k, 1, part] = ((x0 + x2) - (x1 + x3)).astype(jnp.bfloat16)
        odd_ref[k, part] = b0 - b2
        odd_ref[k, rows + first:rows + last] = b1 - b3

    lanes = table_ref.shape[2]
    lane = lax.broadcasted_iota(jnp.int32, (rows, lanes), 1)
    piece = lanes // n_win
    real = lane % piece < piece // 2

    def odd_spectra(k, m):
        both = product(odd_ref[k], table_ref[m])
        second = both[rows:]
        back, forth = pltpu.roll(second, lanes - piece // 2, 1), pltpu.roll(second, piece // 2, 1)
        turned = jnp.where(real, back, -forth)
        return both[:rows] + turned if m == 1 else both[:rows] - turned

    parts = 4
    size = rows // parts
    chunk(0).wait()
    add_quarters(0, 0, rows)
    row = lax.broadcasted_iota(jnp.int32, (rows, 1), 0)
    for k in range(chunks):
        more = k + 1 < chunks
        if more:
            chunk(k + 1).wait()
        spectra = []
        for m in range(4):
            if m % 2:
                spectra.append(odd_spectra(k, m))
            else:
                spectra.append(product(even_ref[k, m // 2], table_ref[m]))
            if more:
                add_quarters(k + 1, m * size, (m + 1) * size)
        squares = sum(jnp.sum(s * s, axis=1, keepdims=True) for s in spectra)
        gain = lax.rsqrt(squares / F + 1e-06)
        keep = jnp.zeros((rows, 1), jnp.float32)
        for t in range(w_step):
            own = (row >= t * r_dev) & (row < (t + 1) * r_dev)
            keep = jnp.where(own, valid_ref[k * w_step + t].astype(jnp.float32), keep)
        gain = gain * keep
        white = [s * gain for s in spectra]
        for d in range(n_win):
            columns = slice(d * piece, (d + 1) * piece)
            block = jnp.concatenate([part[:, columns] for part in white], axis=1)
            white_ref[k, d] = block.astype(jnp.bfloat16)
        count = w_step * n_own
        for j in range(n_win):
            block = white_ref[k, win ^ j]
            r_refs[j][k * rows:(k + 1) * rows, :] = block
            picked = product(sel_ref[...], block).astype(jnp.bfloat16)
            for d in range(n_rcv):
                q_refs[d][j, k * count:(k + 1) * count, :] = picked[d * count:(d + 1) * count]


def spectra_call(traces, valid, src_station, n_win, n_rcv):
    w_dev, r_dev, samples = traces.shape
    n_src = src_station.shape[0]
    n_own = n_src // n_rcv
    chunks = 2
    every = w_dev * r_dev
    rows = every // chunks
    lanes = 2 * F // n_win
    seed, twice = (jnp.asarray(t) for t in table_seeds(samples, F, samples // 16, n_win))
    shapes = [jax.ShapeDtypeStruct((every, lanes), jnp.bfloat16)] * n_win
    shapes += [jax.ShapeDtypeStruct((n_win, w_dev * n_own, lanes), jnp.bfloat16)] * n_rcv
    shapes += [jax.ShapeDtypeStruct((8, 128), jnp.int32), jax.ShapeDtypeStruct((1,), jnp.int32)]
    vmem = pl.BlockSpec(memory_space=VMEM)
    out = pl.pallas_call(
        functools.partial(spectra_kernel, n_win, n_rcv, r_dev),
        in_specs=[pl.BlockSpec(memory_space=pltpu.HBM)] * 5,
        out_specs=[vmem] * (len(shapes) - 1) + [pl.BlockSpec(memory_space=SMEM)],
        out_shape=shapes,
        scratch_shapes=[
            pltpu.VMEM((chunks, rows, samples), jnp.bfloat16),
            pltpu.VMEM((chunks, 2, rows, samples // 4), jnp.bfloat16),
            pltpu.VMEM((chunks, 2 * rows, samples // 4), jnp.bfloat16),
            pltpu.VMEM((chunks, n_win, rows, lanes), jnp.bfloat16),
            pltpu.VMEM((n_src * (w_dev // chunks), rows), jnp.bfloat16),
            pltpu.VMEM((n_src, 128), jnp.float32),
            pltpu.VMEM((4, samples // 4, F // 2), jnp.bfloat16),
            pltpu.VMEM(seed.shape, jnp.float32),
            pltpu.VMEM(twice.shape, jnp.float32),
            pltpu.SMEM(valid.shape, jnp.int32),
            pltpu.SMEM(src_station.shape, jnp.int32),
            pltpu.SemaphoreType.DMA((4,)),
            pltpu.SemaphoreType.DMA((chunks,)),
        ],
        compiler_params=pltpu.CompilerParams(vmem_limit_bytes=36 * 2**20),
        cost_estimate=pl.CostEstimate(
            flops=2 * every * (samples // 4) * 6 * (F // 2), bytes_accessed=every * samples * 2,
            transcendentals=0,
        ),
        name="spectra",
    )(*(in_hbm(x) for x in (valid, src_station, traces.reshape(every, samples), seed, twice)))
    return out[:n_win], out[n_win:n_win + n_rcv], out[-2], out[-1]


def bin_order(lanes):
    quarter = lanes // 8
    lane = lax.broadcasted_iota(jnp.int32, (lanes, lanes), 1)
    row = lax.broadcasted_iota(jnp.int32, (lanes, lanes), 0)
    part = (lane // quarter) % 2
    bin_of = 4 * (lane % quarter) + lane // (2 * quarter)
    hit = row == part * (lanes // 2) + bin_of
    return hit.astype(jnp.float32).astype(jnp.bfloat16)


def turn_kernel(r_dev, *refs):
    x_refs, (out_ref, rows_ref) = refs[:-2], refs[-2:]
    lanes = x_refs[0].shape[1]
    bins = lanes // 2
    w_dev = out_ref.shape[1] // 2
    pad = out_ref.shape[2] // 2
    order = bin_order(lanes)
    windows = [(x, w) for x in x_refs for w in range(x.shape[0] // r_dev)]
    for k, (x_ref, w) in enumerate(windows):
        turned = lax.dot_general(
            order, x_ref[w * r_dev:(w + 1) * r_dev], (((1,), (1,)), ((), ())),
            preferred_element_type=jnp.float32,
        )
        rows_ref[pl.ds(k, lanes, stride=w_dev), :r_dev] = turned
    rr = rows_ref[:bins * w_dev].reshape(bins, w_dev, pad)
    ri = rows_ref[bins * w_dev:].reshape(bins, w_dev, pad)
    out_ref[:, :, :pad] = jnp.concatenate([rr, ri], axis=1).astype(jnp.bfloat16)
    out_ref[:, :, pad:] = jnp.concatenate([ri, -rr], axis=1).astype(jnp.bfloat16)


def turn_call(parts, w_dev, r_dev):
    lanes = parts[0].shape[1]
    pad = 128
    vmem = pl.BlockSpec(memory_space=VMEM)
    return pl.pallas_call(
        functools.partial(turn_kernel, r_dev),
        in_specs=[vmem] * len(parts),
        out_specs=vmem,
        out_shape=jax.ShapeDtypeStruct((lanes // 2, 2 * w_dev, 2 * pad), jnp.bfloat16),
        scratch_shapes=[pltpu.VMEM((lanes * w_dev, pad), jnp.float32)],
        compiler_params=pltpu.CompilerParams(vmem_limit_bytes=16 * 2**20),
        cost_estimate=pl.CostEstimate(
            flops=2 * w_dev * lanes * lanes * pad, bytes_accessed=2 * 2**20, transcendentals=0
        ),
        name="turn",
    )(*parts)


def merge_kernel(n_win, *refs):
    picked, outs = refs[:-n_win], refs[-n_win:]
    for j, out_ref in enumerate(outs):
        total = picked[0][j].astype(jnp.float32)
        for q_ref in picked[1:]:
            total = total + q_ref[j].astype(jnp.float32)
        out_ref[...] = total.astype(jnp.bfloat16)


def merge_call(*picked):
    n_win, rows, lanes = picked[0].shape
    vmem = pl.BlockSpec(memory_space=VMEM)
    return pl.pallas_call(
        functools.partial(merge_kernel, n_win),
        in_specs=[vmem] * len(picked),
        out_specs=[vmem] * n_win,
        out_shape=[jax.ShapeDtypeStruct((rows, lanes), jnp.bfloat16)] * n_win,
        compiler_params=pltpu.CompilerParams(vmem_limit_bytes=4 * 2**20),
        cost_estimate=pl.CostEstimate(flops=2**18, bytes_accessed=2**19, transcendentals=0),
        name="merge",
    )(*picked)


def lefts_kernel(n_win, w_dev, n_own, *refs):
    out_ref, srow_ref, rows_ref = refs[-3:]
    rows, lanes = refs[0].shape
    bins = lanes // 2
    windows = n_win * w_dev
    pad = rows_ref.shape[1]
    for j in range(n_win):
        block = refs[j][...].astype(jnp.float32)
        for h in range(lanes // pad):
            srow_ref[h, j * rows:(j + 1) * rows, :] = block[:, h * pad:(h + 1) * pad]

    lane = lax.broadcasted_iota(jnp.int32, (bins, lanes), 1)
    row = lax.broadcasted_iota(jnp.int32, (bins, lanes), 0)
    quarter = lanes // 8
    bin_of = 4 * (lane % quarter) + lane // (2 * quarter)
    pick = bin_of == 2 * (row % (bins // 2)) + row // (bins // 2)
    pick = pick.astype(jnp.float32).astype(jnp.bfloat16)
    real = (lane[:w_dev] // quarter) % 2 == 0
    low = lax.broadcasted_iota(jnp.int32, (bins // 2, pad), 1) < pad // 2
    for s in range(n_own):
        values = jnp.concatenate(
            [srow_ref[h, pl.ds(s, windows, stride=n_own), :] for h in range(lanes // pad)], axis=1
        )
        stacked = []
        for j in range(n_win):
            own = values[j * w_dev:(j + 1) * w_dev]
            stacked += [jnp.where(real, own, 0.0), jnp.where(real, 0.0, own)]
        stacked = jnp.concatenate(stacked * 2, axis=0).astype(jnp.bfloat16)
        turned = lax.dot_general(
            pick, stacked, (((1,), (1,)), ((), ())), preferred_element_type=jnp.float32
        )
        pairs = jnp.where(low, turned[:bins // 2], turned[bins // 2:])
        rows_ref[pl.ds(s, bins // 2, stride=n_own), :] = pairs
    out_ref[...] = rows_ref[...].reshape(out_ref.shape).astype(jnp.bfloat16)


def lefts_call(blocks, after, later, w_dev):
    rows, lanes = blocks[0].shape
    n_win = len(blocks)
    n_own = rows // w_dev
    pad = 128
    first = n_win + len(after)
    vmem, anywhere = pl.BlockSpec(memory_space=VMEM), pl.BlockSpec(memory_space=pl.ANY)
    out = pl.pallas_call(
        functools.partial(lefts_kernel, n_win, w_dev, n_own),
        in_specs=[vmem] * n_win + [anywhere] * (len(after) + len(later)),
        out_specs=[anywhere] * len(later) + [vmem],
        out_shape=[jax.ShapeDtypeStruct(x.shape, x.dtype) for x in later]
        + [jax.ShapeDtypeStruct((lanes // 8, 2 * n_own, pad), jnp.bfloat16)],
        input_output_aliases={first + k: k for k in range(len(later))},
        scratch_shapes=[
            pltpu.VMEM((lanes // pad, n_win * rows, pad), jnp.float32),
            pltpu.VMEM((lanes // 4 * n_own, pad), jnp.float32),
        ],
        compiler_params=pltpu.CompilerParams(vmem_limit_bytes=6 * 2**20),
        cost_estimate=pl.CostEstimate(flops=2**26, bytes_accessed=2**19, transcendentals=0),
        name="lefts",
    )(*blocks, *after, *later)
    return out[-1], out[:-1]


def gate_kernel(*refs):
    pass


def gate_call(after, arrays):
    anywhere = pl.BlockSpec(memory_space=pl.ANY)
    return pl.pallas_call(
        gate_kernel,
        in_specs=[anywhere] * (len(after) + len(arrays)),
        out_specs=[anywhere] * len(arrays),
        out_shape=[jax.ShapeDtypeStruct(x.shape, x.dtype) for x in arrays],
        input_output_aliases={len(after) + k: k for k in range(len(arrays))},
        compiler_params=pltpu.CompilerParams(vmem_limit_bytes=2**20),
        cost_estimate=pl.CostEstimate(flops=1, bytes_accessed=1, transcendentals=0),
        name="gate",
    )(*after, *arrays)


def stacks_kernel(shares, n_win, w_dev, r_dev, n_own, bins, plan_hbm, *refs):
    t_refs = refs[:n_win]
    s_refs = refs[n_win:n_win + len(shares)]
    out_hbm, prod_ref, out_ref, plan_ref, sems, plan_sem = refs[-6:]
    plan_copy = pltpu.make_async_copy(plan_hbm, plan_ref, plan_sem)
    plan_copy.start()
    windows = n_win * w_dev
    count = len(shares) * n_own
    pitch = prod_ref.shape[1] // bins
    pad = 128
    rcv = lax.axis_index("rcv")

    low = lax.broadcasted_iota(jnp.int32, (count, pad), 1) < pad // 2
    for group in range(bins // 4):
        values = [s_ref[group].astype(jnp.float32) for s_ref in s_refs]
        for p in range(2):
            rows = jnp.concatenate([v[p * n_own:(p + 1) * n_own] for v in values], axis=0)
            left = jnp.concatenate([jnp.where(low, rows, 0.0), jnp.where(low, 0.0, rows)], axis=0)
            first = 4 * group + 2 * p
            right = [t_ref[f] for f in (first, first + 1) for t_ref in t_refs]
            result = jnp.dot(
                left.astype(jnp.bfloat16), jnp.concatenate(right, axis=0),
                preferred_element_type=jnp.float32,
            )
            for k in range(2):
                for c in range(2):
                    block = result[k * count:(k + 1) * count, c * pad:(c + 1) * pad]
                    prod_ref[c, pl.ds((first + k) * pitch, count), :] = block

    scale = 1.0 / math.sqrt(windows)
    plan_copy.wait()
    copies = []
    for s in range(count):
        for c in range(2):
            turned = prod_ref[c, pl.ds(s, bins, stride=pitch), :].T
            out_ref[s, pl.ds(c, r_dev, stride=2), :] = turned[:r_dev] * scale
        row = plan_ref[0, (rcv ^ shares[s // n_own]) * n_own + s % n_own]
        copies.append(pltpu.make_async_copy(out_ref.at[s], out_hbm.at[row], sems.at[s]))
        copies[-1].start()
    for copy in copies:
        copy.wait()


def stacks_call(out, plan, turned, sources, shares, n_rcv, w_dev, r_dev, bins):
    n_win = len(turned)
    n_own = sources[0].shape[1] // 2
    windows = n_win * w_dev
    count = len(shares) * n_own
    whole = pl.BlockSpec(memory_space=VMEM)
    args = [plan] + list(turned) + [sources[i] for i in shares]
    specs = [pl.BlockSpec(memory_space=pl.ANY)] + [whole] * (len(args) - 1)
    aliases = {}
    if out is not None:
        aliases = {len(args): 0}
        args.append(out)
        specs.append(pl.BlockSpec(memory_space=pl.ANY))
    return pl.pallas_call(
        functools.partial(stacks_kernel, shares, n_win, w_dev, r_dev, n_own, bins),
        in_specs=specs,
        out_specs=pl.BlockSpec(memory_space=pltpu.HBM),
        out_shape=jax.ShapeDtypeStruct((n_rcv * n_own, 2 * r_dev, bins), jnp.float32),
        input_output_aliases=aliases,
        scratch_shapes=[
            pltpu.VMEM((2, (count + 8) * bins, 128), jnp.float32),
            pltpu.VMEM((count, 2 * r_dev, bins), jnp.float32),
            pltpu.SMEM(plan.shape, jnp.int32),
            pltpu.SemaphoreType.DMA((count,)),
            pltpu.SemaphoreType.DMA,
        ],
        compiler_params=pltpu.CompilerParams(vmem_limit_bytes=20 * 2**20),
        cost_estimate=pl.CostEstimate(
            flops=8 * windows * count * r_dev * bins, bytes_accessed=6 * 2**20, transcendentals=0
        ),
        name="stacks",
    )(*args)


def swap(value, axis, by):
    size = lax.axis_size(axis)
    return lax.ppermute(value, axis, [(i, i ^ by) for i in range(size)])


def near_and_far(n_rcv, by):
    pairs = [(z, z ^ by) for z in range(n_rcv)]
    return [p for p in pairs if abs(p[0] - p[1]) == 1], [p for p in pairs if abs(p[0] - p[1]) > 1]


def merge_near(picked, near):
    return merge_call(picked[0], *near)


def merge_all(picked, near):
    far = []
    for i in range(1, len(picked)):
        pairs = near_and_far(len(picked), i)[1]
        if pairs:
            far.append(lax.ppermute(picked[i], "rcv", pairs))
    return merge_call(picked[0], *near, *far)


def body(traces, valid, src_station):
    w_dev, r_dev, samples = traces.shape
    n_src = src_station.shape[0]
    n_win = lax.axis_size("win")
    n_rcv = lax.axis_size("rcv")
    bins = F // n_win
    early = n_win // 2

    blocks, picked, plan, flag = spectra_call(traces, valid, src_station, n_win, n_rcv)

    near = {}
    for i in range(1, n_rcv):
        pairs = near_and_far(n_rcv, i)[0]
        if pairs:
            near[i] = lax.ppermute(picked[i], "rcv", pairs)
    picked = [picked[0] + near.pop(n_rcv - 1)] + list(picked[1:])
    near = list(near.values())
    merged = lax.cond(flag.reshape(()) > 0, merge_all, merge_near, picked, near)

    merged = [merged[0]] + [swap(merged[j], "win", j) for j in range(1, n_win)]
    late = [j for j in range(1, n_win) if j != early]
    received = {0: blocks[0], early: swap(blocks[early], "win", early)}
    lefts, later = lefts_call(merged, [received[early]], [blocks[j] for j in late], w_dev)
    received.update({j: swap(block, "win", j) for j, block in zip(late, later)})
    sources = [lefts, swap(lefts, "rcv", 1), swap(lefts, "rcv", 2)]
    turned = [turn_call([received[j]], w_dev, r_dev) for j in range(n_win)]
    sources[2] = gate_call(turned[:-1], [sources[2]])[0]
    sources.append(swap(sources[2], "rcv", 1))

    half = n_rcv // 2
    sizes = (n_rcv, w_dev, r_dev, bins)
    stacks = stacks_call(None, plan, turned, sources, tuple(range(half)), *sizes)
    stacks = stacks_call(stacks, plan, turned, sources, tuple(range(half, n_rcv)), *sizes)
    return stacks.reshape(n_src, r_dev, 2, bins)


def correlate(received, sources):
    rr = received[:, :, 0]
    ri = received[:, :, 1]
    sr = sources[:, :, 0]
    si = sources[:, :, 1]
    real = jnp.einsum("wsf,wrf->srf", sr, rr, preferred_element_type=jnp.float32)
    real = real + jnp.einsum("wsf,wrf->srf", si, ri, preferred_element_type=jnp.float32)
    imag = jnp.einsum("wsf,wrf->srf", sr, ri, preferred_element_type=jnp.float32)
    imag = imag - jnp.einsum("wsf,wrf->srf", si, rr, preferred_element_type=jnp.float32)
    return jnp.stack([real, imag], axis=2)


def body_any(traces, valid, src_station):
    w_dev, r_dev, samples = traces.shape
    n_win = lax.axis_size("win")
    n_rcv = lax.axis_size("rcv")
    bins = F // n_win
    table = jnp.asarray(band_table(samples, F, samples // 16))
    spectra = jnp.dot(
        traces.reshape(w_dev * r_dev, samples), table, preferred_element_type=jnp.float32
    )
    spectra = spectra.reshape(w_dev, r_dev, 2, F)
    power = jnp.sum(spectra * spectra, axis=(2, 3), keepdims=True) / F
    keep = valid.astype(jnp.float32)[:, None, None, None]
    white = (spectra * lax.rsqrt(power + 1e-06) * keep).astype(jnp.bfloat16)
    blocks = white.reshape(w_dev, r_dev, 2, n_win, bins).transpose(3, 0, 1, 2, 4)
    me = lax.axis_index("win")
    offset = lax.axis_index("rcv") * r_dev
    station_ids = offset + jnp.arange(r_dev, dtype=jnp.int32)
    selector = (src_station[:, None] == station_ids[None, :]).astype(jnp.bfloat16)
    received = []
    for j in range(n_win):
        block = lax.dynamic_index_in_dim(blocks, me ^ j, 0, keepdims=False)
        received.append(swap(block, "win", j) if j else block)
    received = jnp.concatenate(received, axis=0)
    rows = jnp.einsum("sr,wrcf->wscf", selector, received, preferred_element_type=jnp.float32)
    rows = lax.all_to_all(rows.astype(jnp.bfloat16), "rcv", 0, 0, tiled=True)
    rows = rows.reshape((n_rcv, -1) + rows.shape[1:])
    merged = jnp.sum(rows.astype(jnp.float32), axis=0).astype(jnp.bfloat16)
    sources = lax.all_gather(merged, "rcv", axis=0, tiled=True)
    return correlate(received, sources) * (1.0 / math.sqrt(w_dev * n_win))


def solution(mesh):
    sizes = (mesh.shape["win"], mesh.shape["rcv"])
    return jax.shard_map(
        body if sizes == (4, 4) else body_any,
        mesh=mesh,
        in_specs=(P("win", ("groups", "rcv"), None), P(("groups", "win")), P("groups")),
        out_specs=P(None, ("groups", "rcv"), None, "win"),
        check_vma=False,
    )
```

```python
import functools
import math

import jax
import jax.numpy as jnp
import numpy as np
from jax import lax
from jax.experimental import pallas as pl
from jax.experimental.pallas import tpu as pltpu
from jax.sharding import PartitionSpec as P

F = 512
SMEM = pltpu.MemorySpace.SMEM
VMEM = pltpu.MemorySpace.VMEM


def angles(samples, freqs, count):
    phase = samples[:, None] * freqs[None, :] % count
    return phase.astype(np.float64) * (2.0 * math.pi / count)


def band_table(count, bins, first):
    angle = angles(np.arange(count), first + np.arange(bins), count)
    return np.concatenate([np.cos(angle), -np.sin(angle)], axis=1).astype(jnp.bfloat16)


BLOCK = 32


def table_seeds(count, bins, first, n_win):
    j = np.arange(bins // 4)
    turn = np.array([0.0, 0.5 * math.pi]).reshape(1, 2, 1)
    seeds, twice = [], []
    for m in range(4):
        freqs = np.broadcast_to((first + 4 * j + m).reshape(n_win, 1, -1), (n_win, 2, j.size // n_win))
        angle = angles(np.arange(2 * BLOCK), freqs.reshape(-1), count)
        angle = angle + np.broadcast_to(turn, freqs.shape).reshape(1, -1)
        seeds.append(np.cos(angle).reshape(2, BLOCK, -1))
        step = angles(np.full(8, BLOCK), freqs.reshape(-1), count)
        twice.append(2.0 * np.cos(step))
    return np.stack(seeds).astype(np.float32), np.stack(twice).astype(np.float32)


def make_tables(seed_ref, twice_ref, table_ref):
    for first in (0, 2):
        state = {}
        for m in (first, first + 1):
            twice = jnp.concatenate([twice_ref[m]] * (BLOCK // 8), axis=0)
            state[m] = (seed_ref[m, 0], seed_ref[m, 1], twice)
        for a in range(table_ref.shape[1] // BLOCK):
            for m, (here, after, twice) in state.items():
                table_ref[m, a * BLOCK:(a + 1) * BLOCK, :] = here.astype(jnp.bfloat16)
                state[m] = (after, twice * after - here, twice)


def in_hbm(value):
    return pltpu.with_memory_space_constraint(value, pltpu.HBM)


def order_sources(src_ref, r_dev, n_own, order_ref, plan_ref, flag_ref):
    n_src = src_ref.shape[0]
    size = order_ref.shape
    down = lax.broadcasted_iota(jnp.int32, size, 0).astype(jnp.float32)
    along = lax.broadcasted_iota(jnp.int32, size, 1).astype(jnp.float32)
    none = jnp.full(size, float(2**20), jnp.float32)
    column, row = none, none
    for s in range(n_src):
        station = src_ref[s].astype(jnp.float32)
        column = jnp.where(down == s, station, column)
        row = jnp.where(along == s, station, row)
    rank_along = jnp.sum((column < row).astype(jnp.float32), axis=0, keepdims=True)
    rank_down = jnp.sum((row < column).astype(jnp.float32), axis=1, keepdims=True)
    sorted_down = jnp.sum(jnp.where(rank_along == down, row, 0.0), axis=1, keepdims=True)
    at_place = rank_down == along
    sorted_along = jnp.sum(jnp.where(at_place, column, 0.0), axis=0, keepdims=True)
    source_along = jnp.sum(jnp.where(at_place, down, 0.0), axis=0, keepdims=True)
    order_ref[...] = jnp.broadcast_to(sorted_down, size)
    place = along[:1]
    owner, share = jnp.zeros_like(place), jnp.zeros_like(place)
    for z in range(1, n_src // n_own):
        owner = owner + (sorted_along >= z * r_dev).astype(jnp.float32)
        share = share + (place >= z * n_own).astype(jnp.float32)
    far = jnp.where((place < n_src) & (jnp.abs(owner - share) > 1.5), 1.0, 0.0)
    plan_ref[...] = jnp.broadcast_to(source_along, plan_ref.shape).astype(jnp.int32)
    flag_ref[0] = jnp.max(far).astype(jnp.int32)


def spectra_kernel(
    n_win, n_rcv, r_dev, valid_hbm, src_hbm, x_hbm, seed_hbm, twice_hbm, *refs
):
    r_refs = refs[:n_win]
    q_refs = refs[n_win:n_win + n_rcv]
    (plan_ref, flag_ref, x_ref, even_ref, odd_ref, white_ref, sel_ref, order_ref, table_ref,
     seed_ref, twice_ref, valid_ref, src_ref, sems, x_sems) = refs[n_win + n_rcv:]
    chunks, rows, samples = x_ref.shape
    w_step = rows // r_dev
    n_own = src_ref.shape[0] // n_rcv
    quarter = samples // 4
    win = lax.axis_index("win")
    rcv = lax.axis_index("rcv")

    def small(k):
        source = (seed_hbm, twice_hbm, src_hbm, valid_hbm)[k]
        target = (seed_ref, twice_ref, src_ref, valid_ref)[k]
        return pltpu.make_async_copy(source, target, sems.at[k])

    def chunk(k):
        return pltpu.make_async_copy(x_hbm.at[pl.ds(k * rows, rows)], x_ref.at[k], x_sems.at[k])

    for k in range(4):
        small(k).start()
    for k in range(chunks):
        chunk(k).start()
    small(0).wait()
    small(1).wait()
    make_tables(seed_ref, twice_ref, table_ref)
    small(2).wait()
    order_sources(src_ref, r_dev, n_own, order_ref, plan_ref, flag_ref)
    stations = []
    for d in range(n_rcv):
        share = pl.multiple_of((rcv ^ d) * n_own, n_own)
        stations += [order_ref[pl.ds(share, n_own), 0:1]] * w_step
    wanted = jnp.concatenate(stations, axis=0).astype(jnp.int32) - rcv * r_dev
    shape = (n_rcv * w_step * n_own, rows)
    out_row = lax.broadcasted_iota(jnp.int32, shape, 0)
    column = lax.broadcasted_iota(jnp.int32, shape, 1)
    inside = (wanted >= 0) & (wanted < r_dev)
    hit = inside & (column == wanted + (out_row // n_own) % w_step * r_dev)
    sel_ref[...] = hit.astype(jnp.float32).astype(jnp.bfloat16)
    small(3).wait()

    def product(lhs, table):
        return jnp.dot(lhs, table, preferred_element_type=jnp.float32)

    def add_quarters(k, first, last):
        part = slice(first, last)
        b0, b1, b2, b3 = (x_ref[k, part, q * quarter:(q + 1) * quarter] for q in range(4))
        x0, x1, x2, x3 = (b.astype(jnp.float32) for b in (b0, b1, b2, b3))
        even_ref[k, 0, part] = ((x0 + x2) + (x1 + x3)).astype(jnp.bfloat16)
        even_ref[k, 1, part] = ((x0 + x2) - (x1 + x3)).astype(jnp.bfloat16)
        odd_ref[k, part] = b0 - b2
        odd_ref[k, rows + first:rows + last] = b1 - b3

    lanes = table_ref.shape[2]
    lane = lax.broadcasted_iota(jnp.int32, (rows, lanes), 1)
    piece = lanes // n_win
    real = lane % piece < piece // 2

    def odd_spectra(k, m):
        both = product(odd_ref[k], table_ref[m])
        second = both[rows:]
        back, forth = pltpu.roll(second, lanes - piece // 2, 1), pltpu.roll(second, piece // 2, 1)
        turned = jnp.where(real, back, -forth)
        return both[:rows] + turned if m == 1 else both[:rows] - turned

    parts = 4
    size = rows // parts
    chunk(0).wait()
    add_quarters(0, 0, rows)
    row = lax.broadcasted_iota(jnp.int32, (rows, 1), 0)
    for k in range(chunks):
        more = k + 1 < chunks
        if more:
            chunk(k + 1).wait()
        spectra = []
        for m in range(4):
            if m % 2:
                spectra.append(odd_spectra(k, m))
            else:
                spectra.append(product(even_ref[k, m // 2], table_ref[m]))
            if more:
                add_quarters(k + 1, m * size, (m + 1) * size)
        squares = sum(jnp.sum(s * s, axis=1, keepdims=True) for s in spectra)
        gain = lax.rsqrt(squares / F + 1e-06)
        keep = jnp.zeros((rows, 1), jnp.float32)
        for t in range(w_step):
            own = (row >= t * r_dev) & (row < (t + 1) * r_dev)
            keep = jnp.where(own, valid_ref[k * w_step + t].astype(jnp.float32), keep)
        gain = gain * keep
        white = [s * gain for s in spectra]
        for d in range(n_win):
            columns = slice(d * piece, (d + 1) * piece)
            block = jnp.concatenate([part[:, columns] for part in white], axis=1)
            white_ref[k, d] = block.astype(jnp.bfloat16)
        count = w_step * n_own
        for j in range(n_win):
            block = white_ref[k, win ^ j]
            r_refs[j][k * rows:(k + 1) * rows, :] = block
            picked = product(sel_ref[...], block).astype(jnp.bfloat16)
            for d in range(n_rcv):
                q_refs[d][j, k * count:(k + 1) * count, :] = picked[d * count:(d + 1) * count]


def spectra_call(traces, valid, src_station, n_win, n_rcv):
    w_dev, r_dev, samples = traces.shape
    n_src = src_station.shape[0]
    n_own = n_src // n_rcv
    chunks = 2
    every = w_dev * r_dev
    rows = every // chunks
    lanes = 2 * F // n_win
    seed, twice = (jnp.asarray(t) for t in table_seeds(samples, F, samples // 16, n_win))
    shapes = [jax.ShapeDtypeStruct((every, lanes), jnp.bfloat16)] * n_win
    shapes += [jax.ShapeDtypeStruct((n_win, w_dev * n_own, lanes), jnp.bfloat16)] * n_rcv
    shapes += [jax.ShapeDtypeStruct((8, 128), jnp.int32), jax.ShapeDtypeStruct((1,), jnp.int32)]
    vmem = pl.BlockSpec(memory_space=VMEM)
    out = pl.pallas_call(
        functools.partial(spectra_kernel, n_win, n_rcv, r_dev),
        in_specs=[pl.BlockSpec(memory_space=pltpu.HBM)] * 5,
        out_specs=[vmem] * (len(shapes) - 1) + [pl.BlockSpec(memory_space=SMEM)],
        out_shape=shapes,
        scratch_shapes=[
            pltpu.VMEM((chunks, rows, samples), jnp.bfloat16),
            pltpu.VMEM((chunks, 2, rows, samples // 4), jnp.bfloat16),
            pltpu.VMEM((chunks, 2 * rows, samples // 4), jnp.bfloat16),
            pltpu.VMEM((chunks, n_win, rows, lanes), jnp.bfloat16),
            pltpu.VMEM((n_src * (w_dev // chunks), rows), jnp.bfloat16),
            pltpu.VMEM((n_src, 128), jnp.float32),
            pltpu.VMEM((4, samples // 4, F // 2), jnp.bfloat16),
            pltpu.VMEM(seed.shape, jnp.float32),
            pltpu.VMEM(twice.shape, jnp.float32),
            pltpu.SMEM(valid.shape, jnp.int32),
            pltpu.SMEM(src_station.shape, jnp.int32),
            pltpu.SemaphoreType.DMA((4,)),
            pltpu.SemaphoreType.DMA((chunks,)),
        ],
        compiler_params=pltpu.CompilerParams(vmem_limit_bytes=36 * 2**20),
        cost_estimate=pl.CostEstimate(
            flops=2 * every * (samples // 4) * 6 * (F // 2), bytes_accessed=every * samples * 2,
            transcendentals=0,
        ),
        name="spectra",
    )(*(in_hbm(x) for x in (valid, src_station, traces.reshape(every, samples), seed, twice)))
    return out[:n_win], out[n_win:n_win + n_rcv], out[-2], out[-1]


def bin_order(lanes):
    quarter = lanes // 8
    lane = lax.broadcasted_iota(jnp.int32, (lanes, lanes), 1)
    row = lax.broadcasted_iota(jnp.int32, (lanes, lanes), 0)
    part = (lane // quarter) % 2
    bin_of = 4 * (lane % quarter) + lane // (2 * quarter)
    hit = row == part * (lanes // 2) + bin_of
    return hit.astype(jnp.float32).astype(jnp.bfloat16)


def turn_kernel(r_dev, *refs):
    x_refs, (out_ref, rows_ref) = refs[:-2], refs[-2:]
    lanes = x_refs[0].shape[1]
    bins = lanes // 2
    w_dev = out_ref.shape[1] // 2
    pad = out_ref.shape[2] // 2
    order = bin_order(lanes)
    windows = [(x, w) for x in x_refs for w in range(x.shape[0] // r_dev)]
    for k, (x_ref, w) in enumerate(windows):
        turned = lax.dot_general(
            order, x_ref[w * r_dev:(w + 1) * r_dev], (((1,), (1,)), ((), ())),
            preferred_element_type=jnp.float32,
        )
        rows_ref[pl.ds(k, lanes, stride=w_dev), :r_dev] = turned
    rr = rows_ref[:bins * w_dev].reshape(bins, w_dev, pad)
    ri = rows_ref[bins * w_dev:].reshape(bins, w_dev, pad)
    out_ref[:, :, :pad] = jnp.concatenate([rr, ri], axis=1).astype(jnp.bfloat16)
    out_ref[:, :, pad:] = jnp.concatenate([ri, -rr], axis=1).astype(jnp.bfloat16)


def turn_call(parts, w_dev, r_dev):
    lanes = parts[0].shape[1]
    pad = 128
    vmem = pl.BlockSpec(memory_space=VMEM)
    return pl.pallas_call(
        functools.partial(turn_kernel, r_dev),
        in_specs=[vmem] * len(parts),
        out_specs=vmem,
        out_shape=jax.ShapeDtypeStruct((lanes // 2, 2 * w_dev, 2 * pad), jnp.bfloat16),
        scratch_shapes=[pltpu.VMEM((lanes * w_dev, pad), jnp.float32)],
        compiler_params=pltpu.CompilerParams(vmem_limit_bytes=16 * 2**20),
        cost_estimate=pl.CostEstimate(
            flops=2 * w_dev * lanes * lanes * pad, bytes_accessed=2 * 2**20, transcendentals=0
        ),
        name="turn",
    )(*parts)


def merge_kernel(n_win, *refs):
    picked, outs = refs[:-n_win], refs[-n_win:]
    for j, out_ref in enumerate(outs):
        total = picked[0][j].astype(jnp.float32)
        for q_ref in picked[1:]:
            total = total + q_ref[j].astype(jnp.float32)
        out_ref[...] = total.astype(jnp.bfloat16)


def merge_call(*picked):
    n_win, rows, lanes = picked[0].shape
    vmem = pl.BlockSpec(memory_space=VMEM)
    return pl.pallas_call(
        functools.partial(merge_kernel, n_win),
        in_specs=[vmem] * len(picked),
        out_specs=[vmem] * n_win,
        out_shape=[jax.ShapeDtypeStruct((rows, lanes), jnp.bfloat16)] * n_win,
        compiler_params=pltpu.CompilerParams(vmem_limit_bytes=4 * 2**20),
        cost_estimate=pl.CostEstimate(flops=2**18, bytes_accessed=2**19, transcendentals=0),
        name="merge",
    )(*picked)


def lefts_kernel(n_win, w_dev, n_own, *refs):
    out_ref, srow_ref, rows_ref = refs[-3:]
    rows, lanes = refs[0].shape
    bins = lanes // 2
    windows = n_win * w_dev
    pad = rows_ref.shape[1]
    for j in range(n_win):
        block = refs[j][...].astype(jnp.float32)
        for h in range(lanes // pad):
            srow_ref[h, j * rows:(j + 1) * rows, :] = block[:, h * pad:(h + 1) * pad]

    lane = lax.broadcasted_iota(jnp.int32, (bins, lanes), 1)
    row = lax.broadcasted_iota(jnp.int32, (bins, lanes), 0)
    quarter = lanes // 8
    bin_of = 4 * (lane % quarter) + lane // (2 * quarter)
    pick = bin_of == 2 * (row % (bins // 2)) + row // (bins // 2)
    pick = pick.astype(jnp.float32).astype(jnp.bfloat16)
    real = (lane[:w_dev] // quarter) % 2 == 0
    low = lax.broadcasted_iota(jnp.int32, (bins // 2, pad), 1) < pad // 2
    for s in range(n_own):
        values = jnp.concatenate(
            [srow_ref[h, pl.ds(s, windows, stride=n_own), :] for h in range(lanes // pad)], axis=1
        )
        stacked = []
        for j in range(n_win):
            own = values[j * w_dev:(j + 1) * w_dev]
            stacked += [jnp.where(real, own, 0.0), jnp.where(real, 0.0, own)]
        stacked = jnp.concatenate(stacked * 2, axis=0).astype(jnp.bfloat16)
        turned = lax.dot_general(
            pick, stacked, (((1,), (1,)), ((), ())), preferred_element_type=jnp.float32
        )
        pairs = jnp.where(low, turned[:bins // 2], turned[bins // 2:])
        rows_ref[pl.ds(s, bins // 2, stride=n_own), :] = pairs
    out_ref[...] = rows_ref[...].reshape(out_ref.shape).astype(jnp.bfloat16)


def lefts_call(blocks, after, later, w_dev):
    rows, lanes = blocks[0].shape
    n_win = len(blocks)
    n_own = rows // w_dev
    pad = 128
    first = n_win + len(after)
    vmem, anywhere = pl.BlockSpec(memory_space=VMEM), pl.BlockSpec(memory_space=pl.ANY)
    out = pl.pallas_call(
        functools.partial(lefts_kernel, n_win, w_dev, n_own),
        in_specs=[vmem] * n_win + [anywhere] * (len(after) + len(later)),
        out_specs=[anywhere] * len(later) + [vmem],
        out_shape=[jax.ShapeDtypeStruct(x.shape, x.dtype) for x in later]
        + [jax.ShapeDtypeStruct((lanes // 8, 2 * n_own, pad), jnp.bfloat16)],
        input_output_aliases={first + k: k for k in range(len(later))},
        scratch_shapes=[
            pltpu.VMEM((lanes // pad, n_win * rows, pad), jnp.float32),
            pltpu.VMEM((lanes // 4 * n_own, pad), jnp.float32),
        ],
        compiler_params=pltpu.CompilerParams(vmem_limit_bytes=6 * 2**20),
        cost_estimate=pl.CostEstimate(flops=2**26, bytes_accessed=2**19, transcendentals=0),
        name="lefts",
    )(*blocks, *after, *later)
    return out[-1], out[:-1]


def gate_kernel(*refs):
    pass


def gate_call(after, arrays):
    anywhere = pl.BlockSpec(memory_space=pl.ANY)
    return pl.pallas_call(
        gate_kernel,
        in_specs=[anywhere] * (len(after) + len(arrays)),
        out_specs=[anywhere] * len(arrays),
        out_shape=[jax.ShapeDtypeStruct(x.shape, x.dtype) for x in arrays],
        input_output_aliases={len(after) + k: k for k in range(len(arrays))},
        compiler_params=pltpu.CompilerParams(vmem_limit_bytes=2**20),
        cost_estimate=pl.CostEstimate(flops=1, bytes_accessed=1, transcendentals=0),
        name="gate",
    )(*after, *arrays)


def stacks_kernel(shares, n_win, w_dev, r_dev, n_own, bins, plan_hbm, *refs):
    t_refs = refs[:n_win]
    s_refs = refs[n_win:n_win + len(shares)]
    out_hbm, prod_ref, out_ref, plan_ref, sems, plan_sem = refs[-6:]
    plan_copy = pltpu.make_async_copy(plan_hbm, plan_ref, plan_sem)
    plan_copy.start()
    windows = n_win * w_dev
    count = len(shares) * n_own
    pitch = prod_ref.shape[1] // bins
    pad = 128
    rcv = lax.axis_index("rcv")

    low = lax.broadcasted_iota(jnp.int32, (count, pad), 1) < pad // 2
    for group in range(bins // 4):
        values = [s_ref[group].astype(jnp.float32) for s_ref in s_refs]
        for p in range(2):
            rows = jnp.concatenate([v[p * n_own:(p + 1) * n_own] for v in values], axis=0)
            left = jnp.concatenate([jnp.where(low, rows, 0.0), jnp.where(low, 0.0, rows)], axis=0)
            first = 4 * group + 2 * p
            right = [t_ref[f] for f in (first, first + 1) for t_ref in t_refs]
            result = jnp.dot(
                left.astype(jnp.bfloat16), jnp.concatenate(right, axis=0),
                preferred_element_type=jnp.float32,
            )
            for k in range(2):
                for c in range(2):
                    block = result[k * count:(k + 1) * count, c * pad:(c + 1) * pad]
                    prod_ref[c, pl.ds((first + k) * pitch, count), :] = block

    scale = 1.0 / math.sqrt(windows)
    plan_copy.wait()
    copies = []
    for s in range(count):
        for c in range(2):
            turned = prod_ref[c, pl.ds(s, bins, stride=pitch), :].T
            out_ref[s, pl.ds(c, r_dev, stride=2), :] = turned[:r_dev] * scale
        row = plan_ref[0, (rcv ^ shares[s // n_own]) * n_own + s % n_own]
        copies.append(pltpu.make_async_copy(out_ref.at[s], out_hbm.at[row], sems.at[s]))
        copies[-1].start()
    for copy in copies:
        copy.wait()


def stacks_call(out, plan, turned, sources, shares, n_rcv, w_dev, r_dev, bins):
    n_win = len(turned)
    n_own = sources[0].shape[1] // 2
    windows = n_win * w_dev
    count = len(shares) * n_own
    whole = pl.BlockSpec(memory_space=VMEM)
    args = [plan] + list(turned) + [sources[i] for i in shares]
    specs = [pl.BlockSpec(memory_space=pl.ANY)] + [whole] * (len(args) - 1)
    aliases = {}
    if out is not None:
        aliases = {len(args): 0}
        args.append(out)
        specs.append(pl.BlockSpec(memory_space=pl.ANY))
    return pl.pallas_call(
        functools.partial(stacks_kernel, shares, n_win, w_dev, r_dev, n_own, bins),
        in_specs=specs,
        out_specs=pl.BlockSpec(memory_space=pltpu.HBM),
        out_shape=jax.ShapeDtypeStruct((n_rcv * n_own, 2 * r_dev, bins), jnp.float32),
        input_output_aliases=aliases,
        scratch_shapes=[
            pltpu.VMEM((2, (count // 8 | 1) * 8 * bins, 128), jnp.float32),
            pltpu.VMEM((count, 2 * r_dev, bins), jnp.float32),
            pltpu.SMEM(plan.shape, jnp.int32),
            pltpu.SemaphoreType.DMA((count,)),
            pltpu.SemaphoreType.DMA,
        ],
        compiler_params=pltpu.CompilerParams(vmem_limit_bytes=20 * 2**20),
        cost_estimate=pl.CostEstimate(
            flops=8 * windows * count * r_dev * bins, bytes_accessed=6 * 2**20, transcendentals=0
        ),
        name="stacks",
    )(*args)


def swap(value, axis, by):
    size = lax.axis_size(axis)
    return lax.ppermute(value, axis, [(i, i ^ by) for i in range(size)])


def near_and_far(n_rcv, by):
    pairs = [(z, z ^ by) for z in range(n_rcv)]
    return [p for p in pairs if abs(p[0] - p[1]) == 1], [p for p in pairs if abs(p[0] - p[1]) > 1]


def merge_near(picked, near):
    return merge_call(picked[0], *near)


def merge_all(picked, near):
    far = []
    for i in range(1, len(picked)):
        pairs = near_and_far(len(picked), i)[1]
        if pairs:
            far.append(lax.ppermute(picked[i], "rcv", pairs))
    return merge_call(picked[0], *near, *far)


def body(traces, valid, src_station):
    w_dev, r_dev, samples = traces.shape
    n_src = src_station.shape[0]
    n_win = lax.axis_size("win")
    n_rcv = lax.axis_size("rcv")
    bins = F // n_win
    early = n_win // 2

    blocks, picked, plan, flag = spectra_call(traces, valid, src_station, n_win, n_rcv)

    near = {}
    for i in range(1, n_rcv):
        pairs = near_and_far(n_rcv, i)[0]
        if pairs:
            near[i] = lax.ppermute(picked[i], "rcv", pairs)
    picked = [picked[0] + near.pop(n_rcv - 1)] + list(picked[1:])
    near = list(near.values())
    merged = lax.cond(flag.reshape(()) > 0, merge_all, merge_near, picked, near)

    merged = [merged[0]] + [swap(merged[j], "win", j) for j in range(1, n_win)]
    late = [j for j in range(1, n_win) if j != early]
    received = {0: blocks[0], early: swap(blocks[early], "win", early)}
    lefts, later = lefts_call(merged, [received[early]], [blocks[j] for j in late], w_dev)
    received.update({j: swap(block, "win", j) for j, block in zip(late, later)})
    sources = [lefts, swap(lefts, "rcv", 1), swap(lefts, "rcv", 2)]
    turned = [turn_call([received[j]], w_dev, r_dev) for j in range(n_win)]
    sources[2] = gate_call(turned[:-1], [sources[2]])[0]
    sources.append(swap(sources[2], "rcv", 1))

    sizes = (n_rcv, w_dev, r_dev, bins)
    stacks = stacks_call(None, plan, turned, sources, tuple(range(n_rcv - 1)), *sizes)
    stacks = stacks_call(stacks, plan, turned, sources, (n_rcv - 1,), *sizes)
    return stacks.reshape(n_src, r_dev, 2, bins)


def correlate(received, sources):
    rr = received[:, :, 0]
    ri = received[:, :, 1]
    sr = sources[:, :, 0]
    si = sources[:, :, 1]
    real = jnp.einsum("wsf,wrf->srf", sr, rr, preferred_element_type=jnp.float32)
    real = real + jnp.einsum("wsf,wrf->srf", si, ri, preferred_element_type=jnp.float32)
    imag = jnp.einsum("wsf,wrf->srf", sr, ri, preferred_element_type=jnp.float32)
    imag = imag - jnp.einsum("wsf,wrf->srf", si, rr, preferred_element_type=jnp.float32)
    return jnp.stack([real, imag], axis=2)


def body_any(traces, valid, src_station):
    w_dev, r_dev, samples = traces.shape
    n_win = lax.axis_size("win")
    n_rcv = lax.axis_size("rcv")
    bins = F // n_win
    table = jnp.asarray(band_table(samples, F, samples // 16))
    spectra = jnp.dot(
        traces.reshape(w_dev * r_dev, samples), table, preferred_element_type=jnp.float32
    )
    spectra = spectra.reshape(w_dev, r_dev, 2, F)
    power = jnp.sum(spectra * spectra, axis=(2, 3), keepdims=True) / F
    keep = valid.astype(jnp.float32)[:, None, None, None]
    white = (spectra * lax.rsqrt(power + 1e-06) * keep).astype(jnp.bfloat16)
    blocks = white.reshape(w_dev, r_dev, 2, n_win, bins).transpose(3, 0, 1, 2, 4)
    me = lax.axis_index("win")
    offset = lax.axis_index("rcv") * r_dev
    station_ids = offset + jnp.arange(r_dev, dtype=jnp.int32)
    selector = (src_station[:, None] == station_ids[None, :]).astype(jnp.bfloat16)
    received = []
    for j in range(n_win):
        block = lax.dynamic_index_in_dim(blocks, me ^ j, 0, keepdims=False)
        received.append(swap(block, "win", j) if j else block)
    received = jnp.concatenate(received, axis=0)
    rows = jnp.einsum("sr,wrcf->wscf", selector, received, preferred_element_type=jnp.float32)
    rows = lax.all_to_all(rows.astype(jnp.bfloat16), "rcv", 0, 0, tiled=True)
    rows = rows.reshape((n_rcv, -1) + rows.shape[1:])
    merged = jnp.sum(rows.astype(jnp.float32), axis=0).astype(jnp.bfloat16)
    sources = lax.all_gather(merged, "rcv", axis=0, tiled=True)
    return correlate(received, sources) * (1.0 / math.sqrt(w_dev * n_win))


def solution(mesh):
    sizes = (mesh.shape["win"], mesh.shape["rcv"])
    return jax.shard_map(
        body if sizes == (4, 4) else body_any,
        mesh=mesh,
        in_specs=(P("win", ("groups", "rcv"), None), P(("groups", "win")), P("groups")),
        out_specs=P(None, ("groups", "rcv"), None, "win"),
        check_vma=False,
    )
```

```python
import functools
import math

import jax
import jax.numpy as jnp
import numpy as np
from jax import lax
from jax.experimental import pallas as pl
from jax.experimental.pallas import tpu as pltpu
from jax.sharding import PartitionSpec as P

F = 512
SMEM = pltpu.MemorySpace.SMEM
VMEM = pltpu.MemorySpace.VMEM


def angles(samples, freqs, count):
    phase = samples[:, None] * freqs[None, :] % count
    return phase.astype(np.float64) * (2.0 * math.pi / count)


def band_table(count, bins, first):
    angle = angles(np.arange(count), first + np.arange(bins), count)
    return np.concatenate([np.cos(angle), -np.sin(angle)], axis=1).astype(jnp.bfloat16)


BLOCK = 32


def table_seeds(count, bins, first, n_win):
    j = np.arange(bins // 4)
    turn = np.array([0.0, 0.5 * math.pi]).reshape(1, 2, 1)
    seeds, twice = [], []
    for m in range(4):
        freqs = np.broadcast_to((first + 4 * j + m).reshape(n_win, 1, -1), (n_win, 2, j.size // n_win))
        angle = angles(np.arange(2 * BLOCK), freqs.reshape(-1), count)
        angle = angle + np.broadcast_to(turn, freqs.shape).reshape(1, -1)
        seeds.append(np.cos(angle).reshape(2, BLOCK, -1))
        step = angles(np.full(8, BLOCK), freqs.reshape(-1), count)
        twice.append(2.0 * np.cos(step))
    return np.stack(seeds).astype(np.float32), np.stack(twice).astype(np.float32)


def make_tables(seed_ref, twice_ref, table_ref):
    for first in (0, 2):
        state = {}
        for m in (first, first + 1):
            twice = jnp.concatenate([twice_ref[m]] * (BLOCK // 8), axis=0)
            state[m] = (seed_ref[m, 0], seed_ref[m, 1], twice)
        for a in range(table_ref.shape[1] // BLOCK):
            for m, (here, after, twice) in state.items():
                table_ref[m, a * BLOCK:(a + 1) * BLOCK, :] = here.astype(jnp.bfloat16)
                state[m] = (after, twice * after - here, twice)


def in_hbm(value):
    return pltpu.with_memory_space_constraint(value, pltpu.HBM)


def order_sources(src_ref, r_dev, n_own, order_ref, plan_ref, flag_ref):
    n_src = src_ref.shape[0]
    size = order_ref.shape
    down = lax.broadcasted_iota(jnp.int32, size, 0).astype(jnp.float32)
    along = lax.broadcasted_iota(jnp.int32, size, 1).astype(jnp.float32)
    none = jnp.full(size, float(2**20), jnp.float32)
    column, row = none, none
    for s in range(n_src):
        station = src_ref[s].astype(jnp.float32)
        column = jnp.where(down == s, station, column)
        row = jnp.where(along == s, station, row)
    rank_along = jnp.sum((column < row).astype(jnp.float32), axis=0, keepdims=True)
    rank_down = jnp.sum((row < column).astype(jnp.float32), axis=1, keepdims=True)
    sorted_down = jnp.sum(jnp.where(rank_along == down, row, 0.0), axis=1, keepdims=True)
    at_place = rank_down == along
    sorted_along = jnp.sum(jnp.where(at_place, column, 0.0), axis=0, keepdims=True)
    source_along = jnp.sum(jnp.where(at_place, down, 0.0), axis=0, keepdims=True)
    order_ref[...] = jnp.broadcast_to(sorted_down, size)
    place = along[:1]
    owner, share = jnp.zeros_like(place), jnp.zeros_like(place)
    for z in range(1, n_src // n_own):
        owner = owner + (sorted_along >= z * r_dev).astype(jnp.float32)
        share = share + (place >= z * n_own).astype(jnp.float32)
    far = jnp.where((place < n_src) & (jnp.abs(owner - share) > 1.5), 1.0, 0.0)
    plan_ref[...] = jnp.broadcast_to(source_along, plan_ref.shape).astype(jnp.int32)
    flag_ref[0] = jnp.max(far).astype(jnp.int32)


def spectra_kernel(
    n_win, n_rcv, r_dev, valid_hbm, src_hbm, x_hbm, seed_hbm, twice_hbm, *refs
):
    r_refs = refs[:n_win]
    q_refs = refs[n_win:n_win + n_rcv]
    (plan_ref, flag_ref, x_ref, even_ref, odd_ref, white_ref, sel_ref, order_ref, table_ref,
     seed_ref, twice_ref, valid_ref, src_ref, sems, x_sems) = refs[n_win + n_rcv:]
    chunks, rows, samples = x_ref.shape
    w_step = rows // r_dev
    n_own = src_ref.shape[0] // n_rcv
    quarter = samples // 4
    win = lax.axis_index("win")
    rcv = lax.axis_index("rcv")

    def small(k):
        source = (seed_hbm, twice_hbm, src_hbm, valid_hbm)[k]
        target = (seed_ref, twice_ref, src_ref, valid_ref)[k]
        return pltpu.make_async_copy(source, target, sems.at[k])

    def chunk(k):
        return pltpu.make_async_copy(x_hbm.at[pl.ds(k * rows, rows)], x_ref.at[k], x_sems.at[k])

    for k in range(4):
        small(k).start()
    for k in range(chunks):
        chunk(k).start()
    small(0).wait()
    small(1).wait()
    make_tables(seed_ref, twice_ref, table_ref)
    small(2).wait()
    order_sources(src_ref, r_dev, n_own, order_ref, plan_ref, flag_ref)
    stations = []
    for d in range(n_rcv):
        share = pl.multiple_of((rcv ^ d) * n_own, n_own)
        stations += [order_ref[pl.ds(share, n_own), 0:1]] * w_step
    wanted = jnp.concatenate(stations, axis=0).astype(jnp.int32) - rcv * r_dev
    shape = (n_rcv * w_step * n_own, rows)
    out_row = lax.broadcasted_iota(jnp.int32, shape, 0)
    column = lax.broadcasted_iota(jnp.int32, shape, 1)
    inside = (wanted >= 0) & (wanted < r_dev)
    hit = inside & (column == wanted + (out_row // n_own) % w_step * r_dev)
    sel_ref[...] = hit.astype(jnp.float32).astype(jnp.bfloat16)
    small(3).wait()

    def product(lhs, table):
        return jnp.dot(lhs, table, preferred_element_type=jnp.float32)

    def add_quarters(k, first, last):
        part = slice(first, last)
        b0, b1, b2, b3 = (x_ref[k, part, q * quarter:(q + 1) * quarter] for q in range(4))
        first_sum, second_sum = b0 + b2, b1 + b3
        even_ref[k, 0, part] = first_sum + second_sum
        even_ref[k, 1, part] = first_sum - second_sum
        odd_ref[k, part] = b0 - b2
        odd_ref[k, rows + first:rows + last] = b1 - b3

    lanes = table_ref.shape[2]
    lane = lax.broadcasted_iota(jnp.int32, (rows, lanes), 1)
    piece = lanes // n_win
    real = lane % piece < piece // 2

    def odd_spectra(k, m):
        both = product(odd_ref[k], table_ref[m])
        second = both[rows:]
        back, forth = pltpu.roll(second, lanes - piece // 2, 1), pltpu.roll(second, piece // 2, 1)
        turned = jnp.where(real, back, -forth)
        return both[:rows] + turned if m == 1 else both[:rows] - turned

    parts = 4
    size = rows // parts
    chunk(0).wait()
    add_quarters(0, 0, rows)
    row = lax.broadcasted_iota(jnp.int32, (rows, 1), 0)
    for k in range(chunks):
        more = k + 1 < chunks
        if more:
            chunk(k + 1).wait()
        spectra = []
        for m in range(4):
            if m % 2:
                spectra.append(odd_spectra(k, m))
            else:
                spectra.append(product(even_ref[k, m // 2], table_ref[m]))
            if more:
                add_quarters(k + 1, m * size, (m + 1) * size)
        squares = sum(jnp.sum(s * s, axis=1, keepdims=True) for s in spectra)
        gain = lax.rsqrt(squares / F + 1e-06)
        keep = jnp.zeros((rows, 1), jnp.float32)
        for t in range(w_step):
            own = (row >= t * r_dev) & (row < (t + 1) * r_dev)
            keep = jnp.where(own, valid_ref[k * w_step + t].astype(jnp.float32), keep)
        gain = gain * keep
        white = [s * gain for s in spectra]
        for d in range(n_win):
            columns = slice(d * piece, (d + 1) * piece)
            block = jnp.concatenate([part[:, columns] for part in white], axis=1)
            white_ref[k, d] = block.astype(jnp.bfloat16)
        count = w_step * n_own
        for j in range(n_win):
            block = white_ref[k, win ^ j]
            r_refs[j][k * rows:(k + 1) * rows, :] = block
            picked = product(sel_ref[...], block).astype(jnp.bfloat16)
            for d in range(n_rcv):
                q_refs[d][j, k * count:(k + 1) * count, :] = picked[d * count:(d + 1) * count]


def spectra_call(traces, valid, src_station, n_win, n_rcv):
    w_dev, r_dev, samples = traces.shape
    n_src = src_station.shape[0]
    n_own = n_src // n_rcv
    chunks = 2
    every = w_dev * r_dev
    rows = every // chunks
    lanes = 2 * F // n_win
    seed, twice = (jnp.asarray(t) for t in table_seeds(samples, F, samples // 16, n_win))
    shapes = [jax.ShapeDtypeStruct((every, lanes), jnp.bfloat16)] * n_win
    shapes += [jax.ShapeDtypeStruct((n_win, w_dev * n_own, lanes), jnp.bfloat16)] * n_rcv
    shapes += [jax.ShapeDtypeStruct((8, 128), jnp.int32), jax.ShapeDtypeStruct((1,), jnp.int32)]
    vmem = pl.BlockSpec(memory_space=VMEM)
    out = pl.pallas_call(
        functools.partial(spectra_kernel, n_win, n_rcv, r_dev),
        in_specs=[pl.BlockSpec(memory_space=pltpu.HBM)] * 5,
        out_specs=[vmem] * (len(shapes) - 1) + [pl.BlockSpec(memory_space=SMEM)],
        out_shape=shapes,
        scratch_shapes=[
            pltpu.VMEM((chunks, rows, samples), jnp.bfloat16),
            pltpu.VMEM((chunks, 2, rows, samples // 4), jnp.bfloat16),
            pltpu.VMEM((chunks, 2 * rows, samples // 4), jnp.bfloat16),
            pltpu.VMEM((chunks, n_win, rows, lanes), jnp.bfloat16),
            pltpu.VMEM((n_src * (w_dev // chunks), rows), jnp.bfloat16),
            pltpu.VMEM((n_src, 128), jnp.float32),
            pltpu.VMEM((4, samples // 4, F // 2), jnp.bfloat16),
            pltpu.VMEM(seed.shape, jnp.float32),
            pltpu.VMEM(twice.shape, jnp.float32),
            pltpu.SMEM(valid.shape, jnp.int32),
            pltpu.SMEM(src_station.shape, jnp.int32),
            pltpu.SemaphoreType.DMA((4,)),
            pltpu.SemaphoreType.DMA((chunks,)),
        ],
        compiler_params=pltpu.CompilerParams(vmem_limit_bytes=36 * 2**20),
        cost_estimate=pl.CostEstimate(
            flops=2 * every * (samples // 4) * 6 * (F // 2), bytes_accessed=every * samples * 2,
            transcendentals=0,
        ),
        name="spectra",
    )(*(in_hbm(x) for x in (valid, src_station, traces.reshape(every, samples), seed, twice)))
    return out[:n_win], out[n_win:n_win + n_rcv], out[-2], out[-1]


def bin_order(lanes):
    quarter = lanes // 8
    lane = lax.broadcasted_iota(jnp.int32, (lanes, lanes), 1)
    row = lax.broadcasted_iota(jnp.int32, (lanes, lanes), 0)
    part = (lane // quarter) % 2
    bin_of = 4 * (lane % quarter) + lane // (2 * quarter)
    hit = row == part * (lanes // 2) + bin_of
    return hit.astype(jnp.float32).astype(jnp.bfloat16)


def turn_kernel(r_dev, *refs):
    x_refs, (out_ref, rows_ref) = refs[:-2], refs[-2:]
    lanes = x_refs[0].shape[1]
    bins = lanes // 2
    w_dev = out_ref.shape[1] // 2
    pad = out_ref.shape[2] // 2
    order = bin_order(lanes)
    windows = [(x, w) for x in x_refs for w in range(x.shape[0] // r_dev)]
    for k, (x_ref, w) in enumerate(windows):
        turned = lax.dot_general(
            order, x_ref[w * r_dev:(w + 1) * r_dev], (((1,), (1,)), ((), ())),
            preferred_element_type=jnp.float32,
        )
        rows_ref[pl.ds(k, lanes, stride=w_dev), :r_dev] = turned
    rr = rows_ref[:bins * w_dev].reshape(bins, w_dev, pad)
    ri = rows_ref[bins * w_dev:].reshape(bins, w_dev, pad)
    out_ref[:, :, :pad] = jnp.concatenate([rr, ri], axis=1).astype(jnp.bfloat16)
    out_ref[:, :, pad:] = jnp.concatenate([ri, -rr], axis=1).astype(jnp.bfloat16)


def turn_call(parts, w_dev, r_dev):
    lanes = parts[0].shape[1]
    pad = 128
    vmem = pl.BlockSpec(memory_space=VMEM)
    return pl.pallas_call(
        functools.partial(turn_kernel, r_dev),
        in_specs=[vmem] * len(parts),
        out_specs=vmem,
        out_shape=jax.ShapeDtypeStruct((lanes // 2, 2 * w_dev, 2 * pad), jnp.bfloat16),
        scratch_shapes=[pltpu.VMEM((lanes * w_dev, pad), jnp.float32)],
        compiler_params=pltpu.CompilerParams(vmem_limit_bytes=16 * 2**20),
        cost_estimate=pl.CostEstimate(
            flops=2 * w_dev * lanes * lanes * pad, bytes_accessed=2 * 2**20, transcendentals=0
        ),
        name="turn",
    )(*parts)


def merge_kernel(n_win, *refs):
    picked, outs = refs[:-n_win], refs[-n_win:]
    for j, out_ref in enumerate(outs):
        total = picked[0][j].astype(jnp.float32)
        for q_ref in picked[1:]:
            total = total + q_ref[j].astype(jnp.float32)
        out_ref[...] = total.astype(jnp.bfloat16)


def merge_call(*picked):
    n_win, rows, lanes = picked[0].shape
    vmem = pl.BlockSpec(memory_space=VMEM)
    return pl.pallas_call(
        functools.partial(merge_kernel, n_win),
        in_specs=[vmem] * len(picked),
        out_specs=[vmem] * n_win,
        out_shape=[jax.ShapeDtypeStruct((rows, lanes), jnp.bfloat16)] * n_win,
        compiler_params=pltpu.CompilerParams(vmem_limit_bytes=4 * 2**20),
        cost_estimate=pl.CostEstimate(flops=2**18, bytes_accessed=2**19, transcendentals=0),
        name="merge",
    )(*picked)


def lefts_kernel(n_win, w_dev, n_own, *refs):
    out_ref, srow_ref, rows_ref = refs[-3:]
    rows, lanes = refs[0].shape
    bins = lanes // 2
    windows = n_win * w_dev
    pad = rows_ref.shape[1]
    for j in range(n_win):
        block = refs[j][...].astype(jnp.float32)
        for h in range(lanes // pad):
            srow_ref[h, j * rows:(j + 1) * rows, :] = block[:, h * pad:(h + 1) * pad]

    lane = lax.broadcasted_iota(jnp.int32, (bins, lanes), 1)
    row = lax.broadcasted_iota(jnp.int32, (bins, lanes), 0)
    quarter = lanes // 8
    bin_of = 4 * (lane % quarter) + lane // (2 * quarter)
    pick = bin_of == 2 * (row % (bins // 2)) + row // (bins // 2)
    pick = pick.astype(jnp.float32).astype(jnp.bfloat16)
    real = (lane[:w_dev] // quarter) % 2 == 0
    low = lax.broadcasted_iota(jnp.int32, (bins // 2, pad), 1) < pad // 2
    for s in range(n_own):
        values = jnp.concatenate(
            [srow_ref[h, pl.ds(s, windows, stride=n_own), :] for h in range(lanes // pad)], axis=1
        )
        stacked = []
        for j in range(n_win):
            own = values[j * w_dev:(j + 1) * w_dev]
            stacked += [jnp.where(real, own, 0.0), jnp.where(real, 0.0, own)]
        stacked = jnp.concatenate(stacked * 2, axis=0).astype(jnp.bfloat16)
        turned = lax.dot_general(
            pick, stacked, (((1,), (1,)), ((), ())), preferred_element_type=jnp.float32
        )
        pairs = jnp.where(low, turned[:bins // 2], turned[bins // 2:])
        rows_ref[pl.ds(s, bins // 2, stride=n_own), :] = pairs
    out_ref[...] = rows_ref[...].reshape(out_ref.shape).astype(jnp.bfloat16)


def lefts_call(blocks, after, later, w_dev):
    rows, lanes = blocks[0].shape
    n_win = len(blocks)
    n_own = rows // w_dev
    pad = 128
    first = n_win + len(after)
    vmem, anywhere = pl.BlockSpec(memory_space=VMEM), pl.BlockSpec(memory_space=pl.ANY)
    out = pl.pallas_call(
        functools.partial(lefts_kernel, n_win, w_dev, n_own),
        in_specs=[vmem] * n_win + [anywhere] * (len(after) + len(later)),
        out_specs=[anywhere] * len(later) + [vmem],
        out_shape=[jax.ShapeDtypeStruct(x.shape, x.dtype) for x in later]
        + [jax.ShapeDtypeStruct((lanes // 8, 2 * n_own, pad), jnp.bfloat16)],
        input_output_aliases={first + k: k for k in range(len(later))},
        scratch_shapes=[
            pltpu.VMEM((lanes // pad, n_win * rows, pad), jnp.float32),
            pltpu.VMEM((lanes // 4 * n_own, pad), jnp.float32),
        ],
        compiler_params=pltpu.CompilerParams(vmem_limit_bytes=6 * 2**20),
        cost_estimate=pl.CostEstimate(flops=2**26, bytes_accessed=2**19, transcendentals=0),
        name="lefts",
    )(*blocks, *after, *later)
    return out[-1], out[:-1]


def gate_kernel(*refs):
    pass


def gate_call(after, arrays):
    anywhere = pl.BlockSpec(memory_space=pl.ANY)
    return pl.pallas_call(
        gate_kernel,
        in_specs=[anywhere] * (len(after) + len(arrays)),
        out_specs=[anywhere] * len(arrays),
        out_shape=[jax.ShapeDtypeStruct(x.shape, x.dtype) for x in arrays],
        input_output_aliases={len(after) + k: k for k in range(len(arrays))},
        compiler_params=pltpu.CompilerParams(vmem_limit_bytes=2**20),
        cost_estimate=pl.CostEstimate(flops=1, bytes_accessed=1, transcendentals=0),
        name="gate",
    )(*after, *arrays)


def stacks_kernel(shares, n_win, w_dev, r_dev, n_own, bins, plan_hbm, *refs):
    t_refs = refs[:n_win]
    s_refs = refs[n_win:n_win + len(shares)]
    out_hbm, prod_ref, out_ref, plan_ref, sems, plan_sem = refs[-6:]
    plan_copy = pltpu.make_async_copy(plan_hbm, plan_ref, plan_sem)
    plan_copy.start()
    windows = n_win * w_dev
    count = len(shares) * n_own
    pitch = prod_ref.shape[1] // bins
    pad = 128
    rcv = lax.axis_index("rcv")

    low = lax.broadcasted_iota(jnp.int32, (count, pad), 1) < pad // 2
    for group in range(bins // 4):
        values = [s_ref[group].astype(jnp.float32) for s_ref in s_refs]
        for p in range(2):
            rows = jnp.concatenate([v[p * n_own:(p + 1) * n_own] for v in values], axis=0)
            left = jnp.concatenate([jnp.where(low, rows, 0.0), jnp.where(low, 0.0, rows)], axis=0)
            first = 4 * group + 2 * p
            right = [t_ref[f] for f in (first, first + 1) for t_ref in t_refs]
            result = jnp.dot(
                left.astype(jnp.bfloat16), jnp.concatenate(right, axis=0),
                preferred_element_type=jnp.float32,
            )
            for k in range(2):
                for c in range(2):
                    block = result[k * count:(k + 1) * count, c * pad:(c + 1) * pad]
                    prod_ref[c, pl.ds((first + k) * pitch, count), :] = block

    scale = 1.0 / math.sqrt(windows)
    plan_copy.wait()
    copies = []
    for s in range(count):
        for c in range(2):
            turned = prod_ref[c, pl.ds(s, bins, stride=pitch), :].T
            out_ref[s, pl.ds(c, r_dev, stride=2), :] = turned[:r_dev] * scale
        row = plan_ref[0, (rcv ^ shares[s // n_own]) * n_own + s % n_own]
        copies.append(pltpu.make_async_copy(out_ref.at[s], out_hbm.at[row], sems.at[s]))
        copies[-1].start()
    for copy in copies:
        copy.wait()


def stacks_call(out, plan, turned, sources, shares, n_rcv, w_dev, r_dev, bins):
    n_win = len(turned)
    n_own = sources[0].shape[1] // 2
    windows = n_win * w_dev
    count = len(shares) * n_own
    whole = pl.BlockSpec(memory_space=VMEM)
    args = [plan] + list(turned) + [sources[i] for i in shares]
    specs = [pl.BlockSpec(memory_space=pl.ANY)] + [whole] * (len(args) - 1)
    aliases = {}
    if out is not None:
        aliases = {len(args): 0}
        args.append(out)
        specs.append(pl.BlockSpec(memory_space=pl.ANY))
    return pl.pallas_call(
        functools.partial(stacks_kernel, shares, n_win, w_dev, r_dev, n_own, bins),
        in_specs=specs,
        out_specs=pl.BlockSpec(memory_space=pltpu.HBM),
        out_shape=jax.ShapeDtypeStruct((n_rcv * n_own, 2 * r_dev, bins), jnp.float32),
        input_output_aliases=aliases,
        scratch_shapes=[
            pltpu.VMEM((2, (count // 8 | 1) * 8 * bins, 128), jnp.float32),
            pltpu.VMEM((count, 2 * r_dev, bins), jnp.float32),
            pltpu.SMEM(plan.shape, jnp.int32),
            pltpu.SemaphoreType.DMA((count,)),
            pltpu.SemaphoreType.DMA,
        ],
        compiler_params=pltpu.CompilerParams(vmem_limit_bytes=20 * 2**20),
        cost_estimate=pl.CostEstimate(
            flops=8 * windows * count * r_dev * bins, bytes_accessed=6 * 2**20, transcendentals=0
        ),
        name="stacks",
    )(*args)


def swap(value, axis, by):
    size = lax.axis_size(axis)
    return lax.ppermute(value, axis, [(i, i ^ by) for i in range(size)])


def near_and_far(n_rcv, by):
    pairs = [(z, z ^ by) for z in range(n_rcv)]
    return [p for p in pairs if abs(p[0] - p[1]) == 1], [p for p in pairs if abs(p[0] - p[1]) > 1]


def merge_near(picked, near):
    return merge_call(picked[0], *near)


def merge_all(picked, near):
    far = []
    for i in range(1, len(picked)):
        pairs = near_and_far(len(picked), i)[1]
        if pairs:
            far.append(lax.ppermute(picked[i], "rcv", pairs))
    return merge_call(picked[0], *near, *far)


def body(traces, valid, src_station):
    w_dev, r_dev, samples = traces.shape
    n_src = src_station.shape[0]
    n_win = lax.axis_size("win")
    n_rcv = lax.axis_size("rcv")
    bins = F // n_win
    early = n_win // 2

    blocks, picked, plan, flag = spectra_call(traces, valid, src_station, n_win, n_rcv)

    near = {}
    for i in range(1, n_rcv):
        pairs = near_and_far(n_rcv, i)[0]
        if pairs:
            near[i] = lax.ppermute(picked[i], "rcv", pairs)
    picked = [picked[0] + near.pop(n_rcv - 1)] + list(picked[1:])
    near = list(near.values())
    merged = lax.cond(flag.reshape(()) > 0, merge_all, merge_near, picked, near)

    merged = [merged[0]] + [swap(merged[j], "win", j) for j in range(1, n_win)]
    late = [j for j in range(1, n_win) if j != early]
    received = {0: blocks[0], early: swap(blocks[early], "win", early)}
    lefts, later = lefts_call(merged, [received[early]], [blocks[j] for j in late], w_dev)
    received.update({j: swap(block, "win", j) for j, block in zip(late, later)})
    sources = [lefts, swap(lefts, "rcv", 1), swap(lefts, "rcv", 2)]
    turned = [turn_call([received[j]], w_dev, r_dev) for j in range(n_win)]
    sources[2] = gate_call(turned[:-1], [sources[2]])[0]
    sources.append(swap(sources[2], "rcv", 1))

    sizes = (n_rcv, w_dev, r_dev, bins)
    stacks = stacks_call(None, plan, turned, sources, tuple(range(n_rcv - 1)), *sizes)
    stacks = stacks_call(stacks, plan, turned, sources, (n_rcv - 1,), *sizes)
    return stacks.reshape(n_src, r_dev, 2, bins)


def correlate(received, sources):
    rr = received[:, :, 0]
    ri = received[:, :, 1]
    sr = sources[:, :, 0]
    si = sources[:, :, 1]
    real = jnp.einsum("wsf,wrf->srf", sr, rr, preferred_element_type=jnp.float32)
    real = real + jnp.einsum("wsf,wrf->srf", si, ri, preferred_element_type=jnp.float32)
    imag = jnp.einsum("wsf,wrf->srf", sr, ri, preferred_element_type=jnp.float32)
    imag = imag - jnp.einsum("wsf,wrf->srf", si, rr, preferred_element_type=jnp.float32)
    return jnp.stack([real, imag], axis=2)


def body_any(traces, valid, src_station):
    w_dev, r_dev, samples = traces.shape
    n_win = lax.axis_size("win")
    n_rcv = lax.axis_size("rcv")
    bins = F // n_win
    table = jnp.asarray(band_table(samples, F, samples // 16))
    spectra = jnp.dot(
        traces.reshape(w_dev * r_dev, samples), table, preferred_element_type=jnp.float32
    )
    spectra = spectra.reshape(w_dev, r_dev, 2, F)
    power = jnp.sum(spectra * spectra, axis=(2, 3), keepdims=True) / F
    keep = valid.astype(jnp.float32)[:, None, None, None]
    white = (spectra * lax.rsqrt(power + 1e-06) * keep).astype(jnp.bfloat16)
    blocks = white.reshape(w_dev, r_dev, 2, n_win, bins).transpose(3, 0, 1, 2, 4)
    me = lax.axis_index("win")
    offset = lax.axis_index("rcv") * r_dev
    station_ids = offset + jnp.arange(r_dev, dtype=jnp.int32)
    selector = (src_station[:, None] == station_ids[None, :]).astype(jnp.bfloat16)
    received = []
    for j in range(n_win):
        block = lax.dynamic_index_in_dim(blocks, me ^ j, 0, keepdims=False)
        received.append(swap(block, "win", j) if j else block)
    received = jnp.concatenate(received, axis=0)
    rows = jnp.einsum("sr,wrcf->wscf", selector, received, preferred_element_type=jnp.float32)
    rows = lax.all_to_all(rows.astype(jnp.bfloat16), "rcv", 0, 0, tiled=True)
    rows = rows.reshape((n_rcv, -1) + rows.shape[1:])
    merged = jnp.sum(rows.astype(jnp.float32), axis=0).astype(jnp.bfloat16)
    sources = lax.all_gather(merged, "rcv", axis=0, tiled=True)
    return correlate(received, sources) * (1.0 / math.sqrt(w_dev * n_win))


def solution(mesh):
    sizes = (mesh.shape["win"], mesh.shape["rcv"])
    return jax.shard_map(
        body if sizes == (4, 4) else body_any,
        mesh=mesh,
        in_specs=(P("win", ("groups", "rcv"), None), P(("groups", "win")), P("groups")),
        out_specs=P(None, ("groups", "rcv"), None, "win"),
        check_vma=False,
    )
```

```python
import functools
import math

import jax
import jax.numpy as jnp
import numpy as np
from jax import lax
from jax.experimental import pallas as pl
from jax.experimental.pallas import tpu as pltpu
from jax.sharding import PartitionSpec as P

F = 512
SMEM = pltpu.MemorySpace.SMEM
VMEM = pltpu.MemorySpace.VMEM


def angles(samples, freqs, count):
    phase = samples[:, None] * freqs[None, :] % count
    return phase.astype(np.float64) * (2.0 * math.pi / count)


def band_table(count, bins, first):
    angle = angles(np.arange(count), first + np.arange(bins), count)
    return np.concatenate([np.cos(angle), -np.sin(angle)], axis=1).astype(jnp.bfloat16)


BLOCK = 32


def table_seeds(count, bins, first, n_win):
    j = np.arange(bins // 4)
    turn = np.array([0.0, 0.5 * math.pi]).reshape(1, 2, 1)
    seeds, twice = [], []
    for m in range(4):
        freqs = np.broadcast_to((first + 4 * j + m).reshape(n_win, 1, -1), (n_win, 2, j.size // n_win))
        angle = angles(np.arange(2 * BLOCK), freqs.reshape(-1), count)
        angle = angle + np.broadcast_to(turn, freqs.shape).reshape(1, -1)
        seeds.append(np.cos(angle).reshape(2, BLOCK, -1))
        step = angles(np.full(8, BLOCK), freqs.reshape(-1), count)
        twice.append(2.0 * np.cos(step))
    return np.stack(seeds).astype(np.float32), np.stack(twice).astype(np.float32)


def make_tables(seed_ref, twice_ref, table_ref):
    for first in (0, 2):
        state = {}
        for m in (first, first + 1):
            twice = jnp.concatenate([twice_ref[m]] * (BLOCK // 8), axis=0)
            state[m] = (seed_ref[m, 0], seed_ref[m, 1], twice)
        for a in range(table_ref.shape[1] // BLOCK):
            for m, (here, after, twice) in state.items():
                table_ref[m, a * BLOCK:(a + 1) * BLOCK, :] = here.astype(jnp.bfloat16)
                state[m] = (after, twice * after - here, twice)


def in_hbm(value):
    return pltpu.with_memory_space_constraint(value, pltpu.HBM)


def order_sources(src_ref, r_dev, n_own, order_ref, plan_ref, flag_ref):
    n_src = src_ref.shape[0]
    size = order_ref.shape
    down = lax.broadcasted_iota(jnp.int32, size, 0).astype(jnp.float32)
    along = lax.broadcasted_iota(jnp.int32, size, 1).astype(jnp.float32)
    none = jnp.full(size, float(2**20), jnp.float32)
    column, row = none, none
    for s in range(n_src):
        station = src_ref[s].astype(jnp.float32)
        column = jnp.where(down == s, station, column)
        row = jnp.where(along == s, station, row)
    rank_along = jnp.sum((column < row).astype(jnp.float32), axis=0, keepdims=True)
    rank_down = jnp.sum((row < column).astype(jnp.float32), axis=1, keepdims=True)
    sorted_down = jnp.sum(jnp.where(rank_along == down, row, 0.0), axis=1, keepdims=True)
    at_place = rank_down == along
    sorted_along = jnp.sum(jnp.where(at_place, column, 0.0), axis=0, keepdims=True)
    source_along = jnp.sum(jnp.where(at_place, down, 0.0), axis=0, keepdims=True)
    order_ref[...] = jnp.broadcast_to(sorted_down, size)
    place = along[:1]
    owner, share = jnp.zeros_like(place), jnp.zeros_like(place)
    for z in range(1, n_src // n_own):
        owner = owner + (sorted_along >= z * r_dev).astype(jnp.float32)
        share = share + (place >= z * n_own).astype(jnp.float32)
    far = jnp.where((place < n_src) & (jnp.abs(owner - share) > 1.5), 1.0, 0.0)
    plan_ref[...] = jnp.broadcast_to(source_along, plan_ref.shape).astype(jnp.int32)
    flag_ref[0] = jnp.max(far).astype(jnp.int32)


def spectra_kernel(
    n_win, n_rcv, r_dev, valid_hbm, src_hbm, x_hbm, seed_hbm, twice_hbm, *refs
):
    r_refs = refs[:n_win]
    q_refs = refs[n_win:n_win + n_rcv]
    (plan_ref, flag_ref, x_ref, even_ref, odd_ref, white_ref, sel_ref, order_ref, table_ref,
     seed_ref, twice_ref, valid_ref, src_ref, sems, x_sems) = refs[n_win + n_rcv:]
    chunks, rows, samples = x_ref.shape
    w_step = rows // r_dev
    n_own = src_ref.shape[0] // n_rcv
    quarter = samples // 4
    win = lax.axis_index("win")
    rcv = lax.axis_index("rcv")

    def small(k):
        source = (seed_hbm, twice_hbm, src_hbm, valid_hbm)[k]
        target = (seed_ref, twice_ref, src_ref, valid_ref)[k]
        return pltpu.make_async_copy(source, target, sems.at[k])

    pieces = x_sems.shape[1]
    height = rows // pieces

    def chunk(k, p):
        return pltpu.make_async_copy(
            x_hbm.at[pl.ds(k * rows + p * height, height)],
            x_ref.at[k, pl.ds(p * height, height)],
            x_sems.at[k, p],
        )

    def wait_for(k):
        for p in range(pieces):
            chunk(k, p).wait()

    for k in range(4):
        small(k).start()
    for k in range(chunks):
        for p in range(pieces):
            chunk(k, p).start()
    small(0).wait()
    small(1).wait()
    make_tables(seed_ref, twice_ref, table_ref)
    small(2).wait()
    order_sources(src_ref, r_dev, n_own, order_ref, plan_ref, flag_ref)
    stations = []
    for d in range(n_rcv):
        share = pl.multiple_of((rcv ^ d) * n_own, n_own)
        stations += [order_ref[pl.ds(share, n_own), 0:1]] * w_step
    wanted = jnp.concatenate(stations, axis=0).astype(jnp.int32) - rcv * r_dev
    shape = (n_rcv * w_step * n_own, rows)
    out_row = lax.broadcasted_iota(jnp.int32, shape, 0)
    column = lax.broadcasted_iota(jnp.int32, shape, 1)
    inside = (wanted >= 0) & (wanted < r_dev)
    hit = inside & (column == wanted + (out_row // n_own) % w_step * r_dev)
    sel_ref[...] = hit.astype(jnp.float32).astype(jnp.bfloat16)
    small(3).wait()

    def product(lhs, table):
        return jnp.dot(lhs, table, preferred_element_type=jnp.float32)

    def add_quarters(k, first, last):
        part = slice(first, last)
        b0, b1, b2, b3 = (x_ref[k, part, q * quarter:(q + 1) * quarter] for q in range(4))
        x0, x1, x2, x3 = (b.astype(jnp.float32) for b in (b0, b1, b2, b3))
        even_ref[k, 0, part] = ((x0 + x2) + (x1 + x3)).astype(jnp.bfloat16)
        even_ref[k, 1, part] = ((x0 + x2) - (x1 + x3)).astype(jnp.bfloat16)
        odd_ref[k, part] = b0 - b2
        odd_ref[k, rows + first:rows + last] = b1 - b3

    lanes = table_ref.shape[2]
    lane = lax.broadcasted_iota(jnp.int32, (rows, lanes), 1)
    piece = lanes // n_win
    real = lane % piece < piece // 2

    def odd_spectra(k, m):
        both = product(odd_ref[k], table_ref[m])
        second = both[rows:]
        back, forth = pltpu.roll(second, lanes - piece // 2, 1), pltpu.roll(second, piece // 2, 1)
        turned = jnp.where(real, back, -forth)
        return both[:rows] + turned if m == 1 else both[:rows] - turned

    parts = 4
    size = rows // parts
    wait_for(0)
    add_quarters(0, 0, rows)
    row = lax.broadcasted_iota(jnp.int32, (rows, 1), 0)
    for k in range(chunks):
        more = k + 1 < chunks
        if more:
            wait_for(k + 1)
        spectra = []
        for m in range(4):
            if m % 2:
                spectra.append(odd_spectra(k, m))
            else:
                spectra.append(product(even_ref[k, m // 2], table_ref[m]))
            if more:
                add_quarters(k + 1, m * size, (m + 1) * size)
        squares = sum(jnp.sum(s * s, axis=1, keepdims=True) for s in spectra)
        gain = lax.rsqrt(squares / F + 1e-06)
        keep = jnp.zeros((rows, 1), jnp.float32)
        for t in range(w_step):
            own = (row >= t * r_dev) & (row < (t + 1) * r_dev)
            keep = jnp.where(own, valid_ref[k * w_step + t].astype(jnp.float32), keep)
        gain = gain * keep
        white = [s * gain for s in spectra]
        for d in range(n_win):
            columns = slice(d * piece, (d + 1) * piece)
            block = jnp.concatenate([part[:, columns] for part in white], axis=1)
            white_ref[k, d] = block.astype(jnp.bfloat16)
        count = w_step * n_own
        for j in range(n_win):
            block = white_ref[k, win ^ j]
            r_refs[j][k * rows:(k + 1) * rows, :] = block
            picked = product(sel_ref[...], block).astype(jnp.bfloat16)
            for d in range(n_rcv):
                q_refs[d][j, k * count:(k + 1) * count, :] = picked[d * count:(d + 1) * count]


def spectra_call(traces, valid, src_station, n_win, n_rcv):
    w_dev, r_dev, samples = traces.shape
    n_src = src_station.shape[0]
    n_own = n_src // n_rcv
    chunks = 2
    every = w_dev * r_dev
    rows = every // chunks
    lanes = 2 * F // n_win
    seed, twice = (jnp.asarray(t) for t in table_seeds(samples, F, samples // 16, n_win))
    shapes = [jax.ShapeDtypeStruct((every, lanes), jnp.bfloat16)] * n_win
    shapes += [jax.ShapeDtypeStruct((n_win, w_dev * n_own, lanes), jnp.bfloat16)] * n_rcv
    shapes += [jax.ShapeDtypeStruct((8, 128), jnp.int32), jax.ShapeDtypeStruct((1,), jnp.int32)]
    vmem = pl.BlockSpec(memory_space=VMEM)
    out = pl.pallas_call(
        functools.partial(spectra_kernel, n_win, n_rcv, r_dev),
        in_specs=[pl.BlockSpec(memory_space=pltpu.HBM)] * 5,
        out_specs=[vmem] * (len(shapes) - 1) + [pl.BlockSpec(memory_space=SMEM)],
        out_shape=shapes,
        scratch_shapes=[
            pltpu.VMEM((chunks, rows, samples), jnp.bfloat16),
            pltpu.VMEM((chunks, 2, rows, samples // 4), jnp.bfloat16),
            pltpu.VMEM((chunks, 2 * rows, samples // 4), jnp.bfloat16),
            pltpu.VMEM((chunks, n_win, rows, lanes), jnp.bfloat16),
            pltpu.VMEM((n_src * (w_dev // chunks), rows), jnp.bfloat16),
            pltpu.VMEM((n_src, 128), jnp.float32),
            pltpu.VMEM((4, samples // 4, F // 2), jnp.bfloat16),
            pltpu.VMEM(seed.shape, jnp.float32),
            pltpu.VMEM(twice.shape, jnp.float32),
            pltpu.SMEM(valid.shape, jnp.int32),
            pltpu.SMEM(src_station.shape, jnp.int32),
            pltpu.SemaphoreType.DMA((4,)),
            pltpu.SemaphoreType.DMA((chunks, 4)),
        ],
        compiler_params=pltpu.CompilerParams(vmem_limit_bytes=36 * 2**20),
        cost_estimate=pl.CostEstimate(
            flops=2 * every * (samples // 4) * 6 * (F // 2), bytes_accessed=every * samples * 2,
            transcendentals=0,
        ),
        name="spectra",
    )(*(in_hbm(x) for x in (valid, src_station, traces.reshape(every, samples), seed, twice)))
    return out[:n_win], out[n_win:n_win + n_rcv], out[-2], out[-1]


def bin_order(lanes):
    quarter = lanes // 8
    lane = lax.broadcasted_iota(jnp.int32, (lanes, lanes), 1)
    row = lax.broadcasted_iota(jnp.int32, (lanes, lanes), 0)
    part = (lane // quarter) % 2
    bin_of = 4 * (lane % quarter) + lane // (2 * quarter)
    hit = row == part * (lanes // 2) + bin_of
    return hit.astype(jnp.float32).astype(jnp.bfloat16)


def turn_kernel(r_dev, *refs):
    x_refs, (out_ref, rows_ref) = refs[:-2], refs[-2:]
    lanes = x_refs[0].shape[1]
    bins = lanes // 2
    w_dev = out_ref.shape[1] // 2
    pad = out_ref.shape[2] // 2
    order = bin_order(lanes)
    windows = [(x, w) for x in x_refs for w in range(x.shape[0] // r_dev)]
    for k, (x_ref, w) in enumerate(windows):
        turned = lax.dot_general(
            order, x_ref[w * r_dev:(w + 1) * r_dev], (((1,), (1,)), ((), ())),
            preferred_element_type=jnp.float32,
        )
        rows_ref[pl.ds(k, lanes, stride=w_dev), :r_dev] = turned
    rr = rows_ref[:bins * w_dev].reshape(bins, w_dev, pad)
    ri = rows_ref[bins * w_dev:].reshape(bins, w_dev, pad)
    out_ref[:, :, :pad] = jnp.concatenate([rr, ri], axis=1).astype(jnp.bfloat16)
    out_ref[:, :, pad:] = jnp.concatenate([ri, -rr], axis=1).astype(jnp.bfloat16)


def turn_call(parts, w_dev, r_dev):
    lanes = parts[0].shape[1]
    pad = 128
    vmem = pl.BlockSpec(memory_space=VMEM)
    return pl.pallas_call(
        functools.partial(turn_kernel, r_dev),
        in_specs=[vmem] * len(parts),
        out_specs=vmem,
        out_shape=jax.ShapeDtypeStruct((lanes // 2, 2 * w_dev, 2 * pad), jnp.bfloat16),
        scratch_shapes=[pltpu.VMEM((lanes * w_dev, pad), jnp.float32)],
        compiler_params=pltpu.CompilerParams(vmem_limit_bytes=16 * 2**20),
        cost_estimate=pl.CostEstimate(
            flops=2 * w_dev * lanes * lanes * pad, bytes_accessed=2 * 2**20, transcendentals=0
        ),
        name="turn",
    )(*parts)


def merge_kernel(n_win, *refs):
    picked, outs = refs[:-n_win], refs[-n_win:]
    for j, out_ref in enumerate(outs):
        total = picked[0][j].astype(jnp.float32)
        for q_ref in picked[1:]:
            total = total + q_ref[j].astype(jnp.float32)
        out_ref[...] = total.astype(jnp.bfloat16)


def merge_call(*picked):
    n_win, rows, lanes = picked[0].shape
    vmem = pl.BlockSpec(memory_space=VMEM)
    return pl.pallas_call(
        functools.partial(merge_kernel, n_win),
        in_specs=[vmem] * len(picked),
        out_specs=[vmem] * n_win,
        out_shape=[jax.ShapeDtypeStruct((rows, lanes), jnp.bfloat16)] * n_win,
        compiler_params=pltpu.CompilerParams(vmem_limit_bytes=4 * 2**20),
        cost_estimate=pl.CostEstimate(flops=2**18, bytes_accessed=2**19, transcendentals=0),
        name="merge",
    )(*picked)


def lefts_kernel(n_win, w_dev, n_own, *refs):
    out_ref, srow_ref, rows_ref = refs[-3:]
    rows, lanes = refs[0].shape
    bins = lanes // 2
    windows = n_win * w_dev
    pad = rows_ref.shape[1]
    for j in range(n_win):
        block = refs[j][...].astype(jnp.float32)
        for h in range(lanes // pad):
            srow_ref[h, j * rows:(j + 1) * rows, :] = block[:, h * pad:(h + 1) * pad]

    lane = lax.broadcasted_iota(jnp.int32, (bins, lanes), 1)
    row = lax.broadcasted_iota(jnp.int32, (bins, lanes), 0)
    quarter = lanes // 8
    bin_of = 4 * (lane % quarter) + lane // (2 * quarter)
    pick = bin_of == 2 * (row % (bins // 2)) + row // (bins // 2)
    pick = pick.astype(jnp.float32).astype(jnp.bfloat16)
    real = (lane[:w_dev] // quarter) % 2 == 0
    low = lax.broadcasted_iota(jnp.int32, (bins // 2, pad), 1) < pad // 2
    for s in range(n_own):
        values = jnp.concatenate(
            [srow_ref[h, pl.ds(s, windows, stride=n_own), :] for h in range(lanes // pad)], axis=1
        )
        stacked = []
        for j in range(n_win):
            own = values[j * w_dev:(j + 1) * w_dev]
            stacked += [jnp.where(real, own, 0.0), jnp.where(real, 0.0, own)]
        stacked = jnp.concatenate(stacked * 2, axis=0).astype(jnp.bfloat16)
        turned = lax.dot_general(
            pick, stacked, (((1,), (1,)), ((), ())), preferred_element_type=jnp.float32
        )
        pairs = jnp.where(low, turned[:bins // 2], turned[bins // 2:])
        rows_ref[pl.ds(s, bins // 2, stride=n_own), :] = pairs
    out_ref[...] = rows_ref[...].reshape(out_ref.shape).astype(jnp.bfloat16)


def lefts_call(blocks, after, later, w_dev):
    rows, lanes = blocks[0].shape
    n_win = len(blocks)
    n_own = rows // w_dev
    pad = 128
    first = n_win + len(after)
    vmem, anywhere = pl.BlockSpec(memory_space=VMEM), pl.BlockSpec(memory_space=pl.ANY)
    out = pl.pallas_call(
        functools.partial(lefts_kernel, n_win, w_dev, n_own),
        in_specs=[vmem] * n_win + [anywhere] * (len(after) + len(later)),
        out_specs=[anywhere] * len(later) + [vmem],
        out_shape=[jax.ShapeDtypeStruct(x.shape, x.dtype) for x in later]
        + [jax.ShapeDtypeStruct((lanes // 8, 2 * n_own, pad), jnp.bfloat16)],
        input_output_aliases={first + k: k for k in range(len(later))},
        scratch_shapes=[
            pltpu.VMEM((lanes // pad, n_win * rows, pad), jnp.float32),
            pltpu.VMEM((lanes // 4 * n_own, pad), jnp.float32),
        ],
        compiler_params=pltpu.CompilerParams(vmem_limit_bytes=6 * 2**20),
        cost_estimate=pl.CostEstimate(flops=2**26, bytes_accessed=2**19, transcendentals=0),
        name="lefts",
    )(*blocks, *after, *later)
    return out[-1], out[:-1]


def gate_kernel(*refs):
    pass


def gate_call(after, arrays):
    anywhere = pl.BlockSpec(memory_space=pl.ANY)
    return pl.pallas_call(
        gate_kernel,
        in_specs=[anywhere] * (len(after) + len(arrays)),
        out_specs=[anywhere] * len(arrays),
        out_shape=[jax.ShapeDtypeStruct(x.shape, x.dtype) for x in arrays],
        input_output_aliases={len(after) + k: k for k in range(len(arrays))},
        compiler_params=pltpu.CompilerParams(vmem_limit_bytes=2**20),
        cost_estimate=pl.CostEstimate(flops=1, bytes_accessed=1, transcendentals=0),
        name="gate",
    )(*after, *arrays)


def stacks_kernel(shares, n_win, w_dev, r_dev, n_own, bins, plan_hbm, *refs):
    t_refs = refs[:n_win]
    s_refs = refs[n_win:n_win + len(shares)]
    out_hbm, prod_ref, out_ref, plan_ref, sems, plan_sem = refs[-6:]
    plan_copy = pltpu.make_async_copy(plan_hbm, plan_ref, plan_sem)
    plan_copy.start()
    windows = n_win * w_dev
    count = len(shares) * n_own
    pitch = prod_ref.shape[1] // bins
    pad = 128
    rcv = lax.axis_index("rcv")

    low = lax.broadcasted_iota(jnp.int32, (count, pad), 1) < pad // 2
    for group in range(bins // 4):
        values = [s_ref[group].astype(jnp.float32) for s_ref in s_refs]
        for p in range(2):
            rows = jnp.concatenate([v[p * n_own:(p + 1) * n_own] for v in values], axis=0)
            left = jnp.concatenate([jnp.where(low, rows, 0.0), jnp.where(low, 0.0, rows)], axis=0)
            first = 4 * group + 2 * p
            right = [t_ref[f] for f in (first, first + 1) for t_ref in t_refs]
            result = jnp.dot(
                left.astype(jnp.bfloat16), jnp.concatenate(right, axis=0),
                preferred_element_type=jnp.float32,
            )
            for k in range(2):
                for c in range(2):
                    block = result[k * count:(k + 1) * count, c * pad:(c + 1) * pad]
                    prod_ref[c, pl.ds((first + k) * pitch, count), :] = block

    scale = 1.0 / math.sqrt(windows)
    plan_copy.wait()
    copies = []
    for s in range(count):
        for c in range(2):
            turned = prod_ref[c, pl.ds(s, bins, stride=pitch), :].T
            out_ref[s, pl.ds(c, r_dev, stride=2), :] = turned[:r_dev] * scale
        row = plan_ref[0, (rcv ^ shares[s // n_own]) * n_own + s % n_own]
        copies.append(pltpu.make_async_copy(out_ref.at[s], out_hbm.at[row], sems.at[s]))
        copies[-1].start()
    for copy in copies:
        copy.wait()


def stacks_call(out, plan, turned, sources, shares, n_rcv, w_dev, r_dev, bins):
    n_win = len(turned)
    n_own = sources[0].shape[1] // 2
    windows = n_win * w_dev
    count = len(shares) * n_own
    whole = pl.BlockSpec(memory_space=VMEM)
    args = [plan] + list(turned) + [sources[i] for i in shares]
    specs = [pl.BlockSpec(memory_space=pl.ANY)] + [whole] * (len(args) - 1)
    aliases = {}
    if out is not None:
        aliases = {len(args): 0}
        args.append(out)
        specs.append(pl.BlockSpec(memory_space=pl.ANY))
    return pl.pallas_call(
        functools.partial(stacks_kernel, shares, n_win, w_dev, r_dev, n_own, bins),
        in_specs=specs,
        out_specs=pl.BlockSpec(memory_space=pltpu.HBM),
        out_shape=jax.ShapeDtypeStruct((n_rcv * n_own, 2 * r_dev, bins), jnp.float32),
        input_output_aliases=aliases,
        scratch_shapes=[
            pltpu.VMEM((2, (count // 8 | 1) * 8 * bins, 128), jnp.float32),
            pltpu.VMEM((count, 2 * r_dev, bins), jnp.float32),
            pltpu.SMEM(plan.shape, jnp.int32),
            pltpu.SemaphoreType.DMA((count,)),
            pltpu.SemaphoreType.DMA,
        ],
        compiler_params=pltpu.CompilerParams(vmem_limit_bytes=20 * 2**20),
        cost_estimate=pl.CostEstimate(
            flops=8 * windows * count * r_dev * bins, bytes_accessed=6 * 2**20, transcendentals=0
        ),
        name="stacks",
    )(*args)


def swap(value, axis, by):
    size = lax.axis_size(axis)
    return lax.ppermute(value, axis, [(i, i ^ by) for i in range(size)])


def near_and_far(n_rcv, by):
    pairs = [(z, z ^ by) for z in range(n_rcv)]
    return [p for p in pairs if abs(p[0] - p[1]) == 1], [p for p in pairs if abs(p[0] - p[1]) > 1]


def merge_near(picked, near):
    return merge_call(picked[0], *near)


def merge_all(picked, near):
    far = []
    for i in range(1, len(picked)):
        pairs = near_and_far(len(picked), i)[1]
        if pairs:
            far.append(lax.ppermute(picked[i], "rcv", pairs))
    return merge_call(picked[0], *near, *far)


def body(traces, valid, src_station):
    w_dev, r_dev, samples = traces.shape
    n_src = src_station.shape[0]
    n_win = lax.axis_size("win")
    n_rcv = lax.axis_size("rcv")
    bins = F // n_win
    early = n_win // 2

    blocks, picked, plan, flag = spectra_call(traces, valid, src_station, n_win, n_rcv)

    near = {}
    for i in range(1, n_rcv):
        pairs = near_and_far(n_rcv, i)[0]
        if pairs:
            near[i] = lax.ppermute(picked[i], "rcv", pairs)
    picked = [picked[0] + near.pop(n_rcv - 1)] + list(picked[1:])
    near = list(near.values())
    merged = lax.cond(flag.reshape(()) > 0, merge_all, merge_near, picked, near)

    merged = [merged[0]] + [swap(merged[j], "win", j) for j in range(1, n_win)]
    late = [j for j in range(1, n_win) if j != early]
    received = {0: blocks[0], early: swap(blocks[early], "win", early)}
    lefts, later = lefts_call(merged, [received[early]], [blocks[j] for j in late], w_dev)
    received.update({j: swap(block, "win", j) for j, block in zip(late, later)})
    sources = [lefts, swap(lefts, "rcv", 1), swap(lefts, "rcv", 2)]
    turned = [turn_call([received[j]], w_dev, r_dev) for j in range(n_win)]
    sources[2] = gate_call(turned[:-1], [sources[2]])[0]
    sources.append(swap(sources[2], "rcv", 1))

    sizes = (n_rcv, w_dev, r_dev, bins)
    stacks = stacks_call(None, plan, turned, sources, tuple(range(n_rcv - 1)), *sizes)
    stacks = stacks_call(stacks, plan, turned, sources, (n_rcv - 1,), *sizes)
    return stacks.reshape(n_src, r_dev, 2, bins)


def correlate(received, sources):
    rr = received[:, :, 0]
    ri = received[:, :, 1]
    sr = sources[:, :, 0]
    si = sources[:, :, 1]
    real = jnp.einsum("wsf,wrf->srf", sr, rr, preferred_element_type=jnp.float32)
    real = real + jnp.einsum("wsf,wrf->srf", si, ri, preferred_element_type=jnp.float32)
    imag = jnp.einsum("wsf,wrf->srf", sr, ri, preferred_element_type=jnp.float32)
    imag = imag - jnp.einsum("wsf,wrf->srf", si, rr, preferred_element_type=jnp.float32)
    return jnp.stack([real, imag], axis=2)


def body_any(traces, valid, src_station):
    w_dev, r_dev, samples = traces.shape
    n_win = lax.axis_size("win")
    n_rcv = lax.axis_size("rcv")
    bins = F // n_win
    table = jnp.asarray(band_table(samples, F, samples // 16))
    spectra = jnp.dot(
        traces.reshape(w_dev * r_dev, samples), table, preferred_element_type=jnp.float32
    )
    spectra = spectra.reshape(w_dev, r_dev, 2, F)
    power = jnp.sum(spectra * spectra, axis=(2, 3), keepdims=True) / F
    keep = valid.astype(jnp.float32)[:, None, None, None]
    white = (spectra * lax.rsqrt(power + 1e-06) * keep).astype(jnp.bfloat16)
    blocks = white.reshape(w_dev, r_dev, 2, n_win, bins).transpose(3, 0, 1, 2, 4)
    me = lax.axis_index("win")
    offset = lax.axis_index("rcv") * r_dev
    station_ids = offset + jnp.arange(r_dev, dtype=jnp.int32)
    selector = (src_station[:, None] == station_ids[None, :]).astype(jnp.bfloat16)
    received = []
    for j in range(n_win):
        block = lax.dynamic_index_in_dim(blocks, me ^ j, 0, keepdims=False)
        received.append(swap(block, "win", j) if j else block)
    received = jnp.concatenate(received, axis=0)
    rows = jnp.einsum("sr,wrcf->wscf", selector, received, preferred_element_type=jnp.float32)
    rows = lax.all_to_all(rows.astype(jnp.bfloat16), "rcv", 0, 0, tiled=True)
    rows = rows.reshape((n_rcv, -1) + rows.shape[1:])
    merged = jnp.sum(rows.astype(jnp.float32), axis=0).astype(jnp.bfloat16)
    sources = lax.all_gather(merged, "rcv", axis=0, tiled=True)
    return correlate(received, sources) * (1.0 / math.sqrt(w_dev * n_win))


def solution(mesh):
    sizes = (mesh.shape["win"], mesh.shape["rcv"])
    return jax.shard_map(
        body if sizes == (4, 4) else body_any,
        mesh=mesh,
        in_specs=(P("win", ("groups", "rcv"), None), P(("groups", "win")), P("groups")),
        out_specs=P(None, ("groups", "rcv"), None, "win"),
        check_vma=False,
    )
```

```python
import functools
import math

import jax
import jax.numpy as jnp
import numpy as np
from jax import lax
from jax.experimental import pallas as pl
from jax.experimental.pallas import tpu as pltpu
from jax.sharding import PartitionSpec as P

F = 512
SMEM = pltpu.MemorySpace.SMEM
VMEM = pltpu.MemorySpace.VMEM


def angles(samples, freqs, count):
    phase = samples[:, None] * freqs[None, :] % count
    return phase.astype(np.float64) * (2.0 * math.pi / count)


def band_table(count, bins, first):
    angle = angles(np.arange(count), first + np.arange(bins), count)
    return np.concatenate([np.cos(angle), -np.sin(angle)], axis=1).astype(jnp.bfloat16)


BLOCK = 32


def table_seeds(count, bins, first, n_win):
    j = np.arange(bins // 4)
    turn = np.array([0.0, 0.5 * math.pi]).reshape(1, 2, 1)
    seeds, twice = [], []
    for m in range(4):
        freqs = np.broadcast_to((first + 4 * j + m).reshape(n_win, 1, -1), (n_win, 2, j.size // n_win))
        angle = angles(np.arange(2 * BLOCK), freqs.reshape(-1), count)
        angle = angle + np.broadcast_to(turn, freqs.shape).reshape(1, -1)
        seeds.append(np.cos(angle).reshape(2, BLOCK, -1))
        step = angles(np.full(8, BLOCK), freqs.reshape(-1), count)
        twice.append(2.0 * np.cos(step))
    return np.stack(seeds).astype(np.float32), np.stack(twice).astype(np.float32)


def make_tables(seed_ref, twice_ref, table_ref):
    for first in (0, 2):
        state = {}
        for m in (first, first + 1):
            twice = jnp.concatenate([twice_ref[m]] * (BLOCK // 8), axis=0)
            state[m] = (seed_ref[m, 0], seed_ref[m, 1], twice)
        for a in range(table_ref.shape[1] // BLOCK):
            for m, (here, after, twice) in state.items():
                table_ref[m, a * BLOCK:(a + 1) * BLOCK, :] = here.astype(jnp.bfloat16)
                state[m] = (after, twice * after - here, twice)


def in_hbm(value):
    return pltpu.with_memory_space_constraint(value, pltpu.HBM)


def order_sources(src_ref, r_dev, n_own, order_ref, plan_ref, flag_ref):
    n_src = src_ref.shape[0]
    size = order_ref.shape
    down = lax.broadcasted_iota(jnp.int32, size, 0).astype(jnp.float32)
    along = lax.broadcasted_iota(jnp.int32, size, 1).astype(jnp.float32)
    none = jnp.full(size, float(2**20), jnp.float32)
    column, row = none, none
    for s in range(n_src):
        station = src_ref[s].astype(jnp.float32)
        column = jnp.where(down == s, station, column)
        row = jnp.where(along == s, station, row)
    rank_along = jnp.sum((column < row).astype(jnp.float32), axis=0, keepdims=True)
    rank_down = jnp.sum((row < column).astype(jnp.float32), axis=1, keepdims=True)
    sorted_down = jnp.sum(jnp.where(rank_along == down, row, 0.0), axis=1, keepdims=True)
    at_place = rank_down == along
    sorted_along = jnp.sum(jnp.where(at_place, column, 0.0), axis=0, keepdims=True)
    source_along = jnp.sum(jnp.where(at_place, down, 0.0), axis=0, keepdims=True)
    order_ref[...] = jnp.broadcast_to(sorted_down, size)
    place = along[:1]
    owner, share = jnp.zeros_like(place), jnp.zeros_like(place)
    for z in range(1, n_src // n_own):
        owner = owner + (sorted_along >= z * r_dev).astype(jnp.float32)
        share = share + (place >= z * n_own).astype(jnp.float32)
    far = jnp.where((place < n_src) & (jnp.abs(owner - share) > 1.5), 1.0, 0.0)
    plan_ref[...] = jnp.broadcast_to(source_along, plan_ref.shape).astype(jnp.int32)
    flag_ref[0] = jnp.max(far).astype(jnp.int32)


def spectra_kernel(
    n_win, n_rcv, r_dev, valid_hbm, src_hbm, x_hbm, seed_hbm, twice_hbm, *refs
):
    r_refs = refs[:n_win]
    q_refs = refs[n_win:n_win + n_rcv]
    (plan_ref, flag_ref, x_ref, even_ref, odd_ref, white_ref, sel_ref, order_ref, table_ref,
     seed_ref, twice_ref, valid_ref, src_ref, sems, x_sems) = refs[n_win + n_rcv:]
    chunks, rows, samples = x_ref.shape
    w_step = rows // r_dev
    n_own = src_ref.shape[0] // n_rcv
    quarter = samples // 4
    win = lax.axis_index("win")
    rcv = lax.axis_index("rcv")

    def small(k):
        source = (seed_hbm, twice_hbm, src_hbm, valid_hbm)[k]
        target = (seed_ref, twice_ref, src_ref, valid_ref)[k]
        return pltpu.make_async_copy(source, target, sems.at[k])

    def chunk(k):
        return pltpu.make_async_copy(x_hbm.at[pl.ds(k * rows, rows)], x_ref.at[k], x_sems.at[k])

    for k in range(4):
        small(k).start()
    for k in range(chunks):
        chunk(k).start()
    small(0).wait()
    small(1).wait()
    make_tables(seed_ref, twice_ref, table_ref)
    small(2).wait()
    order_sources(src_ref, r_dev, n_own, order_ref, plan_ref, flag_ref)
    stations = []
    for d in range(n_rcv):
        share = pl.multiple_of((rcv ^ d) * n_own, n_own)
        stations += [order_ref[pl.ds(share, n_own), 0:1]] * w_step
    wanted = jnp.concatenate(stations, axis=0).astype(jnp.int32) - rcv * r_dev
    shape = (n_rcv * w_step * n_own, rows)
    out_row = lax.broadcasted_iota(jnp.int32, shape, 0)
    column = lax.broadcasted_iota(jnp.int32, shape, 1)
    inside = (wanted >= 0) & (wanted < r_dev)
    hit = inside & (column == wanted + (out_row // n_own) % w_step * r_dev)
    sel_ref[...] = hit.astype(jnp.float32).astype(jnp.bfloat16)
    small(3).wait()

    def product(lhs, table):
        return jnp.dot(lhs, table, preferred_element_type=jnp.float32)

    def add_quarters(k, first, last):
        part = slice(first, last)
        b0, b1, b2, b3 = (x_ref[k, part, q * quarter:(q + 1) * quarter] for q in range(4))
        x0, x1, x2, x3 = (b.astype(jnp.float32) for b in (b0, b1, b2, b3))
        even_ref[k, 0, part] = ((x0 + x2) + (x1 + x3)).astype(jnp.bfloat16)
        even_ref[k, 1, part] = ((x0 + x2) - (x1 + x3)).astype(jnp.bfloat16)
        odd_ref[k, part] = b0 - b2
        odd_ref[k, rows + first:rows + last] = b1 - b3

    lanes = table_ref.shape[2]
    lane = lax.broadcasted_iota(jnp.int32, (rows, lanes), 1)
    piece = lanes // n_win
    real = lane % piece < piece // 2

    def odd_spectra(k, m):
        both = product(odd_ref[k], table_ref[m])
        second = both[rows:]
        back, forth = pltpu.roll(second, lanes - piece // 2, 1), pltpu.roll(second, piece // 2, 1)
        turned = jnp.where(real, back, -forth)
        return both[:rows] + turned if m == 1 else both[:rows] - turned

    parts = 4
    size = rows // parts
    chunk(0).wait()
    add_quarters(0, 0, rows)
    row = lax.broadcasted_iota(jnp.int32, (rows, 1), 0)
    for k in range(chunks):
        more = k + 1 < chunks
        if more:
            chunk(k + 1).wait()
        spectra = []
        for m in range(4):
            if m % 2:
                spectra.append(odd_spectra(k, m))
            else:
                spectra.append(product(even_ref[k, m // 2], table_ref[m]))
            if more:
                add_quarters(k + 1, m * size, (m + 1) * size)
        squares = sum(jnp.sum(s * s, axis=1, keepdims=True) for s in spectra)
        gain = lax.rsqrt(squares / F + 1e-06)
        keep = jnp.zeros((rows, 1), jnp.float32)
        for t in range(w_step):
            own = (row >= t * r_dev) & (row < (t + 1) * r_dev)
            keep = jnp.where(own, valid_ref[k * w_step + t].astype(jnp.float32), keep)
        gain = gain * keep
        white = [s * gain for s in spectra]
        for d in range(n_win):
            columns = slice(d * piece, (d + 1) * piece)
            block = jnp.concatenate([part[:, columns] for part in white], axis=1)
            white_ref[k, d] = block.astype(jnp.bfloat16)
        count = w_step * n_own
        for j in range(n_win):
            block = white_ref[k, win ^ j]
            r_refs[j][k * rows:(k + 1) * rows, :] = block
            picked = product(sel_ref[...], block).astype(jnp.bfloat16)
            for d in range(n_rcv):
                q_refs[d][j, k * count:(k + 1) * count, :] = picked[d * count:(d + 1) * count]


def spectra_call(traces, valid, src_station, n_win, n_rcv):
    w_dev, r_dev, samples = traces.shape
    n_src = src_station.shape[0]
    n_own = n_src // n_rcv
    chunks = 2
    every = w_dev * r_dev
    rows = every // chunks
    lanes = 2 * F // n_win
    seed, twice = (jnp.asarray(t) for t in table_seeds(samples, F, samples // 16, n_win))
    shapes = [jax.ShapeDtypeStruct((every, lanes), jnp.bfloat16)] * n_win
    shapes += [jax.ShapeDtypeStruct((n_win, w_dev * n_own, lanes), jnp.bfloat16)] * n_rcv
    shapes += [jax.ShapeDtypeStruct((8, 128), jnp.int32), jax.ShapeDtypeStruct((1,), jnp.int32)]
    vmem = pl.BlockSpec(memory_space=VMEM)
    out = pl.pallas_call(
        functools.partial(spectra_kernel, n_win, n_rcv, r_dev),
        in_specs=[pl.BlockSpec(memory_space=pltpu.HBM)] * 5,
        out_specs=[vmem] * (len(shapes) - 1) + [pl.BlockSpec(memory_space=SMEM)],
        out_shape=shapes,
        scratch_shapes=[
            pltpu.VMEM((chunks, rows, samples), jnp.bfloat16),
            pltpu.VMEM((chunks, 2, rows, samples // 4), jnp.bfloat16),
            pltpu.VMEM((chunks, 2 * rows, samples // 4), jnp.bfloat16),
            pltpu.VMEM((chunks, n_win, rows, lanes), jnp.bfloat16),
            pltpu.VMEM((n_src * (w_dev // chunks), rows), jnp.bfloat16),
            pltpu.VMEM((n_src, 128), jnp.float32),
            pltpu.VMEM((4, samples // 4, F // 2), jnp.bfloat16),
            pltpu.VMEM(seed.shape, jnp.float32),
            pltpu.VMEM(twice.shape, jnp.float32),
            pltpu.SMEM(valid.shape, jnp.int32),
            pltpu.SMEM(src_station.shape, jnp.int32),
            pltpu.SemaphoreType.DMA((4,)),
            pltpu.SemaphoreType.DMA((chunks,)),
        ],
        compiler_params=pltpu.CompilerParams(vmem_limit_bytes=36 * 2**20),
        cost_estimate=pl.CostEstimate(
            flops=2 * every * (samples // 4) * 6 * (F // 2), bytes_accessed=every * samples * 2,
            transcendentals=0,
        ),
        name="spectra",
    )(*(in_hbm(x) for x in (valid, src_station, traces.reshape(every, samples), seed, twice)))
    return out[:n_win], out[n_win:n_win + n_rcv], out[-2], out[-1]


def bin_order(lanes):
    quarter = lanes // 8
    lane = lax.broadcasted_iota(jnp.int32, (lanes, lanes), 1)
    row = lax.broadcasted_iota(jnp.int32, (lanes, lanes), 0)
    part = (lane // quarter) % 2
    bin_of = 4 * (lane % quarter) + lane // (2 * quarter)
    hit = row == part * (lanes // 2) + bin_of
    return hit.astype(jnp.float32).astype(jnp.bfloat16)


def turn_kernel(r_dev, *refs):
    x_refs, (out_ref, rows_ref) = refs[:-2], refs[-2:]
    lanes = x_refs[0].shape[1]
    bins = lanes // 2
    w_dev = out_ref.shape[1] // 2
    pad = out_ref.shape[2] // 2
    order = bin_order(lanes)
    windows = [(x, w) for x in x_refs for w in range(x.shape[0] // r_dev)]
    for k, (x_ref, w) in enumerate(windows):
        turned = lax.dot_general(
            order, x_ref[w * r_dev:(w + 1) * r_dev], (((1,), (1,)), ((), ())),
            preferred_element_type=jnp.float32,
        )
        rows_ref[pl.ds(k, lanes, stride=w_dev), :r_dev] = turned
    rr = rows_ref[:bins * w_dev].reshape(bins, w_dev, pad)
    ri = rows_ref[bins * w_dev:].reshape(bins, w_dev, pad)
    out_ref[:, :, :pad] = jnp.concatenate([rr, ri], axis=1).astype(jnp.bfloat16)
    out_ref[:, :, pad:] = jnp.concatenate([ri, -rr], axis=1).astype(jnp.bfloat16)


def turn_call(parts, w_dev, r_dev):
    lanes = parts[0].shape[1]
    pad = 128
    vmem = pl.BlockSpec(memory_space=VMEM)
    return pl.pallas_call(
        functools.partial(turn_kernel, r_dev),
        in_specs=[vmem] * len(parts),
        out_specs=vmem,
        out_shape=jax.ShapeDtypeStruct((lanes // 2, 2 * w_dev, 2 * pad), jnp.bfloat16),
        scratch_shapes=[pltpu.VMEM((lanes * w_dev, pad), jnp.float32)],
        compiler_params=pltpu.CompilerParams(vmem_limit_bytes=16 * 2**20),
        cost_estimate=pl.CostEstimate(
            flops=2 * w_dev * lanes * lanes * pad, bytes_accessed=2 * 2**20, transcendentals=0
        ),
        name="turn",
    )(*parts)


def merge_kernel(n_win, *refs):
    picked, outs = refs[:-n_win], refs[-n_win:]
    for j, out_ref in enumerate(outs):
        total = picked[0][j].astype(jnp.float32)
        for q_ref in picked[1:]:
            total = total + q_ref[j].astype(jnp.float32)
        out_ref[...] = total.astype(jnp.bfloat16)


def merge_call(*picked):
    n_win, rows, lanes = picked[0].shape
    vmem = pl.BlockSpec(memory_space=VMEM)
    return pl.pallas_call(
        functools.partial(merge_kernel, n_win),
        in_specs=[vmem] * len(picked),
        out_specs=[vmem] * n_win,
        out_shape=[jax.ShapeDtypeStruct((rows, lanes), jnp.bfloat16)] * n_win,
        compiler_params=pltpu.CompilerParams(vmem_limit_bytes=4 * 2**20),
        cost_estimate=pl.CostEstimate(flops=2**18, bytes_accessed=2**19, transcendentals=0),
        name="merge",
    )(*picked)


def lefts_kernel(n_parts, n_win, w_dev, n_own, *refs):
    *part_refs, out_ref, srow_ref, rows_ref = refs[-3 - n_parts:]
    rows, lanes = refs[0].shape
    bins = lanes // 2
    windows = n_win * w_dev
    pad = rows_ref.shape[1]
    for j in range(n_win):
        block = refs[j][...].astype(jnp.float32)
        for h in range(lanes // pad):
            srow_ref[h, j * rows:(j + 1) * rows, :] = block[:, h * pad:(h + 1) * pad]

    lane = lax.broadcasted_iota(jnp.int32, (bins, lanes), 1)
    row = lax.broadcasted_iota(jnp.int32, (bins, lanes), 0)
    quarter = lanes // 8
    bin_of = 4 * (lane % quarter) + lane // (2 * quarter)
    pick = bin_of == 2 * (row % (bins // 2)) + row // (bins // 2)
    pick = pick.astype(jnp.float32).astype(jnp.bfloat16)
    real = (lane[:w_dev] // quarter) % 2 == 0
    low = lax.broadcasted_iota(jnp.int32, (bins // 2, pad), 1) < pad // 2
    for s in range(n_own):
        values = jnp.concatenate(
            [srow_ref[h, pl.ds(s, windows, stride=n_own), :] for h in range(lanes // pad)], axis=1
        )
        stacked = []
        for j in range(n_win):
            own = values[j * w_dev:(j + 1) * w_dev]
            stacked += [jnp.where(real, own, 0.0), jnp.where(real, 0.0, own)]
        stacked = jnp.concatenate(stacked * 2, axis=0).astype(jnp.bfloat16)
        turned = lax.dot_general(
            pick, stacked, (((1,), (1,)), ((), ())), preferred_element_type=jnp.float32
        )
        pairs = jnp.where(low, turned[:bins // 2], turned[bins // 2:])
        rows_ref[pl.ds(s, bins // 2, stride=n_own), :] = pairs
    whole = rows_ref[...].reshape(out_ref.shape).astype(jnp.bfloat16)
    out_ref[...] = whole
    size = whole.shape[0] // n_parts
    for k, part_ref in enumerate(part_refs):
        part_ref[...] = whole[k * size:(k + 1) * size]


def lefts_call(blocks, after, later, w_dev, n_parts):
    rows, lanes = blocks[0].shape
    n_win = len(blocks)
    n_own = rows // w_dev
    pad = 128
    first = n_win + len(after)
    vmem, anywhere = pl.BlockSpec(memory_space=VMEM), pl.BlockSpec(memory_space=pl.ANY)
    out = pl.pallas_call(
        functools.partial(lefts_kernel, n_parts, n_win, w_dev, n_own),
        in_specs=[vmem] * n_win + [anywhere] * (len(after) + len(later)),
        out_specs=[anywhere] * len(later) + [vmem] * (n_parts + 1),
        out_shape=[jax.ShapeDtypeStruct(x.shape, x.dtype) for x in later]
        + [jax.ShapeDtypeStruct((lanes // 8 // n_parts, 2 * n_own, pad), jnp.bfloat16)] * n_parts
        + [jax.ShapeDtypeStruct((lanes // 8, 2 * n_own, pad), jnp.bfloat16)],
        input_output_aliases={first + k: k for k in range(len(later))},
        scratch_shapes=[
            pltpu.VMEM((lanes // pad, n_win * rows, pad), jnp.float32),
            pltpu.VMEM((lanes // 4 * n_own, pad), jnp.float32),
        ],
        compiler_params=pltpu.CompilerParams(vmem_limit_bytes=6 * 2**20),
        cost_estimate=pl.CostEstimate(flops=2**26, bytes_accessed=2**19, transcendentals=0),
        name="lefts",
    )(*blocks, *after, *later)
    return out[-1], out[len(later):-1], out[:len(later)]


def gate_kernel(*refs):
    pass


def gate_call(after, arrays):
    anywhere = pl.BlockSpec(memory_space=pl.ANY)
    return pl.pallas_call(
        gate_kernel,
        in_specs=[anywhere] * (len(after) + len(arrays)),
        out_specs=[anywhere] * len(arrays),
        out_shape=[jax.ShapeDtypeStruct(x.shape, x.dtype) for x in arrays],
        input_output_aliases={len(after) + k: k for k in range(len(arrays))},
        compiler_params=pltpu.CompilerParams(vmem_limit_bytes=2**20),
        cost_estimate=pl.CostEstimate(flops=1, bytes_accessed=1, transcendentals=0),
        name="gate",
    )(*after, *arrays)


def stacks_kernel(shares, parts, n_win, w_dev, r_dev, n_own, bins, plan_hbm, *refs):
    t_refs = refs[:n_win]
    s_refs, taken = [], n_win
    for n_parts in parts:
        s_refs.append(refs[taken:taken + n_parts])
        taken += n_parts
    out_hbm, prod_ref, out_ref, plan_ref, sems, plan_sem = refs[-6:]
    plan_copy = pltpu.make_async_copy(plan_hbm, plan_ref, plan_sem)
    plan_copy.start()
    windows = n_win * w_dev
    count = len(shares) * n_own
    pitch = prod_ref.shape[1] // bins
    pad = 128
    rcv = lax.axis_index("rcv")

    low = lax.broadcasted_iota(jnp.int32, (count, pad), 1) < pad // 2
    for group in range(bins // 4):
        values = []
        for part_refs in s_refs:
            k, place = divmod(group, bins // 4 // len(part_refs))
            values.append(part_refs[k][place].astype(jnp.float32))
        for p in range(2):
            rows = jnp.concatenate([v[p * n_own:(p + 1) * n_own] for v in values], axis=0)
            left = jnp.concatenate([jnp.where(low, rows, 0.0), jnp.where(low, 0.0, rows)], axis=0)
            first = 4 * group + 2 * p
            right = [t_ref[f] for f in (first, first + 1) for t_ref in t_refs]
            result = jnp.dot(
                left.astype(jnp.bfloat16), jnp.concatenate(right, axis=0),
                preferred_element_type=jnp.float32,
            )
            for k in range(2):
                for c in range(2):
                    block = result[k * count:(k + 1) * count, c * pad:(c + 1) * pad]
                    prod_ref[c, pl.ds((first + k) * pitch, count), :] = block

    scale = 1.0 / math.sqrt(windows)
    plan_copy.wait()
    copies = []
    for s in range(count):
        for c in range(2):
            turned = prod_ref[c, pl.ds(s, bins, stride=pitch), :].T
            out_ref[s, pl.ds(c, r_dev, stride=2), :] = turned[:r_dev] * scale
        row = plan_ref[0, (rcv ^ shares[s // n_own]) * n_own + s % n_own]
        copies.append(pltpu.make_async_copy(out_ref.at[s], out_hbm.at[row], sems.at[s]))
        copies[-1].start()
    for copy in copies:
        copy.wait()


def stacks_call(out, plan, turned, sources, shares, n_rcv, w_dev, r_dev, bins):
    n_win = len(turned)
    n_own = sources[0][0].shape[1] // 2
    parts = [len(sources[i]) for i in shares]
    windows = n_win * w_dev
    count = len(shares) * n_own
    whole = pl.BlockSpec(memory_space=VMEM)
    args = [plan] + list(turned) + [part for i in shares for part in sources[i]]
    specs = [pl.BlockSpec(memory_space=pl.ANY)] + [whole] * (len(args) - 1)
    aliases = {}
    if out is not None:
        aliases = {len(args): 0}
        args.append(out)
        specs.append(pl.BlockSpec(memory_space=pl.ANY))
    return pl.pallas_call(
        functools.partial(stacks_kernel, shares, parts, n_win, w_dev, r_dev, n_own, bins),
        in_specs=specs,
        out_specs=pl.BlockSpec(memory_space=pltpu.HBM),
        out_shape=jax.ShapeDtypeStruct((n_rcv * n_own, 2 * r_dev, bins), jnp.float32),
        input_output_aliases=aliases,
        scratch_shapes=[
            pltpu.VMEM((2, (count // 8 | 1) * 8 * bins, 128), jnp.float32),
            pltpu.VMEM((count, 2 * r_dev, bins), jnp.float32),
            pltpu.SMEM(plan.shape, jnp.int32),
            pltpu.SemaphoreType.DMA((count,)),
            pltpu.SemaphoreType.DMA,
        ],
        compiler_params=pltpu.CompilerParams(vmem_limit_bytes=20 * 2**20),
        cost_estimate=pl.CostEstimate(
            flops=8 * windows * count * r_dev * bins, bytes_accessed=6 * 2**20, transcendentals=0
        ),
        name="stacks",
    )(*args)


def swap(value, axis, by):
    size = lax.axis_size(axis)
    return lax.ppermute(value, axis, [(i, i ^ by) for i in range(size)])


def near_and_far(n_rcv, by):
    pairs = [(z, z ^ by) for z in range(n_rcv)]
    return [p for p in pairs if abs(p[0] - p[1]) == 1], [p for p in pairs if abs(p[0] - p[1]) > 1]


def merge_near(picked, near):
    return merge_call(picked[0], *near)


def merge_all(picked, near):
    far = []
    for i in range(1, len(picked)):
        pairs = near_and_far(len(picked), i)[1]
        if pairs:
            far.append(lax.ppermute(picked[i], "rcv", pairs))
    return merge_call(picked[0], *near, *far)


def body(traces, valid, src_station):
    w_dev, r_dev, samples = traces.shape
    n_src = src_station.shape[0]
    n_win = lax.axis_size("win")
    n_rcv = lax.axis_size("rcv")
    bins = F // n_win
    early = n_win // 2

    blocks, picked, plan, flag = spectra_call(traces, valid, src_station, n_win, n_rcv)

    near = {}
    for i in range(1, n_rcv):
        pairs = near_and_far(n_rcv, i)[0]
        if pairs:
            near[i] = lax.ppermute(picked[i], "rcv", pairs)
    picked = [picked[0] + near.pop(n_rcv - 1)] + list(picked[1:])
    near = list(near.values())
    merged = lax.cond(flag.reshape(()) > 0, merge_all, merge_near, picked, near)

    merged = [merged[0]] + [swap(merged[j], "win", j) for j in range(1, n_win)]
    late = [j for j in range(1, n_win) if j != early]
    received = {0: blocks[0], early: swap(blocks[early], "win", early)}
    lefts, halves, later = lefts_call(merged, [received[early]], [blocks[j] for j in late], w_dev, 2)
    received.update({j: swap(block, "win", j) for j, block in zip(late, later)})
    turned = [turn_call([received[j]], w_dev, r_dev) for j in range(n_win)]
    near = swap(lefts, "rcv", 1)
    middle = [swap(half, "rcv", 2) for half in halves]
    middle[:1] = gate_call(turned[:-1], middle[:1])
    sources = [[lefts], [near], middle, [swap(half, "rcv", 1) for half in middle]]

    sizes = (n_rcv, w_dev, r_dev, bins)
    stacks = stacks_call(None, plan, turned, sources, tuple(range(n_rcv - 1)), *sizes)
    stacks = stacks_call(stacks, plan, turned, sources, (n_rcv - 1,), *sizes)
    return stacks.reshape(n_src, r_dev, 2, bins)


def correlate(received, sources):
    rr = received[:, :, 0]
    ri = received[:, :, 1]
    sr = sources[:, :, 0]
    si = sources[:, :, 1]
    real = jnp.einsum("wsf,wrf->srf", sr, rr, preferred_element_type=jnp.float32)
    real = real + jnp.einsum("wsf,wrf->srf", si, ri, preferred_element_type=jnp.float32)
    imag = jnp.einsum("wsf,wrf->srf", sr, ri, preferred_element_type=jnp.float32)
    imag = imag - jnp.einsum("wsf,wrf->srf", si, rr, preferred_element_type=jnp.float32)
    return jnp.stack([real, imag], axis=2)


def body_any(traces, valid, src_station):
    w_dev, r_dev, samples = traces.shape
    n_win = lax.axis_size("win")
    n_rcv = lax.axis_size("rcv")
    bins = F // n_win
    table = jnp.asarray(band_table(samples, F, samples // 16))
    spectra = jnp.dot(
        traces.reshape(w_dev * r_dev, samples), table, preferred_element_type=jnp.float32
    )
    spectra = spectra.reshape(w_dev, r_dev, 2, F)
    power = jnp.sum(spectra * spectra, axis=(2, 3), keepdims=True) / F
    keep = valid.astype(jnp.float32)[:, None, None, None]
    white = (spectra * lax.rsqrt(power + 1e-06) * keep).astype(jnp.bfloat16)
    blocks = white.reshape(w_dev, r_dev, 2, n_win, bins).transpose(3, 0, 1, 2, 4)
    me = lax.axis_index("win")
    offset = lax.axis_index("rcv") * r_dev
    station_ids = offset + jnp.arange(r_dev, dtype=jnp.int32)
    selector = (src_station[:, None] == station_ids[None, :]).astype(jnp.bfloat16)
    received = []
    for j in range(n_win):
        block = lax.dynamic_index_in_dim(blocks, me ^ j, 0, keepdims=False)
        received.append(swap(block, "win", j) if j else block)
    received = jnp.concatenate(received, axis=0)
    rows = jnp.einsum("sr,wrcf->wscf", selector, received, preferred_element_type=jnp.float32)
    rows = lax.all_to_all(rows.astype(jnp.bfloat16), "rcv", 0, 0, tiled=True)
    rows = rows.reshape((n_rcv, -1) + rows.shape[1:])
    merged = jnp.sum(rows.astype(jnp.float32), axis=0).astype(jnp.bfloat16)
    sources = lax.all_gather(merged, "rcv", axis=0, tiled=True)
    return correlate(received, sources) * (1.0 / math.sqrt(w_dev * n_win))


def solution(mesh):
    sizes = (mesh.shape["win"], mesh.shape["rcv"])
    return jax.shard_map(
        body if sizes == (4, 4) else body_any,
        mesh=mesh,
        in_specs=(P("win", ("groups", "rcv"), None), P(("groups", "win")), P("groups")),
        out_specs=P(None, ("groups", "rcv"), None, "win"),
        check_vma=False,
    )
```

```python
import functools
import math

import jax
import jax.numpy as jnp
import numpy as np
from jax import lax
from jax.experimental import pallas as pl
from jax.experimental.pallas import tpu as pltpu
from jax.sharding import PartitionSpec as P

F = 512
SMEM = pltpu.MemorySpace.SMEM
VMEM = pltpu.MemorySpace.VMEM


def angles(samples, freqs, count):
    phase = samples[:, None] * freqs[None, :] % count
    return phase.astype(np.float64) * (2.0 * math.pi / count)


def band_table(count, bins, first):
    angle = angles(np.arange(count), first + np.arange(bins), count)
    return np.concatenate([np.cos(angle), -np.sin(angle)], axis=1).astype(jnp.bfloat16)


BLOCK = 32


def table_seeds(count, bins, first, n_win):
    j = np.arange(bins // 4)
    turn = np.array([0.0, 0.5 * math.pi]).reshape(1, 2, 1)
    seeds, twice = [], []
    for m in range(4):
        freqs = np.broadcast_to((first + 4 * j + m).reshape(n_win, 1, -1), (n_win, 2, j.size // n_win))
        angle = angles(np.arange(2 * BLOCK), freqs.reshape(-1), count)
        angle = angle + np.broadcast_to(turn, freqs.shape).reshape(1, -1)
        seeds.append(np.cos(angle).reshape(2, BLOCK, -1))
        step = angles(np.full(8, BLOCK), freqs.reshape(-1), count)
        twice.append(2.0 * np.cos(step))
    return np.stack(seeds).astype(np.float32), np.stack(twice).astype(np.float32)


def make_tables(seed_ref, twice_ref, table_ref):
    for first in (0, 2):
        state = {}
        for m in (first, first + 1):
            twice = jnp.concatenate([twice_ref[m]] * (BLOCK // 8), axis=0)
            state[m] = (seed_ref[m, 0], seed_ref[m, 1], twice)
        for a in range(table_ref.shape[1] // BLOCK):
            for m, (here, after, twice) in state.items():
                table_ref[m, a * BLOCK:(a + 1) * BLOCK, :] = here.astype(jnp.bfloat16)
                state[m] = (after, twice * after - here, twice)


def in_hbm(value):
    return pltpu.with_memory_space_constraint(value, pltpu.HBM)


def order_sources(src_ref, r_dev, n_own, order_ref, plan_ref, flag_ref):
    n_src = src_ref.shape[0]
    size = order_ref.shape
    down = lax.broadcasted_iota(jnp.int32, size, 0).astype(jnp.float32)
    along = lax.broadcasted_iota(jnp.int32, size, 1).astype(jnp.float32)
    none = jnp.full(size, float(2**20), jnp.float32)
    column, row = none, none
    for s in range(n_src):
        station = src_ref[s].astype(jnp.float32)
        column = jnp.where(down == s, station, column)
        row = jnp.where(along == s, station, row)
    rank_along = jnp.sum((column < row).astype(jnp.float32), axis=0, keepdims=True)
    rank_down = jnp.sum((row < column).astype(jnp.float32), axis=1, keepdims=True)
    sorted_down = jnp.sum(jnp.where(rank_along == down, row, 0.0), axis=1, keepdims=True)
    at_place = rank_down == along
    sorted_along = jnp.sum(jnp.where(at_place, column, 0.0), axis=0, keepdims=True)
    source_along = jnp.sum(jnp.where(at_place, down, 0.0), axis=0, keepdims=True)
    order_ref[...] = jnp.broadcast_to(sorted_down, size)
    place = along[:1]
    owner, share = jnp.zeros_like(place), jnp.zeros_like(place)
    for z in range(1, n_src // n_own):
        owner = owner + (sorted_along >= z * r_dev).astype(jnp.float32)
        share = share + (place >= z * n_own).astype(jnp.float32)
    far = jnp.where((place < n_src) & (jnp.abs(owner - share) > 1.5), 1.0, 0.0)
    plan_ref[...] = jnp.broadcast_to(source_along, plan_ref.shape).astype(jnp.int32)
    flag_ref[0] = jnp.max(far).astype(jnp.int32)


def spectra_kernel(
    n_win, n_rcv, r_dev, cuts, valid_hbm, src_hbm, x_hbm, seed_hbm, twice_hbm, *refs
):
    r_refs = refs[:n_win]
    q_refs = refs[n_win:n_win + n_rcv]
    (plan_ref, flag_ref, x_ref, even_ref, odd_ref, white_ref, sel_ref, order_ref, table_ref,
     seed_ref, twice_ref, valid_ref, src_ref, sems, x_sems) = refs[n_win + n_rcv:]
    bounds = [(a * r_dev, b * r_dev) for a, b in zip(cuts, cuts[1:])]
    n_own = src_ref.shape[0] // n_rcv
    quarter = x_ref.shape[1] // 4
    win = lax.axis_index("win")
    rcv = lax.axis_index("rcv")

    def small(k):
        source = (seed_hbm, twice_hbm, src_hbm, valid_hbm)[k]
        target = (seed_ref, twice_ref, src_ref, valid_ref)[k]
        return pltpu.make_async_copy(source, target, sems.at[k])

    def chunk(k):
        rows = pl.ds(bounds[k][0], bounds[k][1] - bounds[k][0])
        return pltpu.make_async_copy(x_hbm.at[rows], x_ref.at[rows], x_sems.at[k])

    for k in range(4):
        small(k).start()
    for k in range(len(bounds)):
        chunk(k).start()
    small(0).wait()
    small(1).wait()
    make_tables(seed_ref, twice_ref, table_ref)
    small(2).wait()
    order_sources(src_ref, r_dev, n_own, order_ref, plan_ref, flag_ref)
    stations = []
    for d in range(n_rcv):
        share = pl.multiple_of((rcv ^ d) * n_own, n_own)
        stations.append(order_ref[pl.ds(share, n_own), 0:1])
    per_window = n_rcv * n_own
    wanted = jnp.concatenate(stations * (sel_ref.shape[0] // per_window), axis=0)
    wanted = wanted.astype(jnp.int32) - rcv * r_dev
    out_row = lax.broadcasted_iota(jnp.int32, sel_ref.shape, 0)
    column = lax.broadcasted_iota(jnp.int32, sel_ref.shape, 1)
    inside = (wanted >= 0) & (wanted < r_dev)
    hit = inside & (column == wanted + out_row // per_window * r_dev)
    sel_ref[...] = hit.astype(jnp.float32).astype(jnp.bfloat16)
    small(3).wait()

    def product(lhs, table):
        return jnp.dot(lhs, table, preferred_element_type=jnp.float32)

    def add_quarters(k, first, last):
        start, stop = bounds[k]
        part = slice(start + first, start + last)
        b0, b1, b2, b3 = (x_ref[part, q * quarter:(q + 1) * quarter] for q in range(4))
        x0, x1, x2, x3 = (b.astype(jnp.float32) for b in (b0, b1, b2, b3))
        even_ref[0, part] = ((x0 + x2) + (x1 + x3)).astype(jnp.bfloat16)
        even_ref[1, part] = ((x0 + x2) - (x1 + x3)).astype(jnp.bfloat16)
        odd_ref[2 * start + first:2 * start + last] = b0 - b2
        odd_ref[start + stop + first:start + stop + last] = b1 - b3

    lanes = table_ref.shape[2]
    piece = lanes // n_win

    def odd_spectra(k, m):
        start, stop = bounds[k]
        rows = stop - start
        both = product(odd_ref[2 * start:2 * stop], table_ref[m])
        second = both[rows:]
        back, forth = pltpu.roll(second, lanes - piece // 2, 1), pltpu.roll(second, piece // 2, 1)
        real = lax.broadcasted_iota(jnp.int32, (rows, lanes), 1) % piece < piece // 2
        turned = jnp.where(real, back, -forth)
        return both[:rows] + turned if m == 1 else both[:rows] - turned

    chunk(0).wait()
    add_quarters(0, 0, bounds[0][1])
    for k, (start, stop) in enumerate(bounds):
        rows = stop - start
        windows = cuts[k + 1] - cuts[k]
        more = k + 1 < len(bounds)
        if more:
            chunk(k + 1).wait()
        spectra = []
        for m in range(4):
            if m % 2:
                spectra.append(odd_spectra(k, m))
            else:
                spectra.append(product(even_ref[m // 2, start:stop], table_ref[m]))
            if more and m < cuts[k + 2] - cuts[k + 1]:
                add_quarters(k + 1, m * r_dev, (m + 1) * r_dev)
        squares = sum(jnp.sum(s * s, axis=1, keepdims=True) for s in spectra)
        gain = lax.rsqrt(squares / F + 1e-06)
        row = lax.broadcasted_iota(jnp.int32, (rows, 1), 0)
        keep = jnp.zeros((rows, 1), jnp.float32)
        for t in range(windows):
            own = (row >= t * r_dev) & (row < (t + 1) * r_dev)
            keep = jnp.where(own, valid_ref[cuts[k] + t].astype(jnp.float32), keep)
        gain = gain * keep
        white = [s * gain for s in spectra]
        for d in range(n_win):
            columns = slice(d * piece, (d + 1) * piece)
            block = jnp.concatenate([part[:, columns] for part in white], axis=1)
            white_ref[d, start:stop] = block.astype(jnp.bfloat16)
        select = sel_ref[:windows * per_window, :rows]
        for j in range(n_win):
            block = white_ref[win ^ j, start:stop]
            r_refs[j][start:stop, :] = block
            picked = product(select, block).astype(jnp.bfloat16)
            for t in range(windows):
                place = (cuts[k] + t) * n_own
                for d in range(n_rcv):
                    first = t * per_window + d * n_own
                    q_refs[d][j, place:place + n_own, :] = picked[first:first + n_own]


def spectra_call(traces, valid, src_station, n_win, n_rcv):
    w_dev, r_dev, samples = traces.shape
    n_src = src_station.shape[0]
    n_own = n_src // n_rcv
    cuts = (0, w_dev // 4, w_dev * 5 // 8, w_dev)
    largest = max(b - a for a, b in zip(cuts, cuts[1:]))
    every = w_dev * r_dev
    lanes = 2 * F // n_win
    seed, twice = (jnp.asarray(t) for t in table_seeds(samples, F, samples // 16, n_win))
    shapes = [jax.ShapeDtypeStruct((every, lanes), jnp.bfloat16)] * n_win
    shapes += [jax.ShapeDtypeStruct((n_win, w_dev * n_own, lanes), jnp.bfloat16)] * n_rcv
    shapes += [jax.ShapeDtypeStruct((8, 128), jnp.int32), jax.ShapeDtypeStruct((1,), jnp.int32)]
    vmem = pl.BlockSpec(memory_space=VMEM)
    out = pl.pallas_call(
        functools.partial(spectra_kernel, n_win, n_rcv, r_dev, cuts),
        in_specs=[pl.BlockSpec(memory_space=pltpu.HBM)] * 5,
        out_specs=[vmem] * (len(shapes) - 1) + [pl.BlockSpec(memory_space=SMEM)],
        out_shape=shapes,
        scratch_shapes=[
            pltpu.VMEM((every, samples), jnp.bfloat16),
            pltpu.VMEM((2, every, samples // 4), jnp.bfloat16),
            pltpu.VMEM((2 * every, samples // 4), jnp.bfloat16),
            pltpu.VMEM((n_win, every, lanes), jnp.bfloat16),
            pltpu.VMEM((n_src * largest, r_dev * largest), jnp.bfloat16),
            pltpu.VMEM((n_src, 128), jnp.float32),
            pltpu.VMEM((4, samples // 4, F // 2), jnp.bfloat16),
            pltpu.VMEM(seed.shape, jnp.float32),
            pltpu.VMEM(twice.shape, jnp.float32),
            pltpu.SMEM(valid.shape, jnp.int32),
            pltpu.SMEM(src_station.shape, jnp.int32),
            pltpu.SemaphoreType.DMA((4,)),
            pltpu.SemaphoreType.DMA((len(cuts) - 1,)),
        ],
        compiler_params=pltpu.CompilerParams(vmem_limit_bytes=36 * 2**20),
        cost_estimate=pl.CostEstimate(
            flops=2 * every * (samples // 4) * 6 * (F // 2), bytes_accessed=every * samples * 2,
            transcendentals=0,
        ),
        name="spectra",
    )(*(in_hbm(x) for x in (valid, src_station, traces.reshape(every, samples), seed, twice)))
    return out[:n_win], out[n_win:n_win + n_rcv], out[-2], out[-1]


def bin_order(lanes):
    quarter = lanes // 8
    lane = lax.broadcasted_iota(jnp.int32, (lanes, lanes), 1)
    row = lax.broadcasted_iota(jnp.int32, (lanes, lanes), 0)
    part = (lane // quarter) % 2
    bin_of = 4 * (lane % quarter) + lane // (2 * quarter)
    hit = row == part * (lanes // 2) + bin_of
    return hit.astype(jnp.float32).astype(jnp.bfloat16)


def turn_kernel(r_dev, *refs):
    x_refs, (out_ref, rows_ref) = refs[:-2], refs[-2:]
    lanes = x_refs[0].shape[1]
    bins = lanes // 2
    w_dev = out_ref.shape[1] // 2
    pad = out_ref.shape[2] // 2
    order = bin_order(lanes)
    windows = [(x, w) for x in x_refs for w in range(x.shape[0] // r_dev)]
    for k, (x_ref, w) in enumerate(windows):
        turned = lax.dot_general(
            order, x_ref[w * r_dev:(w + 1) * r_dev], (((1,), (1,)), ((), ())),
            preferred_element_type=jnp.float32,
        )
        rows_ref[pl.ds(k, lanes, stride=w_dev), :r_dev] = turned
    rr = rows_ref[:bins * w_dev].reshape(bins, w_dev, pad)
    ri = rows_ref[bins * w_dev:].reshape(bins, w_dev, pad)
    out_ref[:, :, :pad] = jnp.concatenate([rr, ri], axis=1).astype(jnp.bfloat16)
    out_ref[:, :, pad:] = jnp.concatenate([ri, -rr], axis=1).astype(jnp.bfloat16)


def turn_call(parts, w_dev, r_dev):
    lanes = parts[0].shape[1]
    pad = 128
    vmem = pl.BlockSpec(memory_space=VMEM)
    return pl.pallas_call(
        functools.partial(turn_kernel, r_dev),
        in_specs=[vmem] * len(parts),
        out_specs=vmem,
        out_shape=jax.ShapeDtypeStruct((lanes // 2, 2 * w_dev, 2 * pad), jnp.bfloat16),
        scratch_shapes=[pltpu.VMEM((lanes * w_dev, pad), jnp.float32)],
        compiler_params=pltpu.CompilerParams(vmem_limit_bytes=16 * 2**20),
        cost_estimate=pl.CostEstimate(
            flops=2 * w_dev * lanes * lanes * pad, bytes_accessed=2 * 2**20, transcendentals=0
        ),
        name="turn",
    )(*parts)


def merge_kernel(n_win, *refs):
    picked, outs = refs[:-n_win], refs[-n_win:]
    for j, out_ref in enumerate(outs):
        total = picked[0][j].astype(jnp.float32)
        for q_ref in picked[1:]:
            total = total + q_ref[j].astype(jnp.float32)
        out_ref[...] = total.astype(jnp.bfloat16)


def merge_call(*picked):
    n_win, rows, lanes = picked[0].shape
    vmem = pl.BlockSpec(memory_space=VMEM)
    return pl.pallas_call(
        functools.partial(merge_kernel, n_win),
        in_specs=[vmem] * len(picked),
        out_specs=[vmem] * n_win,
        out_shape=[jax.ShapeDtypeStruct((rows, lanes), jnp.bfloat16)] * n_win,
        compiler_params=pltpu.CompilerParams(vmem_limit_bytes=4 * 2**20),
        cost_estimate=pl.CostEstimate(flops=2**18, bytes_accessed=2**19, transcendentals=0),
        name="merge",
    )(*picked)


def lefts_kernel(n_win, w_dev, n_own, *refs):
    out_ref, srow_ref, rows_ref = refs[-3:]
    rows, lanes = refs[0].shape
    bins = lanes // 2
    windows = n_win * w_dev
    pad = rows_ref.shape[1]
    for j in range(n_win):
        block = refs[j][...].astype(jnp.float32)
        for h in range(lanes // pad):
            srow_ref[h, j * rows:(j + 1) * rows, :] = block[:, h * pad:(h + 1) * pad]

    lane = lax.broadcasted_iota(jnp.int32, (bins, lanes), 1)
    row = lax.broadcasted_iota(jnp.int32, (bins, lanes), 0)
    quarter = lanes // 8
    bin_of = 4 * (lane % quarter) + lane // (2 * quarter)
    pick = bin_of == 2 * (row % (bins // 2)) + row // (bins // 2)
    pick = pick.astype(jnp.float32).astype(jnp.bfloat16)
    real = (lane[:w_dev] // quarter) % 2 == 0
    low = lax.broadcasted_iota(jnp.int32, (bins // 2, pad), 1) < pad // 2
    for s in range(n_own):
        values = jnp.concatenate(
            [srow_ref[h, pl.ds(s, windows, stride=n_own), :] for h in range(lanes // pad)], axis=1
        )
        stacked = []
        for j in range(n_win):
            own = values[j * w_dev:(j + 1) * w_dev]
            stacked += [jnp.where(real, own, 0.0), jnp.where(real, 0.0, own)]
        stacked = jnp.concatenate(stacked * 2, axis=0).astype(jnp.bfloat16)
        turned = lax.dot_general(
            pick, stacked, (((1,), (1,)), ((), ())), preferred_element_type=jnp.float32
        )
        pairs = jnp.where(low, turned[:bins // 2], turned[bins // 2:])
        rows_ref[pl.ds(s, bins // 2, stride=n_own), :] = pairs
    out_ref[...] = rows_ref[...].reshape(out_ref.shape).astype(jnp.bfloat16)


def lefts_call(blocks, after, later, w_dev):
    rows, lanes = blocks[0].shape
    n_win = len(blocks)
    n_own = rows // w_dev
    pad = 128
    first = n_win + len(after)
    vmem, anywhere = pl.BlockSpec(memory_space=VMEM), pl.BlockSpec(memory_space=pl.ANY)
    out = pl.pallas_call(
        functools.partial(lefts_kernel, n_win, w_dev, n_own),
        in_specs=[vmem] * n_win + [anywhere] * (len(after) + len(later)),
        out_specs=[anywhere] * len(later) + [vmem],
        out_shape=[jax.ShapeDtypeStruct(x.shape, x.dtype) for x in later]
        + [jax.ShapeDtypeStruct((lanes // 8, 2 * n_own, pad), jnp.bfloat16)],
        input_output_aliases={first + k: k for k in range(len(later))},
        scratch_shapes=[
            pltpu.VMEM((lanes // pad, n_win * rows, pad), jnp.float32),
            pltpu.VMEM((lanes // 4 * n_own, pad), jnp.float32),
        ],
        compiler_params=pltpu.CompilerParams(vmem_limit_bytes=6 * 2**20),
        cost_estimate=pl.CostEstimate(flops=2**26, bytes_accessed=2**19, transcendentals=0),
        name="lefts",
    )(*blocks, *after, *later)
    return out[-1], out[:-1]


def gate_kernel(*refs):
    pass


def gate_call(after, arrays):
    anywhere = pl.BlockSpec(memory_space=pl.ANY)
    return pl.pallas_call(
        gate_kernel,
        in_specs=[anywhere] * (len(after) + len(arrays)),
        out_specs=[anywhere] * len(arrays),
        out_shape=[jax.ShapeDtypeStruct(x.shape, x.dtype) for x in arrays],
        input_output_aliases={len(after) + k: k for k in range(len(arrays))},
        compiler_params=pltpu.CompilerParams(vmem_limit_bytes=2**20),
        cost_estimate=pl.CostEstimate(flops=1, bytes_accessed=1, transcendentals=0),
        name="gate",
    )(*after, *arrays)


def stacks_kernel(shares, n_win, w_dev, r_dev, n_own, bins, plan_hbm, *refs):
    t_refs = refs[:n_win]
    s_refs = refs[n_win:n_win + len(shares)]
    out_hbm, prod_ref, out_ref, plan_ref, sems, plan_sem = refs[-6:]
    plan_copy = pltpu.make_async_copy(plan_hbm, plan_ref, plan_sem)
    plan_copy.start()
    windows = n_win * w_dev
    count = len(shares) * n_own
    pitch = prod_ref.shape[1] // bins
    pad = 128
    rcv = lax.axis_index("rcv")

    low = lax.broadcasted_iota(jnp.int32, (count, pad), 1) < pad // 2
    for group in range(bins // 4):
        values = [s_ref[group].astype(jnp.float32) for s_ref in s_refs]
        for p in range(2):
            rows = jnp.concatenate([v[p * n_own:(p + 1) * n_own] for v in values], axis=0)
            left = jnp.concatenate([jnp.where(low, rows, 0.0), jnp.where(low, 0.0, rows)], axis=0)
            first = 4 * group + 2 * p
            right = [t_ref[f] for f in (first, first + 1) for t_ref in t_refs]
            result = jnp.dot(
                left.astype(jnp.bfloat16), jnp.concatenate(right, axis=0),
                preferred_element_type=jnp.float32,
            )
            for k in range(2):
                for c in range(2):
                    block = result[k * count:(k + 1) * count, c * pad:(c + 1) * pad]
                    prod_ref[c, pl.ds((first + k) * pitch, count), :] = block

    scale = 1.0 / math.sqrt(windows)
    plan_copy.wait()
    copies = []
    for s in range(count):
        for c in range(2):
            turned = prod_ref[c, pl.ds(s, bins, stride=pitch), :].T
            out_ref[s, pl.ds(c, r_dev, stride=2), :] = turned[:r_dev] * scale
        row = plan_ref[0, (rcv ^ shares[s // n_own]) * n_own + s % n_own]
        copies.append(pltpu.make_async_copy(out_ref.at[s], out_hbm.at[row], sems.at[s]))
        copies[-1].start()
    for copy in copies:
        copy.wait()


def stacks_call(out, plan, turned, sources, shares, n_rcv, w_dev, r_dev, bins):
    n_win = len(turned)
    n_own = sources[0].shape[1] // 2
    windows = n_win * w_dev
    count = len(shares) * n_own
    whole = pl.BlockSpec(memory_space=VMEM)
    args = [plan] + list(turned) + [sources[i] for i in shares]
    specs = [pl.BlockSpec(memory_space=pl.ANY)] + [whole] * (len(args) - 1)
    aliases = {}
    if out is not None:
        aliases = {len(args): 0}
        args.append(out)
        specs.append(pl.BlockSpec(memory_space=pl.ANY))
    return pl.pallas_call(
        functools.partial(stacks_kernel, shares, n_win, w_dev, r_dev, n_own, bins),
        in_specs=specs,
        out_specs=pl.BlockSpec(memory_space=pltpu.HBM),
        out_shape=jax.ShapeDtypeStruct((n_rcv * n_own, 2 * r_dev, bins), jnp.float32),
        input_output_aliases=aliases,
        scratch_shapes=[
            pltpu.VMEM((2, (count // 8 | 1) * 8 * bins, 128), jnp.float32),
            pltpu.VMEM((count, 2 * r_dev, bins), jnp.float32),
            pltpu.SMEM(plan.shape, jnp.int32),
            pltpu.SemaphoreType.DMA((count,)),
            pltpu.SemaphoreType.DMA,
        ],
        compiler_params=pltpu.CompilerParams(vmem_limit_bytes=20 * 2**20),
        cost_estimate=pl.CostEstimate(
            flops=8 * windows * count * r_dev * bins, bytes_accessed=6 * 2**20, transcendentals=0
        ),
        name="stacks",
    )(*args)


def swap(value, axis, by):
    size = lax.axis_size(axis)
    return lax.ppermute(value, axis, [(i, i ^ by) for i in range(size)])


def near_and_far(n_rcv, by):
    pairs = [(z, z ^ by) for z in range(n_rcv)]
    return [p for p in pairs if abs(p[0] - p[1]) == 1], [p for p in pairs if abs(p[0] - p[1]) > 1]


def merge_near(picked, near):
    return merge_call(picked[0], *near)


def merge_all(picked, near):
    far = []
    for i in range(1, len(picked)):
        pairs = near_and_far(len(picked), i)[1]
        if pairs:
            far.append(lax.ppermute(picked[i], "rcv", pairs))
    return merge_call(picked[0], *near, *far)


def body(traces, valid, src_station):
    w_dev, r_dev, samples = traces.shape
    n_src = src_station.shape[0]
    n_win = lax.axis_size("win")
    n_rcv = lax.axis_size("rcv")
    bins = F // n_win
    early = n_win // 2

    blocks, picked, plan, flag = spectra_call(traces, valid, src_station, n_win, n_rcv)

    near = {}
    for i in range(1, n_rcv):
        pairs = near_and_far(n_rcv, i)[0]
        if pairs:
            near[i] = lax.ppermute(picked[i], "rcv", pairs)
    picked = [picked[0] + near.pop(n_rcv - 1)] + list(picked[1:])
    near = list(near.values())
    merged = lax.cond(flag.reshape(()) > 0, merge_all, merge_near, picked, near)

    merged = [merged[0]] + [swap(merged[j], "win", j) for j in range(1, n_win)]
    late = [j for j in range(1, n_win) if j != early]
    received = {0: blocks[0], early: swap(blocks[early], "win", early)}
    lefts, later = lefts_call(merged, [received[early]], [blocks[j] for j in late], w_dev)
    received.update({j: swap(block, "win", j) for j, block in zip(late, later)})
    sources = [lefts, swap(lefts, "rcv", 1), swap(lefts, "rcv", 2)]
    turned = [turn_call([received[j]], w_dev, r_dev) for j in range(n_win)]
    sources[2] = gate_call(turned[:-1], [sources[2]])[0]
    sources.append(swap(sources[2], "rcv", 1))

    sizes = (n_rcv, w_dev, r_dev, bins)
    stacks = stacks_call(None, plan, turned, sources, tuple(range(n_rcv - 1)), *sizes)
    stacks = stacks_call(stacks, plan, turned, sources, (n_rcv - 1,), *sizes)
    return stacks.reshape(n_src, r_dev, 2, bins)


def correlate(received, sources):
    rr = received[:, :, 0]
    ri = received[:, :, 1]
    sr = sources[:, :, 0]
    si = sources[:, :, 1]
    real = jnp.einsum("wsf,wrf->srf", sr, rr, preferred_element_type=jnp.float32)
    real = real + jnp.einsum("wsf,wrf->srf", si, ri, preferred_element_type=jnp.float32)
    imag = jnp.einsum("wsf,wrf->srf", sr, ri, preferred_element_type=jnp.float32)
    imag = imag - jnp.einsum("wsf,wrf->srf", si, rr, preferred_element_type=jnp.float32)
    return jnp.stack([real, imag], axis=2)


def body_any(traces, valid, src_station):
    w_dev, r_dev, samples = traces.shape
    n_win = lax.axis_size("win")
    n_rcv = lax.axis_size("rcv")
    bins = F // n_win
    table = jnp.asarray(band_table(samples, F, samples // 16))
    spectra = jnp.dot(
        traces.reshape(w_dev * r_dev, samples), table, preferred_element_type=jnp.float32
    )
    spectra = spectra.reshape(w_dev, r_dev, 2, F)
    power = jnp.sum(spectra * spectra, axis=(2, 3), keepdims=True) / F
    keep = valid.astype(jnp.float32)[:, None, None, None]
    white = (spectra * lax.rsqrt(power + 1e-06) * keep).astype(jnp.bfloat16)
    blocks = white.reshape(w_dev, r_dev, 2, n_win, bins).transpose(3, 0, 1, 2, 4)
    me = lax.axis_index("win")
    offset = lax.axis_index("rcv") * r_dev
    station_ids = offset + jnp.arange(r_dev, dtype=jnp.int32)
    selector = (src_station[:, None] == station_ids[None, :]).astype(jnp.bfloat16)
    received = []
    for j in range(n_win):
        block = lax.dynamic_index_in_dim(blocks, me ^ j, 0, keepdims=False)
        received.append(swap(block, "win", j) if j else block)
    received = jnp.concatenate(received, axis=0)
    rows = jnp.einsum("sr,wrcf->wscf", selector, received, preferred_element_type=jnp.float32)
    rows = lax.all_to_all(rows.astype(jnp.bfloat16), "rcv", 0, 0, tiled=True)
    rows = rows.reshape((n_rcv, -1) + rows.shape[1:])
    merged = jnp.sum(rows.astype(jnp.float32), axis=0).astype(jnp.bfloat16)
    sources = lax.all_gather(merged, "rcv", axis=0, tiled=True)
    return correlate(received, sources) * (1.0 / math.sqrt(w_dev * n_win))


def solution(mesh):
    sizes = (mesh.shape["win"], mesh.shape["rcv"])
    return jax.shard_map(
        body if sizes == (4, 4) else body_any,
        mesh=mesh,
        in_specs=(P("win", ("groups", "rcv"), None), P(("groups", "win")), P("groups")),
        out_specs=P(None, ("groups", "rcv"), None, "win"),
        check_vma=False,
    )
```

```python
import functools
import math

import jax
import jax.numpy as jnp
import numpy as np
from jax import lax
from jax.experimental import pallas as pl
from jax.experimental.pallas import tpu as pltpu
from jax.sharding import PartitionSpec as P

F = 512
SMEM = pltpu.MemorySpace.SMEM
VMEM = pltpu.MemorySpace.VMEM


def angles(samples, freqs, count):
    phase = samples[:, None] * freqs[None, :] % count
    return phase.astype(np.float64) * (2.0 * math.pi / count)


def band_table(count, bins, first):
    angle = angles(np.arange(count), first + np.arange(bins), count)
    return np.concatenate([np.cos(angle), -np.sin(angle)], axis=1).astype(jnp.bfloat16)


BLOCK = 32


def table_seeds(count, bins, first, n_win):
    j = np.arange(bins // 4)
    turn = np.array([0.0, 0.5 * math.pi]).reshape(1, 2, 1)
    seeds, twice = [], []
    for m in range(4):
        freqs = np.broadcast_to((first + 4 * j + m).reshape(n_win, 1, -1), (n_win, 2, j.size // n_win))
        angle = angles(np.arange(2 * BLOCK), freqs.reshape(-1), count)
        angle = angle + np.broadcast_to(turn, freqs.shape).reshape(1, -1)
        seeds.append(np.cos(angle).reshape(2, BLOCK, -1))
        step = angles(np.full(8, BLOCK), freqs.reshape(-1), count)
        twice.append(2.0 * np.cos(step))
    return np.stack(seeds).astype(np.float32), np.stack(twice).astype(np.float32)


def make_tables(seed_ref, twice_ref, table_ref):
    for first in (0, 2):
        state = {}
        for m in (first, first + 1):
            twice = jnp.concatenate([twice_ref[m]] * (BLOCK // 8), axis=0)
            state[m] = (seed_ref[m, 0], seed_ref[m, 1], twice)
        for a in range(table_ref.shape[1] // BLOCK):
            for m, (here, after, twice) in state.items():
                table_ref[m, a * BLOCK:(a + 1) * BLOCK, :] = here.astype(jnp.bfloat16)
                state[m] = (after, twice * after - here, twice)


def in_hbm(value):
    return pltpu.with_memory_space_constraint(value, pltpu.HBM)


def order_sources(src_ref, r_dev, n_own, order_ref, plan_ref, flag_ref):
    n_src = src_ref.shape[0]
    size = order_ref.shape
    down = lax.broadcasted_iota(jnp.int32, size, 0).astype(jnp.float32)
    along = lax.broadcasted_iota(jnp.int32, size, 1).astype(jnp.float32)
    none = jnp.full(size, float(2**20), jnp.float32)
    column, row = none, none
    for s in range(n_src):
        station = src_ref[s].astype(jnp.float32)
        column = jnp.where(down == s, station, column)
        row = jnp.where(along == s, station, row)
    rank_along = jnp.sum((column < row).astype(jnp.float32), axis=0, keepdims=True)
    rank_down = jnp.sum((row < column).astype(jnp.float32), axis=1, keepdims=True)
    sorted_down = jnp.sum(jnp.where(rank_along == down, row, 0.0), axis=1, keepdims=True)
    at_place = rank_down == along
    sorted_along = jnp.sum(jnp.where(at_place, column, 0.0), axis=0, keepdims=True)
    source_along = jnp.sum(jnp.where(at_place, down, 0.0), axis=0, keepdims=True)
    order_ref[...] = jnp.broadcast_to(sorted_down, size)
    place = along[:1]
    owner, share = jnp.zeros_like(place), jnp.zeros_like(place)
    for z in range(1, n_src // n_own):
        owner = owner + (sorted_along >= z * r_dev).astype(jnp.float32)
        share = share + (place >= z * n_own).astype(jnp.float32)
    far = jnp.where((place < n_src) & (jnp.abs(owner - share) > 1.5), 1.0, 0.0)
    plan_ref[...] = jnp.broadcast_to(source_along, plan_ref.shape).astype(jnp.int32)
    flag_ref[0] = jnp.max(far).astype(jnp.int32)


def spectra_kernel(
    n_win, n_rcv, r_dev, cuts, valid_hbm, src_hbm, x_hbm, seed_hbm, twice_hbm, *refs
):
    r_refs = refs[:n_win]
    q_refs = refs[n_win:n_win + n_rcv]
    (plan_ref, flag_ref, x_ref, even_ref, odd_ref, white_ref, sel_ref, order_ref, table_ref,
     seed_ref, twice_ref, valid_ref, src_ref, sems, x_sems) = refs[n_win + n_rcv:]
    bounds = [(a * r_dev, b * r_dev) for a, b in zip(cuts, cuts[1:])]
    n_own = src_ref.shape[0] // n_rcv
    quarter = x_ref.shape[1] // 4
    win = lax.axis_index("win")
    rcv = lax.axis_index("rcv")

    def small(k):
        source = (seed_hbm, twice_hbm, src_hbm, valid_hbm)[k]
        target = (seed_ref, twice_ref, src_ref, valid_ref)[k]
        return pltpu.make_async_copy(source, target, sems.at[k])

    def chunk(k):
        rows = pl.ds(bounds[k][0], bounds[k][1] - bounds[k][0])
        return pltpu.make_async_copy(x_hbm.at[rows], x_ref.at[rows], x_sems.at[k])

    for k in range(4):
        small(k).start()
    for k in range(len(bounds)):
        chunk(k).start()
    small(0).wait()
    small(1).wait()
    make_tables(seed_ref, twice_ref, table_ref)
    small(2).wait()
    order_sources(src_ref, r_dev, n_own, order_ref, plan_ref, flag_ref)
    stations = []
    for d in range(n_rcv):
        share = pl.multiple_of((rcv ^ d) * n_own, n_own)
        stations.append(order_ref[pl.ds(share, n_own), 0:1])
    per_window = n_rcv * n_own
    wanted = jnp.concatenate(stations * (sel_ref.shape[0] // per_window), axis=0)
    wanted = wanted.astype(jnp.int32) - rcv * r_dev
    out_row = lax.broadcasted_iota(jnp.int32, sel_ref.shape, 0)
    column = lax.broadcasted_iota(jnp.int32, sel_ref.shape, 1)
    inside = (wanted >= 0) & (wanted < r_dev)
    hit = inside & (column == wanted + out_row // per_window * r_dev)
    sel_ref[...] = hit.astype(jnp.float32).astype(jnp.bfloat16)
    small(3).wait()

    def product(lhs, table):
        return jnp.dot(lhs, table, preferred_element_type=jnp.float32)

    def add_quarters(k, first, last):
        start, stop = bounds[k]
        part = slice(start + first, start + last)
        b0, b1, b2, b3 = (x_ref[part, q * quarter:(q + 1) * quarter] for q in range(4))
        x0, x1, x2, x3 = (b.astype(jnp.float32) for b in (b0, b1, b2, b3))
        even_ref[0, part] = ((x0 + x2) + (x1 + x3)).astype(jnp.bfloat16)
        even_ref[1, part] = ((x0 + x2) - (x1 + x3)).astype(jnp.bfloat16)
        odd_ref[2 * start + first:2 * start + last] = b0 - b2
        odd_ref[start + stop + first:start + stop + last] = b1 - b3

    lanes = table_ref.shape[2]
    piece = lanes // n_win

    def odd_spectra(k, m):
        start, stop = bounds[k]
        rows = stop - start
        both = product(odd_ref[2 * start:2 * stop], table_ref[m])
        second = both[rows:]
        back, forth = pltpu.roll(second, lanes - piece // 2, 1), pltpu.roll(second, piece // 2, 1)
        real = lax.broadcasted_iota(jnp.int32, (rows, lanes), 1) % piece < piece // 2
        turned = jnp.where(real, back, -forth)
        return both[:rows] + turned if m == 1 else both[:rows] - turned

    chunk(0).wait()
    add_quarters(0, 0, bounds[0][1])
    for k, (start, stop) in enumerate(bounds):
        rows = stop - start
        windows = cuts[k + 1] - cuts[k]
        more = k + 1 < len(bounds)
        if more:
            chunk(k + 1).wait()
        spectra = []
        for m in range(4):
            if m % 2:
                spectra.append(odd_spectra(k, m))
            else:
                spectra.append(product(even_ref[m // 2, start:stop], table_ref[m]))
            if more:
                ahead = cuts[k + 2] - cuts[k + 1]
                first, last = ahead * m // 4, ahead * (m + 1) // 4
                if first < last:
                    add_quarters(k + 1, first * r_dev, last * r_dev)
        squares = sum(jnp.sum(s * s, axis=1, keepdims=True) for s in spectra)
        gain = lax.rsqrt(squares / F + 1e-06)
        row = lax.broadcasted_iota(jnp.int32, (rows, 1), 0)
        keep = jnp.zeros((rows, 1), jnp.float32)
        for t in range(windows):
            own = (row >= t * r_dev) & (row < (t + 1) * r_dev)
            keep = jnp.where(own, valid_ref[cuts[k] + t].astype(jnp.float32), keep)
        gain = gain * keep
        white = [s * gain for s in spectra]
        for d in range(n_win):
            columns = slice(d * piece, (d + 1) * piece)
            block = jnp.concatenate([part[:, columns] for part in white], axis=1)
            white_ref[d, start:stop] = block.astype(jnp.bfloat16)
        select = sel_ref[:windows * per_window, :rows]
        for j in range(n_win):
            block = white_ref[win ^ j, start:stop]
            r_refs[j][start:stop, :] = block
            picked = product(select, block).astype(jnp.bfloat16)
            for t in range(windows):
                place = (cuts[k] + t) * n_own
                for d in range(n_rcv):
                    first = t * per_window + d * n_own
                    q_refs[d][j, place:place + n_own, :] = picked[first:first + n_own]


def spectra_call(traces, valid, src_station, n_win, n_rcv):
    w_dev, r_dev, samples = traces.shape
    n_src = src_station.shape[0]
    n_own = n_src // n_rcv
    cuts = (0, w_dev * 3 // 8, w_dev)
    largest = max(b - a for a, b in zip(cuts, cuts[1:]))
    every = w_dev * r_dev
    lanes = 2 * F // n_win
    seed, twice = (jnp.asarray(t) for t in table_seeds(samples, F, samples // 16, n_win))
    shapes = [jax.ShapeDtypeStruct((every, lanes), jnp.bfloat16)] * n_win
    shapes += [jax.ShapeDtypeStruct((n_win, w_dev * n_own, lanes), jnp.bfloat16)] * n_rcv
    shapes += [jax.ShapeDtypeStruct((8, 128), jnp.int32), jax.ShapeDtypeStruct((1,), jnp.int32)]
    vmem = pl.BlockSpec(memory_space=VMEM)
    out = pl.pallas_call(
        functools.partial(spectra_kernel, n_win, n_rcv, r_dev, cuts),
        in_specs=[pl.BlockSpec(memory_space=pltpu.HBM)] * 5,
        out_specs=[vmem] * (len(shapes) - 1) + [pl.BlockSpec(memory_space=SMEM)],
        out_shape=shapes,
        scratch_shapes=[
            pltpu.VMEM((every, samples), jnp.bfloat16),
            pltpu.VMEM((2, every, samples // 4), jnp.bfloat16),
            pltpu.VMEM((2 * every, samples // 4), jnp.bfloat16),
            pltpu.VMEM((n_win, every, lanes), jnp.bfloat16),
            pltpu.VMEM((n_src * largest, r_dev * largest), jnp.bfloat16),
            pltpu.VMEM((n_src, 128), jnp.float32),
            pltpu.VMEM((4, samples // 4, F // 2), jnp.bfloat16),
            pltpu.VMEM(seed.shape, jnp.float32),
            pltpu.VMEM(twice.shape, jnp.float32),
            pltpu.SMEM(valid.shape, jnp.int32),
            pltpu.SMEM(src_station.shape, jnp.int32),
            pltpu.SemaphoreType.DMA((4,)),
            pltpu.SemaphoreType.DMA((len(cuts) - 1,)),
        ],
        compiler_params=pltpu.CompilerParams(vmem_limit_bytes=36 * 2**20),
        cost_estimate=pl.CostEstimate(
            flops=2 * every * (samples // 4) * 6 * (F // 2), bytes_accessed=every * samples * 2,
            transcendentals=0,
        ),
        name="spectra",
    )(*(in_hbm(x) for x in (valid, src_station, traces.reshape(every, samples), seed, twice)))
    return out[:n_win], out[n_win:n_win + n_rcv], out[-2], out[-1]


def bin_order(lanes):
    quarter = lanes // 8
    lane = lax.broadcasted_iota(jnp.int32, (lanes, lanes), 1)
    row = lax.broadcasted_iota(jnp.int32, (lanes, lanes), 0)
    part = (lane // quarter) % 2
    bin_of = 4 * (lane % quarter) + lane // (2 * quarter)
    hit = row == part * (lanes // 2) + bin_of
    return hit.astype(jnp.float32).astype(jnp.bfloat16)


def turn_kernel(r_dev, *refs):
    x_refs, (out_ref, rows_ref) = refs[:-2], refs[-2:]
    lanes = x_refs[0].shape[1]
    bins = lanes // 2
    w_dev = out_ref.shape[1] // 2
    pad = out_ref.shape[2] // 2
    order = bin_order(lanes)
    windows = [(x, w) for x in x_refs for w in range(x.shape[0] // r_dev)]
    for k, (x_ref, w) in enumerate(windows):
        turned = lax.dot_general(
            order, x_ref[w * r_dev:(w + 1) * r_dev], (((1,), (1,)), ((), ())),
            preferred_element_type=jnp.float32,
        )
        rows_ref[pl.ds(k, lanes, stride=w_dev), :r_dev] = turned
    rr = rows_ref[:bins * w_dev].reshape(bins, w_dev, pad)
    ri = rows_ref[bins * w_dev:].reshape(bins, w_dev, pad)
    out_ref[:, :, :pad] = jnp.concatenate([rr, ri], axis=1).astype(jnp.bfloat16)
    out_ref[:, :, pad:] = jnp.concatenate([ri, -rr], axis=1).astype(jnp.bfloat16)


def turn_call(parts, w_dev, r_dev):
    lanes = parts[0].shape[1]
    pad = 128
    vmem = pl.BlockSpec(memory_space=VMEM)
    return pl.pallas_call(
        functools.partial(turn_kernel, r_dev),
        in_specs=[vmem] * len(parts),
        out_specs=vmem,
        out_shape=jax.ShapeDtypeStruct((lanes // 2, 2 * w_dev, 2 * pad), jnp.bfloat16),
        scratch_shapes=[pltpu.VMEM((lanes * w_dev, pad), jnp.float32)],
        compiler_params=pltpu.CompilerParams(vmem_limit_bytes=16 * 2**20),
        cost_estimate=pl.CostEstimate(
            flops=2 * w_dev * lanes * lanes * pad, bytes_accessed=2 * 2**20, transcendentals=0
        ),
        name="turn",
    )(*parts)


def merge_kernel(n_win, *refs):
    picked, outs = refs[:-n_win], refs[-n_win:]
    for j, out_ref in enumerate(outs):
        total = picked[0][j].astype(jnp.float32)
        for q_ref in picked[1:]:
            total = total + q_ref[j].astype(jnp.float32)
        out_ref[...] = total.astype(jnp.bfloat16)


def merge_call(*picked):
    n_win, rows, lanes = picked[0].shape
    vmem = pl.BlockSpec(memory_space=VMEM)
    return pl.pallas_call(
        functools.partial(merge_kernel, n_win),
        in_specs=[vmem] * len(picked),
        out_specs=[vmem] * n_win,
        out_shape=[jax.ShapeDtypeStruct((rows, lanes), jnp.bfloat16)] * n_win,
        compiler_params=pltpu.CompilerParams(vmem_limit_bytes=4 * 2**20),
        cost_estimate=pl.CostEstimate(flops=2**18, bytes_accessed=2**19, transcendentals=0),
        name="merge",
    )(*picked)


def lefts_kernel(n_win, w_dev, n_own, *refs):
    out_ref, srow_ref, rows_ref = refs[-3:]
    rows, lanes = refs[0].shape
    bins = lanes // 2
    windows = n_win * w_dev
    pad = rows_ref.shape[1]
    for j in range(n_win):
        block = refs[j][...].astype(jnp.float32)
        for h in range(lanes // pad):
            srow_ref[h, j * rows:(j + 1) * rows, :] = block[:, h * pad:(h + 1) * pad]

    lane = lax.broadcasted_iota(jnp.int32, (bins, lanes), 1)
    row = lax.broadcasted_iota(jnp.int32, (bins, lanes), 0)
    quarter = lanes // 8
    bin_of = 4 * (lane % quarter) + lane // (2 * quarter)
    pick = bin_of == 2 * (row % (bins // 2)) + row // (bins // 2)
    pick = pick.astype(jnp.float32).astype(jnp.bfloat16)
    real = (lane[:w_dev] // quarter) % 2 == 0
    low = lax.broadcasted_iota(jnp.int32, (bins // 2, pad), 1) < pad // 2
    for s in range(n_own):
        values = jnp.concatenate(
            [srow_ref[h, pl.ds(s, windows, stride=n_own), :] for h in range(lanes // pad)], axis=1
        )
        stacked = []
        for j in range(n_win):
            own = values[j * w_dev:(j + 1) * w_dev]
            stacked += [jnp.where(real, own, 0.0), jnp.where(real, 0.0, own)]
        stacked = jnp.concatenate(stacked * 2, axis=0).astype(jnp.bfloat16)
        turned = lax.dot_general(
            pick, stacked, (((1,), (1,)), ((), ())), preferred_element_type=jnp.float32
        )
        pairs = jnp.where(low, turned[:bins // 2], turned[bins // 2:])
        rows_ref[pl.ds(s, bins // 2, stride=n_own), :] = pairs
    out_ref[...] = rows_ref[...].reshape(out_ref.shape).astype(jnp.bfloat16)


def lefts_call(blocks, after, later, w_dev):
    rows, lanes = blocks[0].shape
    n_win = len(blocks)
    n_own = rows // w_dev
    pad = 128
    first = n_win + len(after)
    vmem, anywhere = pl.BlockSpec(memory_space=VMEM), pl.BlockSpec(memory_space=pl.ANY)
    out = pl.pallas_call(
        functools.partial(lefts_kernel, n_win, w_dev, n_own),
        in_specs=[vmem] * n_win + [anywhere] * (len(after) + len(later)),
        out_specs=[anywhere] * len(later) + [vmem],
        out_shape=[jax.ShapeDtypeStruct(x.shape, x.dtype) for x in later]
        + [jax.ShapeDtypeStruct((lanes // 8, 2 * n_own, pad), jnp.bfloat16)],
        input_output_aliases={first + k: k for k in range(len(later))},
        scratch_shapes=[
            pltpu.VMEM((lanes // pad, n_win * rows, pad), jnp.float32),
            pltpu.VMEM((lanes // 4 * n_own, pad), jnp.float32),
        ],
        compiler_params=pltpu.CompilerParams(vmem_limit_bytes=6 * 2**20),
        cost_estimate=pl.CostEstimate(flops=2**26, bytes_accessed=2**19, transcendentals=0),
        name="lefts",
    )(*blocks, *after, *later)
    return out[-1], out[:-1]


def gate_kernel(*refs):
    pass


def gate_call(after, arrays):
    anywhere = pl.BlockSpec(memory_space=pl.ANY)
    return pl.pallas_call(
        gate_kernel,
        in_specs=[anywhere] * (len(after) + len(arrays)),
        out_specs=[anywhere] * len(arrays),
        out_shape=[jax.ShapeDtypeStruct(x.shape, x.dtype) for x in arrays],
        input_output_aliases={len(after) + k: k for k in range(len(arrays))},
        compiler_params=pltpu.CompilerParams(vmem_limit_bytes=2**20),
        cost_estimate=pl.CostEstimate(flops=1, bytes_accessed=1, transcendentals=0),
        name="gate",
    )(*after, *arrays)


def stacks_kernel(shares, n_win, w_dev, r_dev, n_own, bins, plan_hbm, *refs):
    t_refs = refs[:n_win]
    s_refs = refs[n_win:n_win + len(shares)]
    out_hbm, prod_ref, out_ref, plan_ref, sems, plan_sem = refs[-6:]
    plan_copy = pltpu.make_async_copy(plan_hbm, plan_ref, plan_sem)
    plan_copy.start()
    windows = n_win * w_dev
    count = len(shares) * n_own
    pitch = prod_ref.shape[1] // bins
    pad = 128
    rcv = lax.axis_index("rcv")

    low = lax.broadcasted_iota(jnp.int32, (count, pad), 1) < pad // 2
    for group in range(bins // 4):
        values = [s_ref[group].astype(jnp.float32) for s_ref in s_refs]
        for p in range(2):
            rows = jnp.concatenate([v[p * n_own:(p + 1) * n_own] for v in values], axis=0)
            left = jnp.concatenate([jnp.where(low, rows, 0.0), jnp.where(low, 0.0, rows)], axis=0)
            first = 4 * group + 2 * p
            right = [t_ref[f] for f in (first, first + 1) for t_ref in t_refs]
            result = jnp.dot(
                left.astype(jnp.bfloat16), jnp.concatenate(right, axis=0),
                preferred_element_type=jnp.float32,
            )
            for k in range(2):
                for c in range(2):
                    block = result[k * count:(k + 1) * count, c * pad:(c + 1) * pad]
                    prod_ref[c, pl.ds((first + k) * pitch, count), :] = block

    scale = 1.0 / math.sqrt(windows)
    plan_copy.wait()
    copies = []
    for s in range(count):
        for c in range(2):
            turned = prod_ref[c, pl.ds(s, bins, stride=pitch), :].T
            out_ref[s, pl.ds(c, r_dev, stride=2), :] = turned[:r_dev] * scale
        row = plan_ref[0, (rcv ^ shares[s // n_own]) * n_own + s % n_own]
        copies.append(pltpu.make_async_copy(out_ref.at[s], out_hbm.at[row], sems.at[s]))
        copies[-1].start()
    for copy in copies:
        copy.wait()


def stacks_call(out, plan, turned, sources, shares, n_rcv, w_dev, r_dev, bins):
    n_win = len(turned)
    n_own = sources[0].shape[1] // 2
    windows = n_win * w_dev
    count = len(shares) * n_own
    whole = pl.BlockSpec(memory_space=VMEM)
    args = [plan] + list(turned) + [sources[i] for i in shares]
    specs = [pl.BlockSpec(memory_space=pl.ANY)] + [whole] * (len(args) - 1)
    aliases = {}
    if out is not None:
        aliases = {len(args): 0}
        args.append(out)
        specs.append(pl.BlockSpec(memory_space=pl.ANY))
    return pl.pallas_call(
        functools.partial(stacks_kernel, shares, n_win, w_dev, r_dev, n_own, bins),
        in_specs=specs,
        out_specs=pl.BlockSpec(memory_space=pltpu.HBM),
        out_shape=jax.ShapeDtypeStruct((n_rcv * n_own, 2 * r_dev, bins), jnp.float32),
        input_output_aliases=aliases,
        scratch_shapes=[
            pltpu.VMEM((2, (count // 8 | 1) * 8 * bins, 128), jnp.float32),
            pltpu.VMEM((count, 2 * r_dev, bins), jnp.float32),
            pltpu.SMEM(plan.shape, jnp.int32),
            pltpu.SemaphoreType.DMA((count,)),
            pltpu.SemaphoreType.DMA,
        ],
        compiler_params=pltpu.CompilerParams(vmem_limit_bytes=20 * 2**20),
        cost_estimate=pl.CostEstimate(
            flops=8 * windows * count * r_dev * bins, bytes_accessed=6 * 2**20, transcendentals=0
        ),
        name="stacks",
    )(*args)


def swap(value, axis, by):
    size = lax.axis_size(axis)
    return lax.ppermute(value, axis, [(i, i ^ by) for i in range(size)])


def near_and_far(n_rcv, by):
    pairs = [(z, z ^ by) for z in range(n_rcv)]
    return [p for p in pairs if abs(p[0] - p[1]) == 1], [p for p in pairs if abs(p[0] - p[1]) > 1]


def merge_near(picked, near):
    return merge_call(picked[0], *near)


def merge_all(picked, near):
    far = []
    for i in range(1, len(picked)):
        pairs = near_and_far(len(picked), i)[1]
        if pairs:
            far.append(lax.ppermute(picked[i], "rcv", pairs))
    return merge_call(picked[0], *near, *far)


def body(traces, valid, src_station):
    w_dev, r_dev, samples = traces.shape
    n_src = src_station.shape[0]
    n_win = lax.axis_size("win")
    n_rcv = lax.axis_size("rcv")
    bins = F // n_win
    early = n_win // 2

    blocks, picked, plan, flag = spectra_call(traces, valid, src_station, n_win, n_rcv)

    near = {}
    for i in range(1, n_rcv):
        pairs = near_and_far(n_rcv, i)[0]
        if pairs:
            near[i] = lax.ppermute(picked[i], "rcv", pairs)
    picked = [picked[0] + near.pop(n_rcv - 1)] + list(picked[1:])
    near = list(near.values())
    merged = lax.cond(flag.reshape(()) > 0, merge_all, merge_near, picked, near)

    merged = [merged[0]] + [swap(merged[j], "win", j) for j in range(1, n_win)]
    late = [j for j in range(1, n_win) if j != early]
    received = {0: blocks[0], early: swap(blocks[early], "win", early)}
    lefts, later = lefts_call(merged, [received[early]], [blocks[j] for j in late], w_dev)
    received.update({j: swap(block, "win", j) for j, block in zip(late, later)})
    sources = [lefts, swap(lefts, "rcv", 1), swap(lefts, "rcv", 2)]
    turned = [turn_call([received[j]], w_dev, r_dev) for j in range(n_win)]
    sources[2] = gate_call(turned[:-1], [sources[2]])[0]
    sources.append(swap(sources[2], "rcv", 1))

    sizes = (n_rcv, w_dev, r_dev, bins)
    stacks = stacks_call(None, plan, turned, sources, tuple(range(n_rcv - 1)), *sizes)
    stacks = stacks_call(stacks, plan, turned, sources, (n_rcv - 1,), *sizes)
    return stacks.reshape(n_src, r_dev, 2, bins)


def correlate(received, sources):
    rr = received[:, :, 0]
    ri = received[:, :, 1]
    sr = sources[:, :, 0]
    si = sources[:, :, 1]
    real = jnp.einsum("wsf,wrf->srf", sr, rr, preferred_element_type=jnp.float32)
    real = real + jnp.einsum("wsf,wrf->srf", si, ri, preferred_element_type=jnp.float32)
    imag = jnp.einsum("wsf,wrf->srf", sr, ri, preferred_element_type=jnp.float32)
    imag = imag - jnp.einsum("wsf,wrf->srf", si, rr, preferred_element_type=jnp.float32)
    return jnp.stack([real, imag], axis=2)


def body_any(traces, valid, src_station):
    w_dev, r_dev, samples = traces.shape
    n_win = lax.axis_size("win")
    n_rcv = lax.axis_size("rcv")
    bins = F // n_win
    table = jnp.asarray(band_table(samples, F, samples // 16))
    spectra = jnp.dot(
        traces.reshape(w_dev * r_dev, samples), table, preferred_element_type=jnp.float32
    )
    spectra = spectra.reshape(w_dev, r_dev, 2, F)
    power = jnp.sum(spectra * spectra, axis=(2, 3), keepdims=True) / F
    keep = valid.astype(jnp.float32)[:, None, None, None]
    white = (spectra * lax.rsqrt(power + 1e-06) * keep).astype(jnp.bfloat16)
    blocks = white.reshape(w_dev, r_dev, 2, n_win, bins).transpose(3, 0, 1, 2, 4)
    me = lax.axis_index("win")
    offset = lax.axis_index("rcv") * r_dev
    station_ids = offset + jnp.arange(r_dev, dtype=jnp.int32)
    selector = (src_station[:, None] == station_ids[None, :]).astype(jnp.bfloat16)
    received = []
    for j in range(n_win):
        block = lax.dynamic_index_in_dim(blocks, me ^ j, 0, keepdims=False)
        received.append(swap(block, "win", j) if j else block)
    received = jnp.concatenate(received, axis=0)
    rows = jnp.einsum("sr,wrcf->wscf", selector, received, preferred_element_type=jnp.float32)
    rows = lax.all_to_all(rows.astype(jnp.bfloat16), "rcv", 0, 0, tiled=True)
    rows = rows.reshape((n_rcv, -1) + rows.shape[1:])
    merged = jnp.sum(rows.astype(jnp.float32), axis=0).astype(jnp.bfloat16)
    sources = lax.all_gather(merged, "rcv", axis=0, tiled=True)
    return correlate(received, sources) * (1.0 / math.sqrt(w_dev * n_win))


def solution(mesh):
    sizes = (mesh.shape["win"], mesh.shape["rcv"])
    return jax.shard_map(
        body if sizes == (4, 4) else body_any,
        mesh=mesh,
        in_specs=(P("win", ("groups", "rcv"), None), P(("groups", "win")), P("groups")),
        out_specs=P(None, ("groups", "rcv"), None, "win"),
        check_vma=False,
    )
```

```python
import functools
import math

import jax
import jax.numpy as jnp
import numpy as np
from jax import lax
from jax.experimental import pallas as pl
from jax.experimental.pallas import tpu as pltpu
from jax.sharding import PartitionSpec as P

F = 512
SMEM = pltpu.MemorySpace.SMEM
VMEM = pltpu.MemorySpace.VMEM


def angles(samples, freqs, count):
    phase = samples[:, None] * freqs[None, :] % count
    return phase.astype(np.float64) * (2.0 * math.pi / count)


def band_table(count, bins, first):
    angle = angles(np.arange(count), first + np.arange(bins), count)
    return np.concatenate([np.cos(angle), -np.sin(angle)], axis=1).astype(jnp.bfloat16)


BLOCK = 32


def table_seeds(count, bins, first, n_win):
    j = np.arange(bins // 4)
    turn = np.array([0.0, 0.5 * math.pi]).reshape(1, 2, 1)
    seeds, twice = [], []
    for m in range(4):
        freqs = np.broadcast_to((first + 4 * j + m).reshape(n_win, 1, -1), (n_win, 2, j.size // n_win))
        angle = angles(np.arange(2 * BLOCK), freqs.reshape(-1), count)
        angle = angle + np.broadcast_to(turn, freqs.shape).reshape(1, -1)
        seeds.append(np.cos(angle).reshape(2, BLOCK, -1))
        step = angles(np.full(8, BLOCK), freqs.reshape(-1), count)
        twice.append(2.0 * np.cos(step))
    blocks = np.stack(seeds).reshape(4, 2 * BLOCK, -1)
    return np.concatenate([blocks, np.stack(twice)], axis=1).astype(np.float32)


def make_tables(seed_ref, table_ref):
    for first in (0, 2):
        state = {}
        for m in (first, first + 1):
            twice = jnp.concatenate([seed_ref[m, 2 * BLOCK:]] * (BLOCK // 8), axis=0)
            state[m] = (seed_ref[m, :BLOCK], seed_ref[m, BLOCK:2 * BLOCK], twice)
        for a in range(table_ref.shape[1] // BLOCK):
            for m, (here, after, twice) in state.items():
                table_ref[m, a * BLOCK:(a + 1) * BLOCK, :] = here.astype(jnp.bfloat16)
                state[m] = (after, twice * after - here, twice)


def in_hbm(value):
    return pltpu.with_memory_space_constraint(value, pltpu.HBM)


def order_sources(src_ref, r_dev, n_own, order_ref, plan_ref, flag_ref):
    n_src = src_ref.shape[0]
    size = order_ref.shape
    down = lax.broadcasted_iota(jnp.int32, size, 0).astype(jnp.float32)
    along = lax.broadcasted_iota(jnp.int32, size, 1).astype(jnp.float32)
    none = jnp.full(size, float(2**20), jnp.float32)
    column, row = none, none
    for s in range(n_src):
        station = src_ref[s].astype(jnp.float32)
        column = jnp.where(down == s, station, column)
        row = jnp.where(along == s, station, row)
    rank_along = jnp.sum((column < row).astype(jnp.float32), axis=0, keepdims=True)
    rank_down = jnp.sum((row < column).astype(jnp.float32), axis=1, keepdims=True)
    sorted_down = jnp.sum(jnp.where(rank_along == down, row, 0.0), axis=1, keepdims=True)
    at_place = rank_down == along
    sorted_along = jnp.sum(jnp.where(at_place, column, 0.0), axis=0, keepdims=True)
    source_along = jnp.sum(jnp.where(at_place, down, 0.0), axis=0, keepdims=True)
    order_ref[...] = jnp.broadcast_to(sorted_down, size)
    place = along[:1]
    owner, share = jnp.zeros_like(place), jnp.zeros_like(place)
    for z in range(1, n_src // n_own):
        owner = owner + (sorted_along >= z * r_dev).astype(jnp.float32)
        share = share + (place >= z * n_own).astype(jnp.float32)
    far = jnp.where((place < n_src) & (jnp.abs(owner - share) > 1.5), 1.0, 0.0)
    plan_ref[...] = jnp.broadcast_to(source_along, plan_ref.shape).astype(jnp.int32)
    flag_ref[0] = jnp.max(far).astype(jnp.int32)


def spectra_kernel(
    n_win, n_rcv, r_dev, valid_hbm, src_hbm, x_hbm, seed_hbm, *refs
):
    r_refs = refs[:n_win]
    q_refs = refs[n_win:n_win + n_rcv]
    (plan_ref, flag_ref, x_ref, even_ref, odd_ref, white_ref, sel_ref, order_ref, table_ref,
     seed_ref, valid_ref, src_ref, sems, x_sems) = refs[n_win + n_rcv:]
    chunks, rows, samples = x_ref.shape
    w_step = rows // r_dev
    n_own = src_ref.shape[0] // n_rcv
    quarter = samples // 4
    win = lax.axis_index("win")
    rcv = lax.axis_index("rcv")

    def small(k):
        source = (seed_hbm, src_hbm, valid_hbm)[k]
        target = (seed_ref, src_ref, valid_ref)[k]
        return pltpu.make_async_copy(source, target, sems.at[k])

    def chunk(k):
        return pltpu.make_async_copy(x_hbm.at[pl.ds(k * rows, rows)], x_ref.at[k], x_sems.at[k])

    for k in range(3):
        small(k).start()
    for k in range(chunks):
        chunk(k).start()
    small(0).wait()
    make_tables(seed_ref, table_ref)
    small(1).wait()
    order_sources(src_ref, r_dev, n_own, order_ref, plan_ref, flag_ref)
    stations = []
    for d in range(n_rcv):
        share = pl.multiple_of((rcv ^ d) * n_own, n_own)
        stations += [order_ref[pl.ds(share, n_own), 0:1]] * w_step
    wanted = jnp.concatenate(stations, axis=0).astype(jnp.int32) - rcv * r_dev
    shape = (n_rcv * w_step * n_own, rows)
    out_row = lax.broadcasted_iota(jnp.int32, shape, 0)
    column = lax.broadcasted_iota(jnp.int32, shape, 1)
    inside = (wanted >= 0) & (wanted < r_dev)
    hit = inside & (column == wanted + (out_row // n_own) % w_step * r_dev)
    sel_ref[...] = hit.astype(jnp.float32).astype(jnp.bfloat16)
    small(2).wait()

    def product(lhs, table):
        return jnp.dot(lhs, table, preferred_element_type=jnp.float32)

    def add_quarters(k, first, last):
        part = slice(first, last)
        b0, b1, b2, b3 = (x_ref[k, part, q * quarter:(q + 1) * quarter] for q in range(4))
        x0, x1, x2, x3 = (b.astype(jnp.float32) for b in (b0, b1, b2, b3))
        even_ref[k, 0, part] = ((x0 + x2) + (x1 + x3)).astype(jnp.bfloat16)
        even_ref[k, 1, part] = ((x0 + x2) - (x1 + x3)).astype(jnp.bfloat16)
        odd_ref[k, part] = b0 - b2
        odd_ref[k, rows + first:rows + last] = b1 - b3

    lanes = table_ref.shape[2]
    lane = lax.broadcasted_iota(jnp.int32, (rows, lanes), 1)
    piece = lanes // n_win
    real = lane % piece < piece // 2

    def odd_spectra(k, m):
        both = product(odd_ref[k], table_ref[m])
        second = both[rows:]
        back, forth = pltpu.roll(second, lanes - piece // 2, 1), pltpu.roll(second, piece // 2, 1)
        turned = jnp.where(real, back, -forth)
        return both[:rows] + turned if m == 1 else both[:rows] - turned

    parts = 4
    size = rows // parts
    chunk(0).wait()
    add_quarters(0, 0, rows)
    row = lax.broadcasted_iota(jnp.int32, (rows, 1), 0)
    for k in range(chunks):
        more = k + 1 < chunks
        if more:
            chunk(k + 1).wait()
        spectra = []
        for m in range(4):
            if m % 2:
                spectra.append(odd_spectra(k, m))
            else:
                spectra.append(product(even_ref[k, m // 2], table_ref[m]))
            if more:
                add_quarters(k + 1, m * size, (m + 1) * size)
        squares = sum(jnp.sum(s * s, axis=1, keepdims=True) for s in spectra)
        gain = lax.rsqrt(squares / F + 1e-06)
        keep = jnp.zeros((rows, 1), jnp.float32)
        for t in range(w_step):
            own = (row >= t * r_dev) & (row < (t + 1) * r_dev)
            keep = jnp.where(own, valid_ref[k * w_step + t].astype(jnp.float32), keep)
        gain = gain * keep
        white = [s * gain for s in spectra]
        for d in range(n_win):
            columns = slice(d * piece, (d + 1) * piece)
            block = jnp.concatenate([part[:, columns] for part in white], axis=1)
            white_ref[k, d] = block.astype(jnp.bfloat16)
        count = w_step * n_own
        for j in range(n_win):
            block = white_ref[k, win ^ j]
            r_refs[j][k * rows:(k + 1) * rows, :] = block
            picked = product(sel_ref[...], block).astype(jnp.bfloat16)
            for d in range(n_rcv):
                q_refs[d][j, k * count:(k + 1) * count, :] = picked[d * count:(d + 1) * count]


def spectra_call(traces, valid, src_station, n_win, n_rcv):
    w_dev, r_dev, samples = traces.shape
    n_src = src_station.shape[0]
    n_own = n_src // n_rcv
    chunks = 2
    every = w_dev * r_dev
    rows = every // chunks
    lanes = 2 * F // n_win
    seed = jnp.asarray(table_seeds(samples, F, samples // 16, n_win))
    shapes = [jax.ShapeDtypeStruct((every, lanes), jnp.bfloat16)] * n_win
    shapes += [jax.ShapeDtypeStruct((n_win, w_dev * n_own, lanes), jnp.bfloat16)] * n_rcv
    shapes += [jax.ShapeDtypeStruct((8, 128), jnp.int32), jax.ShapeDtypeStruct((1,), jnp.int32)]
    vmem = pl.BlockSpec(memory_space=VMEM)
    out = pl.pallas_call(
        functools.partial(spectra_kernel, n_win, n_rcv, r_dev),
        in_specs=[pl.BlockSpec(memory_space=pltpu.HBM)] * 4,
        out_specs=[vmem] * (len(shapes) - 1) + [pl.BlockSpec(memory_space=SMEM)],
        out_shape=shapes,
        scratch_shapes=[
            pltpu.VMEM((chunks, rows, samples), jnp.bfloat16),
            pltpu.VMEM((chunks, 2, rows, samples // 4), jnp.bfloat16),
            pltpu.VMEM((chunks, 2 * rows, samples // 4), jnp.bfloat16),
            pltpu.VMEM((chunks, n_win, rows, lanes), jnp.bfloat16),
            pltpu.VMEM((n_src * (w_dev // chunks), rows), jnp.bfloat16),
            pltpu.VMEM((n_src, 128), jnp.float32),
            pltpu.VMEM((4, samples // 4, F // 2), jnp.bfloat16),
            pltpu.VMEM(seed.shape, jnp.float32),
            pltpu.SMEM(valid.shape, jnp.int32),
            pltpu.SMEM(src_station.shape, jnp.int32),
            pltpu.SemaphoreType.DMA((3,)),
            pltpu.SemaphoreType.DMA((chunks,)),
        ],
        compiler_params=pltpu.CompilerParams(vmem_limit_bytes=36 * 2**20),
        cost_estimate=pl.CostEstimate(
            flops=2 * every * (samples // 4) * 6 * (F // 2), bytes_accessed=every * samples * 2,
            transcendentals=0,
        ),
        name="spectra",
    )(*(in_hbm(x) for x in (valid, src_station, traces.reshape(every, samples), seed)))
    return out[:n_win], out[n_win:n_win + n_rcv], out[-2], out[-1]


def bin_order(lanes):
    quarter = lanes // 8
    lane = lax.broadcasted_iota(jnp.int32, (lanes, lanes), 1)
    row = lax.broadcasted_iota(jnp.int32, (lanes, lanes), 0)
    part = (lane // quarter) % 2
    bin_of = 4 * (lane % quarter) + lane // (2 * quarter)
    hit = row == part * (lanes // 2) + bin_of
    return hit.astype(jnp.float32).astype(jnp.bfloat16)


def turn_kernel(r_dev, *refs):
    x_refs, (out_ref, rows_ref) = refs[:-2], refs[-2:]
    lanes = x_refs[0].shape[1]
    bins = lanes // 2
    w_dev = out_ref.shape[1] // 2
    pad = out_ref.shape[2] // 2
    order = bin_order(lanes)
    windows = [(x, w) for x in x_refs for w in range(x.shape[0] // r_dev)]
    for k, (x_ref, w) in enumerate(windows):
        turned = lax.dot_general(
            order, x_ref[w * r_dev:(w + 1) * r_dev], (((1,), (1,)), ((), ())),
            preferred_element_type=jnp.float32,
        )
        rows_ref[pl.ds(k, lanes, stride=w_dev), :r_dev] = turned
    rr = rows_ref[:bins * w_dev].reshape(bins, w_dev, pad)
    ri = rows_ref[bins * w_dev:].reshape(bins, w_dev, pad)
    out_ref[:, :, :pad] = jnp.concatenate([rr, ri], axis=1).astype(jnp.bfloat16)
    out_ref[:, :, pad:] = jnp.concatenate([ri, -rr], axis=1).astype(jnp.bfloat16)


def turn_call(parts, w_dev, r_dev):
    lanes = parts[0].shape[1]
    pad = 128
    vmem = pl.BlockSpec(memory_space=VMEM)
    return pl.pallas_call(
        functools.partial(turn_kernel, r_dev),
        in_specs=[vmem] * len(parts),
        out_specs=vmem,
        out_shape=jax.ShapeDtypeStruct((lanes // 2, 2 * w_dev, 2 * pad), jnp.bfloat16),
        scratch_shapes=[pltpu.VMEM((lanes * w_dev, pad), jnp.float32)],
        compiler_params=pltpu.CompilerParams(vmem_limit_bytes=16 * 2**20),
        cost_estimate=pl.CostEstimate(
            flops=2 * w_dev * lanes * lanes * pad, bytes_accessed=2 * 2**20, transcendentals=0
        ),
        name="turn",
    )(*parts)


def merge_kernel(n_win, *refs):
    picked, outs = refs[:-n_win], refs[-n_win:]
    for j, out_ref in enumerate(outs):
        total = picked[0][j].astype(jnp.float32)
        for q_ref in picked[1:]:
            total = total + q_ref[j].astype(jnp.float32)
        out_ref[...] = total.astype(jnp.bfloat16)


def merge_call(*picked):
    n_win, rows, lanes = picked[0].shape
    vmem = pl.BlockSpec(memory_space=VMEM)
    return pl.pallas_call(
        functools.partial(merge_kernel, n_win),
        in_specs=[vmem] * len(picked),
        out_specs=[vmem] * n_win,
        out_shape=[jax.ShapeDtypeStruct((rows, lanes), jnp.bfloat16)] * n_win,
        compiler_params=pltpu.CompilerParams(vmem_limit_bytes=4 * 2**20),
        cost_estimate=pl.CostEstimate(flops=2**18, bytes_accessed=2**19, transcendentals=0),
        name="merge",
    )(*picked)


def lefts_kernel(n_win, w_dev, n_own, *refs):
    out_ref, srow_ref, rows_ref = refs[-3:]
    rows, lanes = refs[0].shape
    bins = lanes // 2
    windows = n_win * w_dev
    pad = rows_ref.shape[1]
    for j in range(n_win):
        block = refs[j][...].astype(jnp.float32)
        for h in range(lanes // pad):
            srow_ref[h, j * rows:(j + 1) * rows, :] = block[:, h * pad:(h + 1) * pad]

    lane = lax.broadcasted_iota(jnp.int32, (bins, lanes), 1)
    row = lax.broadcasted_iota(jnp.int32, (bins, lanes), 0)
    quarter = lanes // 8
    bin_of = 4 * (lane % quarter) + lane // (2 * quarter)
    pick = bin_of == 2 * (row % (bins // 2)) + row // (bins // 2)
    pick = pick.astype(jnp.float32).astype(jnp.bfloat16)
    real = (lane[:w_dev] // quarter) % 2 == 0
    low = lax.broadcasted_iota(jnp.int32, (bins // 2, pad), 1) < pad // 2
    for s in range(n_own):
        values = jnp.concatenate(
            [srow_ref[h, pl.ds(s, windows, stride=n_own), :] for h in range(lanes // pad)], axis=1
        )
        stacked = []
        for j in range(n_win):
            own = values[j * w_dev:(j + 1) * w_dev]
            stacked += [jnp.where(real, own, 0.0), jnp.where(real, 0.0, own)]
        stacked = jnp.concatenate(stacked * 2, axis=0).astype(jnp.bfloat16)
        turned = lax.dot_general(
            pick, stacked, (((1,), (1,)), ((), ())), preferred_element_type=jnp.float32
        )
        pairs = jnp.where(low, turned[:bins // 2], turned[bins // 2:])
        rows_ref[pl.ds(s, bins // 2, stride=n_own), :] = pairs
    out_ref[...] = rows_ref[...].reshape(out_ref.shape).astype(jnp.bfloat16)


def lefts_call(blocks, after, later, w_dev):
    rows, lanes = blocks[0].shape
    n_win = len(blocks)
    n_own = rows // w_dev
    pad = 128
    first = n_win + len(after)
    vmem, anywhere = pl.BlockSpec(memory_space=VMEM), pl.BlockSpec(memory_space=pl.ANY)
    out = pl.pallas_call(
        functools.partial(lefts_kernel, n_win, w_dev, n_own),
        in_specs=[vmem] * n_win + [anywhere] * (len(after) + len(later)),
        out_specs=[anywhere] * len(later) + [vmem],
        out_shape=[jax.ShapeDtypeStruct(x.shape, x.dtype) for x in later]
        + [jax.ShapeDtypeStruct((lanes // 8, 2 * n_own, pad), jnp.bfloat16)],
        input_output_aliases={first + k: k for k in range(len(later))},
        scratch_shapes=[
            pltpu.VMEM((lanes // pad, n_win * rows, pad), jnp.float32),
            pltpu.VMEM((lanes // 4 * n_own, pad), jnp.float32),
        ],
        compiler_params=pltpu.CompilerParams(vmem_limit_bytes=6 * 2**20),
        cost_estimate=pl.CostEstimate(flops=2**26, bytes_accessed=2**19, transcendentals=0),
        name="lefts",
    )(*blocks, *after, *later)
    return out[-1], out[:-1]


def gate_kernel(*refs):
    pass


def gate_call(after, arrays):
    anywhere = pl.BlockSpec(memory_space=pl.ANY)
    return pl.pallas_call(
        gate_kernel,
        in_specs=[anywhere] * (len(after) + len(arrays)),
        out_specs=[anywhere] * len(arrays),
        out_shape=[jax.ShapeDtypeStruct(x.shape, x.dtype) for x in arrays],
        input_output_aliases={len(after) + k: k for k in range(len(arrays))},
        compiler_params=pltpu.CompilerParams(vmem_limit_bytes=2**20),
        cost_estimate=pl.CostEstimate(flops=1, bytes_accessed=1, transcendentals=0),
        name="gate",
    )(*after, *arrays)


def stacks_kernel(shares, n_win, w_dev, r_dev, n_own, bins, plan_hbm, *refs):
    t_refs = refs[:n_win]
    s_refs = refs[n_win:n_win + len(shares)]
    out_hbm, prod_ref, out_ref, plan_ref, sem, plan_sem = refs[-6:]
    plan_copy = pltpu.make_async_copy(plan_hbm, plan_ref, plan_sem)
    plan_copy.start()
    windows = n_win * w_dev
    count = len(shares) * n_own
    pitch = prod_ref.shape[1] // bins
    pad = 128
    rcv = lax.axis_index("rcv")

    low = lax.broadcasted_iota(jnp.int32, (count, pad), 1) < pad // 2
    for group in range(bins // 4):
        values = [s_ref[group].astype(jnp.float32) for s_ref in s_refs]
        for p in range(2):
            rows = jnp.concatenate([v[p * n_own:(p + 1) * n_own] for v in values], axis=0)
            left = jnp.concatenate([jnp.where(low, rows, 0.0), jnp.where(low, 0.0, rows)], axis=0)
            first = 4 * group + 2 * p
            right = [t_ref[f] for f in (first, first + 1) for t_ref in t_refs]
            result = jnp.dot(
                left.astype(jnp.bfloat16), jnp.concatenate(right, axis=0),
                preferred_element_type=jnp.float32,
            )
            for k in range(2):
                for c in range(2):
                    block = result[k * count:(k + 1) * count, c * pad:(c + 1) * pad]
                    prod_ref[c, pl.ds((first + k) * pitch, count), :] = block

    scale = 1.0 / math.sqrt(windows)
    plan_copy.wait()
    for s in range(count):
        for c in range(2):
            turned = prod_ref[c, pl.ds(s, bins, stride=pitch), :].T
            out_ref[s, pl.ds(c, r_dev, stride=2), :] = turned[:r_dev] * scale
        row = plan_ref[0, (rcv ^ shares[s // n_own]) * n_own + s % n_own]
        pltpu.make_async_copy(out_ref.at[s], out_hbm.at[row], sem).start()
    pltpu.make_async_copy(out_ref, out_hbm.at[pl.ds(0, count)], sem).wait()


def stacks_call(out, plan, turned, sources, shares, n_rcv, w_dev, r_dev, bins):
    n_win = len(turned)
    n_own = sources[0].shape[1] // 2
    windows = n_win * w_dev
    count = len(shares) * n_own
    whole = pl.BlockSpec(memory_space=VMEM)
    args = [plan] + list(turned) + [sources[i] for i in shares]
    specs = [pl.BlockSpec(memory_space=pl.ANY)] + [whole] * (len(args) - 1)
    aliases = {}
    if out is not None:
        aliases = {len(args): 0}
        args.append(out)
        specs.append(pl.BlockSpec(memory_space=pl.ANY))
    return pl.pallas_call(
        functools.partial(stacks_kernel, shares, n_win, w_dev, r_dev, n_own, bins),
        in_specs=specs,
        out_specs=pl.BlockSpec(memory_space=pltpu.HBM),
        out_shape=jax.ShapeDtypeStruct((n_rcv * n_own, 2 * r_dev, bins), jnp.float32),
        input_output_aliases=aliases,
        scratch_shapes=[
            pltpu.VMEM((2, (count // 8 | 1) * 8 * bins, 128), jnp.float32),
            pltpu.VMEM((count, 2 * r_dev, bins), jnp.float32),
            pltpu.SMEM(plan.shape, jnp.int32),
            pltpu.SemaphoreType.DMA,
            pltpu.SemaphoreType.DMA,
        ],
        compiler_params=pltpu.CompilerParams(vmem_limit_bytes=20 * 2**20),
        cost_estimate=pl.CostEstimate(
            flops=8 * windows * count * r_dev * bins, bytes_accessed=6 * 2**20, transcendentals=0
        ),
        name="stacks",
    )(*args)


def swap(value, axis, by):
    size = lax.axis_size(axis)
    return lax.ppermute(value, axis, [(i, i ^ by) for i in range(size)])


def near_and_far(n_rcv, by):
    pairs = [(z, z ^ by) for z in range(n_rcv)]
    return [p for p in pairs if abs(p[0] - p[1]) == 1], [p for p in pairs if abs(p[0] - p[1]) > 1]


def merge_near(picked, near):
    return merge_call(picked[0], *near)


def merge_all(picked, near):
    far = []
    for i in range(1, len(picked)):
        pairs = near_and_far(len(picked), i)[1]
        if pairs:
            far.append(lax.ppermute(picked[i], "rcv", pairs))
    return merge_call(picked[0], *near, *far)


def body(traces, valid, src_station):
    w_dev, r_dev, samples = traces.shape
    n_src = src_station.shape[0]
    n_win = lax.axis_size("win")
    n_rcv = lax.axis_size("rcv")
    bins = F // n_win
    early = n_win // 2

    blocks, picked, plan, flag = spectra_call(traces, valid, src_station, n_win, n_rcv)

    near = {}
    for i in range(1, n_rcv):
        pairs = near_and_far(n_rcv, i)[0]
        if pairs:
            near[i] = lax.ppermute(picked[i], "rcv", pairs)
    picked = [picked[0] + near.pop(n_rcv - 1)] + list(picked[1:])
    near = list(near.values())
    merged = lax.cond(flag.reshape(()) > 0, merge_all, merge_near, picked, near)

    merged = [merged[0]] + [swap(merged[j], "win", j) for j in range(1, n_win)]
    late = [j for j in range(1, n_win) if j != early]
    received = {0: blocks[0], early: swap(blocks[early], "win", early)}
    lefts, later = lefts_call(merged, [received[early]], [blocks[j] for j in late], w_dev)
    received.update({j: swap(block, "win", j) for j, block in zip(late, later)})
    sources = [lefts, swap(lefts, "rcv", 1), swap(lefts, "rcv", 2)]
    turned = [turn_call([received[j]], w_dev, r_dev) for j in range(n_win)]
    sources[2] = gate_call(turned[:-1], [sources[2]])[0]
    sources.append(swap(sources[2], "rcv", 1))

    sizes = (n_rcv, w_dev, r_dev, bins)
    stacks = stacks_call(None, plan, turned, sources, tuple(range(n_rcv - 1)), *sizes)
    stacks = stacks_call(stacks, plan, turned, sources, (n_rcv - 1,), *sizes)
    return stacks.reshape(n_src, r_dev, 2, bins)


def correlate(received, sources):
    rr = received[:, :, 0]
    ri = received[:, :, 1]
    sr = sources[:, :, 0]
    si = sources[:, :, 1]
    real = jnp.einsum("wsf,wrf->srf", sr, rr, preferred_element_type=jnp.float32)
    real = real + jnp.einsum("wsf,wrf->srf", si, ri, preferred_element_type=jnp.float32)
    imag = jnp.einsum("wsf,wrf->srf", sr, ri, preferred_element_type=jnp.float32)
    imag = imag - jnp.einsum("wsf,wrf->srf", si, rr, preferred_element_type=jnp.float32)
    return jnp.stack([real, imag], axis=2)


def body_any(traces, valid, src_station):
    w_dev, r_dev, samples = traces.shape
    n_win = lax.axis_size("win")
    n_rcv = lax.axis_size("rcv")
    bins = F // n_win
    table = jnp.asarray(band_table(samples, F, samples // 16))
    spectra = jnp.dot(
        traces.reshape(w_dev * r_dev, samples), table, preferred_element_type=jnp.float32
    )
    spectra = spectra.reshape(w_dev, r_dev, 2, F)
    power = jnp.sum(spectra * spectra, axis=(2, 3), keepdims=True) / F
    keep = valid.astype(jnp.float32)[:, None, None, None]
    white = (spectra * lax.rsqrt(power + 1e-06) * keep).astype(jnp.bfloat16)
    blocks = white.reshape(w_dev, r_dev, 2, n_win, bins).transpose(3, 0, 1, 2, 4)
    me = lax.axis_index("win")
    offset = lax.axis_index("rcv") * r_dev
    station_ids = offset + jnp.arange(r_dev, dtype=jnp.int32)
    selector = (src_station[:, None] == station_ids[None, :]).astype(jnp.bfloat16)
    received = []
    for j in range(n_win):
        block = lax.dynamic_index_in_dim(blocks, me ^ j, 0, keepdims=False)
        received.append(swap(block, "win", j) if j else block)
    received = jnp.concatenate(received, axis=0)
    rows = jnp.einsum("sr,wrcf->wscf", selector, received, preferred_element_type=jnp.float32)
    rows = lax.all_to_all(rows.astype(jnp.bfloat16), "rcv", 0, 0, tiled=True)
    rows = rows.reshape((n_rcv, -1) + rows.shape[1:])
    merged = jnp.sum(rows.astype(jnp.float32), axis=0).astype(jnp.bfloat16)
    sources = lax.all_gather(merged, "rcv", axis=0, tiled=True)
    return correlate(received, sources) * (1.0 / math.sqrt(w_dev * n_win))


def solution(mesh):
    sizes = (mesh.shape["win"], mesh.shape["rcv"])
    return jax.shard_map(
        body if sizes == (4, 4) else body_any,
        mesh=mesh,
        in_specs=(P("win", ("groups", "rcv"), None), P(("groups", "win")), P("groups")),
        out_specs=P(None, ("groups", "rcv"), None, "win"),
        check_vma=False,
    )
```
